32 devices in a mesh: grp: 2 (over y), row: 8 (over z, x), col: 2 (over core).
Axes of the slice: x: 2, y: 2, z: 4, core: 2. Of those that a mesh axis runs over, the one named last changes fastest.
Arguments:
- activations: bfloat16 [8192, 8192], P(('grp', 'row'), 'col'), parts along dimension 0, may hold values from -2 to 2, as said below
- start_sketch: bfloat16 [8192, 128], P(('grp', 'row')), parts along dimension 0, may hold values from -4 to 4, as said below
Outputs:
- basis: float32 [8192, 128], P(('grp', 'row')), parts along dimension 0
- projection: float32 [256, 8192], P(('grp', 'row'), 'col'), parts along dimension 0
The draws below stay inside these ranges and needn't reach their ends.
There are 2 independent parts, one for each index of `grp`. The reference program is written for one: setup_inputs(seed, part) draws one part's arguments, and reference() takes and returns one part's arrays. A program takes and returns all parts, laid end to end along the dimension named above; each array names one. Nothing has to cross between parts.
Inputs may be any that keep to these rules, and one draw needn't show every extreme that they name: Real-valued activations with row and column scales that vary. `start_sketch`: Real-valued entries of order one.
All inputs are finite; a program needn't handle non-finite values.
Results may differ from the reference program's by a relative error of at most 0.0027.
Values may be sent and summed in bfloat16 or wider, within the bound.
No kernel may reach another device: no remote copies, remote signals or barrier semaphores. Data moves between devices by JAX's collectives and lax.ppermute only.
A program may use at most 64 MiB of HBM per device.

```python
import math
import jax
import jax.numpy as jnp
from jax import lax

COLS = 8192
SKETCH = 128
ROWS = 4096


def draw_activations(key, part):
    key = jax.random.fold_in(key, 11)
    key_rows, key_cols, key_base = jax.random.split(key, 3)
    row_scale = jnp.exp(jax.random.uniform(key_rows, (ROWS, 1), jnp.float32) * math.log(2.0))
    col_scale = jnp.exp(jax.random.uniform(key_cols, (1, COLS), jnp.float32) * math.log(2.0))
    base = jnp.clip(jax.random.normal(key_base, (ROWS, COLS), jnp.float32), -4.0, 4.0)
    return (0.1 * base * row_scale * col_scale).astype(jnp.bfloat16)


def draw_start_sketch(key, part):
    key = jax.random.fold_in(key, 23)
    values = jnp.clip(jax.random.normal(key, (ROWS, SKETCH), jnp.float32), -4.0, 4.0)
    return values.astype(jnp.bfloat16)


def setup_inputs(seed: int = 0, part: int = 0) -> dict:
    arg_keys = jax.random.split(jax.random.key(seed), 3)
    own_keys = jax.random.split(jax.random.fold_in(arg_keys[2], part), 3)
    activations = draw_activations(jax.random.fold_in(jax.random.fold_in(arg_keys[2], part), 71), part)
    start_sketch = draw_start_sketch(jax.random.fold_in(jax.random.fold_in(arg_keys[2], part), 71), part)
    return dict(activations=activations, start_sketch=start_sketch)


def reference(activations, start_sketch):
    root_rows = math.sqrt(ROWS)
    sketch_cols = (lax.dot_general(activations.astype(jnp.float32), start_sketch.astype(jnp.float32), (((0,), (0,)), ((), ())), preferred_element_type=jnp.float32) / root_rows).astype(jnp.bfloat16)
    sketch = jnp.dot(activations.astype(jnp.float32), sketch_cols.astype(jnp.float32), preferred_element_type=jnp.float32) / COLS
    gram = lax.dot_general(sketch, sketch, (((0,), (0,)), ((), ())), precision=lax.Precision.HIGHEST)
    factor = jnp.linalg.cholesky(gram)
    solved = jax.scipy.linalg.solve_triangular(factor, sketch.T, lower=True)
    basis = solved.T * root_rows
    basis_low = basis.astype(jnp.bfloat16)
    projection = lax.dot_general(basis_low.astype(jnp.float32), activations.astype(jnp.float32), (((0,), (0,)), ((), ())), preferred_element_type=jnp.float32) / ROWS
    return (basis, projection)
```

```python
import math

import jax
import jax.numpy as jnp
from jax import lax
from jax.sharding import PartitionSpec as P


def exchange_sum(value, axis):
    size = lax.axis_size(axis)
    step = 1
    while step < size:
        pairs = [(i, i ^ step) for i in range(size)]
        value = value + lax.ppermute(value, axis, pairs)
        step *= 2
    return value


def scatter_sum(blocks, axis):
    landed = lax.all_to_all(blocks.astype(jnp.bfloat16), axis, 0, 0, tiled=True)
    return jnp.sum(landed.astype(jnp.float32), axis=0)


def gather(block, axis):
    copies = jnp.broadcast_to(block[None], (lax.axis_size(axis),) + block.shape)
    return lax.all_to_all(copies, axis, 0, 0, tiled=True)


def per_device(activations, start_sketch):
    rows_here, cols_here = activations.shape
    width = start_sketch.shape[1]
    parts = lax.axis_size("row")
    total_rows = rows_here * parts
    total_cols = cols_here * lax.axis_size("col")
    root_rows = math.sqrt(total_rows)

    local_cols = lax.dot_general(
        activations, start_sketch, (((0,), (0,)), ((), ())), preferred_element_type=jnp.float32
    )
    share = scatter_sum(local_cols.reshape(parts, cols_here // parts, width), "row")
    sketch_cols = gather((share / root_rows).astype(jnp.bfloat16), "row").reshape(cols_here, width)

    partial_sketch = jnp.dot(activations, sketch_cols, preferred_element_type=jnp.float32)
    sketch = exchange_sum(partial_sketch, "col") / total_cols

    local_gram = lax.dot_general(
        sketch, sketch, (((0,), (0,)), ((), ())), precision=lax.Precision.HIGHEST
    )
    gram = exchange_sum(local_gram, "row")
    factor = jnp.linalg.cholesky(gram)
    solved = jax.scipy.linalg.solve_triangular(factor, sketch.T, lower=True)
    basis = solved.T * root_rows

    high = basis.astype(jnp.bfloat16)
    low = (basis - high.astype(jnp.float32)).astype(jnp.bfloat16)
    pair = jnp.concatenate([high, low], axis=1)
    local_pair = lax.dot_general(
        pair, activations, (((0,), (0,)), ((), ())), preferred_element_type=jnp.float32
    )
    local_proj = local_pair[:width] + local_pair[width:]
    projection = (
        scatter_sum(local_proj.reshape(parts, width // parts, cols_here), "row") / total_rows
    )
    return (basis, projection)


def solution(mesh):
    return jax.shard_map(
        per_device,
        mesh=mesh,
        in_specs=(P(("grp", "row"), "col"), P(("grp", "row"), None)),
        out_specs=(P(("grp", "row"), None), P(("grp", "row"), "col")),
        check_vma=False,
    )
```

```python
import math

import jax
import jax.numpy as jnp
from jax import lax
from jax.sharding import PartitionSpec as P

CHUNKS = 2


def levels_of(size):
    levels, stride = [], 1
    while stride < size:
        radix = 2 if stride == 1 else min(4, size // stride)
        levels.append((stride, radix))
        stride *= radix
    return levels


def swap(value, axis, distance):
    size = lax.axis_size(axis)
    return lax.ppermute(value, axis, [(i, i ^ distance) for i in range(size)])


def exchange_sum(value, axis):
    step = 1
    while step < lax.axis_size(axis):
        value = value + swap(value, axis, step)
        step *= 2
    return value


def digit_of(axis, stride, radix):
    return lax.rem(lax.div(lax.axis_index(axis), stride), radix)


def scatter_level(blocks, axis, stride, radix):
    digit = digit_of(axis, stride, radix)
    view = blocks.reshape((blocks.shape[0] // radix, radix) + blocks.shape[1:])
    total = lax.dynamic_index_in_dim(view, digit, 1, keepdims=False)
    for t in range(1, radix):
        part = lax.dynamic_index_in_dim(view, jnp.bitwise_xor(digit, t), 1, keepdims=False)
        landed = swap(part.astype(jnp.bfloat16), axis, t * stride)
        total = total + landed.astype(jnp.float32)
    return total


def scatter_sum(blocks, axis):
    for stride, radix in levels_of(lax.axis_size(axis)):
        blocks = scatter_level(blocks, axis, stride, radix)
    return blocks[0]


def gather_level(blocks, axis, stride, radix):
    digit = digit_of(axis, stride, radix)
    held = [blocks] + [swap(blocks, axis, t * stride) for t in range(1, radix)]
    bit = 1
    while bit < radix:
        flip = jnp.bitwise_and(digit, bit) != 0
        held = [jnp.where(flip, held[j ^ bit], held[j]) for j in range(radix)]
        bit *= 2
    whole = jnp.stack(held, axis=1)
    return whole.reshape((blocks.shape[0] * radix,) + blocks.shape[1:])


def gather(block, axis):
    blocks = block[None]
    for stride, radix in reversed(levels_of(lax.axis_size(axis))):
        blocks = gather_level(blocks, axis, stride, radix)
    return blocks


def per_device(activations, start_sketch):
    rows_here, cols_here = activations.shape
    width = start_sketch.shape[1]
    parts = lax.axis_size("row")
    total_rows = rows_here * parts
    total_cols = cols_here * lax.axis_size("col")
    root_rows = math.sqrt(total_rows)

    cols_chunk = cols_here // CHUNKS
    spans = [slice(c * cols_chunk, (c + 1) * cols_chunk) for c in range(CHUNKS)]

    partial_sketch = 0.0
    for span in spans:
        local_cols = lax.dot_general(
            activations[:, span],
            start_sketch,
            (((0,), (0,)), ((), ())),
            preferred_element_type=jnp.float32,
        )
        share = scatter_sum(local_cols.reshape(parts, cols_chunk // parts, width), "row")
        chunk = gather((share / root_rows).astype(jnp.bfloat16), "row")
        partial_sketch = partial_sketch + jnp.dot(
            activations[:, span],
            chunk.reshape(cols_chunk, width),
            preferred_element_type=jnp.float32,
        )
    sketch = exchange_sum(partial_sketch, "col") / total_cols

    local_gram = lax.dot_general(
        sketch, sketch, (((0,), (0,)), ((), ())), precision=lax.Precision.HIGHEST
    )
    gram = exchange_sum(local_gram, "row")
    factor = jnp.linalg.cholesky(gram)
    solved = jax.scipy.linalg.solve_triangular(factor, sketch.T, lower=True)
    basis = solved.T * root_rows

    high = basis.astype(jnp.bfloat16)
    low = (basis - high.astype(jnp.float32)).astype(jnp.bfloat16)
    pair = jnp.concatenate([high, low], axis=1)
    pieces = []
    for span in spans:
        local_pair = lax.dot_general(
            pair, activations[:, span], (((0,), (0,)), ((), ())), preferred_element_type=jnp.float32
        )
        local_proj = local_pair[:width] + local_pair[width:]
        pieces.append(
            scatter_sum(local_proj.reshape(parts, width // parts, cols_chunk), "row") / total_rows
        )
    return (basis, jnp.concatenate(pieces, axis=1))


def solution(mesh):
    return jax.shard_map(
        per_device,
        mesh=mesh,
        in_specs=(P(("grp", "row"), "col"), P(("grp", "row"), None)),
        out_specs=(P(("grp", "row"), None), P(("grp", "row"), "col")),
        check_vma=False,
    )
```

```python
import functools
import math

import jax
import jax.numpy as jnp
from jax import lax
from jax.experimental import pallas as pl
from jax.experimental.pallas import tpu as pltpu
from jax.sharding import PartitionSpec as P

CHUNKS = 2


def levels_of(size):
    levels, stride = [], 1
    while stride < size:
        radix = 2 if stride == 1 else min(4, size // stride)
        levels.append((stride, radix))
        stride *= radix
    return levels


def swap(value, axis, distance):
    size = lax.axis_size(axis)
    return lax.ppermute(value, axis, [(i, i ^ distance) for i in range(size)])


def exchange_sum(value, axis):
    step = 1
    while step < lax.axis_size(axis):
        value = value + swap(value, axis, step)
        step *= 2
    return value


def digit_of(axis, stride, radix):
    return lax.rem(lax.div(lax.axis_index(axis), stride), radix)


def scatter_level(blocks, axis, stride, radix):
    digit = digit_of(axis, stride, radix)
    view = blocks.reshape((blocks.shape[0] // radix, radix) + blocks.shape[1:])
    total = lax.dynamic_index_in_dim(view, digit, 1, keepdims=False)
    for t in range(1, radix):
        part = lax.dynamic_index_in_dim(view, jnp.bitwise_xor(digit, t), 1, keepdims=False)
        landed = swap(part.astype(jnp.bfloat16), axis, t * stride)
        total = total + landed.astype(jnp.float32)
    return total


def scatter_sum(blocks, axis):
    for stride, radix in levels_of(lax.axis_size(axis)):
        blocks = scatter_level(blocks, axis, stride, radix)
    return blocks[0]


def gather_level(blocks, axis, stride, radix):
    digit = digit_of(axis, stride, radix)
    held = [blocks] + [swap(blocks, axis, t * stride) for t in range(1, radix)]
    bit = 1
    while bit < radix:
        flip = jnp.bitwise_and(digit, bit) != 0
        held = [jnp.where(flip, held[j ^ bit], held[j]) for j in range(radix)]
        bit *= 2
    whole = jnp.stack(held, axis=1)
    return whole.reshape((blocks.shape[0] * radix,) + blocks.shape[1:])


def gather(block, axis):
    blocks = block[None]
    for stride, radix in reversed(levels_of(lax.axis_size(axis))):
        blocks = gather_level(blocks, axis, stride, radix)
    return blocks


def matmul(left, right, exact=True):
    if not exact:
        left, right = left.astype(jnp.bfloat16), right.astype(jnp.bfloat16)
    return lax.dot_general(
        left,
        right,
        (((1,), (0,)), ((), ())),
        precision=lax.Precision.HIGHEST if exact else None,
        preferred_element_type=jnp.float32,
    )


def matmul_t(left, right, exact=True):
    if not exact:
        left, right = left.astype(jnp.bfloat16), right.astype(jnp.bfloat16)
    return lax.dot_general(
        left,
        right,
        (((1,), (1,)), ((), ())),
        precision=lax.Precision.HIGHEST if exact else None,
        preferred_element_type=jnp.float32,
    )


UPDATES = 4
LOOSE_UPDATES = 2
CLOSE = 1e-5


def basis_kernel(total_cols, root_rows, gram_ref, mine_ref, other_ref, *refs):
    basis_ref, pair_ref, work_ref, inverse_ref = refs
    width = gram_ref.shape[0]
    row = lax.broadcasted_iota(jnp.int32, (width, width), 0)
    col = lax.broadcasted_iota(jnp.int32, (width, width), 1)
    on_diag = row == col
    unit = jnp.where(on_diag, 1.0, 0.0)
    half = jnp.where(row > col, 1.0, jnp.where(on_diag, 0.5, 0.0))

    gram = gram_ref[...]
    diagonal = jnp.where(on_diag, gram, 0.0)
    down = lax.rsqrt(jnp.sum(diagonal, axis=1, keepdims=True))
    across = lax.rsqrt(jnp.sum(diagonal, axis=0, keepdims=True))
    scaled = gram * down * across

    error = scaled - unit
    step = error * half
    inverse = unit - step + matmul(step, step, False)
    for update in range(1, UPDATES):
        exact = update >= LOOSE_UPDATES
        error = matmul_t(matmul(inverse, scaled, exact), inverse, exact) - unit
        step = error * half
        inverse = inverse - matmul(step, inverse - matmul(step, inverse, exact), exact)
    inverse_ref[...] = inverse * across
    far = jnp.sum(error * error)

    @pl.when(jnp.logical_not(far <= CLOSE))
    def _():
        work_ref[...] = gram
        inverse_ref[...] = unit

        def eliminate(k, carry):
            whole = work_ref[...]
            pivot_row = work_ref[pl.ds(k, 1), :]
            pivot = jnp.sum(
                jnp.where(col[:1] == k, pivot_row, 0.0), axis=1, keepdims=True
            )
            column = jnp.sum(jnp.where(col == k, whole, 0.0), axis=1, keepdims=True)
            factor = jnp.where(row[:, :1] > k, column / pivot, 0.0)
            work_ref[...] = whole - factor * pivot_row
            inverse_ref[...] = inverse_ref[...] - factor * inverse_ref[pl.ds(k, 1), :]
            return carry

        lax.fori_loop(0, width, eliminate, 0)
        pivots = jnp.sum(jnp.where(on_diag, work_ref[...], 0.0), axis=1, keepdims=True)
        inverse_ref[...] = inverse_ref[...] * lax.rsqrt(pivots)

    sketch = (mine_ref[...] + other_ref[...]) / total_cols
    basis = matmul_t(sketch, inverse_ref[...]) * root_rows
    basis_ref[...] = basis
    high = basis.astype(jnp.bfloat16)
    pair_ref[:, :width] = high
    pair_ref[:, width:] = (basis - high.astype(jnp.float32)).astype(jnp.bfloat16)


def make_basis(gram, mine, other, total_cols, root_rows):
    rows, width = mine.shape
    return pl.pallas_call(
        functools.partial(basis_kernel, total_cols, root_rows),
        out_shape=(
            jax.ShapeDtypeStruct((rows, width), jnp.float32),
            jax.ShapeDtypeStruct((rows, 2 * width), jnp.bfloat16),
        ),
        in_specs=[pl.BlockSpec(memory_space=pltpu.VMEM)] * 3,
        out_specs=[pl.BlockSpec(memory_space=pltpu.VMEM)] * 2,
        scratch_shapes=[
            pltpu.VMEM((width, width), jnp.float32),
            pltpu.VMEM((width, width), jnp.float32),
        ],
        name="make_basis",
    )(gram, mine, other)


def per_device(activations, start_sketch):
    rows_here, cols_here = activations.shape
    width = start_sketch.shape[1]
    parts = lax.axis_size("row")
    total_rows = rows_here * parts
    total_cols = cols_here * lax.axis_size("col")
    root_rows = math.sqrt(total_rows)

    cols_chunk = cols_here // CHUNKS
    spans = [slice(c * cols_chunk, (c + 1) * cols_chunk) for c in range(CHUNKS)]

    partial_sketch = 0.0
    for span in spans:
        local_cols = lax.dot_general(
            activations[:, span],
            start_sketch,
            (((0,), (0,)), ((), ())),
            preferred_element_type=jnp.float32,
        )
        share = scatter_sum(local_cols.reshape(parts, cols_chunk // parts, width), "row")
        chunk = gather((share / root_rows).astype(jnp.bfloat16), "row")
        partial_sketch = partial_sketch + jnp.dot(
            activations[:, span],
            chunk.reshape(cols_chunk, width),
            preferred_element_type=jnp.float32,
        )
    other_sketch = swap(partial_sketch, "col", 1)
    sketch = (partial_sketch + other_sketch) / total_cols

    local_gram = lax.dot_general(
        sketch, sketch, (((0,), (0,)), ((), ())), precision=lax.Precision.HIGHEST
    )
    gram = exchange_sum(local_gram, "row")
    basis, pair = make_basis(gram, partial_sketch, other_sketch, total_cols, root_rows)

    pieces = []
    for span in spans:
        local_pair = lax.dot_general(
            pair, activations[:, span], (((0,), (0,)), ((), ())), preferred_element_type=jnp.float32
        )
        local_proj = local_pair[:width] + local_pair[width:]
        pieces.append(
            scatter_sum(local_proj.reshape(parts, width // parts, cols_chunk), "row") / total_rows
        )
    return (basis, jnp.concatenate(pieces, axis=1))


def solution(mesh):
    return jax.shard_map(
        per_device,
        mesh=mesh,
        in_specs=(P(("grp", "row"), "col"), P(("grp", "row"), None)),
        out_specs=(P(("grp", "row"), None), P(("grp", "row"), "col")),
        check_vma=False,
    )
```

```python
import functools
import math

import jax
import jax.numpy as jnp
from jax import lax
from jax.experimental import pallas as pl
from jax.experimental.pallas import tpu as pltpu
from jax.sharding import PartitionSpec as P

CHUNKS = 2


def levels_of(size):
    levels, stride = [], 1
    while stride < size:
        radix = 2 if stride == 1 else min(4, size // stride)
        levels.append((stride, radix))
        stride *= radix
    return levels


def swap(value, axis, distance):
    size = lax.axis_size(axis)
    return lax.ppermute(value, axis, [(i, i ^ distance) for i in range(size)])


def exchange_sum(value, axis):
    step = 1
    while step < lax.axis_size(axis):
        value = value + swap(value, axis, step)
        step *= 2
    return value


def digit_of(axis, stride, radix):
    return lax.rem(lax.div(lax.axis_index(axis), stride), radix)


def scatter_level(blocks, axis, stride, radix):
    digit = digit_of(axis, stride, radix)
    view = blocks.reshape((blocks.shape[0] // radix, radix) + blocks.shape[1:])
    total = lax.dynamic_index_in_dim(view, digit, 1, keepdims=False)
    for t in range(1, radix):
        part = lax.dynamic_index_in_dim(view, jnp.bitwise_xor(digit, t), 1, keepdims=False)
        landed = swap(part.astype(jnp.bfloat16), axis, t * stride)
        total = total + landed.astype(jnp.float32)
    return total


def scatter_sum(blocks, axis):
    for stride, radix in levels_of(lax.axis_size(axis)):
        blocks = scatter_level(blocks, axis, stride, radix)
    return blocks[0]


def gather_level(blocks, axis, stride, radix):
    digit = digit_of(axis, stride, radix)
    held = [blocks] + [swap(blocks, axis, t * stride) for t in range(1, radix)]
    bit = 1
    while bit < radix:
        flip = jnp.bitwise_and(digit, bit) != 0
        held = [jnp.where(flip, held[j ^ bit], held[j]) for j in range(radix)]
        bit *= 2
    whole = jnp.stack(held, axis=1)
    return whole.reshape((blocks.shape[0] * radix,) + blocks.shape[1:])


def gather(block, axis):
    blocks = block[None]
    for stride, radix in reversed(levels_of(lax.axis_size(axis))):
        blocks = gather_level(blocks, axis, stride, radix)
    return blocks


def matmul(left, right, exact=True):
    if not exact:
        left, right = left.astype(jnp.bfloat16), right.astype(jnp.bfloat16)
    return lax.dot_general(
        left,
        right,
        (((1,), (0,)), ((), ())),
        precision=lax.Precision.HIGHEST if exact else None,
        preferred_element_type=jnp.float32,
    )


def matmul_t(left, right, exact=True):
    if not exact:
        left, right = left.astype(jnp.bfloat16), right.astype(jnp.bfloat16)
    return lax.dot_general(
        left,
        right,
        (((1,), (1,)), ((), ())),
        precision=lax.Precision.HIGHEST if exact else None,
        preferred_element_type=jnp.float32,
    )


UPDATES = 4
LOOSE_UPDATES = 2
CLOSE = 1e-5
TILE = 1024


def basis_kernel(
    total_cols, root_rows, gram_ref, mine_ref, other_ref, slab_ref,
    basis_ref, product_ref, work_ref, inverse_ref,
):
    width = gram_ref.shape[0]
    row = lax.broadcasted_iota(jnp.int32, (width, width), 0)
    col = lax.broadcasted_iota(jnp.int32, (width, width), 1)
    on_diag = row == col
    unit = jnp.where(on_diag, 1.0, 0.0)
    half = jnp.where(row > col, 1.0, jnp.where(on_diag, 0.5, 0.0))

    gram = gram_ref[...]
    diagonal = jnp.where(on_diag, gram, 0.0)
    down = lax.rsqrt(jnp.sum(diagonal, axis=1, keepdims=True))
    across = lax.rsqrt(jnp.sum(diagonal, axis=0, keepdims=True))
    scaled = gram * down * across

    error = scaled - unit
    step = error * half
    inverse = unit - step + matmul(step, step, False)
    for update in range(1, UPDATES):
        exact = update >= LOOSE_UPDATES
        error = matmul_t(matmul(inverse, scaled, exact), inverse, exact) - unit
        step = error * half
        inverse = inverse - matmul(step, inverse - matmul(step, inverse, exact), exact)
    inverse_ref[...] = inverse * across
    far = jnp.sum(error * error)

    @pl.when(jnp.logical_not(far <= CLOSE))
    def _():
        work_ref[...] = gram
        inverse_ref[...] = unit

        def eliminate(k, carry):
            whole = work_ref[...]
            pivot_row = work_ref[pl.ds(k, 1), :]
            pivot = jnp.sum(
                jnp.where(col[:1] == k, pivot_row, 0.0), axis=1, keepdims=True
            )
            column = jnp.sum(jnp.where(col == k, whole, 0.0), axis=1, keepdims=True)
            factor = jnp.where(row[:, :1] > k, column / pivot, 0.0)
            work_ref[...] = whole - factor * pivot_row
            inverse_ref[...] = inverse_ref[...] - factor * inverse_ref[pl.ds(k, 1), :]
            return carry

        lax.fori_loop(0, width, eliminate, 0)
        pivots = jnp.sum(jnp.where(on_diag, work_ref[...], 0.0), axis=1, keepdims=True)
        inverse_ref[...] = inverse_ref[...] * lax.rsqrt(pivots)

    sketch = (mine_ref[...] + other_ref[...]) / total_cols
    basis = matmul_t(sketch, inverse_ref[...]) * root_rows
    basis_ref[...] = basis
    high = basis.astype(jnp.bfloat16)
    low = (basis - high.astype(jnp.float32)).astype(jnp.bfloat16)
    pair = jnp.concatenate([high, low], axis=1).T
    for start in range(0, slab_ref.shape[1], TILE):
        tile = slab_ref[:, start : start + TILE]
        both = lax.dot_general(
            pair, tile, (((1,), (0,)), ((), ())), preferred_element_type=jnp.float32
        )
        product_ref[:, start : start + TILE] = both[:width] + both[width:]


def make_basis(gram, mine, other, slab, total_cols, root_rows):
    rows, width = mine.shape
    return pl.pallas_call(
        functools.partial(basis_kernel, total_cols, root_rows),
        out_shape=(
            jax.ShapeDtypeStruct((rows, width), jnp.float32),
            jax.ShapeDtypeStruct((width, slab.shape[1]), jnp.float32),
        ),
        in_specs=[pl.BlockSpec(memory_space=pltpu.VMEM)] * 4,
        out_specs=[pl.BlockSpec(memory_space=pltpu.VMEM)] * 2,
        scratch_shapes=[
            pltpu.VMEM((width, width), jnp.float32),
            pltpu.VMEM((width, width), jnp.float32),
        ],
        compiler_params=pltpu.CompilerParams(vmem_limit_bytes=24 * 2**20),
        name="make_basis",
    )(gram, mine, other, slab)


def per_device(activations, start_sketch):
    rows_here, cols_here = activations.shape
    width = start_sketch.shape[1]
    parts = lax.axis_size("row")
    total_rows = rows_here * parts
    total_cols = cols_here * lax.axis_size("col")
    root_rows = math.sqrt(total_rows)

    cols_chunk = cols_here // CHUNKS
    spans = [slice(c * cols_chunk, (c + 1) * cols_chunk) for c in range(CHUNKS)]

    partial_sketch = 0.0
    for span in spans:
        local_cols = lax.dot_general(
            activations[:, span],
            start_sketch,
            (((0,), (0,)), ((), ())),
            preferred_element_type=jnp.float32,
        )
        share = scatter_sum(local_cols.reshape(parts, cols_chunk // parts, width), "row")
        chunk = gather((share / root_rows).astype(jnp.bfloat16), "row")
        partial_sketch = partial_sketch + jnp.dot(
            activations[:, span],
            chunk.reshape(cols_chunk, width),
            preferred_element_type=jnp.float32,
        )
    other_sketch = swap(partial_sketch, "col", 1)
    sketch = (partial_sketch + other_sketch) / total_cols

    local_gram = lax.dot_general(
        sketch, sketch, (((0,), (0,)), ((), ())), precision=lax.Precision.HIGHEST
    )
    gram = exchange_sum(local_gram, "row")
    basis, local_proj = make_basis(
        gram, partial_sketch, other_sketch, activations, total_cols, root_rows
    )

    pieces = []
    for span in spans:
        blocks = local_proj[:, span].reshape(parts, width // parts, cols_chunk)
        pieces.append(scatter_sum(blocks, "row") / total_rows)
    return (basis, jnp.concatenate(pieces, axis=1))


def solution(mesh):
    return jax.shard_map(
        per_device,
        mesh=mesh,
        in_specs=(P(("grp", "row"), "col"), P(("grp", "row"), None)),
        out_specs=(P(("grp", "row"), None), P(("grp", "row"), "col")),
        check_vma=False,
    )
```

```python
import functools
import math

import jax
import jax.numpy as jnp
from jax import lax
from jax.experimental import pallas as pl
from jax.experimental.pallas import tpu as pltpu
from jax.sharding import PartitionSpec as P

CHUNKS = 2


def levels_of(size):
    levels, stride = [], 1
    while stride < size:
        radix = 2 if stride == 1 else min(4, size // stride)
        levels.append((stride, radix))
        stride *= radix
    return levels


def swap(value, axis, distance):
    size = lax.axis_size(axis)
    return lax.ppermute(value, axis, [(i, i ^ distance) for i in range(size)])


def exchange_sum(value, axis):
    step = 1
    while step < lax.axis_size(axis):
        value = value + swap(value, axis, step)
        step *= 2
    return value


def digit_of(axis, stride, radix):
    return lax.rem(lax.div(lax.axis_index(axis), stride), radix)


def groups_of(axis, stride, radix):
    size = lax.axis_size(axis)
    return [
        [i + j * stride for j in range(radix)]
        for i in range(size)
        if (i // stride) % radix == 0
    ]


def scatter_level(blocks, axis, stride, radix):
    digit = digit_of(axis, stride, radix)
    view = blocks.reshape((blocks.shape[0] // radix, radix) + blocks.shape[1:])
    own = lax.dynamic_index_in_dim(view, digit, 1, keepdims=False)
    if radix == 2:
        part = lax.dynamic_index_in_dim(view, 1 - digit, 1, keepdims=False)
        landed = swap(part.astype(jnp.bfloat16), axis, stride)
        return own + landed.astype(jnp.float32)
    landed = lax.all_to_all(
        view.astype(jnp.bfloat16),
        axis,
        1,
        1,
        axis_index_groups=groups_of(axis, stride, radix),
        tiled=True,
    )
    kept = own - own.astype(jnp.bfloat16).astype(jnp.float32)
    return kept + jnp.sum(landed.astype(jnp.float32), axis=1)


def scatter_sum(blocks, axis):
    for stride, radix in levels_of(lax.axis_size(axis)):
        blocks = scatter_level(blocks, axis, stride, radix)
    return blocks[0]


def gather_level(blocks, axis, stride, radix):
    digit = digit_of(axis, stride, radix)
    if radix == 2:
        other = swap(blocks, axis, stride)
        pair = [jnp.where(digit == 0, blocks, other), jnp.where(digit == 0, other, blocks)]
        whole = jnp.stack(pair, axis=1)
    else:
        copies = jnp.broadcast_to(
            blocks[:, None], (blocks.shape[0], radix) + blocks.shape[1:]
        )
        whole = lax.all_to_all(
            copies, axis, 1, 1, axis_index_groups=groups_of(axis, stride, radix), tiled=True
        )
    return whole.reshape((blocks.shape[0] * radix,) + blocks.shape[1:])


def gather(block, axis):
    blocks = block[None]
    for stride, radix in reversed(levels_of(lax.axis_size(axis))):
        blocks = gather_level(blocks, axis, stride, radix)
    return blocks


def matmul(left, right, exact=True):
    if not exact:
        left, right = left.astype(jnp.bfloat16), right.astype(jnp.bfloat16)
    return lax.dot_general(
        left,
        right,
        (((1,), (0,)), ((), ())),
        precision=lax.Precision.HIGHEST if exact else None,
        preferred_element_type=jnp.float32,
    )


def matmul_t(left, right, exact=True):
    if not exact:
        left, right = left.astype(jnp.bfloat16), right.astype(jnp.bfloat16)
    return lax.dot_general(
        left,
        right,
        (((1,), (1,)), ((), ())),
        precision=lax.Precision.HIGHEST if exact else None,
        preferred_element_type=jnp.float32,
    )


UPDATES = 4
LOOSE_UPDATES = 2
CLOSE = 1e-5
TILE = 1024


def basis_kernel(
    total_cols, root_rows, gram_ref, mine_ref, other_ref, slab_ref,
    basis_ref, product_ref, work_ref, inverse_ref,
):
    width = gram_ref.shape[0]
    row = lax.broadcasted_iota(jnp.int32, (width, width), 0)
    col = lax.broadcasted_iota(jnp.int32, (width, width), 1)
    on_diag = row == col
    unit = jnp.where(on_diag, 1.0, 0.0)
    half = jnp.where(row > col, 1.0, jnp.where(on_diag, 0.5, 0.0))

    gram = gram_ref[...]
    diagonal = jnp.where(on_diag, gram, 0.0)
    down = lax.rsqrt(jnp.sum(diagonal, axis=1, keepdims=True))
    across = lax.rsqrt(jnp.sum(diagonal, axis=0, keepdims=True))
    scaled = gram * down * across

    error = scaled - unit
    step = error * half
    inverse = unit - step + matmul(step, step, False)
    for update in range(1, UPDATES):
        exact = update >= LOOSE_UPDATES
        error = matmul_t(matmul(inverse, scaled, exact), inverse, exact) - unit
        step = error * half
        inverse = inverse - matmul(step, inverse - matmul(step, inverse, exact), exact)
    inverse_ref[...] = inverse * across
    far = jnp.sum(error * error)

    @pl.when(jnp.logical_not(far <= CLOSE))
    def _():
        work_ref[...] = gram
        inverse_ref[...] = unit

        def eliminate(k, carry):
            whole = work_ref[...]
            pivot_row = work_ref[pl.ds(k, 1), :]
            pivot = jnp.sum(
                jnp.where(col[:1] == k, pivot_row, 0.0), axis=1, keepdims=True
            )
            column = jnp.sum(jnp.where(col == k, whole, 0.0), axis=1, keepdims=True)
            factor = jnp.where(row[:, :1] > k, column / pivot, 0.0)
            work_ref[...] = whole - factor * pivot_row
            inverse_ref[...] = inverse_ref[...] - factor * inverse_ref[pl.ds(k, 1), :]
            return carry

        lax.fori_loop(0, width, eliminate, 0)
        pivots = jnp.sum(jnp.where(on_diag, work_ref[...], 0.0), axis=1, keepdims=True)
        inverse_ref[...] = inverse_ref[...] * lax.rsqrt(pivots)

    sketch = (mine_ref[...] + other_ref[...]) / total_cols
    basis = matmul_t(sketch, inverse_ref[...]) * root_rows
    basis_ref[...] = basis
    high = basis.astype(jnp.bfloat16)
    low = (basis - high.astype(jnp.float32)).astype(jnp.bfloat16)
    pair = jnp.concatenate([high, low], axis=1).T
    for start in range(0, slab_ref.shape[1], TILE):
        tile = slab_ref[:, start : start + TILE]
        both = lax.dot_general(
            pair, tile, (((1,), (0,)), ((), ())), preferred_element_type=jnp.float32
        )
        product_ref[:, start : start + TILE] = both[:width] + both[width:]


def make_basis(gram, mine, other, slab, total_cols, root_rows):
    rows, width = mine.shape
    return pl.pallas_call(
        functools.partial(basis_kernel, total_cols, root_rows),
        out_shape=(
            jax.ShapeDtypeStruct((rows, width), jnp.float32),
            jax.ShapeDtypeStruct((width, slab.shape[1]), jnp.float32),
        ),
        in_specs=[pl.BlockSpec(memory_space=pltpu.VMEM)] * 4,
        out_specs=[pl.BlockSpec(memory_space=pltpu.VMEM)] * 2,
        scratch_shapes=[
            pltpu.VMEM((width, width), jnp.float32),
            pltpu.VMEM((width, width), jnp.float32),
        ],
        compiler_params=pltpu.CompilerParams(vmem_limit_bytes=24 * 2**20),
        name="make_basis",
    )(gram, mine, other, slab)


def per_device(activations, start_sketch):
    rows_here, cols_here = activations.shape
    width = start_sketch.shape[1]
    parts = lax.axis_size("row")
    total_rows = rows_here * parts
    total_cols = cols_here * lax.axis_size("col")
    root_rows = math.sqrt(total_rows)

    cols_chunk = cols_here // CHUNKS
    spans = [slice(c * cols_chunk, (c + 1) * cols_chunk) for c in range(CHUNKS)]

    partial_sketch = 0.0
    for span in spans:
        local_cols = lax.dot_general(
            activations[:, span],
            start_sketch,
            (((0,), (0,)), ((), ())),
            preferred_element_type=jnp.float32,
        )
        share = scatter_sum(local_cols.reshape(parts, cols_chunk // parts, width), "row")
        chunk = gather((share / root_rows).astype(jnp.bfloat16), "row")
        partial_sketch = partial_sketch + jnp.dot(
            activations[:, span],
            chunk.reshape(cols_chunk, width),
            preferred_element_type=jnp.float32,
        )
    other_sketch = swap(partial_sketch, "col", 1)
    sketch = (partial_sketch + other_sketch) / total_cols

    local_gram = lax.dot_general(
        sketch, sketch, (((0,), (0,)), ((), ())), precision=lax.Precision.HIGHEST
    )
    gram = exchange_sum(local_gram, "row")
    basis, local_proj = make_basis(
        gram, partial_sketch, other_sketch, activations, total_cols, root_rows
    )

    pieces = []
    for span in spans:
        blocks = local_proj[:, span].reshape(parts, width // parts, cols_chunk)
        pieces.append(scatter_sum(blocks, "row") / total_rows)
    return (basis, jnp.concatenate(pieces, axis=1))


def solution(mesh):
    return jax.shard_map(
        per_device,
        mesh=mesh,
        in_specs=(P(("grp", "row"), "col"), P(("grp", "row"), None)),
        out_specs=(P(("grp", "row"), None), P(("grp", "row"), "col")),
        check_vma=False,
    )
```

```python
import functools
import math

import jax
import jax.numpy as jnp
from jax import lax
from jax.experimental import pallas as pl
from jax.experimental.pallas import tpu as pltpu
from jax.sharding import PartitionSpec as P

CHUNKS = 2


def levels_of(size):
    levels, stride = [], 1
    while stride < size:
        radix = 2 if stride == 1 else min(4, size // stride)
        levels.append((stride, radix))
        stride *= radix
    return levels


def swap(value, axis, distance):
    size = lax.axis_size(axis)
    return lax.ppermute(value, axis, [(i, i ^ distance) for i in range(size)])


def exchange_sum(value, axis):
    step = 1
    while step < lax.axis_size(axis):
        value = value + swap(value, axis, step)
        step *= 2
    return value


def digit_of(axis, stride, radix):
    return lax.rem(lax.div(lax.axis_index(axis), stride), radix)


def scatter_level(blocks, axis, stride, radix):
    digit = digit_of(axis, stride, radix)
    view = blocks.reshape((blocks.shape[0] // radix, radix) + blocks.shape[1:])
    total = lax.dynamic_index_in_dim(view, digit, 1, keepdims=False)
    for t in range(1, radix):
        part = lax.dynamic_index_in_dim(view, jnp.bitwise_xor(digit, t), 1, keepdims=False)
        landed = swap(part.astype(jnp.bfloat16), axis, t * stride)
        total = total + landed.astype(jnp.float32)
    return total


def scatter_sum(blocks, axis):
    for stride, radix in levels_of(lax.axis_size(axis)):
        blocks = scatter_level(blocks, axis, stride, radix)
    return blocks[0]


def bit_of(axis, bit):
    return lax.rem(lax.div(lax.axis_index(axis), 1 << bit), 2)


def halve(value, upper):
    width = value.shape[1] // 2
    low, high = value[:, :width], value[:, width:]
    return jnp.where(upper, high, low), jnp.where(upper, low, high)


def sum_and_share(keep, send, axis, scale):
    bits = (lax.axis_size(axis) - 1).bit_length()
    total = keep + swap(send, axis, 1).astype(jnp.float32)
    for bit in range(1, bits - 1):
        keep, send = halve(total, bit_of(axis, bit) == 1)
        total = keep + swap(send.astype(jnp.bfloat16), axis, 1 << bit).astype(jnp.float32)
    other = swap(total.astype(jnp.bfloat16), axis, 1 << (bits - 1))
    block = ((total + other.astype(jnp.float32)) * scale).astype(jnp.bfloat16)
    for bit in reversed(range(bits - 1)):
        other = swap(block, axis, 1 << bit)
        upper = bit_of(axis, bit) == 1
        block = jnp.concatenate(
            [jnp.where(upper, other, block), jnp.where(upper, block, other)], axis=1
        )
    return block


def sketch_kernel(plan, half, sketch_ref, slab_ref, *refs):
    outs, buffers, arrived = refs[-2 - len(plan) : -2], refs[-2], refs[-1]
    digit = bit_of("row", 0)
    jobs = []
    for out, (first, sent) in enumerate(plan):
        begin = (first + (1 - digit if sent else digit)) * half
        for tile in range(half // SKETCH_TILE):
            here = pl.multiple_of(begin + tile * SKETCH_TILE, SKETCH_TILE)
            slot = len(jobs)
            copy = pltpu.make_async_copy(
                slab_ref.at[:, pl.ds(here, SKETCH_TILE)], buffers.at[slot], arrived.at[slot]
            )
            copy.start()
            jobs.append((out, tile, copy))
    left = sketch_ref[...].T
    for slot, (out, tile, copy) in enumerate(jobs):
        copy.wait()
        product = lax.dot_general(
            left, buffers[slot], (((1,), (0,)), ((), ())), preferred_element_type=jnp.float32
        )
        span = slice(tile * SKETCH_TILE, (tile + 1) * SKETCH_TILE)
        outs[out][:, span] = product.astype(outs[out].dtype)


def sketch_halves(slab, start, plan, half, after=()):
    rows, width = start.shape
    tiles = len(plan) * (half // SKETCH_TILE)
    return pl.pallas_call(
        functools.partial(sketch_kernel, plan, half),
        out_shape=[
            jax.ShapeDtypeStruct((width, half), jnp.bfloat16 if sent else jnp.float32)
            for _, sent in plan
        ],
        in_specs=[
            pl.BlockSpec(memory_space=pltpu.VMEM),
            pl.BlockSpec(memory_space=pl.ANY),
        ]
        + [pl.BlockSpec(memory_space=pl.ANY)] * len(after),
        out_specs=[pl.BlockSpec(memory_space=pltpu.VMEM)] * len(plan),
        scratch_shapes=[
            pltpu.VMEM((tiles, rows, SKETCH_TILE), jnp.bfloat16),
            pltpu.SemaphoreType.DMA((tiles,)),
        ],
        compiler_params=pltpu.CompilerParams(vmem_limit_bytes=57 * 2**20),
        cost_estimate=pl.CostEstimate(
            flops=2 * rows * width * half * len(plan),
            bytes_accessed=2 * rows * half * len(plan),
            transcendentals=0,
        ),
        name="sketch_halves",
    )(start, slab, *after)


def matmul(left, right, exact=True):
    if not exact:
        left, right = left.astype(jnp.bfloat16), right.astype(jnp.bfloat16)
    return lax.dot_general(
        left,
        right,
        (((1,), (0,)), ((), ())),
        precision=lax.Precision.HIGHEST if exact else None,
        preferred_element_type=jnp.float32,
    )


def matmul_t(left, right, exact=True):
    if not exact:
        left, right = left.astype(jnp.bfloat16), right.astype(jnp.bfloat16)
    return lax.dot_general(
        left,
        right,
        (((1,), (1,)), ((), ())),
        precision=lax.Precision.HIGHEST if exact else None,
        preferred_element_type=jnp.float32,
    )


UPDATES = 4
LOOSE_UPDATES = 2
CLOSE = 1e-5
TILE = 1024
SKETCH_TILE = 512


def basis_kernel(
    total_cols, root_rows, gram_ref, mine_ref, other_ref, slab_ref,
    basis_ref, product_ref, work_ref, inverse_ref,
):
    width = gram_ref.shape[0]
    row = lax.broadcasted_iota(jnp.int32, (width, width), 0)
    col = lax.broadcasted_iota(jnp.int32, (width, width), 1)
    on_diag = row == col
    unit = jnp.where(on_diag, 1.0, 0.0)
    half = jnp.where(row > col, 1.0, jnp.where(on_diag, 0.5, 0.0))

    gram = gram_ref[...]
    diagonal = jnp.where(on_diag, gram, 0.0)
    down = lax.rsqrt(jnp.sum(diagonal, axis=1, keepdims=True))
    across = lax.rsqrt(jnp.sum(diagonal, axis=0, keepdims=True))
    scaled = gram * down * across

    error = scaled - unit
    step = error * half
    inverse = unit - step + matmul(step, step, False)
    for update in range(1, UPDATES):
        exact = update >= LOOSE_UPDATES
        error = matmul_t(matmul(inverse, scaled, exact), inverse, exact) - unit
        step = error * half
        inverse = inverse - matmul(step, inverse - matmul(step, inverse, exact), exact)
    inverse_ref[...] = inverse * across
    far = jnp.sum(error * error)

    @pl.when(jnp.logical_not(far <= CLOSE))
    def _():
        work_ref[...] = gram
        inverse_ref[...] = unit

        def eliminate(k, carry):
            whole = work_ref[...]
            pivot_row = work_ref[pl.ds(k, 1), :]
            pivot = jnp.sum(
                jnp.where(col[:1] == k, pivot_row, 0.0), axis=1, keepdims=True
            )
            column = jnp.sum(jnp.where(col == k, whole, 0.0), axis=1, keepdims=True)
            factor = jnp.where(row[:, :1] > k, column / pivot, 0.0)
            work_ref[...] = whole - factor * pivot_row
            inverse_ref[...] = inverse_ref[...] - factor * inverse_ref[pl.ds(k, 1), :]
            return carry

        lax.fori_loop(0, width, eliminate, 0)
        pivots = jnp.sum(jnp.where(on_diag, work_ref[...], 0.0), axis=1, keepdims=True)
        inverse_ref[...] = inverse_ref[...] * lax.rsqrt(pivots)

    sketch = (mine_ref[...] + other_ref[...]) / total_cols
    basis = matmul_t(sketch, inverse_ref[...]) * root_rows
    basis_ref[...] = basis
    high = basis.astype(jnp.bfloat16)
    low = (basis - high.astype(jnp.float32)).astype(jnp.bfloat16)
    pair = jnp.concatenate([high, low], axis=1).T
    for start in range(0, slab_ref.shape[1], TILE):
        tile = slab_ref[:, start : start + TILE]
        both = lax.dot_general(
            pair, tile, (((1,), (0,)), ((), ())), preferred_element_type=jnp.float32
        )
        product_ref[:, start : start + TILE] = both[:width] + both[width:]


def make_basis(gram, mine, other, slab, total_cols, root_rows):
    rows, width = mine.shape
    return pl.pallas_call(
        functools.partial(basis_kernel, total_cols, root_rows),
        out_shape=(
            jax.ShapeDtypeStruct((rows, width), jnp.float32),
            jax.ShapeDtypeStruct((width, slab.shape[1]), jnp.float32),
        ),
        in_specs=[pl.BlockSpec(memory_space=pltpu.VMEM)] * 4,
        out_specs=[pl.BlockSpec(memory_space=pltpu.VMEM)] * 2,
        scratch_shapes=[
            pltpu.VMEM((width, width), jnp.float32),
            pltpu.VMEM((width, width), jnp.float32),
        ],
        compiler_params=pltpu.CompilerParams(vmem_limit_bytes=24 * 2**20),
        name="make_basis",
    )(gram, mine, other, slab)


def per_device(activations, start_sketch):
    rows_here, cols_here = activations.shape
    width = start_sketch.shape[1]
    parts = lax.axis_size("row")
    total_rows = rows_here * parts
    total_cols = cols_here * lax.axis_size("col")
    root_rows = math.sqrt(total_rows)

    cols_chunk = cols_here // CHUNKS
    spans = [slice(c * cols_chunk, (c + 1) * cols_chunk) for c in range(CHUNKS)]

    half = cols_chunk // 2
    (send,) = sketch_halves(activations, start_sketch, [(0, True)], half)
    sends, keeps = [send], []
    plan = [(0, False)]
    for c in range(1, CHUNKS):
        plan += [(2 * c, True), (2 * c, False)]
    rest = sketch_halves(activations, start_sketch, plan, half, (send,))
    for (_, sent), out in zip(plan, rest):
        (sends if sent else keeps).append(out)

    partial_sketch = 0.0
    for span, keep, send in zip(spans, keeps, sends):
        shared = sum_and_share(keep, send, "row", 1.0 / root_rows)
        partial_sketch = partial_sketch + lax.dot_general(
            activations[:, span],
            shared,
            (((1,), (1,)), ((), ())),
            preferred_element_type=jnp.float32,
        )
    other_sketch = swap(partial_sketch, "col", 1)
    sketch = (partial_sketch + other_sketch) / total_cols

    local_gram = lax.dot_general(
        sketch, sketch, (((0,), (0,)), ((), ())), precision=lax.Precision.HIGHEST
    )
    gram = exchange_sum(local_gram, "row")
    basis, local_proj = make_basis(
        gram, partial_sketch, other_sketch, activations, total_cols, root_rows
    )

    pieces = []
    for span in spans:
        blocks = local_proj[:, span].reshape(parts, width // parts, cols_chunk)
        pieces.append(scatter_sum(blocks, "row") / total_rows)
    return (basis, jnp.concatenate(pieces, axis=1))


def solution(mesh):
    return jax.shard_map(
        per_device,
        mesh=mesh,
        in_specs=(P(("grp", "row"), "col"), P(("grp", "row"), None)),
        out_specs=(P(("grp", "row"), None), P(("grp", "row"), "col")),
        check_vma=False,
    )
```

```python
import functools
import math

import jax
import jax.numpy as jnp
from jax import lax
from jax.experimental import pallas as pl
from jax.experimental.pallas import tpu as pltpu
from jax.sharding import PartitionSpec as P

CHUNKS = 2


def levels_of(size):
    levels, stride = [], 1
    while stride < size:
        radix = 2 if stride == 1 else min(4, size // stride)
        levels.append((stride, radix))
        stride *= radix
    return levels


def swap(value, axis, distance):
    size = lax.axis_size(axis)
    return lax.ppermute(value, axis, [(i, i ^ distance) for i in range(size)])


def exchange_sum(value, axis):
    step = 1
    while step < lax.axis_size(axis):
        value = value + swap(value, axis, step)
        step *= 2
    return value


def digit_of(axis, stride, radix):
    return lax.rem(lax.div(lax.axis_index(axis), stride), radix)


def scatter_level(blocks, axis, stride, radix):
    digit = digit_of(axis, stride, radix)
    view = blocks.reshape((blocks.shape[0] // radix, radix) + blocks.shape[1:])
    total = lax.dynamic_index_in_dim(view, digit, 1, keepdims=False)
    for t in range(1, radix):
        part = lax.dynamic_index_in_dim(view, jnp.bitwise_xor(digit, t), 1, keepdims=False)
        landed = swap(part.astype(jnp.bfloat16), axis, t * stride)
        total = total + landed.astype(jnp.float32)
    return total


def scatter_sum(blocks, axis):
    for stride, radix in levels_of(lax.axis_size(axis)):
        blocks = scatter_level(blocks, axis, stride, radix)
    return blocks[0]


def bit_of(axis, bit):
    return lax.rem(lax.div(lax.axis_index(axis), 1 << bit), 2)


def sum_and_share(value, axis, order, scale):
    for bit in order[:-1]:
        upper = bit_of(axis, bit) == 1
        half = value.shape[0] // 2
        low, high = value[:half], value[half:]
        send = jnp.where(upper, low, high).astype(jnp.bfloat16)
        landed = swap(send, axis, 1 << bit)
        value = jnp.where(upper, high, low) + landed.astype(jnp.float32)
    landed = swap(value.astype(jnp.bfloat16), axis, 1 << order[-1])
    block = ((value + landed.astype(jnp.float32)) * scale).astype(jnp.bfloat16)
    for bit in reversed(order[:-1]):
        upper = bit_of(axis, bit) == 1
        other = swap(block, axis, 1 << bit)
        block = jnp.concatenate(
            [jnp.where(upper, other, block), jnp.where(upper, block, other)], axis=0
        )
    return block


def orders_of(axis):
    bits = list(range((lax.axis_size(axis) - 1).bit_length()))
    if len(bits) < 3:
        return [bits, bits]
    return [bits, [bits[1], bits[0]] + bits[2:]]


def matmul(left, right, exact=True):
    if not exact:
        left, right = left.astype(jnp.bfloat16), right.astype(jnp.bfloat16)
    return lax.dot_general(
        left,
        right,
        (((1,), (0,)), ((), ())),
        precision=lax.Precision.HIGHEST if exact else None,
        preferred_element_type=jnp.float32,
    )


def matmul_t(left, right, exact=True):
    if not exact:
        left, right = left.astype(jnp.bfloat16), right.astype(jnp.bfloat16)
    return lax.dot_general(
        left,
        right,
        (((1,), (1,)), ((), ())),
        precision=lax.Precision.HIGHEST if exact else None,
        preferred_element_type=jnp.float32,
    )


UPDATES = 4
LOOSE_UPDATES = 2
CLOSE = 1e-5
TILE = 1024


def basis_kernel(
    total_cols, root_rows, gram_ref, mine_ref, other_ref, slab_ref,
    basis_ref, product_ref, work_ref, inverse_ref,
):
    width = gram_ref.shape[0]
    row = lax.broadcasted_iota(jnp.int32, (width, width), 0)
    col = lax.broadcasted_iota(jnp.int32, (width, width), 1)
    on_diag = row == col
    unit = jnp.where(on_diag, 1.0, 0.0)
    half = jnp.where(row > col, 1.0, jnp.where(on_diag, 0.5, 0.0))

    gram = gram_ref[...]
    diagonal = jnp.where(on_diag, gram, 0.0)
    down = lax.rsqrt(jnp.sum(diagonal, axis=1, keepdims=True))
    across = lax.rsqrt(jnp.sum(diagonal, axis=0, keepdims=True))
    scaled = gram * down * across

    error = scaled - unit
    step = error * half
    inverse = unit - step + matmul(step, step, False)
    for update in range(1, UPDATES):
        exact = update >= LOOSE_UPDATES
        error = matmul_t(matmul(inverse, scaled, exact), inverse, exact) - unit
        step = error * half
        inverse = inverse - matmul(step, inverse - matmul(step, inverse, exact), exact)
    inverse_ref[...] = inverse * across
    far = jnp.sum(error * error)

    @pl.when(jnp.logical_not(far <= CLOSE))
    def _():
        work_ref[...] = gram
        inverse_ref[...] = unit

        def eliminate(k, carry):
            whole = work_ref[...]
            pivot_row = work_ref[pl.ds(k, 1), :]
            pivot = jnp.sum(
                jnp.where(col[:1] == k, pivot_row, 0.0), axis=1, keepdims=True
            )
            column = jnp.sum(jnp.where(col == k, whole, 0.0), axis=1, keepdims=True)
            factor = jnp.where(row[:, :1] > k, column / pivot, 0.0)
            work_ref[...] = whole - factor * pivot_row
            inverse_ref[...] = inverse_ref[...] - factor * inverse_ref[pl.ds(k, 1), :]
            return carry

        lax.fori_loop(0, width, eliminate, 0)
        pivots = jnp.sum(jnp.where(on_diag, work_ref[...], 0.0), axis=1, keepdims=True)
        inverse_ref[...] = inverse_ref[...] * lax.rsqrt(pivots)

    sketch = (mine_ref[...] + other_ref[...]) / total_cols
    basis = matmul_t(sketch, inverse_ref[...]) * root_rows
    basis_ref[...] = basis
    high = basis.astype(jnp.bfloat16)
    low = (basis - high.astype(jnp.float32)).astype(jnp.bfloat16)
    pair = jnp.concatenate([high, low], axis=1).T
    for start in range(0, slab_ref.shape[1], TILE):
        tile = slab_ref[:, start : start + TILE]
        both = lax.dot_general(
            pair, tile, (((1,), (0,)), ((), ())), preferred_element_type=jnp.float32
        )
        product_ref[:, start : start + TILE] = both[:width] + both[width:]


def make_basis(gram, mine, other, slab, total_cols, root_rows):
    rows, width = mine.shape
    return pl.pallas_call(
        functools.partial(basis_kernel, total_cols, root_rows),
        out_shape=(
            jax.ShapeDtypeStruct((rows, width), jnp.float32),
            jax.ShapeDtypeStruct((width, slab.shape[1]), jnp.float32),
        ),
        in_specs=[pl.BlockSpec(memory_space=pltpu.VMEM)] * 4,
        out_specs=[pl.BlockSpec(memory_space=pltpu.VMEM)] * 2,
        scratch_shapes=[
            pltpu.VMEM((width, width), jnp.float32),
            pltpu.VMEM((width, width), jnp.float32),
        ],
        compiler_params=pltpu.CompilerParams(vmem_limit_bytes=24 * 2**20),
        name="make_basis",
    )(gram, mine, other, slab)


def per_device(activations, start_sketch):
    rows_here, cols_here = activations.shape
    width = start_sketch.shape[1]
    parts = lax.axis_size("row")
    total_rows = rows_here * parts
    total_cols = cols_here * lax.axis_size("col")
    root_rows = math.sqrt(total_rows)

    cols_chunk = cols_here // CHUNKS
    spans = [slice(c * cols_chunk, (c + 1) * cols_chunk) for c in range(CHUNKS)]

    partial_sketch = 0.0
    for span, order in zip(spans, orders_of("row")):
        local_cols = lax.dot_general(
            activations[:, span],
            start_sketch,
            (((0,), (0,)), ((), ())),
            preferred_element_type=jnp.float32,
        )
        partial_sketch = partial_sketch + jnp.dot(
            activations[:, span],
            sum_and_share(local_cols, "row", order, 1.0 / root_rows),
            preferred_element_type=jnp.float32,
        )
    other_sketch = swap(partial_sketch, "col", 1)
    sketch = (partial_sketch + other_sketch) / total_cols

    local_gram = lax.dot_general(
        sketch, sketch, (((0,), (0,)), ((), ())), precision=lax.Precision.HIGHEST
    )
    gram = exchange_sum(local_gram, "row")
    basis, local_proj = make_basis(
        gram, partial_sketch, other_sketch, activations, total_cols, root_rows
    )

    pieces = []
    for span in spans:
        blocks = local_proj[:, span].reshape(parts, width // parts, cols_chunk)
        pieces.append(scatter_sum(blocks, "row") / total_rows)
    return (basis, jnp.concatenate(pieces, axis=1))


def solution(mesh):
    return jax.shard_map(
        per_device,
        mesh=mesh,
        in_specs=(P(("grp", "row"), "col"), P(("grp", "row"), None)),
        out_specs=(P(("grp", "row"), None), P(("grp", "row"), "col")),
        check_vma=False,
    )
```

```python
import functools
import math

import jax
import jax.numpy as jnp
from jax import lax
from jax.experimental import pallas as pl
from jax.experimental.pallas import tpu as pltpu
from jax.sharding import PartitionSpec as P

SKETCH_CHUNKS = 4
CHUNKS = 2


def levels_of(size):
    levels, stride = [], 1
    while stride < size:
        radix = 2 if stride == 1 else min(4, size // stride)
        levels.append((stride, radix))
        stride *= radix
    return levels


def swap(value, axis, distance):
    size = lax.axis_size(axis)
    return lax.ppermute(value, axis, [(i, i ^ distance) for i in range(size)])


def exchange_sum(value, axis):
    step = 1
    while step < lax.axis_size(axis):
        value = value + swap(value, axis, step)
        step *= 2
    return value


def digit_of(axis, stride, radix):
    return lax.rem(lax.div(lax.axis_index(axis), stride), radix)


def scatter_level(blocks, axis, stride, radix):
    digit = digit_of(axis, stride, radix)
    view = blocks.reshape((blocks.shape[0] // radix, radix) + blocks.shape[1:])
    total = lax.dynamic_index_in_dim(view, digit, 1, keepdims=False)
    for t in range(1, radix):
        part = lax.dynamic_index_in_dim(view, jnp.bitwise_xor(digit, t), 1, keepdims=False)
        landed = swap(part.astype(jnp.bfloat16), axis, t * stride)
        total = total + landed.astype(jnp.float32)
    return total


def scatter_sum(blocks, axis):
    for stride, radix in levels_of(lax.axis_size(axis)):
        blocks = scatter_level(blocks, axis, stride, radix)
    return blocks[0]


def bit_of(axis, bit):
    return lax.rem(lax.div(lax.axis_index(axis), 1 << bit), 2)


def sum_and_share(value, axis, order, scale):
    for bit in order[:-1]:
        upper = bit_of(axis, bit) == 1
        half = value.shape[0] // 2
        low, high = value[:half], value[half:]
        send = jnp.where(upper, low, high).astype(jnp.bfloat16)
        landed = swap(send, axis, 1 << bit)
        value = jnp.where(upper, high, low) + landed.astype(jnp.float32)
    landed = swap(value.astype(jnp.bfloat16), axis, 1 << order[-1])
    block = ((value + landed.astype(jnp.float32)) * scale).astype(jnp.bfloat16)
    for bit in reversed(order[:-1]):
        upper = bit_of(axis, bit) == 1
        other = swap(block, axis, 1 << bit)
        block = jnp.concatenate(
            [jnp.where(upper, other, block), jnp.where(upper, block, other)], axis=0
        )
    return block


def orders_of(axis):
    bits = list(range((lax.axis_size(axis) - 1).bit_length()))
    if len(bits) < 3:
        return [bits, bits]
    return [bits, [bits[1], bits[0]] + bits[2:]]


def matmul(left, right, exact=True):
    if not exact:
        left, right = left.astype(jnp.bfloat16), right.astype(jnp.bfloat16)
    return lax.dot_general(
        left,
        right,
        (((1,), (0,)), ((), ())),
        precision=lax.Precision.HIGHEST if exact else None,
        preferred_element_type=jnp.float32,
    )


def matmul_t(left, right, exact=True):
    if not exact:
        left, right = left.astype(jnp.bfloat16), right.astype(jnp.bfloat16)
    return lax.dot_general(
        left,
        right,
        (((1,), (1,)), ((), ())),
        precision=lax.Precision.HIGHEST if exact else None,
        preferred_element_type=jnp.float32,
    )


UPDATES = 4
LOOSE_UPDATES = 2
CLOSE = 1e-5
TILE = 1024


def basis_kernel(
    total_cols, root_rows, gram_ref, mine_ref, other_ref, slab_ref,
    basis_ref, product_ref, work_ref, inverse_ref,
):
    width = gram_ref.shape[0]
    row = lax.broadcasted_iota(jnp.int32, (width, width), 0)
    col = lax.broadcasted_iota(jnp.int32, (width, width), 1)
    on_diag = row == col
    unit = jnp.where(on_diag, 1.0, 0.0)
    half = jnp.where(row > col, 1.0, jnp.where(on_diag, 0.5, 0.0))

    gram = gram_ref[...]
    diagonal = jnp.where(on_diag, gram, 0.0)
    down = lax.rsqrt(jnp.sum(diagonal, axis=1, keepdims=True))
    across = lax.rsqrt(jnp.sum(diagonal, axis=0, keepdims=True))
    scaled = gram * down * across

    error = scaled - unit
    step = error * half
    inverse = unit - step + matmul(step, step, False)
    for update in range(1, UPDATES):
        exact = update >= LOOSE_UPDATES
        error = matmul_t(matmul(inverse, scaled, exact), inverse, exact) - unit
        step = error * half
        inverse = inverse - matmul(step, inverse - matmul(step, inverse, exact), exact)
    inverse_ref[...] = inverse * across
    far = jnp.sum(error * error)

    @pl.when(jnp.logical_not(far <= CLOSE))
    def _():
        work_ref[...] = gram
        inverse_ref[...] = unit

        def eliminate(k, carry):
            whole = work_ref[...]
            pivot_row = work_ref[pl.ds(k, 1), :]
            pivot = jnp.sum(
                jnp.where(col[:1] == k, pivot_row, 0.0), axis=1, keepdims=True
            )
            column = jnp.sum(jnp.where(col == k, whole, 0.0), axis=1, keepdims=True)
            factor = jnp.where(row[:, :1] > k, column / pivot, 0.0)
            work_ref[...] = whole - factor * pivot_row
            inverse_ref[...] = inverse_ref[...] - factor * inverse_ref[pl.ds(k, 1), :]
            return carry

        lax.fori_loop(0, width, eliminate, 0)
        pivots = jnp.sum(jnp.where(on_diag, work_ref[...], 0.0), axis=1, keepdims=True)
        inverse_ref[...] = inverse_ref[...] * lax.rsqrt(pivots)

    sketch = (mine_ref[...] + other_ref[...]) / total_cols
    basis = matmul_t(sketch, inverse_ref[...]) * root_rows
    basis_ref[...] = basis
    high = basis.astype(jnp.bfloat16)
    low = (basis - high.astype(jnp.float32)).astype(jnp.bfloat16)
    pair = jnp.concatenate([high, low], axis=1).T
    for start in range(0, slab_ref.shape[1], TILE):
        tile = slab_ref[:, start : start + TILE]
        both = lax.dot_general(
            pair, tile, (((1,), (0,)), ((), ())), preferred_element_type=jnp.float32
        )
        product_ref[:, start : start + TILE] = both[:width] + both[width:]


def make_basis(gram, mine, other, slab, total_cols, root_rows):
    rows, width = mine.shape
    return pl.pallas_call(
        functools.partial(basis_kernel, total_cols, root_rows),
        out_shape=(
            jax.ShapeDtypeStruct((rows, width), jnp.float32),
            jax.ShapeDtypeStruct((width, slab.shape[1]), jnp.float32),
        ),
        in_specs=[pl.BlockSpec(memory_space=pltpu.VMEM)] * 4,
        out_specs=[pl.BlockSpec(memory_space=pltpu.VMEM)] * 2,
        scratch_shapes=[
            pltpu.VMEM((width, width), jnp.float32),
            pltpu.VMEM((width, width), jnp.float32),
        ],
        compiler_params=pltpu.CompilerParams(vmem_limit_bytes=24 * 2**20),
        name="make_basis",
    )(gram, mine, other, slab)


def per_device(activations, start_sketch):
    rows_here, cols_here = activations.shape
    width = start_sketch.shape[1]
    parts = lax.axis_size("row")
    total_rows = rows_here * parts
    total_cols = cols_here * lax.axis_size("col")
    root_rows = math.sqrt(total_rows)

    cols_chunk = cols_here // CHUNKS
    spans = [slice(c * cols_chunk, (c + 1) * cols_chunk) for c in range(CHUNKS)]

    partial_sketch = 0.0
    orders = orders_of("row")
    step = cols_here // SKETCH_CHUNKS
    for c in range(SKETCH_CHUNKS):
        span, order = slice(c * step, (c + 1) * step), orders[c % 2]
        local_cols = lax.dot_general(
            activations[:, span],
            start_sketch,
            (((0,), (0,)), ((), ())),
            preferred_element_type=jnp.float32,
        )
        partial_sketch = partial_sketch + jnp.dot(
            activations[:, span],
            sum_and_share(local_cols, "row", order, 1.0 / root_rows),
            preferred_element_type=jnp.float32,
        )
    other_sketch = swap(partial_sketch, "col", 1)
    sketch = (partial_sketch + other_sketch) / total_cols

    local_gram = lax.dot_general(
        sketch, sketch, (((0,), (0,)), ((), ())), precision=lax.Precision.HIGHEST
    )
    gram = exchange_sum(local_gram, "row")
    basis, local_proj = make_basis(
        gram, partial_sketch, other_sketch, activations, total_cols, root_rows
    )

    pieces = []
    for span in spans:
        blocks = local_proj[:, span].reshape(parts, width // parts, cols_chunk)
        pieces.append(scatter_sum(blocks, "row") / total_rows)
    return (basis, jnp.concatenate(pieces, axis=1))


def solution(mesh):
    return jax.shard_map(
        per_device,
        mesh=mesh,
        in_specs=(P(("grp", "row"), "col"), P(("grp", "row"), None)),
        out_specs=(P(("grp", "row"), None), P(("grp", "row"), "col")),
        check_vma=False,
    )
```

```python
import functools
import math

import jax
import jax.numpy as jnp
from jax import lax
from jax.experimental import pallas as pl
from jax.experimental.pallas import tpu as pltpu
from jax.sharding import PartitionSpec as P

SKETCH_CHUNKS = 4
CHUNKS = 2
TILE = 512
KERNEL_VMEM = 50 * 2**20


def levels_of(size):
    levels, stride = [], 1
    while stride < size:
        radix = 2 if stride == 1 else min(4, size // stride)
        levels.append((stride, radix))
        stride *= radix
    return levels


def swap(value, axis, distance):
    size = lax.axis_size(axis)
    return lax.ppermute(value, axis, [(i, i ^ distance) for i in range(size)])


def exchange_sum(value, axis):
    step = 1
    while step < lax.axis_size(axis):
        value = value + swap(value, axis, step)
        step *= 2
    return value


def digit_of(axis, stride, radix):
    return lax.rem(lax.div(lax.axis_index(axis), stride), radix)


def scatter_level(blocks, axis, stride, radix):
    digit = digit_of(axis, stride, radix)
    view = blocks.reshape((blocks.shape[0] // radix, radix) + blocks.shape[1:])
    total = lax.dynamic_index_in_dim(view, digit, 1, keepdims=False)
    for t in range(1, radix):
        part = lax.dynamic_index_in_dim(view, jnp.bitwise_xor(digit, t), 1, keepdims=False)
        landed = swap(part.astype(jnp.bfloat16), axis, t * stride)
        total = total + landed.astype(jnp.float32)
    return total


def scatter_sum(blocks, axis):
    for stride, radix in levels_of(lax.axis_size(axis)):
        blocks = scatter_level(blocks, axis, stride, radix)
    return blocks[0]


def bit_of(axis, bit):
    return lax.rem(lax.div(lax.axis_index(axis), 1 << bit), 2)


def sum_and_share(value, axis, order, scale):
    for bit in order[:-1]:
        upper = bit_of(axis, bit) == 1
        half = value.shape[1] // 2
        low, high = value[:, :half], value[:, half:]
        send = jnp.where(upper, low, high).astype(jnp.bfloat16)
        landed = swap(send, axis, 1 << bit)
        value = jnp.where(upper, high, low) + landed.astype(jnp.float32)
    landed = swap(value.astype(jnp.bfloat16), axis, 1 << order[-1])
    block = ((value + landed.astype(jnp.float32)) * scale).astype(jnp.bfloat16)
    for bit in reversed(order[:-1]):
        upper = bit_of(axis, bit) == 1
        other = swap(block, axis, 1 << bit)
        block = jnp.concatenate(
            [jnp.where(upper, other, block), jnp.where(upper, block, other)], axis=1
        )
    return block


def orders_of(axis):
    bits = list(range((lax.axis_size(axis) - 1).bit_length()))
    if len(bits) < 3:
        return [bits, bits]
    return [bits, [bits[1], bits[0]] + bits[2:]]


def fetch_tiles(slab_ref, buffer, arrived):
    copies = []
    for tile in range(buffer.shape[0]):
        span = pl.ds(tile * TILE, TILE)
        copies.append(
            pltpu.make_async_copy(slab_ref.at[:, span], buffer.at[tile], arrived.at[tile])
        )
    for copy in copies:
        copy.start()
    return copies


def sketch_kernel(start_ref, slab_ref, *refs):
    outs, (start_buffer, buffer, start_here, arrived) = refs[:-4], refs[-4:]
    start = pltpu.make_async_copy(start_ref, start_buffer, start_here)
    start.start()
    copies = fetch_tiles(slab_ref, buffer, arrived)
    start.wait()
    left = start_buffer[...].T
    for tile, copy in enumerate(copies):
        copy.wait()
        out, inner = divmod(tile * TILE, outs[0].shape[1])
        outs[out][:, inner : inner + TILE] = lax.dot_general(
            left, buffer[tile], (((1,), (0,)), ((), ())), preferred_element_type=jnp.float32
        )


def first_product(start, slab, chunks):
    rows, width = start.shape
    cols = slab.shape[1]
    return pl.pallas_call(
        sketch_kernel,
        out_shape=[jax.ShapeDtypeStruct((width, cols // chunks), jnp.float32)] * chunks,
        in_specs=[pl.BlockSpec(memory_space=pl.ANY)] * 2,
        out_specs=[pl.BlockSpec(memory_space=pltpu.VMEM)] * chunks,
        scratch_shapes=[
            pltpu.VMEM((rows, width), jnp.bfloat16),
            pltpu.VMEM((cols // TILE, rows, TILE), jnp.bfloat16),
            pltpu.SemaphoreType.DMA,
            pltpu.SemaphoreType.DMA((cols // TILE,)),
        ],
        compiler_params=pltpu.CompilerParams(vmem_limit_bytes=KERNEL_VMEM),
        cost_estimate=pl.CostEstimate(
            flops=2 * rows * width * cols, bytes_accessed=2 * rows * cols, transcendentals=0
        ),
        name="first_product",
    )(start, slab)


def matmul(left, right, exact=True):
    if not exact:
        left, right = left.astype(jnp.bfloat16), right.astype(jnp.bfloat16)
    return lax.dot_general(
        left,
        right,
        (((1,), (0,)), ((), ())),
        precision=lax.Precision.HIGHEST if exact else None,
        preferred_element_type=jnp.float32,
    )


def matmul_t(left, right, exact=True):
    if not exact:
        left, right = left.astype(jnp.bfloat16), right.astype(jnp.bfloat16)
    return lax.dot_general(
        left,
        right,
        (((1,), (1,)), ((), ())),
        precision=lax.Precision.HIGHEST if exact else None,
        preferred_element_type=jnp.float32,
    )


UPDATES = 4
LOOSE_UPDATES = 2
CLOSE = 1e-5


def basis_kernel(
    total_cols, root_rows, gram_ref, mine_ref, other_ref, slab_ref,
    basis_ref, product_ref, work_ref, inverse_ref, buffer, arrived,
):
    copies = fetch_tiles(slab_ref, buffer, arrived)
    width = gram_ref.shape[0]
    row = lax.broadcasted_iota(jnp.int32, (width, width), 0)
    col = lax.broadcasted_iota(jnp.int32, (width, width), 1)
    on_diag = row == col
    unit = jnp.where(on_diag, 1.0, 0.0)
    half = jnp.where(row > col, 1.0, jnp.where(on_diag, 0.5, 0.0))

    gram = gram_ref[...]
    diagonal = jnp.where(on_diag, gram, 0.0)
    down = lax.rsqrt(jnp.sum(diagonal, axis=1, keepdims=True))
    across = lax.rsqrt(jnp.sum(diagonal, axis=0, keepdims=True))
    scaled = gram * down * across

    error = scaled - unit
    step = error * half
    inverse = unit - step + matmul(step, step, False)
    for update in range(1, UPDATES):
        exact = update >= LOOSE_UPDATES
        error = matmul_t(matmul(inverse, scaled, exact), inverse, exact) - unit
        step = error * half
        inverse = inverse - matmul(step, inverse - matmul(step, inverse, exact), exact)
    inverse_ref[...] = inverse * across
    far = jnp.sum(error * error)

    @pl.when(jnp.logical_not(far <= CLOSE))
    def _():
        work_ref[...] = gram
        inverse_ref[...] = unit

        def eliminate(k, carry):
            whole = work_ref[...]
            pivot_row = work_ref[pl.ds(k, 1), :]
            pivot = jnp.sum(
                jnp.where(col[:1] == k, pivot_row, 0.0), axis=1, keepdims=True
            )
            column = jnp.sum(jnp.where(col == k, whole, 0.0), axis=1, keepdims=True)
            factor = jnp.where(row[:, :1] > k, column / pivot, 0.0)
            work_ref[...] = whole - factor * pivot_row
            inverse_ref[...] = inverse_ref[...] - factor * inverse_ref[pl.ds(k, 1), :]
            return carry

        lax.fori_loop(0, width, eliminate, 0)
        pivots = jnp.sum(jnp.where(on_diag, work_ref[...], 0.0), axis=1, keepdims=True)
        inverse_ref[...] = inverse_ref[...] * lax.rsqrt(pivots)

    sketch = (mine_ref[...] + other_ref[...]) / total_cols
    basis = matmul_t(sketch, inverse_ref[...]) * root_rows
    basis_ref[...] = basis
    high = basis.astype(jnp.bfloat16)
    low = (basis - high.astype(jnp.float32)).astype(jnp.bfloat16)
    pair = jnp.concatenate([high, low], axis=1).T
    for tile, copy in enumerate(copies):
        copy.wait()
        both = lax.dot_general(
            pair, buffer[tile], (((1,), (0,)), ((), ())), preferred_element_type=jnp.float32
        )
        product_ref[:, tile * TILE : (tile + 1) * TILE] = both[:width] + both[width:]


def make_basis(gram, mine, other, slab, total_cols, root_rows):
    rows, width = mine.shape
    return pl.pallas_call(
        functools.partial(basis_kernel, total_cols, root_rows),
        out_shape=(
            jax.ShapeDtypeStruct((rows, width), jnp.float32),
            jax.ShapeDtypeStruct((width, slab.shape[1]), jnp.float32),
        ),
        in_specs=[pl.BlockSpec(memory_space=pltpu.VMEM)] * 3
        + [pl.BlockSpec(memory_space=pl.ANY)],
        out_specs=[pl.BlockSpec(memory_space=pltpu.VMEM)] * 2,
        scratch_shapes=[
            pltpu.VMEM((width, width), jnp.float32),
            pltpu.VMEM((width, width), jnp.float32),
            pltpu.VMEM((slab.shape[1] // TILE, rows, TILE), jnp.bfloat16),
            pltpu.SemaphoreType.DMA((slab.shape[1] // TILE,)),
        ],
        compiler_params=pltpu.CompilerParams(vmem_limit_bytes=KERNEL_VMEM),
        name="make_basis",
    )(gram, mine, other, slab)


def per_device(activations, start_sketch):
    rows_here, cols_here = activations.shape
    width = start_sketch.shape[1]
    parts = lax.axis_size("row")
    total_rows = rows_here * parts
    total_cols = cols_here * lax.axis_size("col")
    root_rows = math.sqrt(total_rows)

    cols_chunk = cols_here // CHUNKS
    spans = [slice(c * cols_chunk, (c + 1) * cols_chunk) for c in range(CHUNKS)]

    local_cols = first_product(start_sketch, activations, SKETCH_CHUNKS)
    partial_sketch = 0.0
    orders = orders_of("row")
    step = cols_here // SKETCH_CHUNKS
    for c in range(SKETCH_CHUNKS):
        span = slice(c * step, (c + 1) * step)
        shared = sum_and_share(local_cols[c], "row", orders[c % 2], 1.0 / root_rows)
        partial_sketch = partial_sketch + lax.dot_general(
            activations[:, span],
            shared,
            (((1,), (1,)), ((), ())),
            preferred_element_type=jnp.float32,
        )
    other_sketch = swap(partial_sketch, "col", 1)
    sketch = (partial_sketch + other_sketch) / total_cols

    local_gram = lax.dot_general(
        sketch, sketch, (((0,), (0,)), ((), ())), precision=lax.Precision.HIGHEST
    )
    gram = exchange_sum(local_gram, "row")
    basis, local_proj = make_basis(
        gram, partial_sketch, other_sketch, activations, total_cols, root_rows
    )

    pieces = []
    for span in spans:
        blocks = local_proj[:, span].reshape(parts, width // parts, cols_chunk)
        pieces.append(scatter_sum(blocks, "row") / total_rows)
    return (basis, jnp.concatenate(pieces, axis=1))


def solution(mesh):
    return jax.shard_map(
        per_device,
        mesh=mesh,
        in_specs=(P(("grp", "row"), "col"), P(("grp", "row"), None)),
        out_specs=(P(("grp", "row"), None), P(("grp", "row"), "col")),
        check_vma=False,
    )
```

```python
import functools
import math

import jax
import jax.numpy as jnp
from jax import lax
from jax.experimental import pallas as pl
from jax.experimental.pallas import tpu as pltpu
from jax.sharding import PartitionSpec as P

SKETCH_CHUNKS = 4
CHUNKS = 2
TILE = 512
KERNEL_VMEM = 50 * 2**20


def levels_of(size):
    levels, stride = [], 1
    while stride < size:
        radix = 2 if stride == 1 else min(4, size // stride)
        levels.append((stride, radix))
        stride *= radix
    return levels


def swap(value, axis, distance):
    size = lax.axis_size(axis)
    return lax.ppermute(value, axis, [(i, i ^ distance) for i in range(size)])


def exchange_sum(value, axis):
    for stride, radix in levels_of(lax.axis_size(axis)):
        terms = [value] + [swap(value, axis, t * stride) for t in range(1, radix)]
        while len(terms) > 1:
            terms = [terms[i] + terms[i + 1] for i in range(0, len(terms), 2)]
        value = terms[0]
    return value


def digit_of(axis, stride, radix):
    return lax.rem(lax.div(lax.axis_index(axis), stride), radix)


def scatter_level(blocks, axis, stride, radix):
    digit = digit_of(axis, stride, radix)
    view = blocks.reshape((blocks.shape[0] // radix, radix) + blocks.shape[1:])
    total = lax.dynamic_index_in_dim(view, digit, 1, keepdims=False)
    for t in range(1, radix):
        part = lax.dynamic_index_in_dim(view, jnp.bitwise_xor(digit, t), 1, keepdims=False)
        landed = swap(part.astype(jnp.bfloat16), axis, t * stride)
        total = total + landed.astype(jnp.float32)
    return total


def scatter_sum(blocks, axis):
    for stride, radix in levels_of(lax.axis_size(axis)):
        blocks = scatter_level(blocks, axis, stride, radix)
    return blocks[0]


def bit_of(axis, bit):
    return lax.rem(lax.div(lax.axis_index(axis), 1 << bit), 2)


def sum_and_share(value, axis, order, scale):
    for bit in order[:-1]:
        upper = bit_of(axis, bit) == 1
        half = value.shape[1] // 2
        low, high = value[:, :half], value[:, half:]
        send = jnp.where(upper, low, high).astype(jnp.bfloat16)
        landed = swap(send, axis, 1 << bit)
        value = jnp.where(upper, high, low) + landed.astype(jnp.float32)
    landed = swap(value.astype(jnp.bfloat16), axis, 1 << order[-1])
    block = ((value + landed.astype(jnp.float32)) * scale).astype(jnp.bfloat16)
    for bit in reversed(order[:-1]):
        upper = bit_of(axis, bit) == 1
        other = swap(block, axis, 1 << bit)
        block = jnp.concatenate(
            [jnp.where(upper, other, block), jnp.where(upper, block, other)], axis=1
        )
    return block


def orders_of(axis):
    bits = list(range((lax.axis_size(axis) - 1).bit_length()))
    if len(bits) < 3:
        return [bits, bits]
    return [bits, [bits[1], bits[0]] + bits[2:]]


def fetch_tiles(slab_ref, buffer, arrived):
    copies = []
    for tile in range(buffer.shape[0]):
        span = pl.ds(tile * TILE, TILE)
        copies.append(
            pltpu.make_async_copy(slab_ref.at[:, span], buffer.at[tile], arrived.at[tile])
        )
    for copy in copies:
        copy.start()
    return copies


def sketch_kernel(start_ref, slab_ref, *refs):
    outs, (buffer, arrived) = refs[:-2], refs[-2:]
    copies = fetch_tiles(slab_ref, buffer, arrived)
    left = start_ref[...].T
    for tile, copy in enumerate(copies):
        copy.wait()
        out, inner = divmod(tile * TILE, outs[0].shape[1])
        outs[out][:, inner : inner + TILE] = lax.dot_general(
            left, buffer[tile], (((1,), (0,)), ((), ())), preferred_element_type=jnp.float32
        )


def first_product(start, slab, chunks):
    rows, width = start.shape
    cols = slab.shape[1]
    return pl.pallas_call(
        sketch_kernel,
        out_shape=[jax.ShapeDtypeStruct((width, cols // chunks), jnp.float32)] * chunks,
        in_specs=[
            pl.BlockSpec(memory_space=pltpu.VMEM),
            pl.BlockSpec(memory_space=pl.ANY),
        ],
        out_specs=[pl.BlockSpec(memory_space=pltpu.VMEM)] * chunks,
        scratch_shapes=[
            pltpu.VMEM((cols // TILE, rows, TILE), jnp.bfloat16),
            pltpu.SemaphoreType.DMA((cols // TILE,)),
        ],
        compiler_params=pltpu.CompilerParams(vmem_limit_bytes=KERNEL_VMEM),
        cost_estimate=pl.CostEstimate(
            flops=2 * rows * width * cols, bytes_accessed=2 * rows * cols, transcendentals=0
        ),
        name="first_product",
    )(start, slab)


def matmul(left, right, exact=True):
    if not exact:
        left, right = left.astype(jnp.bfloat16), right.astype(jnp.bfloat16)
    return lax.dot_general(
        left,
        right,
        (((1,), (0,)), ((), ())),
        precision=lax.Precision.HIGHEST if exact else None,
        preferred_element_type=jnp.float32,
    )


def matmul_t(left, right, exact=True):
    if not exact:
        left, right = left.astype(jnp.bfloat16), right.astype(jnp.bfloat16)
    return lax.dot_general(
        left,
        right,
        (((1,), (1,)), ((), ())),
        precision=lax.Precision.HIGHEST if exact else None,
        preferred_element_type=jnp.float32,
    )


def gram_kernel(total_cols, mine_ref, other_ref, packed_ref):
    sketch = (mine_ref[...] + other_ref[...]) / total_cols
    gram = matmul(sketch.T, sketch)
    half = gram.shape[0] // 2
    row = lax.broadcasted_iota(jnp.int32, (half, 2 * half), 0)
    col = lax.broadcasted_iota(jnp.int32, (half, 2 * half), 1)
    top, bottom = gram[:half], pltpu.roll(gram[half:], half, 1)
    packed_ref[:half] = jnp.where(row > col, bottom, top)
    diagonal = jnp.sum(jnp.where(row == col, bottom, 0.0), axis=0, keepdims=True)
    packed_ref[half:] = jnp.broadcast_to(diagonal, (8, 2 * half))


def unpack_gram(packed):
    width = packed.shape[1]
    half = width // 2
    row = lax.broadcasted_iota(jnp.int32, (half, width), 0)
    col = lax.broadcasted_iota(jnp.int32, (half, width), 1)
    square = packed[:half]
    top = jnp.where(row > col, 0.0, square)
    lower = jnp.where(row > col, square, jnp.where(row == col, packed[half : half + 1], 0.0))
    parts = jnp.concatenate([top, pltpu.roll(lower, half, 1)], axis=0)
    row = lax.broadcasted_iota(jnp.int32, (width, width), 0)
    col = lax.broadcasted_iota(jnp.int32, (width, width), 1)
    return jnp.where(row == col, parts, parts + parts.T)


def make_gram(mine, other, total_cols):
    rows, width = mine.shape
    return pl.pallas_call(
        functools.partial(gram_kernel, total_cols),
        out_shape=jax.ShapeDtypeStruct((width // 2 + 8, width), jnp.float32),
        in_specs=[pl.BlockSpec(memory_space=pltpu.VMEM)] * 2,
        out_specs=pl.BlockSpec(memory_space=pltpu.VMEM),
        compiler_params=pltpu.CompilerParams(vmem_limit_bytes=16 * 2**20),
        name="make_gram",
    )(mine, other)


UPDATES = 4
LOOSE_UPDATES = 2
CLOSE = 1e-5


def basis_kernel(
    total_cols, root_rows, gram_ref, mine_ref, other_ref, slab_ref,
    basis_ref, product_ref, work_ref, inverse_ref, buffer, arrived,
):
    fetch = pltpu.make_async_copy(slab_ref, buffer, arrived)
    fetch.start()
    width = gram_ref.shape[1]
    row = lax.broadcasted_iota(jnp.int32, (width, width), 0)
    col = lax.broadcasted_iota(jnp.int32, (width, width), 1)
    on_diag = row == col
    unit = jnp.where(on_diag, 1.0, 0.0)
    half = jnp.where(row > col, 1.0, jnp.where(on_diag, 0.5, 0.0))

    gram = unpack_gram(gram_ref[...])
    diagonal = jnp.where(on_diag, gram, 0.0)
    down = lax.rsqrt(jnp.sum(diagonal, axis=1, keepdims=True))
    across = lax.rsqrt(jnp.sum(diagonal, axis=0, keepdims=True))
    scaled = gram * down * across

    error = scaled - unit
    step = error * half
    inverse = unit - step + matmul(step, step, False)
    for update in range(1, UPDATES):
        exact = update >= LOOSE_UPDATES
        error = matmul_t(matmul(inverse, scaled, exact), inverse, exact) - unit
        step = error * half
        inverse = inverse - matmul(step, inverse - matmul(step, inverse, exact), exact)
    inverse_ref[...] = inverse * across
    far = jnp.sum(error * error)

    @pl.when(jnp.logical_not(far <= CLOSE))
    def _():
        work_ref[...] = gram
        inverse_ref[...] = unit

        def eliminate(k, carry):
            whole = work_ref[...]
            pivot_row = work_ref[pl.ds(k, 1), :]
            pivot = jnp.sum(
                jnp.where(col[:1] == k, pivot_row, 0.0), axis=1, keepdims=True
            )
            column = jnp.sum(jnp.where(col == k, whole, 0.0), axis=1, keepdims=True)
            factor = jnp.where(row[:, :1] > k, column / pivot, 0.0)
            work_ref[...] = whole - factor * pivot_row
            inverse_ref[...] = inverse_ref[...] - factor * inverse_ref[pl.ds(k, 1), :]
            return carry

        lax.fori_loop(0, width, eliminate, 0)
        pivots = jnp.sum(jnp.where(on_diag, work_ref[...], 0.0), axis=1, keepdims=True)
        inverse_ref[...] = inverse_ref[...] * lax.rsqrt(pivots)

    sketch = (mine_ref[...] + other_ref[...]) / total_cols
    basis = matmul_t(sketch, inverse_ref[...]) * root_rows
    basis_ref[...] = basis
    high = basis.astype(jnp.bfloat16)
    low = (basis - high.astype(jnp.float32)).astype(jnp.bfloat16)
    pair = jnp.concatenate([high, low], axis=1).T
    fetch.wait()
    for start in range(0, buffer.shape[1], TILE):
        both = lax.dot_general(
            pair,
            buffer[:, start : start + TILE],
            (((1,), (0,)), ((), ())),
            preferred_element_type=jnp.float32,
        )
        product_ref[:, start : start + TILE] = both[:width] + both[width:]


def make_basis(gram, mine, other, slab, total_cols, root_rows):
    rows, width = mine.shape
    return pl.pallas_call(
        functools.partial(basis_kernel, total_cols, root_rows),
        out_shape=(
            jax.ShapeDtypeStruct((rows, width), jnp.float32),
            jax.ShapeDtypeStruct((width, slab.shape[1]), jnp.float32),
        ),
        in_specs=[pl.BlockSpec(memory_space=pltpu.VMEM)] * 3
        + [pl.BlockSpec(memory_space=pl.ANY)],
        out_specs=[pl.BlockSpec(memory_space=pltpu.VMEM)] * 2,
        scratch_shapes=[
            pltpu.VMEM((width, width), jnp.float32),
            pltpu.VMEM((width, width), jnp.float32),
            pltpu.VMEM(slab.shape, jnp.bfloat16),
            pltpu.SemaphoreType.DMA,
        ],
        compiler_params=pltpu.CompilerParams(vmem_limit_bytes=KERNEL_VMEM),
        name="make_basis",
    )(gram, mine, other, slab)


def per_device(activations, start_sketch):
    rows_here, cols_here = activations.shape
    width = start_sketch.shape[1]
    parts = lax.axis_size("row")
    total_rows = rows_here * parts
    total_cols = cols_here * lax.axis_size("col")
    root_rows = math.sqrt(total_rows)

    cols_chunk = cols_here // CHUNKS
    spans = [slice(c * cols_chunk, (c + 1) * cols_chunk) for c in range(CHUNKS)]

    local_cols = first_product(start_sketch, activations, SKETCH_CHUNKS)
    partial_sketch = 0.0
    orders = orders_of("row")
    step = cols_here // SKETCH_CHUNKS
    for c in range(SKETCH_CHUNKS):
        span = slice(c * step, (c + 1) * step)
        shared = sum_and_share(local_cols[c], "row", orders[c % 2], 1.0 / root_rows)
        partial_sketch = partial_sketch + lax.dot_general(
            activations[:, span],
            shared,
            (((1,), (1,)), ((), ())),
            preferred_element_type=jnp.float32,
        )
    other_sketch = swap(partial_sketch, "col", 1)
    gram = exchange_sum(make_gram(partial_sketch, other_sketch, total_cols), "row")
    basis, local_proj = make_basis(
        gram, partial_sketch, other_sketch, activations, total_cols, root_rows
    )

    pieces = []
    for span in spans:
        blocks = local_proj[:, span].reshape(parts, width // parts, cols_chunk)
        pieces.append(scatter_sum(blocks, "row") / total_rows)
    return (basis, jnp.concatenate(pieces, axis=1))


def solution(mesh):
    return jax.shard_map(
        per_device,
        mesh=mesh,
        in_specs=(P(("grp", "row"), "col"), P(("grp", "row"), None)),
        out_specs=(P(("grp", "row"), None), P(("grp", "row"), "col")),
        check_vma=False,
    )
```

```python
import functools
import math

import jax
import jax.numpy as jnp
from jax import lax
from jax.experimental import pallas as pl
from jax.experimental.pallas import tpu as pltpu
from jax.sharding import PartitionSpec as P

SKETCH_CHUNKS = 2
CHUNKS = 2
TILE = 512
KERNEL_VMEM = 50 * 2**20


def levels_of(size):
    levels, stride = [], 1
    while stride < size:
        radix = 2 if stride == 1 else min(4, size // stride)
        levels.append((stride, radix))
        stride *= radix
    return levels


def swap(value, axis, distance):
    size = lax.axis_size(axis)
    return lax.ppermute(value, axis, [(i, i ^ distance) for i in range(size)])


def exchange_sum(value, axis):
    for stride, radix in levels_of(lax.axis_size(axis)):
        terms = [value] + [swap(value, axis, t * stride) for t in range(1, radix)]
        while len(terms) > 1:
            terms = [terms[i] + terms[i + 1] for i in range(0, len(terms), 2)]
        value = terms[0]
    return value


def digit_of(axis, stride, radix):
    return lax.rem(lax.div(lax.axis_index(axis), stride), radix)


def scatter_level(blocks, axis, stride, radix):
    digit = digit_of(axis, stride, radix)
    view = blocks.reshape((blocks.shape[0] // radix, radix) + blocks.shape[1:])
    total = lax.dynamic_index_in_dim(view, digit, 1, keepdims=False)
    for t in range(1, radix):
        part = lax.dynamic_index_in_dim(view, jnp.bitwise_xor(digit, t), 1, keepdims=False)
        landed = swap(part.astype(jnp.bfloat16), axis, t * stride)
        total = total + landed.astype(jnp.float32)
    return total


def scatter_sum(blocks, axis):
    for stride, radix in levels_of(lax.axis_size(axis)):
        blocks = scatter_level(blocks, axis, stride, radix)
    return blocks[0]


def orders_of(size):
    bits = list(range((size - 1).bit_length()))
    return [bits, [bits[1], bits[0]] + bits[2:] if len(bits) > 2 else bits]


def core_swap(value, bits):
    rows, cores = lax.axis_size("row"), lax.axis_size("col")
    pairs = [
        (row * cores + core, (row ^ (1 << bits[core % 2])) * cores + core)
        for row in range(rows)
        for core in range(cores)
    ]
    return lax.ppermute(value, ("row", "col"), pairs)


def core_upper(bits):
    odd = lax.rem(lax.axis_index("col"), 2) == 1
    weight = jnp.where(odd, 1 << bits[1], 1 << bits[0])
    return jnp.bitwise_and(lax.axis_index("row"), weight) != 0


def sum_and_share(value, scale):
    steps = list(zip(*orders_of(lax.axis_size("row"))))
    for bits in steps[:-1]:
        upper = core_upper(bits)
        half = value.shape[1] // 2
        low, high = value[:, :half], value[:, half:]
        send = jnp.where(upper, low, high).astype(jnp.bfloat16)
        landed = core_swap(send, bits)
        value = jnp.where(upper, high, low) + landed.astype(jnp.float32)
    landed = core_swap(value.astype(jnp.bfloat16), steps[-1])
    block = ((value + landed.astype(jnp.float32)) * scale).astype(jnp.bfloat16)
    for bits in reversed(steps[:-1]):
        upper = core_upper(bits)
        other = core_swap(block, bits)
        block = jnp.concatenate(
            [jnp.where(upper, other, block), jnp.where(upper, block, other)], axis=1
        )
    return block


def fetch_tiles(slab_ref, buffer, arrived):
    copies = []
    for tile in range(buffer.shape[0]):
        span = pl.ds(tile * TILE, TILE)
        copies.append(
            pltpu.make_async_copy(slab_ref.at[:, span], buffer.at[tile], arrived.at[tile])
        )
    for copy in copies:
        copy.start()
    return copies


def sketch_kernel(start_ref, slab_ref, *refs):
    outs, (buffer, arrived) = refs[:-2], refs[-2:]
    copies = fetch_tiles(slab_ref, buffer, arrived)
    left = start_ref[...].T
    for tile, copy in enumerate(copies):
        copy.wait()
        out, inner = divmod(tile * TILE, outs[0].shape[1])
        outs[out][:, inner : inner + TILE] = lax.dot_general(
            left, buffer[tile], (((1,), (0,)), ((), ())), preferred_element_type=jnp.float32
        )


def first_product(start, slab, chunks):
    rows, width = start.shape
    cols = slab.shape[1]
    return pl.pallas_call(
        sketch_kernel,
        out_shape=[jax.ShapeDtypeStruct((width, cols // chunks), jnp.float32)] * chunks,
        in_specs=[
            pl.BlockSpec(memory_space=pltpu.VMEM),
            pl.BlockSpec(memory_space=pl.ANY),
        ],
        out_specs=[pl.BlockSpec(memory_space=pltpu.VMEM)] * chunks,
        scratch_shapes=[
            pltpu.VMEM((cols // TILE, rows, TILE), jnp.bfloat16),
            pltpu.SemaphoreType.DMA((cols // TILE,)),
        ],
        compiler_params=pltpu.CompilerParams(vmem_limit_bytes=KERNEL_VMEM),
        cost_estimate=pl.CostEstimate(
            flops=2 * rows * width * cols, bytes_accessed=2 * rows * cols, transcendentals=0
        ),
        name="first_product",
    )(start, slab)


def matmul(left, right, exact=True):
    if not exact:
        left, right = left.astype(jnp.bfloat16), right.astype(jnp.bfloat16)
    return lax.dot_general(
        left,
        right,
        (((1,), (0,)), ((), ())),
        precision=lax.Precision.HIGHEST if exact else None,
        preferred_element_type=jnp.float32,
    )


def matmul_t(left, right, exact=True):
    if not exact:
        left, right = left.astype(jnp.bfloat16), right.astype(jnp.bfloat16)
    return lax.dot_general(
        left,
        right,
        (((1,), (1,)), ((), ())),
        precision=lax.Precision.HIGHEST if exact else None,
        preferred_element_type=jnp.float32,
    )


def gram_kernel(total_cols, mine_ref, other_ref, packed_ref):
    sketch = (mine_ref[...] + other_ref[...]) / total_cols
    gram = matmul(sketch.T, sketch)
    half = gram.shape[0] // 2
    row = lax.broadcasted_iota(jnp.int32, (half, 2 * half), 0)
    col = lax.broadcasted_iota(jnp.int32, (half, 2 * half), 1)
    top, bottom = gram[:half], pltpu.roll(gram[half:], half, 1)
    packed_ref[:half] = jnp.where(row > col, bottom, top)
    diagonal = jnp.sum(jnp.where(row == col, bottom, 0.0), axis=0, keepdims=True)
    packed_ref[half:] = jnp.broadcast_to(diagonal, (8, 2 * half))


def unpack_gram(packed):
    width = packed.shape[1]
    half = width // 2
    row = lax.broadcasted_iota(jnp.int32, (half, width), 0)
    col = lax.broadcasted_iota(jnp.int32, (half, width), 1)
    square = packed[:half]
    top = jnp.where(row > col, 0.0, square)
    lower = jnp.where(row > col, square, jnp.where(row == col, packed[half : half + 1], 0.0))
    parts = jnp.concatenate([top, pltpu.roll(lower, half, 1)], axis=0)
    row = lax.broadcasted_iota(jnp.int32, (width, width), 0)
    col = lax.broadcasted_iota(jnp.int32, (width, width), 1)
    return jnp.where(row == col, parts, parts + parts.T)


def make_gram(mine, other, total_cols):
    rows, width = mine.shape
    return pl.pallas_call(
        functools.partial(gram_kernel, total_cols),
        out_shape=jax.ShapeDtypeStruct((width // 2 + 8, width), jnp.float32),
        in_specs=[pl.BlockSpec(memory_space=pltpu.VMEM)] * 2,
        out_specs=pl.BlockSpec(memory_space=pltpu.VMEM),
        compiler_params=pltpu.CompilerParams(vmem_limit_bytes=16 * 2**20),
        name="make_gram",
    )(mine, other)


UPDATES = 4
LOOSE_UPDATES = 2
CLOSE = 1e-5


def basis_kernel(
    total_cols, root_rows, gram_ref, mine_ref, other_ref, slab_ref,
    basis_ref, product_ref, work_ref, inverse_ref, buffer, arrived,
):
    fetch = pltpu.make_async_copy(slab_ref, buffer, arrived)
    fetch.start()
    width = gram_ref.shape[1]
    row = lax.broadcasted_iota(jnp.int32, (width, width), 0)
    col = lax.broadcasted_iota(jnp.int32, (width, width), 1)
    on_diag = row == col
    unit = jnp.where(on_diag, 1.0, 0.0)
    half = jnp.where(row > col, 1.0, jnp.where(on_diag, 0.5, 0.0))

    gram = unpack_gram(gram_ref[...])
    diagonal = jnp.where(on_diag, gram, 0.0)
    down = lax.rsqrt(jnp.sum(diagonal, axis=1, keepdims=True))
    across = lax.rsqrt(jnp.sum(diagonal, axis=0, keepdims=True))
    scaled = gram * down * across

    error = scaled - unit
    step = error * half
    inverse = unit - step + matmul(step, step, False)
    for update in range(1, UPDATES):
        exact = update >= LOOSE_UPDATES
        error = matmul_t(matmul(inverse, scaled, exact), inverse, exact) - unit
        step = error * half
        inverse = inverse - matmul(step, inverse - matmul(step, inverse, exact), exact)
    inverse_ref[...] = inverse * across
    far = jnp.sum(error * error)

    @pl.when(jnp.logical_not(far <= CLOSE))
    def _():
        work_ref[...] = gram
        inverse_ref[...] = unit

        def eliminate(k, carry):
            whole = work_ref[...]
            pivot_row = work_ref[pl.ds(k, 1), :]
            pivot = jnp.sum(
                jnp.where(col[:1] == k, pivot_row, 0.0), axis=1, keepdims=True
            )
            column = jnp.sum(jnp.where(col == k, whole, 0.0), axis=1, keepdims=True)
            factor = jnp.where(row[:, :1] > k, column / pivot, 0.0)
            work_ref[...] = whole - factor * pivot_row
            inverse_ref[...] = inverse_ref[...] - factor * inverse_ref[pl.ds(k, 1), :]
            return carry

        lax.fori_loop(0, width, eliminate, 0)
        pivots = jnp.sum(jnp.where(on_diag, work_ref[...], 0.0), axis=1, keepdims=True)
        inverse_ref[...] = inverse_ref[...] * lax.rsqrt(pivots)

    sketch = (mine_ref[...] + other_ref[...]) / total_cols
    basis = matmul_t(sketch, inverse_ref[...]) * root_rows
    basis_ref[...] = basis
    high = basis.astype(jnp.bfloat16)
    low = (basis - high.astype(jnp.float32)).astype(jnp.bfloat16)
    pair = jnp.concatenate([high, low], axis=1).T
    fetch.wait()
    for start in range(0, buffer.shape[1], TILE):
        both = lax.dot_general(
            pair,
            buffer[:, start : start + TILE],
            (((1,), (0,)), ((), ())),
            preferred_element_type=jnp.float32,
        )
        product_ref[:, start : start + TILE] = both[:width] + both[width:]


def make_basis(gram, mine, other, slab, total_cols, root_rows):
    rows, width = mine.shape
    return pl.pallas_call(
        functools.partial(basis_kernel, total_cols, root_rows),
        out_shape=(
            jax.ShapeDtypeStruct((rows, width), jnp.float32),
            jax.ShapeDtypeStruct((width, slab.shape[1]), jnp.float32),
        ),
        in_specs=[pl.BlockSpec(memory_space=pltpu.VMEM)] * 3
        + [pl.BlockSpec(memory_space=pl.ANY)],
        out_specs=[pl.BlockSpec(memory_space=pltpu.VMEM)] * 2,
        scratch_shapes=[
            pltpu.VMEM((width, width), jnp.float32),
            pltpu.VMEM((width, width), jnp.float32),
            pltpu.VMEM(slab.shape, jnp.bfloat16),
            pltpu.SemaphoreType.DMA,
        ],
        compiler_params=pltpu.CompilerParams(vmem_limit_bytes=KERNEL_VMEM),
        name="make_basis",
    )(gram, mine, other, slab)


def per_device(activations, start_sketch):
    rows_here, cols_here = activations.shape
    width = start_sketch.shape[1]
    parts = lax.axis_size("row")
    total_rows = rows_here * parts
    total_cols = cols_here * lax.axis_size("col")
    root_rows = math.sqrt(total_rows)

    cols_chunk = cols_here // CHUNKS
    spans = [slice(c * cols_chunk, (c + 1) * cols_chunk) for c in range(CHUNKS)]

    local_cols = first_product(start_sketch, activations, SKETCH_CHUNKS)
    partial_sketch = 0.0
    step = cols_here // SKETCH_CHUNKS
    for c in range(SKETCH_CHUNKS):
        span = slice(c * step, (c + 1) * step)
        shared = sum_and_share(local_cols[c], 1.0 / root_rows)
        partial_sketch = partial_sketch + lax.dot_general(
            activations[:, span],
            shared,
            (((1,), (1,)), ((), ())),
            preferred_element_type=jnp.float32,
        )
    other_sketch = swap(partial_sketch, "col", 1)
    gram = exchange_sum(make_gram(partial_sketch, other_sketch, total_cols), "row")
    basis, local_proj = make_basis(
        gram, partial_sketch, other_sketch, activations, total_cols, root_rows
    )

    pieces = []
    for span in spans:
        blocks = local_proj[:, span].reshape(parts, width // parts, cols_chunk)
        pieces.append(scatter_sum(blocks, "row") / total_rows)
    return (basis, jnp.concatenate(pieces, axis=1))


def solution(mesh):
    return jax.shard_map(
        per_device,
        mesh=mesh,
        in_specs=(P(("grp", "row"), "col"), P(("grp", "row"), None)),
        out_specs=(P(("grp", "row"), None), P(("grp", "row"), "col")),
        check_vma=False,
    )
```

```python
import functools
import math

import jax
import jax.numpy as jnp
from jax import lax
from jax.experimental import pallas as pl
from jax.experimental.pallas import tpu as pltpu
from jax.sharding import PartitionSpec as P

SKETCH_CHUNKS = 4
CHUNKS = 2
TILE = 512
KERNEL_VMEM = 50 * 2**20


def levels_of(size):
    levels, stride = [], 1
    while stride < size:
        radix = 2 if stride == 1 else min(4, size // stride)
        levels.append((stride, radix))
        stride *= radix
    return levels


def swap(value, axis, distance):
    size = lax.axis_size(axis)
    return lax.ppermute(value, axis, [(i, i ^ distance) for i in range(size)])


def row_sum(value):
    rows, cores = lax.axis_size("row"), lax.axis_size("col")
    assert cores == 2
    first = lax.axis_index("col") == 0
    stride = 1
    while stride < rows:
        radix = min(8, rows // stride)
        terms = []
        for t in range(radix // 2):
            pairs = []
            for row in range(rows):
                for core, digit in ((0, t), (1, t + radix // 2)):
                    if digit:
                        pairs.append((row * cores + core, (row ^ digit * stride) * cores + core))
            terms.append(lax.ppermute(value, ("row", "col"), pairs))
        terms[0] = jnp.where(first, value, terms[0])
        while len(terms) > 1:
            terms = [terms[i] + terms[i + 1] for i in range(0, len(terms), 2)]
        value = terms[0] + swap(terms[0], "col", 1)
        stride *= radix
    return value


def digit_of(axis, stride, radix):
    return lax.rem(lax.div(lax.axis_index(axis), stride), radix)


def scatter_level(blocks, axis, stride, radix):
    digit = digit_of(axis, stride, radix)
    view = blocks.reshape((blocks.shape[0] // radix, radix) + blocks.shape[1:])
    total = lax.dynamic_index_in_dim(view, digit, 1, keepdims=False)
    for t in range(1, radix):
        part = lax.dynamic_index_in_dim(view, jnp.bitwise_xor(digit, t), 1, keepdims=False)
        landed = swap(part.astype(jnp.bfloat16), axis, t * stride)
        total = total + landed.astype(jnp.float32)
    return total


def scatter_sum(blocks, axis):
    for stride, radix in levels_of(lax.axis_size(axis)):
        blocks = scatter_level(blocks, axis, stride, radix)
    return blocks[0]


def bit_of(axis, bit):
    return lax.rem(lax.div(lax.axis_index(axis), 1 << bit), 2)


def sum_and_share(value, axis, order, scale):
    for bit in order[:-1]:
        upper = bit_of(axis, bit) == 1
        half = value.shape[1] // 2
        low, high = value[:, :half], value[:, half:]
        send = jnp.where(upper, low, high).astype(jnp.bfloat16)
        landed = swap(send, axis, 1 << bit)
        value = jnp.where(upper, high, low) + landed.astype(jnp.float32)
    landed = swap(value.astype(jnp.bfloat16), axis, 1 << order[-1])
    block = ((value + landed.astype(jnp.float32)) * scale).astype(jnp.bfloat16)
    for bit in reversed(order[:-1]):
        upper = bit_of(axis, bit) == 1
        other = swap(block, axis, 1 << bit)
        block = jnp.concatenate(
            [jnp.where(upper, other, block), jnp.where(upper, block, other)], axis=1
        )
    return block


def orders_of(axis):
    bits = list(range((lax.axis_size(axis) - 1).bit_length()))
    if len(bits) < 3:
        return [bits, bits]
    return [bits, [bits[1], bits[0]] + bits[2:]]


def fetch_tiles(slab_ref, buffer, arrived):
    copies = []
    for tile in range(buffer.shape[0]):
        span = pl.ds(tile * TILE, TILE)
        copies.append(
            pltpu.make_async_copy(slab_ref.at[:, span], buffer.at[tile], arrived.at[tile])
        )
    for copy in copies:
        copy.start()
    return copies


def sketch_kernel(start_ref, slab_ref, *refs):
    outs, (buffer, arrived) = refs[:-2], refs[-2:]
    copies = fetch_tiles(slab_ref, buffer, arrived)
    left = start_ref[...].T
    for tile, copy in enumerate(copies):
        copy.wait()
        out, inner = divmod(tile * TILE, outs[0].shape[1])
        outs[out][:, inner : inner + TILE] = lax.dot_general(
            left, buffer[tile], (((1,), (0,)), ((), ())), preferred_element_type=jnp.float32
        )


def first_product(start, slab, chunks):
    rows, width = start.shape
    cols = slab.shape[1]
    return pl.pallas_call(
        sketch_kernel,
        out_shape=[jax.ShapeDtypeStruct((width, cols // chunks), jnp.float32)] * chunks,
        in_specs=[
            pl.BlockSpec(memory_space=pltpu.VMEM),
            pl.BlockSpec(memory_space=pl.ANY),
        ],
        out_specs=[pl.BlockSpec(memory_space=pltpu.VMEM)] * chunks,
        scratch_shapes=[
            pltpu.VMEM((cols // TILE, rows, TILE), jnp.bfloat16),
            pltpu.SemaphoreType.DMA((cols // TILE,)),
        ],
        compiler_params=pltpu.CompilerParams(vmem_limit_bytes=KERNEL_VMEM),
        cost_estimate=pl.CostEstimate(
            flops=2 * rows * width * cols, bytes_accessed=2 * rows * cols, transcendentals=0
        ),
        name="first_product",
    )(start, slab)


def matmul(left, right, exact=True):
    if not exact:
        left, right = left.astype(jnp.bfloat16), right.astype(jnp.bfloat16)
    return lax.dot_general(
        left,
        right,
        (((1,), (0,)), ((), ())),
        precision=lax.Precision.HIGHEST if exact else None,
        preferred_element_type=jnp.float32,
    )


def matmul_t(left, right, exact=True):
    if not exact:
        left, right = left.astype(jnp.bfloat16), right.astype(jnp.bfloat16)
    return lax.dot_general(
        left,
        right,
        (((1,), (1,)), ((), ())),
        precision=lax.Precision.HIGHEST if exact else None,
        preferred_element_type=jnp.float32,
    )


def gram_kernel(total_cols, mine_ref, other_ref, packed_ref):
    sketch = (mine_ref[...] + other_ref[...]) / total_cols
    gram = matmul(sketch.T, sketch)
    half = gram.shape[0] // 2
    row = lax.broadcasted_iota(jnp.int32, (half, 2 * half), 0)
    col = lax.broadcasted_iota(jnp.int32, (half, 2 * half), 1)
    top, bottom = gram[:half], pltpu.roll(gram[half:], half, 1)
    packed_ref[:half] = jnp.where(row > col, bottom, top)
    diagonal = jnp.sum(jnp.where(row == col, bottom, 0.0), axis=0, keepdims=True)
    packed_ref[half:] = jnp.broadcast_to(diagonal, (8, 2 * half))


def unpack_gram(packed):
    width = packed.shape[1]
    half = width // 2
    row = lax.broadcasted_iota(jnp.int32, (half, width), 0)
    col = lax.broadcasted_iota(jnp.int32, (half, width), 1)
    square = packed[:half]
    top = jnp.where(row > col, 0.0, square)
    lower = jnp.where(row > col, square, jnp.where(row == col, packed[half : half + 1], 0.0))
    parts = jnp.concatenate([top, pltpu.roll(lower, half, 1)], axis=0)
    row = lax.broadcasted_iota(jnp.int32, (width, width), 0)
    col = lax.broadcasted_iota(jnp.int32, (width, width), 1)
    return jnp.where(row == col, parts, parts + parts.T)


def make_gram(mine, other, total_cols):
    rows, width = mine.shape
    return pl.pallas_call(
        functools.partial(gram_kernel, total_cols),
        out_shape=jax.ShapeDtypeStruct((width // 2 + 8, width), jnp.float32),
        in_specs=[pl.BlockSpec(memory_space=pltpu.VMEM)] * 2,
        out_specs=pl.BlockSpec(memory_space=pltpu.VMEM),
        compiler_params=pltpu.CompilerParams(vmem_limit_bytes=16 * 2**20),
        name="make_gram",
    )(mine, other)


UPDATES = 4
LOOSE_UPDATES = 2
CLOSE = 1e-5


def basis_kernel(
    total_cols, root_rows, gram_ref, mine_ref, other_ref, slab_ref,
    basis_ref, product_ref, work_ref, inverse_ref, buffer, arrived,
):
    fetch = pltpu.make_async_copy(slab_ref, buffer, arrived)
    fetch.start()
    width = gram_ref.shape[1]
    row = lax.broadcasted_iota(jnp.int32, (width, width), 0)
    col = lax.broadcasted_iota(jnp.int32, (width, width), 1)
    on_diag = row == col
    unit = jnp.where(on_diag, 1.0, 0.0)
    half = jnp.where(row > col, 1.0, jnp.where(on_diag, 0.5, 0.0))

    gram = unpack_gram(gram_ref[...])
    diagonal = jnp.where(on_diag, gram, 0.0)
    down = lax.rsqrt(jnp.sum(diagonal, axis=1, keepdims=True))
    across = lax.rsqrt(jnp.sum(diagonal, axis=0, keepdims=True))
    scaled = gram * down * across

    error = scaled - unit
    step = error * half
    inverse = unit - step + matmul(step, step, False)
    for update in range(1, UPDATES):
        exact = update >= LOOSE_UPDATES
        error = matmul_t(matmul(inverse, scaled, exact), inverse, exact) - unit
        step = error * half
        inverse = inverse - matmul(step, inverse - matmul(step, inverse, exact), exact)
    inverse_ref[...] = inverse * across
    far = jnp.sum(error * error)

    @pl.when(jnp.logical_not(far <= CLOSE))
    def _():
        work_ref[...] = gram
        inverse_ref[...] = unit

        def eliminate(k, carry):
            whole = work_ref[...]
            pivot_row = work_ref[pl.ds(k, 1), :]
            pivot = jnp.sum(
                jnp.where(col[:1] == k, pivot_row, 0.0), axis=1, keepdims=True
            )
            column = jnp.sum(jnp.where(col == k, whole, 0.0), axis=1, keepdims=True)
            factor = jnp.where(row[:, :1] > k, column / pivot, 0.0)
            work_ref[...] = whole - factor * pivot_row
            inverse_ref[...] = inverse_ref[...] - factor * inverse_ref[pl.ds(k, 1), :]
            return carry

        lax.fori_loop(0, width, eliminate, 0)
        pivots = jnp.sum(jnp.where(on_diag, work_ref[...], 0.0), axis=1, keepdims=True)
        inverse_ref[...] = inverse_ref[...] * lax.rsqrt(pivots)

    sketch = (mine_ref[...] + other_ref[...]) / total_cols
    basis = matmul_t(sketch, inverse_ref[...]) * root_rows
    basis_ref[...] = basis
    high = basis.astype(jnp.bfloat16)
    low = (basis - high.astype(jnp.float32)).astype(jnp.bfloat16)
    pair = jnp.concatenate([high, low], axis=1).T
    fetch.wait()
    for start in range(0, buffer.shape[1], TILE):
        both = lax.dot_general(
            pair,
            buffer[:, start : start + TILE],
            (((1,), (0,)), ((), ())),
            preferred_element_type=jnp.float32,
        )
        product_ref[:, start : start + TILE] = both[:width] + both[width:]


def make_basis(gram, mine, other, slab, total_cols, root_rows):
    rows, width = mine.shape
    return pl.pallas_call(
        functools.partial(basis_kernel, total_cols, root_rows),
        out_shape=(
            jax.ShapeDtypeStruct((rows, width), jnp.float32),
            jax.ShapeDtypeStruct((width, slab.shape[1]), jnp.float32),
        ),
        in_specs=[pl.BlockSpec(memory_space=pltpu.VMEM)] * 3
        + [pl.BlockSpec(memory_space=pl.ANY)],
        out_specs=[pl.BlockSpec(memory_space=pltpu.VMEM)] * 2,
        scratch_shapes=[
            pltpu.VMEM((width, width), jnp.float32),
            pltpu.VMEM((width, width), jnp.float32),
            pltpu.VMEM(slab.shape, jnp.bfloat16),
            pltpu.SemaphoreType.DMA,
        ],
        compiler_params=pltpu.CompilerParams(vmem_limit_bytes=KERNEL_VMEM),
        name="make_basis",
    )(gram, mine, other, slab)


def per_device(activations, start_sketch):
    rows_here, cols_here = activations.shape
    width = start_sketch.shape[1]
    parts = lax.axis_size("row")
    total_rows = rows_here * parts
    total_cols = cols_here * lax.axis_size("col")
    root_rows = math.sqrt(total_rows)

    cols_chunk = cols_here // CHUNKS
    spans = [slice(c * cols_chunk, (c + 1) * cols_chunk) for c in range(CHUNKS)]

    local_cols = first_product(start_sketch, activations, SKETCH_CHUNKS)
    partial_sketch = 0.0
    orders = orders_of("row")
    step = cols_here // SKETCH_CHUNKS
    for c in range(SKETCH_CHUNKS):
        span = slice(c * step, (c + 1) * step)
        shared = sum_and_share(local_cols[c], "row", orders[c % 2], 1.0 / root_rows)
        partial_sketch = partial_sketch + lax.dot_general(
            activations[:, span],
            shared,
            (((1,), (1,)), ((), ())),
            preferred_element_type=jnp.float32,
        )
    other_sketch = swap(partial_sketch, "col", 1)
    gram = row_sum(make_gram(partial_sketch, other_sketch, total_cols))
    basis, local_proj = make_basis(
        gram, partial_sketch, other_sketch, activations, total_cols, root_rows
    )

    pieces = []
    for span in spans:
        blocks = local_proj[:, span].reshape(parts, width // parts, cols_chunk)
        pieces.append(scatter_sum(blocks, "row") / total_rows)
    return (basis, jnp.concatenate(pieces, axis=1))


def solution(mesh):
    return jax.shard_map(
        per_device,
        mesh=mesh,
        in_specs=(P(("grp", "row"), "col"), P(("grp", "row"), None)),
        out_specs=(P(("grp", "row"), None), P(("grp", "row"), "col")),
        check_vma=False,
    )
```

```python
import functools
import math

import jax
import jax.numpy as jnp
from jax import lax
from jax.experimental import pallas as pl
from jax.experimental.pallas import tpu as pltpu
from jax.sharding import PartitionSpec as P

SKETCH_CHUNKS = 4
TILE = 512
KERNEL_VMEM = 50 * 2**20


def levels_of(size):
    levels, stride = [], 1
    while stride < size:
        radix = 2 if stride == 1 else min(4, size // stride)
        levels.append((stride, radix))
        stride *= radix
    return levels


def swap(value, axis, distance):
    size = lax.axis_size(axis)
    return lax.ppermute(value, axis, [(i, i ^ distance) for i in range(size)])


def row_sum(value):
    rows, cores = lax.axis_size("row"), lax.axis_size("col")
    assert cores == 2
    first = lax.axis_index("col") == 0
    stride = 1
    while stride < rows:
        radix = min(8, rows // stride)
        split = min(2, radix // 2)
        terms = []
        for near in [digit for digit in range(radix) if not digit & split]:
            pairs = []
            for row in range(rows):
                for core, digit in ((0, near), (1, near | split)):
                    if digit:
                        pairs.append((row * cores + core, (row ^ digit * stride) * cores + core))
            terms.append(lax.ppermute(value, ("row", "col"), pairs))
        terms[0] = jnp.where(first, value, terms[0])
        while len(terms) > 1:
            terms = [terms[i] + terms[i + 1] for i in range(0, len(terms), 2)]
        value = terms[0] + swap(terms[0], "col", 1)
        stride *= radix
    return value


def digit_of(axis, stride, radix):
    return lax.rem(lax.div(lax.axis_index(axis), stride), radix)


def scatter_sum(value, axis, reverse):
    levels = levels_of(lax.axis_size(axis))
    rows = value.shape[0] // lax.axis_size(axis)
    total = value.reshape([radix for _, radix in reversed(levels)] + [rows, value.shape[1]])
    order = range(len(levels))
    for level in reversed(order) if reverse else order:
        stride, radix = levels[level]
        dim = len(levels) - 1 - level
        digit = digit_of(axis, stride, radix)
        parts = total
        total = lax.dynamic_slice_in_dim(parts, digit, 1, dim)
        for t in range(1, radix):
            part = lax.dynamic_slice_in_dim(parts, jnp.bitwise_xor(digit, t), 1, dim)
            landed = swap(part.astype(jnp.bfloat16), axis, t * stride)
            total = total + landed.astype(jnp.float32)
    return total.reshape(rows, value.shape[1])


def bit_of(axis, bit):
    return lax.rem(lax.div(lax.axis_index(axis), 1 << bit), 2)


def sum_and_share(value, axis, order, scale):
    for bit in order[:-1]:
        upper = bit_of(axis, bit) == 1
        half = value.shape[1] // 2
        low, high = value[:, :half], value[:, half:]
        send = jnp.where(upper, low, high).astype(jnp.bfloat16)
        landed = swap(send, axis, 1 << bit)
        value = jnp.where(upper, high, low) + landed.astype(jnp.float32)
    landed = swap(value.astype(jnp.bfloat16), axis, 1 << order[-1])
    block = ((value + landed.astype(jnp.float32)) * scale).astype(jnp.bfloat16)
    for bit in reversed(order[:-1]):
        upper = bit_of(axis, bit) == 1
        other = swap(block, axis, 1 << bit)
        block = jnp.concatenate(
            [jnp.where(upper, other, block), jnp.where(upper, block, other)], axis=1
        )
    return block


def orders_of(axis):
    bits = list(range((lax.axis_size(axis) - 1).bit_length()))
    if len(bits) < 3:
        return [bits, bits]
    return [bits, [bits[1], bits[0]] + bits[2:]]


def fetch_tiles(slab_ref, buffer, arrived):
    copies = []
    for tile in range(buffer.shape[0]):
        span = pl.ds(tile * TILE, TILE)
        copies.append(
            pltpu.make_async_copy(slab_ref.at[:, span], buffer.at[tile], arrived.at[tile])
        )
    for copy in copies:
        copy.start()
    return copies


def sketch_kernel(start_ref, slab_ref, *refs):
    outs, (buffer, arrived) = refs[:-2], refs[-2:]
    copies = fetch_tiles(slab_ref, buffer, arrived)
    left = start_ref[...].T
    for tile, copy in enumerate(copies):
        copy.wait()
        out, inner = divmod(tile * TILE, outs[0].shape[1])
        outs[out][:, inner : inner + TILE] = lax.dot_general(
            left, buffer[tile], (((1,), (0,)), ((), ())), preferred_element_type=jnp.float32
        )


def first_product(start, slab, chunks):
    rows, width = start.shape
    cols = slab.shape[1]
    return pl.pallas_call(
        sketch_kernel,
        out_shape=[jax.ShapeDtypeStruct((width, cols // chunks), jnp.float32)] * chunks,
        in_specs=[
            pl.BlockSpec(memory_space=pltpu.VMEM),
            pl.BlockSpec(memory_space=pl.ANY),
        ],
        out_specs=[pl.BlockSpec(memory_space=pltpu.VMEM)] * chunks,
        scratch_shapes=[
            pltpu.VMEM((cols // TILE, rows, TILE), jnp.bfloat16),
            pltpu.SemaphoreType.DMA((cols // TILE,)),
        ],
        compiler_params=pltpu.CompilerParams(vmem_limit_bytes=KERNEL_VMEM),
        cost_estimate=pl.CostEstimate(
            flops=2 * rows * width * cols, bytes_accessed=2 * rows * cols, transcendentals=0
        ),
        name="first_product",
    )(start, slab)


def matmul(left, right, exact=True):
    if not exact:
        left, right = left.astype(jnp.bfloat16), right.astype(jnp.bfloat16)
    return lax.dot_general(
        left,
        right,
        (((1,), (0,)), ((), ())),
        precision=lax.Precision.HIGHEST if exact else None,
        preferred_element_type=jnp.float32,
    )


def matmul_t(left, right, exact=True):
    if not exact:
        left, right = left.astype(jnp.bfloat16), right.astype(jnp.bfloat16)
    return lax.dot_general(
        left,
        right,
        (((1,), (1,)), ((), ())),
        precision=lax.Precision.HIGHEST if exact else None,
        preferred_element_type=jnp.float32,
    )


def gram_kernel(total_cols, mine_ref, other_ref, packed_ref):
    sketch = (mine_ref[...] + other_ref[...]) / total_cols
    gram = matmul(sketch.T, sketch)
    half = gram.shape[0] // 2
    row = lax.broadcasted_iota(jnp.int32, (half, 2 * half), 0)
    col = lax.broadcasted_iota(jnp.int32, (half, 2 * half), 1)
    top, bottom = gram[:half], pltpu.roll(gram[half:], half, 1)
    packed_ref[:half] = jnp.where(row > col, bottom, top)
    diagonal = jnp.sum(jnp.where(row == col, bottom, 0.0), axis=0, keepdims=True)
    packed_ref[half:] = jnp.broadcast_to(diagonal, (8, 2 * half))


def unpack_gram(packed):
    width = packed.shape[1]
    half = width // 2
    row = lax.broadcasted_iota(jnp.int32, (half, width), 0)
    col = lax.broadcasted_iota(jnp.int32, (half, width), 1)
    square = packed[:half]
    top = jnp.where(row > col, 0.0, square)
    lower = jnp.where(row > col, square, jnp.where(row == col, packed[half : half + 1], 0.0))
    parts = jnp.concatenate([top, pltpu.roll(lower, half, 1)], axis=0)
    row = lax.broadcasted_iota(jnp.int32, (width, width), 0)
    col = lax.broadcasted_iota(jnp.int32, (width, width), 1)
    return jnp.where(row == col, parts, parts + parts.T)


def make_gram(mine, other, total_cols):
    rows, width = mine.shape
    return pl.pallas_call(
        functools.partial(gram_kernel, total_cols),
        out_shape=jax.ShapeDtypeStruct((width // 2 + 8, width), jnp.float32),
        in_specs=[pl.BlockSpec(memory_space=pltpu.VMEM)] * 2,
        out_specs=pl.BlockSpec(memory_space=pltpu.VMEM),
        compiler_params=pltpu.CompilerParams(vmem_limit_bytes=16 * 2**20),
        name="make_gram",
    )(mine, other)


UPDATES = 4
LOOSE_UPDATES = 2
CLOSE = 1e-5


def basis_kernel(
    total_cols, root_rows, gram_ref, mine_ref, other_ref, slab_ref,
    basis_ref, product_ref, work_ref, inverse_ref, buffer, arrived,
):
    fetch = pltpu.make_async_copy(slab_ref, buffer, arrived)
    fetch.start()
    width = gram_ref.shape[1]
    row = lax.broadcasted_iota(jnp.int32, (width, width), 0)
    col = lax.broadcasted_iota(jnp.int32, (width, width), 1)
    on_diag = row == col
    unit = jnp.where(on_diag, 1.0, 0.0)
    half = jnp.where(row > col, 1.0, jnp.where(on_diag, 0.5, 0.0))

    gram = unpack_gram(gram_ref[...])
    diagonal = jnp.where(on_diag, gram, 0.0)
    down = lax.rsqrt(jnp.sum(diagonal, axis=1, keepdims=True))
    across = lax.rsqrt(jnp.sum(diagonal, axis=0, keepdims=True))
    scaled = gram * down * across

    error = scaled - unit
    step = error * half
    inverse = unit - step + matmul(step, step, False)
    for update in range(1, UPDATES):
        exact = update >= LOOSE_UPDATES
        error = matmul_t(matmul(inverse, scaled, exact), inverse, exact) - unit
        step = error * half
        inverse = inverse - matmul(step, inverse - matmul(step, inverse, exact), exact)
    inverse_ref[...] = inverse * across
    far = jnp.sum(error * error)

    @pl.when(jnp.logical_not(far <= CLOSE))
    def _():
        work_ref[...] = gram
        inverse_ref[...] = unit

        def eliminate(k, carry):
            whole = work_ref[...]
            pivot_row = work_ref[pl.ds(k, 1), :]
            pivot = jnp.sum(
                jnp.where(col[:1] == k, pivot_row, 0.0), axis=1, keepdims=True
            )
            column = jnp.sum(jnp.where(col == k, whole, 0.0), axis=1, keepdims=True)
            factor = jnp.where(row[:, :1] > k, column / pivot, 0.0)
            work_ref[...] = whole - factor * pivot_row
            inverse_ref[...] = inverse_ref[...] - factor * inverse_ref[pl.ds(k, 1), :]
            return carry

        lax.fori_loop(0, width, eliminate, 0)
        pivots = jnp.sum(jnp.where(on_diag, work_ref[...], 0.0), axis=1, keepdims=True)
        inverse_ref[...] = inverse_ref[...] * lax.rsqrt(pivots)

    sketch = (mine_ref[...] + other_ref[...]) / total_cols
    basis = matmul_t(sketch, inverse_ref[...]) * root_rows
    basis_ref[...] = basis
    high = basis.astype(jnp.bfloat16)
    low = (basis - high.astype(jnp.float32)).astype(jnp.bfloat16)
    pair = jnp.concatenate([high, low], axis=1).T
    fetch.wait()
    for start in range(0, buffer.shape[1], TILE):
        both = lax.dot_general(
            pair,
            buffer[:, start : start + TILE],
            (((1,), (0,)), ((), ())),
            preferred_element_type=jnp.float32,
        )
        product_ref[:, start : start + TILE] = both[:width] + both[width:]


def make_basis(gram, mine, other, slab, total_cols, root_rows):
    rows, width = mine.shape
    return pl.pallas_call(
        functools.partial(basis_kernel, total_cols, root_rows),
        out_shape=(
            jax.ShapeDtypeStruct((rows, width), jnp.float32),
            jax.ShapeDtypeStruct((width, slab.shape[1]), jnp.float32),
        ),
        in_specs=[pl.BlockSpec(memory_space=pltpu.VMEM)] * 3
        + [pl.BlockSpec(memory_space=pl.ANY)],
        out_specs=[pl.BlockSpec(memory_space=pltpu.VMEM)] * 2,
        scratch_shapes=[
            pltpu.VMEM((width, width), jnp.float32),
            pltpu.VMEM((width, width), jnp.float32),
            pltpu.VMEM(slab.shape, jnp.bfloat16),
            pltpu.SemaphoreType.DMA,
        ],
        compiler_params=pltpu.CompilerParams(vmem_limit_bytes=KERNEL_VMEM),
        name="make_basis",
    )(gram, mine, other, slab)


def per_device(activations, start_sketch):
    rows_here, cols_here = activations.shape
    width = start_sketch.shape[1]
    parts = lax.axis_size("row")
    total_rows = rows_here * parts
    total_cols = cols_here * lax.axis_size("col")
    root_rows = math.sqrt(total_rows)

    local_cols = first_product(start_sketch, activations, SKETCH_CHUNKS)
    partial_sketch = 0.0
    orders = orders_of("row")
    step = cols_here // SKETCH_CHUNKS
    for c in range(SKETCH_CHUNKS):
        span = slice(c * step, (c + 1) * step)
        shared = sum_and_share(local_cols[c], "row", orders[c % 2], 1.0 / root_rows)
        partial_sketch = partial_sketch + lax.dot_general(
            activations[:, span],
            shared,
            (((1,), (1,)), ((), ())),
            preferred_element_type=jnp.float32,
        )
    other_sketch = swap(partial_sketch, "col", 1)
    gram = row_sum(make_gram(partial_sketch, other_sketch, total_cols))
    basis, local_proj = make_basis(
        gram, partial_sketch, other_sketch, activations, total_cols, root_rows
    )

    cut = cols_here * 5 // 8
    pieces = [
        scatter_sum(local_proj[:, :cut], "row", False) / total_rows,
        scatter_sum(local_proj[:, cut:], "row", True) / total_rows,
    ]
    return (basis, jnp.concatenate(pieces, axis=1))


def solution(mesh):
    return jax.shard_map(
        per_device,
        mesh=mesh,
        in_specs=(P(("grp", "row"), "col"), P(("grp", "row"), None)),
        out_specs=(P(("grp", "row"), None), P(("grp", "row"), "col")),
        check_vma=False,
    )
```

```python
import functools
import math

import jax
import jax.numpy as jnp
from jax import lax
from jax.experimental import pallas as pl
from jax.experimental.pallas import tpu as pltpu
from jax.sharding import PartitionSpec as P

SKETCH_CHUNKS = 4
TILE = 512
KERNEL_VMEM = 50 * 2**20


def levels_of(size):
    levels, stride = [], 1
    while stride < size:
        radix = 2 if stride == 1 else min(4, size // stride)
        levels.append((stride, radix))
        stride *= radix
    return levels


def swap(value, axis, distance):
    size = lax.axis_size(axis)
    return lax.ppermute(value, axis, [(i, i ^ distance) for i in range(size)])


def row_sum(value):
    rows, cores = lax.axis_size("row"), lax.axis_size("col")
    assert cores == 2
    first = lax.axis_index("col") == 0
    stride = 1
    while stride < rows:
        radix = min(8, rows // stride)
        split = min(2, radix // 2)
        terms = []
        for near in [digit for digit in range(radix) if not digit & split]:
            pairs = []
            for row in range(rows):
                for core, digit in ((0, near), (1, near | split)):
                    if digit:
                        pairs.append((row * cores + core, (row ^ digit * stride) * cores + core))
            terms.append(lax.ppermute(value, ("row", "col"), pairs))
        terms[0] = jnp.where(first, value, terms[0])
        while len(terms) > 1:
            terms = [terms[i] + terms[i + 1] for i in range(0, len(terms), 2)]
        value = terms[0] + swap(terms[0], "col", 1)
        stride *= radix
    return value


def digit_of(axis, stride, radix):
    return lax.rem(lax.div(lax.axis_index(axis), stride), radix)


def core_swap(value, bits):
    rows, cores = lax.axis_size("row"), lax.axis_size("col")
    pairs = [
        (row * cores + core, (row ^ (1 << bits[core % 2])) * cores + core)
        for row in range(rows)
        for core in range(cores)
    ]
    return lax.ppermute(value, ("row", "col"), pairs)


def core_upper(bits):
    odd = lax.rem(lax.axis_index("col"), 2) == 1
    weight = jnp.where(odd, 1 << bits[1], 1 << bits[0])
    return jnp.bitwise_and(lax.axis_index("row"), weight) != 0


def scatter_sum(value):
    n = lax.axis_size("row")
    bits = (n - 1).bit_length()
    rows, cols = value.shape[0] // n, value.shape[1]
    odd = lax.rem(lax.axis_index("col"), 2) == 1
    view = value.reshape(n // 4, 2, 2, rows, cols)
    low = jnp.where(odd, view[:, 0], view[:, :, 0])
    high = jnp.where(odd, view[:, 1], view[:, :, 1])
    for step in [(0, 1), (1, 0)] + [(bit, bit) for bit in range(2, bits)]:
        upper = core_upper(step)
        landed = core_swap(jnp.where(upper, low, high).astype(jnp.bfloat16), step)
        total = jnp.where(upper, high, low) + landed.astype(jnp.float32)
        total = total.reshape(-1, 2, rows, cols) if step[0] < bits - 1 else total
        low, high = total[:, 0], total[:, -1]
    return total.reshape(rows, cols)


def bit_of(axis, bit):
    return lax.rem(lax.div(lax.axis_index(axis), 1 << bit), 2)


def sum_and_share(value, axis, order, scale):
    for bit in order[:-1]:
        upper = bit_of(axis, bit) == 1
        half = value.shape[1] // 2
        low, high = value[:, :half], value[:, half:]
        send = jnp.where(upper, low, high).astype(jnp.bfloat16)
        landed = swap(send, axis, 1 << bit)
        value = jnp.where(upper, high, low) + landed.astype(jnp.float32)
    landed = swap(value.astype(jnp.bfloat16), axis, 1 << order[-1])
    block = ((value + landed.astype(jnp.float32)) * scale).astype(jnp.bfloat16)
    for bit in reversed(order[:-1]):
        upper = bit_of(axis, bit) == 1
        other = swap(block, axis, 1 << bit)
        block = jnp.concatenate(
            [jnp.where(upper, other, block), jnp.where(upper, block, other)], axis=1
        )
    return block


def orders_of(axis):
    bits = list(range((lax.axis_size(axis) - 1).bit_length()))
    if len(bits) < 3:
        return [bits, bits]
    return [bits, [bits[1], bits[0]] + bits[2:]]


def fetch_tiles(slab_ref, buffer, arrived):
    copies = []
    for tile in range(buffer.shape[0]):
        span = pl.ds(tile * TILE, TILE)
        copies.append(
            pltpu.make_async_copy(slab_ref.at[:, span], buffer.at[tile], arrived.at[tile])
        )
    for copy in copies:
        copy.start()
    return copies


def sketch_kernel(start_ref, slab_ref, *refs):
    outs, (buffer, arrived) = refs[:-2], refs[-2:]
    copies = fetch_tiles(slab_ref, buffer, arrived)
    left = start_ref[...].T
    for tile, copy in enumerate(copies):
        copy.wait()
        out, inner = divmod(tile * TILE, outs[0].shape[1])
        outs[out][:, inner : inner + TILE] = lax.dot_general(
            left, buffer[tile], (((1,), (0,)), ((), ())), preferred_element_type=jnp.float32
        )


def first_product(start, slab, chunks):
    rows, width = start.shape
    cols = slab.shape[1]
    return pl.pallas_call(
        sketch_kernel,
        out_shape=[jax.ShapeDtypeStruct((width, cols // chunks), jnp.float32)] * chunks,
        in_specs=[
            pl.BlockSpec(memory_space=pltpu.VMEM),
            pl.BlockSpec(memory_space=pl.ANY),
        ],
        out_specs=[pl.BlockSpec(memory_space=pltpu.VMEM)] * chunks,
        scratch_shapes=[
            pltpu.VMEM((cols // TILE, rows, TILE), jnp.bfloat16),
            pltpu.SemaphoreType.DMA((cols // TILE,)),
        ],
        compiler_params=pltpu.CompilerParams(vmem_limit_bytes=KERNEL_VMEM),
        cost_estimate=pl.CostEstimate(
            flops=2 * rows * width * cols, bytes_accessed=2 * rows * cols, transcendentals=0
        ),
        name="first_product",
    )(start, slab)


def matmul(left, right, exact=True):
    if not exact:
        left, right = left.astype(jnp.bfloat16), right.astype(jnp.bfloat16)
    return lax.dot_general(
        left,
        right,
        (((1,), (0,)), ((), ())),
        precision=lax.Precision.HIGHEST if exact else None,
        preferred_element_type=jnp.float32,
    )


def matmul_t(left, right, exact=True):
    if not exact:
        left, right = left.astype(jnp.bfloat16), right.astype(jnp.bfloat16)
    return lax.dot_general(
        left,
        right,
        (((1,), (1,)), ((), ())),
        precision=lax.Precision.HIGHEST if exact else None,
        preferred_element_type=jnp.float32,
    )


def gram_kernel(total_cols, mine_ref, other_ref, packed_ref):
    sketch = (mine_ref[...] + other_ref[...]) / total_cols
    gram = matmul(sketch.T, sketch)
    half = gram.shape[0] // 2
    row = lax.broadcasted_iota(jnp.int32, (half, 2 * half), 0)
    col = lax.broadcasted_iota(jnp.int32, (half, 2 * half), 1)
    top, bottom = gram[:half], pltpu.roll(gram[half:], half, 1)
    packed_ref[:half] = jnp.where(row > col, bottom, top)
    diagonal = jnp.sum(jnp.where(row == col, bottom, 0.0), axis=0, keepdims=True)
    packed_ref[half:] = jnp.broadcast_to(diagonal, (8, 2 * half))


def unpack_gram(packed):
    width = packed.shape[1]
    half = width // 2
    row = lax.broadcasted_iota(jnp.int32, (half, width), 0)
    col = lax.broadcasted_iota(jnp.int32, (half, width), 1)
    square = packed[:half]
    top = jnp.where(row > col, 0.0, square)
    lower = jnp.where(row > col, square, jnp.where(row == col, packed[half : half + 1], 0.0))
    parts = jnp.concatenate([top, pltpu.roll(lower, half, 1)], axis=0)
    row = lax.broadcasted_iota(jnp.int32, (width, width), 0)
    col = lax.broadcasted_iota(jnp.int32, (width, width), 1)
    return jnp.where(row == col, parts, parts + parts.T)


def make_gram(mine, other, total_cols):
    rows, width = mine.shape
    return pl.pallas_call(
        functools.partial(gram_kernel, total_cols),
        out_shape=jax.ShapeDtypeStruct((width // 2 + 8, width), jnp.float32),
        in_specs=[pl.BlockSpec(memory_space=pltpu.VMEM)] * 2,
        out_specs=pl.BlockSpec(memory_space=pltpu.VMEM),
        compiler_params=pltpu.CompilerParams(vmem_limit_bytes=16 * 2**20),
        name="make_gram",
    )(mine, other)


UPDATES = 4
LOOSE_UPDATES = 2
CLOSE = 1e-5


def basis_kernel(
    total_cols, root_rows, gram_ref, mine_ref, other_ref, slab_ref,
    basis_ref, product_ref, work_ref, inverse_ref, buffer, arrived,
):
    fetch = pltpu.make_async_copy(slab_ref, buffer, arrived)
    fetch.start()
    width = gram_ref.shape[1]
    row = lax.broadcasted_iota(jnp.int32, (width, width), 0)
    col = lax.broadcasted_iota(jnp.int32, (width, width), 1)
    on_diag = row == col
    unit = jnp.where(on_diag, 1.0, 0.0)
    half = jnp.where(row > col, 1.0, jnp.where(on_diag, 0.5, 0.0))

    gram = unpack_gram(gram_ref[...])
    diagonal = jnp.where(on_diag, gram, 0.0)
    down = lax.rsqrt(jnp.sum(diagonal, axis=1, keepdims=True))
    across = lax.rsqrt(jnp.sum(diagonal, axis=0, keepdims=True))
    scaled = gram * down * across

    error = scaled - unit
    step = error * half
    inverse = unit - step + matmul(step, step, False)
    for update in range(1, UPDATES):
        exact = update >= LOOSE_UPDATES
        error = matmul_t(matmul(inverse, scaled, exact), inverse, exact) - unit
        step = error * half
        inverse = inverse - matmul(step, inverse - matmul(step, inverse, exact), exact)
    inverse_ref[...] = inverse * across
    far = jnp.sum(error * error)

    @pl.when(jnp.logical_not(far <= CLOSE))
    def _():
        work_ref[...] = gram
        inverse_ref[...] = unit

        def eliminate(k, carry):
            whole = work_ref[...]
            pivot_row = work_ref[pl.ds(k, 1), :]
            pivot = jnp.sum(
                jnp.where(col[:1] == k, pivot_row, 0.0), axis=1, keepdims=True
            )
            column = jnp.sum(jnp.where(col == k, whole, 0.0), axis=1, keepdims=True)
            factor = jnp.where(row[:, :1] > k, column / pivot, 0.0)
            work_ref[...] = whole - factor * pivot_row
            inverse_ref[...] = inverse_ref[...] - factor * inverse_ref[pl.ds(k, 1), :]
            return carry

        lax.fori_loop(0, width, eliminate, 0)
        pivots = jnp.sum(jnp.where(on_diag, work_ref[...], 0.0), axis=1, keepdims=True)
        inverse_ref[...] = inverse_ref[...] * lax.rsqrt(pivots)

    sketch = (mine_ref[...] + other_ref[...]) / total_cols
    basis = matmul_t(sketch, inverse_ref[...]) * root_rows
    basis_ref[...] = basis
    high = basis.astype(jnp.bfloat16)
    low = (basis - high.astype(jnp.float32)).astype(jnp.bfloat16)
    pair = jnp.concatenate([high, low], axis=1).T
    fetch.wait()
    for start in range(0, buffer.shape[1], TILE):
        both = lax.dot_general(
            pair,
            buffer[:, start : start + TILE],
            (((1,), (0,)), ((), ())),
            preferred_element_type=jnp.float32,
        )
        product_ref[:, start : start + TILE] = both[:width] + both[width:]


def make_basis(gram, mine, other, slab, total_cols, root_rows):
    rows, width = mine.shape
    return pl.pallas_call(
        functools.partial(basis_kernel, total_cols, root_rows),
        out_shape=(
            jax.ShapeDtypeStruct((rows, width), jnp.float32),
            jax.ShapeDtypeStruct((width, slab.shape[1]), jnp.float32),
        ),
        in_specs=[pl.BlockSpec(memory_space=pltpu.VMEM)] * 3
        + [pl.BlockSpec(memory_space=pl.ANY)],
        out_specs=[pl.BlockSpec(memory_space=pltpu.VMEM)] * 2,
        scratch_shapes=[
            pltpu.VMEM((width, width), jnp.float32),
            pltpu.VMEM((width, width), jnp.float32),
            pltpu.VMEM(slab.shape, jnp.bfloat16),
            pltpu.SemaphoreType.DMA,
        ],
        compiler_params=pltpu.CompilerParams(vmem_limit_bytes=KERNEL_VMEM),
        name="make_basis",
    )(gram, mine, other, slab)


def per_device(activations, start_sketch):
    rows_here, cols_here = activations.shape
    width = start_sketch.shape[1]
    parts = lax.axis_size("row")
    total_rows = rows_here * parts
    total_cols = cols_here * lax.axis_size("col")
    root_rows = math.sqrt(total_rows)

    local_cols = first_product(start_sketch, activations, SKETCH_CHUNKS)
    partial_sketch = 0.0
    orders = orders_of("row")
    step = cols_here // SKETCH_CHUNKS
    for c in range(SKETCH_CHUNKS):
        span = slice(c * step, (c + 1) * step)
        shared = sum_and_share(local_cols[c], "row", orders[c % 2], 1.0 / root_rows)
        partial_sketch = partial_sketch + lax.dot_general(
            activations[:, span],
            shared,
            (((1,), (1,)), ((), ())),
            preferred_element_type=jnp.float32,
        )
    other_sketch = swap(partial_sketch, "col", 1)
    gram = row_sum(make_gram(partial_sketch, other_sketch, total_cols))
    basis, local_proj = make_basis(
        gram, partial_sketch, other_sketch, activations, total_cols, root_rows
    )

    projection = scatter_sum(local_proj) / total_rows
    return (basis, projection)


def solution(mesh):
    return jax.shard_map(
        per_device,
        mesh=mesh,
        in_specs=(P(("grp", "row"), "col"), P(("grp", "row"), None)),
        out_specs=(P(("grp", "row"), None), P(("grp", "row"), "col")),
        check_vma=False,
    )
```

```python
import functools
import math

import jax
import jax.numpy as jnp
from jax import lax
from jax.experimental import pallas as pl
from jax.experimental.pallas import tpu as pltpu
from jax.sharding import PartitionSpec as P

CHUNKS = 4
TILE = 512
KERNEL_VMEM = 50 * 2**20


def swap(value, axis, distance):
    size = lax.axis_size(axis)
    return lax.ppermute(value, axis, [(i, i ^ distance) for i in range(size)])


def row_sum(value):
    rows, cores = lax.axis_size("row"), lax.axis_size("col")
    assert cores == 2
    first = lax.axis_index("col") == 0
    stride = 1
    while stride < rows:
        radix = min(8, rows // stride)
        split = min(2, radix // 2)
        terms = []
        for near in [digit for digit in range(radix) if not digit & split]:
            pairs = []
            for row in range(rows):
                for core, digit in ((0, near), (1, near | split)):
                    if digit:
                        pairs.append((row * cores + core, (row ^ digit * stride) * cores + core))
            terms.append(lax.ppermute(value, ("row", "col"), pairs))
        terms[0] = jnp.where(first, value, terms[0])
        while len(terms) > 1:
            terms = [terms[i] + terms[i + 1] for i in range(0, len(terms), 2)]
        value = terms[0] + swap(terms[0], "col", 1)
        stride *= radix
    return value


def scatter_sum(value, axis, order):
    rows, cols = value.shape[0] >> len(order), value.shape[1]
    total = value.reshape([2] * len(order) + [rows, cols])
    left = sorted(order, reverse=True)
    for bit in order:
        dim = left.index(bit)
        left.remove(bit)
        low = lax.index_in_dim(total, 0, dim, keepdims=False)
        high = lax.index_in_dim(total, 1, dim, keepdims=False)
        upper = bit_of(axis, bit) == 1
        send = jnp.where(upper, low, high).astype(jnp.bfloat16)
        landed = swap(send, axis, 1 << bit)
        total = jnp.where(upper, high, low) + landed.astype(jnp.float32)
    return total


def bit_of(axis, bit):
    return lax.rem(lax.div(lax.axis_index(axis), 1 << bit), 2)


def sum_and_share(value, axis, order, scale):
    for bit in order[:-1]:
        upper = bit_of(axis, bit) == 1
        half = value.shape[1] // 2
        low, high = value[:, :half], value[:, half:]
        send = jnp.where(upper, low, high).astype(jnp.bfloat16)
        landed = swap(send, axis, 1 << bit)
        value = jnp.where(upper, high, low) + landed.astype(jnp.float32)
    landed = swap(value.astype(jnp.bfloat16), axis, 1 << order[-1])
    block = ((value + landed.astype(jnp.float32)) * scale).astype(jnp.bfloat16)
    for bit in reversed(order[:-1]):
        upper = bit_of(axis, bit) == 1
        other = swap(block, axis, 1 << bit)
        block = jnp.concatenate(
            [jnp.where(upper, other, block), jnp.where(upper, block, other)], axis=1
        )
    return block


def orders_of(axis):
    bits = list(range((lax.axis_size(axis) - 1).bit_length()))
    if len(bits) < 3:
        return [bits, bits]
    return [bits, [bits[1], bits[0]] + bits[2:]]


def fetch_tiles(slab_ref, buffer, arrived):
    copies = []
    for tile in range(buffer.shape[0]):
        span = pl.ds(tile * TILE, TILE)
        copies.append(
            pltpu.make_async_copy(slab_ref.at[:, span], buffer.at[tile], arrived.at[tile])
        )
    for copy in copies:
        copy.start()
    return copies


def sketch_kernel(start_ref, slab_ref, *refs):
    outs, (buffer, arrived) = refs[:-2], refs[-2:]
    copies = fetch_tiles(slab_ref, buffer, arrived)
    left = start_ref[...].T
    for tile, copy in enumerate(copies):
        copy.wait()
        out, inner = divmod(tile * TILE, outs[0].shape[1])
        outs[out][:, inner : inner + TILE] = lax.dot_general(
            left, buffer[tile], (((1,), (0,)), ((), ())), preferred_element_type=jnp.float32
        )


def first_product(start, slab, chunks):
    rows, width = start.shape
    cols = slab.shape[1]
    return pl.pallas_call(
        sketch_kernel,
        out_shape=[jax.ShapeDtypeStruct((width, cols // chunks), jnp.float32)] * chunks,
        in_specs=[
            pl.BlockSpec(memory_space=pltpu.VMEM),
            pl.BlockSpec(memory_space=pl.ANY),
        ],
        out_specs=[pl.BlockSpec(memory_space=pltpu.VMEM)] * chunks,
        scratch_shapes=[
            pltpu.VMEM((cols // TILE, rows, TILE), jnp.bfloat16),
            pltpu.SemaphoreType.DMA((cols // TILE,)),
        ],
        compiler_params=pltpu.CompilerParams(vmem_limit_bytes=KERNEL_VMEM),
        cost_estimate=pl.CostEstimate(
            flops=2 * rows * width * cols, bytes_accessed=2 * rows * cols, transcendentals=0
        ),
        name="first_product",
    )(start, slab)


def matmul(left, right, exact=True):
    if not exact:
        left, right = left.astype(jnp.bfloat16), right.astype(jnp.bfloat16)
    return lax.dot_general(
        left,
        right,
        (((1,), (0,)), ((), ())),
        precision=lax.Precision.HIGHEST if exact else None,
        preferred_element_type=jnp.float32,
    )


def matmul_t(left, right, exact=True):
    if not exact:
        left, right = left.astype(jnp.bfloat16), right.astype(jnp.bfloat16)
    return lax.dot_general(
        left,
        right,
        (((1,), (1,)), ((), ())),
        precision=lax.Precision.HIGHEST if exact else None,
        preferred_element_type=jnp.float32,
    )


def gram_kernel(total_cols, mine_ref, other_ref, packed_ref):
    sketch = (mine_ref[...] + other_ref[...]) / total_cols
    gram = matmul(sketch.T, sketch)
    half = gram.shape[0] // 2
    row = lax.broadcasted_iota(jnp.int32, (half, 2 * half), 0)
    col = lax.broadcasted_iota(jnp.int32, (half, 2 * half), 1)
    top, bottom = gram[:half], pltpu.roll(gram[half:], half, 1)
    packed_ref[:half] = jnp.where(row > col, bottom, top)
    diagonal = jnp.sum(jnp.where(row == col, bottom, 0.0), axis=0, keepdims=True)
    packed_ref[half:] = jnp.broadcast_to(diagonal, (8, 2 * half))


def unpack_gram(packed):
    width = packed.shape[1]
    half = width // 2
    row = lax.broadcasted_iota(jnp.int32, (half, width), 0)
    col = lax.broadcasted_iota(jnp.int32, (half, width), 1)
    square = packed[:half]
    top = jnp.where(row > col, 0.0, square)
    lower = jnp.where(row > col, square, jnp.where(row == col, packed[half : half + 1], 0.0))
    parts = jnp.concatenate([top, pltpu.roll(lower, half, 1)], axis=0)
    row = lax.broadcasted_iota(jnp.int32, (width, width), 0)
    col = lax.broadcasted_iota(jnp.int32, (width, width), 1)
    return jnp.where(row == col, parts, parts + parts.T)


def make_gram(mine, other, total_cols):
    rows, width = mine.shape
    return pl.pallas_call(
        functools.partial(gram_kernel, total_cols),
        out_shape=jax.ShapeDtypeStruct((width // 2 + 8, width), jnp.float32),
        in_specs=[pl.BlockSpec(memory_space=pltpu.VMEM)] * 2,
        out_specs=pl.BlockSpec(memory_space=pltpu.VMEM),
        compiler_params=pltpu.CompilerParams(vmem_limit_bytes=16 * 2**20),
        name="make_gram",
    )(mine, other)


UPDATES = 4
LOOSE_UPDATES = 2
CLOSE = 1e-5


def basis_kernel(
    total_cols, root_rows, gram_ref, mine_ref, other_ref, slab_ref,
    basis_ref, *refs,
):
    products, (work_ref, inverse_ref, buffer, arrived) = refs[:-4], refs[-4:]
    fetch = pltpu.make_async_copy(slab_ref, buffer, arrived)
    fetch.start()
    width = gram_ref.shape[1]
    row = lax.broadcasted_iota(jnp.int32, (width, width), 0)
    col = lax.broadcasted_iota(jnp.int32, (width, width), 1)
    on_diag = row == col
    unit = jnp.where(on_diag, 1.0, 0.0)
    half = jnp.where(row > col, 1.0, jnp.where(on_diag, 0.5, 0.0))

    gram = unpack_gram(gram_ref[...])
    diagonal = jnp.where(on_diag, gram, 0.0)
    down = lax.rsqrt(jnp.sum(diagonal, axis=1, keepdims=True))
    across = lax.rsqrt(jnp.sum(diagonal, axis=0, keepdims=True))
    scaled = gram * down * across

    error = scaled - unit
    step = error * half
    inverse = unit - step + matmul(step, step, False)
    for update in range(1, UPDATES):
        exact = update >= LOOSE_UPDATES
        error = matmul_t(matmul(inverse, scaled, exact), inverse, exact) - unit
        step = error * half
        inverse = inverse - matmul(step, inverse - matmul(step, inverse, exact), exact)
    inverse_ref[...] = inverse * across
    far = jnp.sum(error * error)

    @pl.when(jnp.logical_not(far <= CLOSE))
    def _():
        work_ref[...] = gram
        inverse_ref[...] = unit

        def eliminate(k, carry):
            whole = work_ref[...]
            pivot_row = work_ref[pl.ds(k, 1), :]
            pivot = jnp.sum(
                jnp.where(col[:1] == k, pivot_row, 0.0), axis=1, keepdims=True
            )
            column = jnp.sum(jnp.where(col == k, whole, 0.0), axis=1, keepdims=True)
            factor = jnp.where(row[:, :1] > k, column / pivot, 0.0)
            work_ref[...] = whole - factor * pivot_row
            inverse_ref[...] = inverse_ref[...] - factor * inverse_ref[pl.ds(k, 1), :]
            return carry

        lax.fori_loop(0, width, eliminate, 0)
        pivots = jnp.sum(jnp.where(on_diag, work_ref[...], 0.0), axis=1, keepdims=True)
        inverse_ref[...] = inverse_ref[...] * lax.rsqrt(pivots)

    sketch = (mine_ref[...] + other_ref[...]) / total_cols
    basis = matmul_t(sketch, inverse_ref[...]) * root_rows
    basis_ref[...] = basis
    high = basis.astype(jnp.bfloat16)
    low = (basis - high.astype(jnp.float32)).astype(jnp.bfloat16)
    pair = jnp.concatenate([high, low], axis=1).T
    fetch.wait()
    for start in range(0, buffer.shape[1], TILE):
        both = lax.dot_general(
            pair,
            buffer[:, start : start + TILE],
            (((1,), (0,)), ((), ())),
            preferred_element_type=jnp.float32,
        )
        out, inner = divmod(start, products[0].shape[1])
        products[out][:, inner : inner + TILE] = both[:width] + both[width:]


def make_basis(gram, mine, other, slab, total_cols, root_rows, chunks):
    rows, width = mine.shape
    cols = slab.shape[1]
    return pl.pallas_call(
        functools.partial(basis_kernel, total_cols, root_rows),
        out_shape=[jax.ShapeDtypeStruct((rows, width), jnp.float32)]
        + [jax.ShapeDtypeStruct((width, cols // chunks), jnp.float32)] * chunks,
        in_specs=[pl.BlockSpec(memory_space=pltpu.VMEM)] * 3
        + [pl.BlockSpec(memory_space=pl.ANY)],
        out_specs=[pl.BlockSpec(memory_space=pltpu.VMEM)] * (1 + chunks),
        scratch_shapes=[
            pltpu.VMEM((width, width), jnp.float32),
            pltpu.VMEM((width, width), jnp.float32),
            pltpu.VMEM(slab.shape, jnp.bfloat16),
            pltpu.SemaphoreType.DMA,
        ],
        compiler_params=pltpu.CompilerParams(vmem_limit_bytes=KERNEL_VMEM),
        name="make_basis",
    )(gram, mine, other, slab)


def per_device(activations, start_sketch):
    rows_here, cols_here = activations.shape
    width = start_sketch.shape[1]
    parts = lax.axis_size("row")
    total_rows = rows_here * parts
    total_cols = cols_here * lax.axis_size("col")
    root_rows = math.sqrt(total_rows)

    local_cols = first_product(start_sketch, activations, CHUNKS)
    partial_sketch = 0.0
    orders = orders_of("row")
    step = cols_here // CHUNKS
    for c in range(CHUNKS):
        span = slice(c * step, (c + 1) * step)
        shared = sum_and_share(local_cols[c], "row", orders[c % 2], 1.0 / root_rows)
        partial_sketch = partial_sketch + lax.dot_general(
            activations[:, span],
            shared,
            (((1,), (1,)), ((), ())),
            preferred_element_type=jnp.float32,
        )
    other_sketch = swap(partial_sketch, "col", 1)
    gram = row_sum(make_gram(partial_sketch, other_sketch, total_cols))
    basis, *products = make_basis(
        gram, partial_sketch, other_sketch, activations, total_cols, root_rows, CHUNKS
    )

    pieces = [
        scatter_sum(product, "row", orders[c % 2]) / total_rows
        for c, product in enumerate(products)
    ]
    return (basis, jnp.concatenate(pieces, axis=1))


def solution(mesh):
    return jax.shard_map(
        per_device,
        mesh=mesh,
        in_specs=(P(("grp", "row"), "col"), P(("grp", "row"), None)),
        out_specs=(P(("grp", "row"), None), P(("grp", "row"), "col")),
        check_vma=False,
    )
```

```python
import functools
import math

import jax
import jax.numpy as jnp
from jax import lax
from jax.experimental import pallas as pl
from jax.experimental.pallas import tpu as pltpu
from jax.sharding import PartitionSpec as P

CHUNKS = 4
TILE = 512
KERNEL_VMEM = 50 * 2**20


def swap(value, axis, distance):
    size = lax.axis_size(axis)
    return lax.ppermute(value, axis, [(i, i ^ distance) for i in range(size)])


def row_sum(value):
    rows, cores = lax.axis_size("row"), lax.axis_size("col")
    assert cores == 2
    first = lax.axis_index("col") == 0
    stride = 1
    while stride < rows:
        radix = min(8, rows // stride)
        split = min(2, radix // 2)
        terms = []
        for near in [digit for digit in range(radix) if not digit & split]:
            pairs = []
            for row in range(rows):
                for core, digit in ((0, near), (1, near | split)):
                    if digit:
                        pairs.append((row * cores + core, (row ^ digit * stride) * cores + core))
            terms.append(lax.ppermute(value, ("row", "col"), pairs))
        terms[0] = jnp.where(first, value, terms[0])
        while len(terms) > 1:
            terms = [terms[i] + terms[i + 1] for i in range(0, len(terms), 2)]
        value = terms[0] + swap(terms[0], "col", 1)
        stride *= radix
    return value


def levels_of(size):
    levels, stride = [], 1
    while stride < size:
        radix = 2 if stride == 1 else min(4, size // stride)
        levels.append((stride, radix))
        stride *= radix
    return levels


def own_block(total, axis, stride, radix, dim):
    digit = lax.rem(lax.div(lax.axis_index(axis), stride), radix)
    return lax.dynamic_slice_in_dim(total, digit, 1, dim)


def sent_blocks(total, axis, stride, radix, dim):
    digit = lax.rem(lax.div(lax.axis_index(axis), stride), radix)
    return [
        lax.dynamic_slice_in_dim(total, jnp.bitwise_xor(digit, t), 1, dim).astype(jnp.bfloat16)
        for t in range(1, radix)
    ]


def after(value, *others):
    return lax.optimization_barrier((value, others))[0]


def scatter_sums(values, axis):
    levels = levels_of(lax.axis_size(axis))
    shape = [radix for _, radix in reversed(levels)]
    rows = values[0].shape[0] // lax.axis_size(axis)
    totals = [value.reshape(shape + [rows, value.shape[1]]) for value in values]
    orders = [list(range(len(levels))), list(range(len(levels)))[::-1]]
    landed = [[], []]
    for step in range(len(levels)):
        for which in range(2):
            level = orders[which][step]
            stride, radix = levels[level]
            dim = len(levels) - 1 - level
            total = add_terms(totals[which], landed[which])
            sends = sent_blocks(total, axis, stride, radix, dim)
            if step:
                landed[1 - which] = after(landed[1 - which], sends)
            elif which == 0:
                totals[1] = after(totals[1], sends)
            landed[which] = [swap(send, axis, t * stride) for t, send in enumerate(sends, 1)]
            totals[which] = own_block(total, axis, stride, radix, dim)
    return [
        add_terms(total, terms).reshape(rows, total.shape[-1])
        for total, terms in zip(totals, landed)
    ]


def add_terms(total, terms):
    for term in terms:
        total = total + term.astype(jnp.float32)
    return total


def bit_of(axis, bit):
    return lax.rem(lax.div(lax.axis_index(axis), 1 << bit), 2)


def sum_and_share(value, axis, order, scale):
    for bit in order[:-1]:
        upper = bit_of(axis, bit) == 1
        half = value.shape[1] // 2
        low, high = value[:, :half], value[:, half:]
        send = jnp.where(upper, low, high).astype(jnp.bfloat16)
        landed = swap(send, axis, 1 << bit)
        value = jnp.where(upper, high, low) + landed.astype(jnp.float32)
    landed = swap(value.astype(jnp.bfloat16), axis, 1 << order[-1])
    block = ((value + landed.astype(jnp.float32)) * scale).astype(jnp.bfloat16)
    for bit in reversed(order[:-1]):
        upper = bit_of(axis, bit) == 1
        other = swap(block, axis, 1 << bit)
        block = jnp.concatenate(
            [jnp.where(upper, other, block), jnp.where(upper, block, other)], axis=1
        )
    return block


def orders_of(axis):
    bits = list(range((lax.axis_size(axis) - 1).bit_length()))
    if len(bits) < 3:
        return [bits, bits]
    return [bits, [bits[1], bits[0]] + bits[2:]]


def fetch_tiles(slab_ref, buffer, arrived):
    copies = []
    for tile in range(buffer.shape[0]):
        span = pl.ds(tile * TILE, TILE)
        copies.append(
            pltpu.make_async_copy(slab_ref.at[:, span], buffer.at[tile], arrived.at[tile])
        )
    for copy in copies:
        copy.start()
    return copies


def sketch_kernel(start_ref, slab_ref, *refs):
    outs, (buffer, arrived) = refs[:-2], refs[-2:]
    copies = fetch_tiles(slab_ref, buffer, arrived)
    left = start_ref[...].T
    for tile, copy in enumerate(copies):
        copy.wait()
        out, inner = divmod(tile * TILE, outs[0].shape[1])
        outs[out][:, inner : inner + TILE] = lax.dot_general(
            left, buffer[tile], (((1,), (0,)), ((), ())), preferred_element_type=jnp.float32
        )


def first_product(start, slab, chunks):
    rows, width = start.shape
    cols = slab.shape[1]
    return pl.pallas_call(
        sketch_kernel,
        out_shape=[jax.ShapeDtypeStruct((width, cols // chunks), jnp.float32)] * chunks,
        in_specs=[
            pl.BlockSpec(memory_space=pltpu.VMEM),
            pl.BlockSpec(memory_space=pl.ANY),
        ],
        out_specs=[pl.BlockSpec(memory_space=pltpu.VMEM)] * chunks,
        scratch_shapes=[
            pltpu.VMEM((cols // TILE, rows, TILE), jnp.bfloat16),
            pltpu.SemaphoreType.DMA((cols // TILE,)),
        ],
        compiler_params=pltpu.CompilerParams(vmem_limit_bytes=KERNEL_VMEM),
        cost_estimate=pl.CostEstimate(
            flops=2 * rows * width * cols, bytes_accessed=2 * rows * cols, transcendentals=0
        ),
        name="first_product",
    )(start, slab)


def matmul(left, right, exact=True):
    if not exact:
        left, right = left.astype(jnp.bfloat16), right.astype(jnp.bfloat16)
    return lax.dot_general(
        left,
        right,
        (((1,), (0,)), ((), ())),
        precision=lax.Precision.HIGHEST if exact else None,
        preferred_element_type=jnp.float32,
    )


def matmul_t(left, right, exact=True):
    if not exact:
        left, right = left.astype(jnp.bfloat16), right.astype(jnp.bfloat16)
    return lax.dot_general(
        left,
        right,
        (((1,), (1,)), ((), ())),
        precision=lax.Precision.HIGHEST if exact else None,
        preferred_element_type=jnp.float32,
    )


def gram_kernel(total_cols, mine_ref, other_ref, packed_ref):
    sketch = (mine_ref[...] + other_ref[...]) / total_cols
    gram = matmul(sketch.T, sketch)
    half = gram.shape[0] // 2
    row = lax.broadcasted_iota(jnp.int32, (half, 2 * half), 0)
    col = lax.broadcasted_iota(jnp.int32, (half, 2 * half), 1)
    top, bottom = gram[:half], pltpu.roll(gram[half:], half, 1)
    packed_ref[:half] = jnp.where(row > col, bottom, top)
    diagonal = jnp.sum(jnp.where(row == col, bottom, 0.0), axis=0, keepdims=True)
    packed_ref[half:] = jnp.broadcast_to(diagonal, (8, 2 * half))


def unpack_gram(packed):
    width = packed.shape[1]
    half = width // 2
    row = lax.broadcasted_iota(jnp.int32, (half, width), 0)
    col = lax.broadcasted_iota(jnp.int32, (half, width), 1)
    square = packed[:half]
    top = jnp.where(row > col, 0.0, square)
    lower = jnp.where(row > col, square, jnp.where(row == col, packed[half : half + 1], 0.0))
    parts = jnp.concatenate([top, pltpu.roll(lower, half, 1)], axis=0)
    row = lax.broadcasted_iota(jnp.int32, (width, width), 0)
    col = lax.broadcasted_iota(jnp.int32, (width, width), 1)
    return jnp.where(row == col, parts, parts + parts.T)


def make_gram(mine, other, total_cols):
    rows, width = mine.shape
    return pl.pallas_call(
        functools.partial(gram_kernel, total_cols),
        out_shape=jax.ShapeDtypeStruct((width // 2 + 8, width), jnp.float32),
        in_specs=[pl.BlockSpec(memory_space=pltpu.VMEM)] * 2,
        out_specs=pl.BlockSpec(memory_space=pltpu.VMEM),
        compiler_params=pltpu.CompilerParams(vmem_limit_bytes=16 * 2**20),
        name="make_gram",
    )(mine, other)


UPDATES = 4
LOOSE_UPDATES = 2
CLOSE = 1e-5


def basis_kernel(
    total_cols, root_rows, gram_ref, mine_ref, other_ref, slab_ref,
    basis_ref, *refs,
):
    products, (work_ref, inverse_ref, buffer, arrived) = refs[:-4], refs[-4:]
    fetch = pltpu.make_async_copy(slab_ref, buffer, arrived)
    fetch.start()
    width = gram_ref.shape[1]
    row = lax.broadcasted_iota(jnp.int32, (width, width), 0)
    col = lax.broadcasted_iota(jnp.int32, (width, width), 1)
    on_diag = row == col
    unit = jnp.where(on_diag, 1.0, 0.0)
    half = jnp.where(row > col, 1.0, jnp.where(on_diag, 0.5, 0.0))

    gram = unpack_gram(gram_ref[...])
    diagonal = jnp.where(on_diag, gram, 0.0)
    down = lax.rsqrt(jnp.sum(diagonal, axis=1, keepdims=True))
    across = lax.rsqrt(jnp.sum(diagonal, axis=0, keepdims=True))
    scaled = gram * down * across

    error = scaled - unit
    step = error * half
    inverse = unit - step + matmul(step, step, False)
    for update in range(1, UPDATES):
        exact = update >= LOOSE_UPDATES
        error = matmul_t(matmul(inverse, scaled, exact), inverse, exact) - unit
        step = error * half
        inverse = inverse - matmul(step, inverse - matmul(step, inverse, exact), exact)
    inverse_ref[...] = inverse * across
    far = jnp.sum(error * error)

    @pl.when(jnp.logical_not(far <= CLOSE))
    def _():
        work_ref[...] = gram
        inverse_ref[...] = unit

        def eliminate(k, carry):
            whole = work_ref[...]
            pivot_row = work_ref[pl.ds(k, 1), :]
            pivot = jnp.sum(
                jnp.where(col[:1] == k, pivot_row, 0.0), axis=1, keepdims=True
            )
            column = jnp.sum(jnp.where(col == k, whole, 0.0), axis=1, keepdims=True)
            factor = jnp.where(row[:, :1] > k, column / pivot, 0.0)
            work_ref[...] = whole - factor * pivot_row
            inverse_ref[...] = inverse_ref[...] - factor * inverse_ref[pl.ds(k, 1), :]
            return carry

        lax.fori_loop(0, width, eliminate, 0)
        pivots = jnp.sum(jnp.where(on_diag, work_ref[...], 0.0), axis=1, keepdims=True)
        inverse_ref[...] = inverse_ref[...] * lax.rsqrt(pivots)

    sketch = (mine_ref[...] + other_ref[...]) / total_cols
    basis = matmul_t(sketch, inverse_ref[...]) * root_rows
    basis_ref[...] = basis
    high = basis.astype(jnp.bfloat16)
    low = (basis - high.astype(jnp.float32)).astype(jnp.bfloat16)
    pair = jnp.concatenate([high, low], axis=1).T
    fetch.wait()
    for start in range(0, buffer.shape[1], TILE):
        both = lax.dot_general(
            pair,
            buffer[:, start : start + TILE],
            (((1,), (0,)), ((), ())),
            preferred_element_type=jnp.float32,
        )
        out = 0 if start < products[0].shape[1] else 1
        inner = start - out * products[0].shape[1]
        products[out][:, inner : inner + TILE] = both[:width] + both[width:]


def make_basis(gram, mine, other, slab, total_cols, root_rows, cut):
    rows, width = mine.shape
    cols = slab.shape[1]
    return pl.pallas_call(
        functools.partial(basis_kernel, total_cols, root_rows),
        out_shape=[jax.ShapeDtypeStruct((rows, width), jnp.float32)]
        + [jax.ShapeDtypeStruct((width, part), jnp.float32) for part in (cut, cols - cut)],
        in_specs=[pl.BlockSpec(memory_space=pltpu.VMEM)] * 3
        + [pl.BlockSpec(memory_space=pl.ANY)],
        out_specs=[pl.BlockSpec(memory_space=pltpu.VMEM)] * 3,
        scratch_shapes=[
            pltpu.VMEM((width, width), jnp.float32),
            pltpu.VMEM((width, width), jnp.float32),
            pltpu.VMEM(slab.shape, jnp.bfloat16),
            pltpu.SemaphoreType.DMA,
        ],
        compiler_params=pltpu.CompilerParams(vmem_limit_bytes=KERNEL_VMEM),
        name="make_basis",
    )(gram, mine, other, slab)


def per_device(activations, start_sketch):
    rows_here, cols_here = activations.shape
    width = start_sketch.shape[1]
    parts = lax.axis_size("row")
    total_rows = rows_here * parts
    total_cols = cols_here * lax.axis_size("col")
    root_rows = math.sqrt(total_rows)

    local_cols = first_product(start_sketch, activations, CHUNKS)
    partial_sketch = 0.0
    orders = orders_of("row")
    step = cols_here // CHUNKS
    for c in range(CHUNKS):
        span = slice(c * step, (c + 1) * step)
        shared = sum_and_share(local_cols[c], "row", orders[c % 2], 1.0 / root_rows)
        partial_sketch = partial_sketch + lax.dot_general(
            activations[:, span],
            shared,
            (((1,), (1,)), ((), ())),
            preferred_element_type=jnp.float32,
        )
    other_sketch = swap(partial_sketch, "col", 1)
    gram = row_sum(make_gram(partial_sketch, other_sketch, total_cols))
    cut = cols_here * 5 // 8
    basis, *products = make_basis(
        gram, partial_sketch, other_sketch, activations, total_cols, root_rows, cut
    )

    pieces = [total / total_rows for total in scatter_sums(products, "row")]
    return (basis, jnp.concatenate(pieces, axis=1))


def solution(mesh):
    return jax.shard_map(
        per_device,
        mesh=mesh,
        in_specs=(P(("grp", "row"), "col"), P(("grp", "row"), None)),
        out_specs=(P(("grp", "row"), None), P(("grp", "row"), "col")),
        check_vma=False,
    )
```

```python
import functools
import math

import jax
import jax.numpy as jnp
from jax import lax
from jax.experimental import pallas as pl
from jax.experimental.pallas import tpu as pltpu
from jax.sharding import PartitionSpec as P

CHUNKS = 4
TILE = 512
KERNEL_VMEM = 50 * 2**20


def swap(value, axis, distance):
    size = lax.axis_size(axis)
    return lax.ppermute(value, axis, [(i, i ^ distance) for i in range(size)])


def row_sum(value):
    rows, cores = lax.axis_size("row"), lax.axis_size("col")
    assert cores == 2
    first = lax.axis_index("col") == 0
    stride = 1
    while stride < rows:
        radix = min(8, rows // stride)
        split = min(2, radix // 2)
        terms = []
        for near in [digit for digit in range(radix) if not digit & split]:
            pairs = []
            for row in range(rows):
                for core, digit in ((0, near), (1, near | split)):
                    if digit:
                        pairs.append((row * cores + core, (row ^ digit * stride) * cores + core))
            terms.append(lax.ppermute(value, ("row", "col"), pairs))
        terms[0] = jnp.where(first, value, terms[0])
        while len(terms) > 1:
            terms = [terms[i] + terms[i + 1] for i in range(0, len(terms), 2)]
        value = terms[0] + swap(terms[0], "col", 1)
        stride *= radix
    return value


def bit_of(axis, bit):
    return lax.rem(lax.div(lax.axis_index(axis), 1 << bit), 2)


def halve_columns(value, axis, bit):
    upper = bit_of(axis, bit) == 1
    half = value.shape[1] // 2
    low, high = value[:, :half], value[:, half:]
    landed = swap(jnp.where(upper, low, high).astype(jnp.bfloat16), axis, 1 << bit)
    return jnp.where(upper, high, low) + landed.astype(jnp.float32)


def join_columns(block, axis, bit):
    upper = bit_of(axis, bit) == 1
    other = swap(block, axis, 1 << bit)
    return jnp.concatenate(
        [jnp.where(upper, other, block), jnp.where(upper, block, other)], axis=1
    )


def sum_and_share(first, second, axis, scale):
    bits = (lax.axis_size(axis) - 1).bit_length()
    first = halve_columns(first, axis, 0)
    second = halve_columns(second, axis, 1)
    first = halve_columns(first, axis, 1)
    second = halve_columns(second, axis, 0)
    both = jnp.concatenate([first, second], axis=1)
    for bit in range(2, bits - 1):
        both = halve_columns(both, axis, bit)
    landed = swap(both.astype(jnp.bfloat16), axis, 1 << (bits - 1))
    block = ((both + landed.astype(jnp.float32)) * scale).astype(jnp.bfloat16)
    for bit in reversed(range(2, bits - 1)):
        block = join_columns(block, axis, bit)
    half = block.shape[1] // 2
    first, second = block[:, :half], block[:, half:]
    first = join_columns(first, axis, 1)
    second = join_columns(second, axis, 0)
    return join_columns(first, axis, 0), join_columns(second, axis, 1)


def halve_rows(value, axis, bit, dim):
    upper = bit_of(axis, bit) == 1
    low = lax.index_in_dim(value, 0, dim, keepdims=False)
    high = lax.index_in_dim(value, 1, dim, keepdims=False)
    landed = swap(jnp.where(upper, low, high).astype(jnp.bfloat16), axis, 1 << bit)
    return jnp.where(upper, high, low) + landed.astype(jnp.float32)


def scatter_sum(first, second, axis):
    n = lax.axis_size(axis)
    rows, cols = first.shape[0] // n, first.shape[1]
    shape = (n // 4, 2, 2, rows, cols)
    first = halve_rows(first.reshape(shape), axis, 0, 2)
    second = halve_rows(second.reshape(shape), axis, 1, 1)
    first = halve_rows(first, axis, 1, 1)
    second = halve_rows(second, axis, 0, 1)
    both = jnp.concatenate([first, second], axis=-1)
    for bit in range(2, (n - 1).bit_length()):
        both = both.reshape(both.shape[0] // 2, 2, rows, 2 * cols)
        both = halve_rows(both, axis, bit, 1)
    return both.reshape(rows, 2 * cols)


def fetch_tiles(slab_ref, buffer, arrived):
    copies = []
    for tile in range(buffer.shape[0]):
        span = pl.ds(tile * TILE, TILE)
        copies.append(
            pltpu.make_async_copy(slab_ref.at[:, span], buffer.at[tile], arrived.at[tile])
        )
    for copy in copies:
        copy.start()
    return copies


def sketch_kernel(start_ref, slab_ref, *refs):
    outs, (buffer, arrived) = refs[:-2], refs[-2:]
    copies = fetch_tiles(slab_ref, buffer, arrived)
    left = start_ref[...].T
    for tile, copy in enumerate(copies):
        copy.wait()
        out, inner = divmod(tile * TILE, outs[0].shape[1])
        outs[out][:, inner : inner + TILE] = lax.dot_general(
            left, buffer[tile], (((1,), (0,)), ((), ())), preferred_element_type=jnp.float32
        )


def first_product(start, slab, chunks):
    rows, width = start.shape
    cols = slab.shape[1]
    return pl.pallas_call(
        sketch_kernel,
        out_shape=[jax.ShapeDtypeStruct((width, cols // chunks), jnp.float32)] * chunks,
        in_specs=[
            pl.BlockSpec(memory_space=pltpu.VMEM),
            pl.BlockSpec(memory_space=pl.ANY),
        ],
        out_specs=[pl.BlockSpec(memory_space=pltpu.VMEM)] * chunks,
        scratch_shapes=[
            pltpu.VMEM((cols // TILE, rows, TILE), jnp.bfloat16),
            pltpu.SemaphoreType.DMA((cols // TILE,)),
        ],
        compiler_params=pltpu.CompilerParams(vmem_limit_bytes=KERNEL_VMEM),
        cost_estimate=pl.CostEstimate(
            flops=2 * rows * width * cols, bytes_accessed=2 * rows * cols, transcendentals=0
        ),
        name="first_product",
    )(start, slab)


def matmul(left, right, exact=True):
    if not exact:
        left, right = left.astype(jnp.bfloat16), right.astype(jnp.bfloat16)
    return lax.dot_general(
        left,
        right,
        (((1,), (0,)), ((), ())),
        precision=lax.Precision.HIGHEST if exact else None,
        preferred_element_type=jnp.float32,
    )


def matmul_t(left, right, exact=True):
    if not exact:
        left, right = left.astype(jnp.bfloat16), right.astype(jnp.bfloat16)
    return lax.dot_general(
        left,
        right,
        (((1,), (1,)), ((), ())),
        precision=lax.Precision.HIGHEST if exact else None,
        preferred_element_type=jnp.float32,
    )


def gram_kernel(total_cols, mine_ref, other_ref, packed_ref):
    sketch = (mine_ref[...] + other_ref[...]) / total_cols
    gram = matmul(sketch.T, sketch)
    half = gram.shape[0] // 2
    row = lax.broadcasted_iota(jnp.int32, (half, 2 * half), 0)
    col = lax.broadcasted_iota(jnp.int32, (half, 2 * half), 1)
    top, bottom = gram[:half], pltpu.roll(gram[half:], half, 1)
    packed_ref[:half] = jnp.where(row > col, bottom, top)
    diagonal = jnp.sum(jnp.where(row == col, bottom, 0.0), axis=0, keepdims=True)
    packed_ref[half:] = jnp.broadcast_to(diagonal, (8, 2 * half))


def unpack_gram(packed):
    width = packed.shape[1]
    half = width // 2
    row = lax.broadcasted_iota(jnp.int32, (half, width), 0)
    col = lax.broadcasted_iota(jnp.int32, (half, width), 1)
    square = packed[:half]
    top = jnp.where(row > col, 0.0, square)
    lower = jnp.where(row > col, square, jnp.where(row == col, packed[half : half + 1], 0.0))
    parts = jnp.concatenate([top, pltpu.roll(lower, half, 1)], axis=0)
    row = lax.broadcasted_iota(jnp.int32, (width, width), 0)
    col = lax.broadcasted_iota(jnp.int32, (width, width), 1)
    return jnp.where(row == col, parts, parts + parts.T)


def make_gram(mine, other, total_cols):
    rows, width = mine.shape
    return pl.pallas_call(
        functools.partial(gram_kernel, total_cols),
        out_shape=jax.ShapeDtypeStruct((width // 2 + 8, width), jnp.float32),
        in_specs=[pl.BlockSpec(memory_space=pltpu.VMEM)] * 2,
        out_specs=pl.BlockSpec(memory_space=pltpu.VMEM),
        compiler_params=pltpu.CompilerParams(vmem_limit_bytes=16 * 2**20),
        name="make_gram",
    )(mine, other)


UPDATES = 4
LOOSE_UPDATES = 2
CLOSE = 1e-5


def basis_kernel(
    total_cols, root_rows, gram_ref, mine_ref, other_ref, slab_ref,
    basis_ref, *refs,
):
    products, (work_ref, inverse_ref, buffer, arrived) = refs[:-4], refs[-4:]
    fetch = pltpu.make_async_copy(slab_ref, buffer, arrived)
    fetch.start()
    width = gram_ref.shape[1]
    row = lax.broadcasted_iota(jnp.int32, (width, width), 0)
    col = lax.broadcasted_iota(jnp.int32, (width, width), 1)
    on_diag = row == col
    unit = jnp.where(on_diag, 1.0, 0.0)
    half = jnp.where(row > col, 1.0, jnp.where(on_diag, 0.5, 0.0))

    gram = unpack_gram(gram_ref[...])
    diagonal = jnp.where(on_diag, gram, 0.0)
    down = lax.rsqrt(jnp.sum(diagonal, axis=1, keepdims=True))
    across = lax.rsqrt(jnp.sum(diagonal, axis=0, keepdims=True))
    scaled = gram * down * across

    error = scaled - unit
    step = error * half
    inverse = unit - step + matmul(step, step, False)
    for update in range(1, UPDATES):
        exact = update >= LOOSE_UPDATES
        error = matmul_t(matmul(inverse, scaled, exact), inverse, exact) - unit
        step = error * half
        inverse = inverse - matmul(step, inverse - matmul(step, inverse, exact), exact)
    inverse_ref[...] = inverse * across
    far = jnp.sum(error * error)

    @pl.when(jnp.logical_not(far <= CLOSE))
    def _():
        work_ref[...] = gram
        inverse_ref[...] = unit

        def eliminate(k, carry):
            whole = work_ref[...]
            pivot_row = work_ref[pl.ds(k, 1), :]
            pivot = jnp.sum(
                jnp.where(col[:1] == k, pivot_row, 0.0), axis=1, keepdims=True
            )
            column = jnp.sum(jnp.where(col == k, whole, 0.0), axis=1, keepdims=True)
            factor = jnp.where(row[:, :1] > k, column / pivot, 0.0)
            work_ref[...] = whole - factor * pivot_row
            inverse_ref[...] = inverse_ref[...] - factor * inverse_ref[pl.ds(k, 1), :]
            return carry

        lax.fori_loop(0, width, eliminate, 0)
        pivots = jnp.sum(jnp.where(on_diag, work_ref[...], 0.0), axis=1, keepdims=True)
        inverse_ref[...] = inverse_ref[...] * lax.rsqrt(pivots)

    sketch = (mine_ref[...] + other_ref[...]) / total_cols
    basis = matmul_t(sketch, inverse_ref[...]) * root_rows
    basis_ref[...] = basis
    high = basis.astype(jnp.bfloat16)
    low = (basis - high.astype(jnp.float32)).astype(jnp.bfloat16)
    pair = jnp.concatenate([high, low], axis=1).T
    fetch.wait()
    for start in range(0, buffer.shape[1], TILE):
        both = lax.dot_general(
            pair,
            buffer[:, start : start + TILE],
            (((1,), (0,)), ((), ())),
            preferred_element_type=jnp.float32,
        )
        out, inner = divmod(start, products[0].shape[1])
        products[out][:, inner : inner + TILE] = both[:width] + both[width:]


def make_basis(gram, mine, other, slab, total_cols, root_rows, chunks):
    rows, width = mine.shape
    cols = slab.shape[1]
    return pl.pallas_call(
        functools.partial(basis_kernel, total_cols, root_rows),
        out_shape=[jax.ShapeDtypeStruct((rows, width), jnp.float32)]
        + [jax.ShapeDtypeStruct((width, cols // chunks), jnp.float32)] * chunks,
        in_specs=[pl.BlockSpec(memory_space=pltpu.VMEM)] * 3
        + [pl.BlockSpec(memory_space=pl.ANY)],
        out_specs=[pl.BlockSpec(memory_space=pltpu.VMEM)] * (1 + chunks),
        scratch_shapes=[
            pltpu.VMEM((width, width), jnp.float32),
            pltpu.VMEM((width, width), jnp.float32),
            pltpu.VMEM(slab.shape, jnp.bfloat16),
            pltpu.SemaphoreType.DMA,
        ],
        compiler_params=pltpu.CompilerParams(vmem_limit_bytes=KERNEL_VMEM),
        name="make_basis",
    )(gram, mine, other, slab)


def per_device(activations, start_sketch):
    rows_here, cols_here = activations.shape
    width = start_sketch.shape[1]
    parts = lax.axis_size("row")
    total_rows = rows_here * parts
    total_cols = cols_here * lax.axis_size("col")
    root_rows = math.sqrt(total_rows)

    local_cols = first_product(start_sketch, activations, CHUNKS)
    partial_sketch = 0.0
    step = cols_here // CHUNKS
    for c in range(0, CHUNKS, 2):
        shared = sum_and_share(local_cols[c], local_cols[c + 1], "row", 1.0 / root_rows)
        for i in range(2):
            partial_sketch = partial_sketch + lax.dot_general(
                activations[:, (c + i) * step : (c + i + 1) * step],
                shared[i],
                (((1,), (1,)), ((), ())),
                preferred_element_type=jnp.float32,
            )
    other_sketch = swap(partial_sketch, "col", 1)
    gram = row_sum(make_gram(partial_sketch, other_sketch, total_cols))
    basis, *products = make_basis(
        gram, partial_sketch, other_sketch, activations, total_cols, root_rows, CHUNKS
    )

    pieces = [
        scatter_sum(products[c], products[c + 1], "row") / total_rows
        for c in range(0, CHUNKS, 2)
    ]
    return (basis, jnp.concatenate(pieces, axis=1))


def solution(mesh):
    return jax.shard_map(
        per_device,
        mesh=mesh,
        in_specs=(P(("grp", "row"), "col"), P(("grp", "row"), None)),
        out_specs=(P(("grp", "row"), None), P(("grp", "row"), "col")),
        check_vma=False,
    )
```

```python
import functools
import math

import jax
import jax.numpy as jnp
from jax import lax
from jax.experimental import pallas as pl
from jax.experimental.pallas import tpu as pltpu
from jax.sharding import PartitionSpec as P

CHUNKS = (1, 1, 3, 3)
TILE = 512
KERNEL_VMEM = 50 * 2**20


def swap(value, axis, distance):
    size = lax.axis_size(axis)
    return lax.ppermute(value, axis, [(i, i ^ distance) for i in range(size)])


def row_sum(value):
    rows, cores = lax.axis_size("row"), lax.axis_size("col")
    assert cores == 2
    first = lax.axis_index("col") == 0
    stride = 1
    while stride < rows:
        radix = min(8, rows // stride)
        split = min(2, radix // 2)
        terms = []
        for near in [digit for digit in range(radix) if not digit & split]:
            pairs = []
            for row in range(rows):
                for core, digit in ((0, near), (1, near | split)):
                    if digit:
                        pairs.append((row * cores + core, (row ^ digit * stride) * cores + core))
            terms.append(lax.ppermute(value, ("row", "col"), pairs))
        terms[0] = jnp.where(first, value, terms[0])
        while len(terms) > 1:
            terms = [terms[i] + terms[i + 1] for i in range(0, len(terms), 2)]
        value = terms[0] + swap(terms[0], "col", 1)
        stride *= radix
    return value


def scatter_sum(value, axis, order):
    rows, cols = value.shape[0] >> len(order), value.shape[1]
    total = value.reshape([2] * len(order) + [rows, cols])
    left = sorted(order, reverse=True)
    for bit in order:
        dim = left.index(bit)
        left.remove(bit)
        low = lax.index_in_dim(total, 0, dim, keepdims=False)
        high = lax.index_in_dim(total, 1, dim, keepdims=False)
        upper = bit_of(axis, bit) == 1
        send = jnp.where(upper, low, high).astype(jnp.bfloat16)
        landed = swap(send, axis, 1 << bit)
        total = jnp.where(upper, high, low) + landed.astype(jnp.float32)
    return total


def bit_of(axis, bit):
    return lax.rem(lax.div(lax.axis_index(axis), 1 << bit), 2)


def sum_and_share(value, axis, order, scale):
    for bit in order[:-1]:
        upper = bit_of(axis, bit) == 1
        half = value.shape[1] // 2
        low, high = value[:, :half], value[:, half:]
        send = jnp.where(upper, low, high).astype(jnp.bfloat16)
        landed = swap(send, axis, 1 << bit)
        value = jnp.where(upper, high, low) + landed.astype(jnp.float32)
    landed = swap(value.astype(jnp.bfloat16), axis, 1 << order[-1])
    block = ((value + landed.astype(jnp.float32)) * scale).astype(jnp.bfloat16)
    for bit in reversed(order[:-1]):
        upper = bit_of(axis, bit) == 1
        other = swap(block, axis, 1 << bit)
        block = jnp.concatenate(
            [jnp.where(upper, other, block), jnp.where(upper, block, other)], axis=1
        )
    return block


def orders_of(axis):
    bits = list(range((lax.axis_size(axis) - 1).bit_length()))
    if len(bits) < 3:
        return [bits, bits]
    return [bits, [bits[1], bits[0]] + bits[2:]]


def fetch_tiles(slab_ref, buffer, arrived):
    copies = []
    for tile in range(buffer.shape[0]):
        span = pl.ds(tile * TILE, TILE)
        copies.append(
            pltpu.make_async_copy(slab_ref.at[:, span], buffer.at[tile], arrived.at[tile])
        )
    for copy in copies:
        copy.start()
    return copies


def store(outs, start, tile):
    for out in outs:
        if start < out.shape[1]:
            out[:, start : start + TILE] = tile
            return
        start -= out.shape[1]


def widths_of(cols):
    return [cols // sum(CHUNKS) * part for part in CHUNKS]


def sketch_kernel(start_ref, slab_ref, *refs):
    outs, (buffer, arrived) = refs[:-2], refs[-2:]
    copies = fetch_tiles(slab_ref, buffer, arrived)
    left = start_ref[...].T
    for tile, copy in enumerate(copies):
        copy.wait()
        store(
            outs,
            tile * TILE,
            lax.dot_general(
                left, buffer[tile], (((1,), (0,)), ((), ())), preferred_element_type=jnp.float32
            ),
        )


def first_product(start, slab):
    rows, width = start.shape
    cols = slab.shape[1]
    return pl.pallas_call(
        sketch_kernel,
        out_shape=[
            jax.ShapeDtypeStruct((width, part), jnp.float32) for part in widths_of(cols)
        ],
        in_specs=[
            pl.BlockSpec(memory_space=pltpu.VMEM),
            pl.BlockSpec(memory_space=pl.ANY),
        ],
        out_specs=[pl.BlockSpec(memory_space=pltpu.VMEM)] * len(CHUNKS),
        scratch_shapes=[
            pltpu.VMEM((cols // TILE, rows, TILE), jnp.bfloat16),
            pltpu.SemaphoreType.DMA((cols // TILE,)),
        ],
        compiler_params=pltpu.CompilerParams(vmem_limit_bytes=KERNEL_VMEM),
        cost_estimate=pl.CostEstimate(
            flops=2 * rows * width * cols, bytes_accessed=2 * rows * cols, transcendentals=0
        ),
        name="first_product",
    )(start, slab)


def matmul(left, right, exact=True):
    if not exact:
        left, right = left.astype(jnp.bfloat16), right.astype(jnp.bfloat16)
    return lax.dot_general(
        left,
        right,
        (((1,), (0,)), ((), ())),
        precision=lax.Precision.HIGHEST if exact else None,
        preferred_element_type=jnp.float32,
    )


def matmul_t(left, right, exact=True):
    if not exact:
        left, right = left.astype(jnp.bfloat16), right.astype(jnp.bfloat16)
    return lax.dot_general(
        left,
        right,
        (((1,), (1,)), ((), ())),
        precision=lax.Precision.HIGHEST if exact else None,
        preferred_element_type=jnp.float32,
    )


def gram_kernel(total_cols, mine_ref, other_ref, packed_ref):
    sketch = (mine_ref[...] + other_ref[...]) / total_cols
    gram = matmul(sketch.T, sketch)
    half = gram.shape[0] // 2
    row = lax.broadcasted_iota(jnp.int32, (half, 2 * half), 0)
    col = lax.broadcasted_iota(jnp.int32, (half, 2 * half), 1)
    top, bottom = gram[:half], pltpu.roll(gram[half:], half, 1)
    packed_ref[:half] = jnp.where(row > col, bottom, top)
    diagonal = jnp.sum(jnp.where(row == col, bottom, 0.0), axis=0, keepdims=True)
    packed_ref[half:] = jnp.broadcast_to(diagonal, (8, 2 * half))


def unpack_gram(packed):
    width = packed.shape[1]
    half = width // 2
    row = lax.broadcasted_iota(jnp.int32, (half, width), 0)
    col = lax.broadcasted_iota(jnp.int32, (half, width), 1)
    square = packed[:half]
    top = jnp.where(row > col, 0.0, square)
    lower = jnp.where(row > col, square, jnp.where(row == col, packed[half : half + 1], 0.0))
    parts = jnp.concatenate([top, pltpu.roll(lower, half, 1)], axis=0)
    row = lax.broadcasted_iota(jnp.int32, (width, width), 0)
    col = lax.broadcasted_iota(jnp.int32, (width, width), 1)
    return jnp.where(row == col, parts, parts + parts.T)


def make_gram(mine, other, total_cols):
    rows, width = mine.shape
    return pl.pallas_call(
        functools.partial(gram_kernel, total_cols),
        out_shape=jax.ShapeDtypeStruct((width // 2 + 8, width), jnp.float32),
        in_specs=[pl.BlockSpec(memory_space=pltpu.VMEM)] * 2,
        out_specs=pl.BlockSpec(memory_space=pltpu.VMEM),
        compiler_params=pltpu.CompilerParams(vmem_limit_bytes=16 * 2**20),
        name="make_gram",
    )(mine, other)


UPDATES = 4
LOOSE_UPDATES = 2
CLOSE = 1e-5


def basis_kernel(
    total_cols, root_rows, gram_ref, mine_ref, other_ref, slab_ref,
    basis_ref, *refs,
):
    products, (work_ref, inverse_ref, buffer, arrived) = refs[:-4], refs[-4:]
    fetch = pltpu.make_async_copy(slab_ref, buffer, arrived)
    fetch.start()
    width = gram_ref.shape[1]
    row = lax.broadcasted_iota(jnp.int32, (width, width), 0)
    col = lax.broadcasted_iota(jnp.int32, (width, width), 1)
    on_diag = row == col
    unit = jnp.where(on_diag, 1.0, 0.0)
    half = jnp.where(row > col, 1.0, jnp.where(on_diag, 0.5, 0.0))

    gram = unpack_gram(gram_ref[...])
    diagonal = jnp.where(on_diag, gram, 0.0)
    down = lax.rsqrt(jnp.sum(diagonal, axis=1, keepdims=True))
    across = lax.rsqrt(jnp.sum(diagonal, axis=0, keepdims=True))
    scaled = gram * down * across

    error = scaled - unit
    step = error * half
    inverse = unit - step + matmul(step, step, False)
    for update in range(1, UPDATES):
        exact = update >= LOOSE_UPDATES
        error = matmul_t(matmul(inverse, scaled, exact), inverse, exact) - unit
        step = error * half
        inverse = inverse - matmul(step, inverse - matmul(step, inverse, exact), exact)
    inverse_ref[...] = inverse * across
    far = jnp.sum(error * error)

    @pl.when(jnp.logical_not(far <= CLOSE))
    def _():
        work_ref[...] = gram
        inverse_ref[...] = unit

        def eliminate(k, carry):
            whole = work_ref[...]
            pivot_row = work_ref[pl.ds(k, 1), :]
            pivot = jnp.sum(
                jnp.where(col[:1] == k, pivot_row, 0.0), axis=1, keepdims=True
            )
            column = jnp.sum(jnp.where(col == k, whole, 0.0), axis=1, keepdims=True)
            factor = jnp.where(row[:, :1] > k, column / pivot, 0.0)
            work_ref[...] = whole - factor * pivot_row
            inverse_ref[...] = inverse_ref[...] - factor * inverse_ref[pl.ds(k, 1), :]
            return carry

        lax.fori_loop(0, width, eliminate, 0)
        pivots = jnp.sum(jnp.where(on_diag, work_ref[...], 0.0), axis=1, keepdims=True)
        inverse_ref[...] = inverse_ref[...] * lax.rsqrt(pivots)

    sketch = (mine_ref[...] + other_ref[...]) / total_cols
    basis = matmul_t(sketch, inverse_ref[...]) * root_rows
    basis_ref[...] = basis
    high = basis.astype(jnp.bfloat16)
    low = (basis - high.astype(jnp.float32)).astype(jnp.bfloat16)
    pair = jnp.concatenate([high, low], axis=1).T
    fetch.wait()
    for start in range(0, buffer.shape[1], TILE):
        both = lax.dot_general(
            pair,
            buffer[:, start : start + TILE],
            (((1,), (0,)), ((), ())),
            preferred_element_type=jnp.float32,
        )
        store(products, start, both[:width] + both[width:])


def make_basis(gram, mine, other, slab, total_cols, root_rows):
    rows, width = mine.shape
    cols = slab.shape[1]
    return pl.pallas_call(
        functools.partial(basis_kernel, total_cols, root_rows),
        out_shape=[jax.ShapeDtypeStruct((rows, width), jnp.float32)]
        + [jax.ShapeDtypeStruct((width, part), jnp.float32) for part in widths_of(cols)],
        in_specs=[pl.BlockSpec(memory_space=pltpu.VMEM)] * 3
        + [pl.BlockSpec(memory_space=pl.ANY)],
        out_specs=[pl.BlockSpec(memory_space=pltpu.VMEM)] * (1 + len(CHUNKS)),
        scratch_shapes=[
            pltpu.VMEM((width, width), jnp.float32),
            pltpu.VMEM((width, width), jnp.float32),
            pltpu.VMEM(slab.shape, jnp.bfloat16),
            pltpu.SemaphoreType.DMA,
        ],
        compiler_params=pltpu.CompilerParams(vmem_limit_bytes=KERNEL_VMEM),
        name="make_basis",
    )(gram, mine, other, slab)


def per_device(activations, start_sketch):
    rows_here, cols_here = activations.shape
    width = start_sketch.shape[1]
    parts = lax.axis_size("row")
    total_rows = rows_here * parts
    total_cols = cols_here * lax.axis_size("col")
    root_rows = math.sqrt(total_rows)

    local_cols = first_product(start_sketch, activations)
    partial_sketch = 0.0
    orders = orders_of("row")
    begin = 0
    for c, local in enumerate(local_cols):
        span = slice(begin, begin + local.shape[1])
        begin = span.stop
        shared = sum_and_share(local, "row", orders[c % 2], 1.0 / root_rows)
        partial_sketch = partial_sketch + lax.dot_general(
            activations[:, span],
            shared,
            (((1,), (1,)), ((), ())),
            preferred_element_type=jnp.float32,
        )
    other_sketch = swap(partial_sketch, "col", 1)
    gram = row_sum(make_gram(partial_sketch, other_sketch, total_cols))
    basis, *products = make_basis(
        gram, partial_sketch, other_sketch, activations, total_cols, root_rows
    )

    pieces = [
        scatter_sum(product, "row", orders[c % 2]) / total_rows
        for c, product in enumerate(products)
    ]
    return (basis, jnp.concatenate(pieces, axis=1))


def solution(mesh):
    return jax.shard_map(
        per_device,
        mesh=mesh,
        in_specs=(P(("grp", "row"), "col"), P(("grp", "row"), None)),
        out_specs=(P(("grp", "row"), None), P(("grp", "row"), "col")),
        check_vma=False,
    )
```

```python
import functools
import math

import jax
import jax.numpy as jnp
from jax import lax
from jax.experimental import pallas as pl
from jax.experimental.pallas import tpu as pltpu
from jax.sharding import PartitionSpec as P

CHUNKS = 4
TILE = 512
KERNEL_VMEM = 50 * 2**20


def swap(value, axis, distance):
    size = lax.axis_size(axis)
    return lax.ppermute(value, axis, [(i, i ^ distance) for i in range(size)])


def row_sum(value):
    rows, cores = lax.axis_size("row"), lax.axis_size("col")
    assert cores == 2
    first = lax.axis_index("col") == 0
    stride = 1
    while stride < rows:
        radix = min(8, rows // stride)
        split = min(2, radix // 2)
        terms = []
        for near in [digit for digit in range(radix) if not digit & split]:
            pairs = []
            for row in range(rows):
                for core, digit in ((0, near), (1, near | split)):
                    if digit:
                        pairs.append((row * cores + core, (row ^ digit * stride) * cores + core))
            terms.append(lax.ppermute(value, ("row", "col"), pairs))
        terms[0] = jnp.where(first, value, terms[0])
        while len(terms) > 1:
            terms = [terms[i] + terms[i + 1] for i in range(0, len(terms), 2)]
        value = terms[0] + swap(terms[0], "col", 1)
        stride *= radix
    return value


def bit_of(axis, bit):
    return lax.rem(lax.div(lax.axis_index(axis), 1 << bit), 2)


def pick(upper, low, high):
    return jnp.where(upper, high, low), jnp.where(upper, low, high).astype(jnp.bfloat16)


def sum_and_share(value, axis, order, scale):
    for bit in order[:-1]:
        half = value.shape[1] // 2
        keep, send = pick(bit_of(axis, bit) == 1, value[:, :half], value[:, half:])
        landed = yield send, bit
        value = keep + landed.astype(jnp.float32)
    landed = yield value.astype(jnp.bfloat16), order[-1]
    block = ((value + landed.astype(jnp.float32)) * scale).astype(jnp.bfloat16)
    for bit in reversed(order[:-1]):
        upper = bit_of(axis, bit) == 1
        other = yield block, bit
        block = jnp.concatenate(
            [jnp.where(upper, other, block), jnp.where(upper, block, other)], axis=1
        )
    return block


def scatter_sum(value, axis, order):
    rows, cols = value.shape[0] >> len(order), value.shape[1]
    total = value.reshape([2] * len(order) + [rows, cols])
    left = sorted(order, reverse=True)
    for bit in order:
        dim = left.index(bit)
        left.remove(bit)
        low = lax.index_in_dim(total, 0, dim, keepdims=False)
        high = lax.index_in_dim(total, 1, dim, keepdims=False)
        keep, send = pick(bit_of(axis, bit) == 1, low, high)
        landed = yield send, bit
        total = keep + landed.astype(jnp.float32)
    return total


def after(value, others):
    return lax.optimization_barrier((value, others))[0] if others else value


def staggered(steps, values, axis, *args):
    orders = orders_of(axis)
    pairs = [range(c, c + 2) for c in range(0, len(values), 2)]
    running, landed, results = {}, {}, {}
    sends, turn = [], 0
    while len(results) < len(values):
        for number, pair in enumerate(pairs):
            if turn < number or pair[0] in results:
                continue
            made = []
            for c in pair:
                try:
                    if c in running:
                        send, bit = running[c].send(after(landed[c], sends))
                    else:
                        value = after(values[c], sends)
                        running[c] = steps(value, axis, orders[c % 2], *args)
                        send, bit = next(running[c])
                except StopIteration as end:
                    results[c] = end.value
                    continue
                made.append(send)
                landed[c] = swap(send, axis, 1 << bit)
            sends = made or sends
        turn += 1
    return [results[c] for c in range(len(values))]


def orders_of(axis):
    bits = list(range((lax.axis_size(axis) - 1).bit_length()))
    if len(bits) < 3:
        return [bits, bits]
    return [bits, [bits[1], bits[0]] + bits[2:]]


def fetch_tiles(slab_ref, buffer, arrived):
    copies = []
    for tile in range(buffer.shape[0]):
        span = pl.ds(tile * TILE, TILE)
        copies.append(
            pltpu.make_async_copy(slab_ref.at[:, span], buffer.at[tile], arrived.at[tile])
        )
    for copy in copies:
        copy.start()
    return copies


def sketch_kernel(start_ref, slab_ref, *refs):
    outs, (buffer, arrived) = refs[:-2], refs[-2:]
    copies = fetch_tiles(slab_ref, buffer, arrived)
    left = start_ref[...].T
    for tile, copy in enumerate(copies):
        copy.wait()
        out, inner = divmod(tile * TILE, outs[0].shape[1])
        outs[out][:, inner : inner + TILE] = lax.dot_general(
            left, buffer[tile], (((1,), (0,)), ((), ())), preferred_element_type=jnp.float32
        )


def first_product(start, slab, chunks):
    rows, width = start.shape
    cols = slab.shape[1]
    return pl.pallas_call(
        sketch_kernel,
        out_shape=[jax.ShapeDtypeStruct((width, cols // chunks), jnp.float32)] * chunks,
        in_specs=[
            pl.BlockSpec(memory_space=pltpu.VMEM),
            pl.BlockSpec(memory_space=pl.ANY),
        ],
        out_specs=[pl.BlockSpec(memory_space=pltpu.VMEM)] * chunks,
        scratch_shapes=[
            pltpu.VMEM((cols // TILE, rows, TILE), jnp.bfloat16),
            pltpu.SemaphoreType.DMA((cols // TILE,)),
        ],
        compiler_params=pltpu.CompilerParams(vmem_limit_bytes=KERNEL_VMEM),
        cost_estimate=pl.CostEstimate(
            flops=2 * rows * width * cols, bytes_accessed=2 * rows * cols, transcendentals=0
        ),
        name="first_product",
    )(start, slab)


def matmul(left, right, exact=True):
    if not exact:
        left, right = left.astype(jnp.bfloat16), right.astype(jnp.bfloat16)
    return lax.dot_general(
        left,
        right,
        (((1,), (0,)), ((), ())),
        precision=lax.Precision.HIGHEST if exact else None,
        preferred_element_type=jnp.float32,
    )


def matmul_t(left, right, exact=True):
    if not exact:
        left, right = left.astype(jnp.bfloat16), right.astype(jnp.bfloat16)
    return lax.dot_general(
        left,
        right,
        (((1,), (1,)), ((), ())),
        precision=lax.Precision.HIGHEST if exact else None,
        preferred_element_type=jnp.float32,
    )


def gram_kernel(total_cols, mine_ref, other_ref, packed_ref):
    sketch = (mine_ref[...] + other_ref[...]) / total_cols
    gram = matmul(sketch.T, sketch)
    half = gram.shape[0] // 2
    row = lax.broadcasted_iota(jnp.int32, (half, 2 * half), 0)
    col = lax.broadcasted_iota(jnp.int32, (half, 2 * half), 1)
    top, bottom = gram[:half], pltpu.roll(gram[half:], half, 1)
    packed_ref[:half] = jnp.where(row > col, bottom, top)
    diagonal = jnp.sum(jnp.where(row == col, bottom, 0.0), axis=0, keepdims=True)
    packed_ref[half:] = jnp.broadcast_to(diagonal, (8, 2 * half))


def unpack_gram(packed):
    width = packed.shape[1]
    half = width // 2
    row = lax.broadcasted_iota(jnp.int32, (half, width), 0)
    col = lax.broadcasted_iota(jnp.int32, (half, width), 1)
    square = packed[:half]
    top = jnp.where(row > col, 0.0, square)
    lower = jnp.where(row > col, square, jnp.where(row == col, packed[half : half + 1], 0.0))
    parts = jnp.concatenate([top, pltpu.roll(lower, half, 1)], axis=0)
    row = lax.broadcasted_iota(jnp.int32, (width, width), 0)
    col = lax.broadcasted_iota(jnp.int32, (width, width), 1)
    return jnp.where(row == col, parts, parts + parts.T)


def make_gram(mine, other, total_cols):
    rows, width = mine.shape
    return pl.pallas_call(
        functools.partial(gram_kernel, total_cols),
        out_shape=jax.ShapeDtypeStruct((width // 2 + 8, width), jnp.float32),
        in_specs=[pl.BlockSpec(memory_space=pltpu.VMEM)] * 2,
        out_specs=pl.BlockSpec(memory_space=pltpu.VMEM),
        compiler_params=pltpu.CompilerParams(vmem_limit_bytes=16 * 2**20),
        name="make_gram",
    )(mine, other)


UPDATES = 4
LOOSE_UPDATES = 2
CLOSE = 1e-5


def basis_kernel(
    total_cols, root_rows, gram_ref, mine_ref, other_ref, slab_ref,
    basis_ref, *refs,
):
    products, (work_ref, inverse_ref, buffer, arrived) = refs[:-4], refs[-4:]
    fetch = pltpu.make_async_copy(slab_ref, buffer, arrived)
    fetch.start()
    width = gram_ref.shape[1]
    row = lax.broadcasted_iota(jnp.int32, (width, width), 0)
    col = lax.broadcasted_iota(jnp.int32, (width, width), 1)
    on_diag = row == col
    unit = jnp.where(on_diag, 1.0, 0.0)
    half = jnp.where(row > col, 1.0, jnp.where(on_diag, 0.5, 0.0))

    gram = unpack_gram(gram_ref[...])
    diagonal = jnp.where(on_diag, gram, 0.0)
    down = lax.rsqrt(jnp.sum(diagonal, axis=1, keepdims=True))
    across = lax.rsqrt(jnp.sum(diagonal, axis=0, keepdims=True))
    scaled = gram * down * across

    error = scaled - unit
    step = error * half
    inverse = unit - step + matmul(step, step, False)
    for update in range(1, UPDATES):
        exact = update >= LOOSE_UPDATES
        error = matmul_t(matmul(inverse, scaled, exact), inverse, exact) - unit
        step = error * half
        inverse = inverse - matmul(step, inverse - matmul(step, inverse, exact), exact)
    inverse_ref[...] = inverse * across
    far = jnp.sum(error * error)

    @pl.when(jnp.logical_not(far <= CLOSE))
    def _():
        work_ref[...] = gram
        inverse_ref[...] = unit

        def eliminate(k, carry):
            whole = work_ref[...]
            pivot_row = work_ref[pl.ds(k, 1), :]
            pivot = jnp.sum(
                jnp.where(col[:1] == k, pivot_row, 0.0), axis=1, keepdims=True
            )
            column = jnp.sum(jnp.where(col == k, whole, 0.0), axis=1, keepdims=True)
            factor = jnp.where(row[:, :1] > k, column / pivot, 0.0)
            work_ref[...] = whole - factor * pivot_row
            inverse_ref[...] = inverse_ref[...] - factor * inverse_ref[pl.ds(k, 1), :]
            return carry

        lax.fori_loop(0, width, eliminate, 0)
        pivots = jnp.sum(jnp.where(on_diag, work_ref[...], 0.0), axis=1, keepdims=True)
        inverse_ref[...] = inverse_ref[...] * lax.rsqrt(pivots)

    sketch = (mine_ref[...] + other_ref[...]) / total_cols
    basis = matmul_t(sketch, inverse_ref[...]) * root_rows
    basis_ref[...] = basis
    high = basis.astype(jnp.bfloat16)
    low = (basis - high.astype(jnp.float32)).astype(jnp.bfloat16)
    pair = jnp.concatenate([high, low], axis=1).T
    fetch.wait()
    for start in range(0, buffer.shape[1], TILE):
        both = lax.dot_general(
            pair,
            buffer[:, start : start + TILE],
            (((1,), (0,)), ((), ())),
            preferred_element_type=jnp.float32,
        )
        out, inner = divmod(start, products[0].shape[1])
        products[out][:, inner : inner + TILE] = both[:width] + both[width:]


def make_basis(gram, mine, other, slab, total_cols, root_rows, chunks):
    rows, width = mine.shape
    cols = slab.shape[1]
    return pl.pallas_call(
        functools.partial(basis_kernel, total_cols, root_rows),
        out_shape=[jax.ShapeDtypeStruct((rows, width), jnp.float32)]
        + [jax.ShapeDtypeStruct((width, cols // chunks), jnp.float32)] * chunks,
        in_specs=[pl.BlockSpec(memory_space=pltpu.VMEM)] * 3
        + [pl.BlockSpec(memory_space=pl.ANY)],
        out_specs=[pl.BlockSpec(memory_space=pltpu.VMEM)] * (1 + chunks),
        scratch_shapes=[
            pltpu.VMEM((width, width), jnp.float32),
            pltpu.VMEM((width, width), jnp.float32),
            pltpu.VMEM(slab.shape, jnp.bfloat16),
            pltpu.SemaphoreType.DMA,
        ],
        compiler_params=pltpu.CompilerParams(vmem_limit_bytes=KERNEL_VMEM),
        name="make_basis",
    )(gram, mine, other, slab)


def per_device(activations, start_sketch):
    rows_here, cols_here = activations.shape
    width = start_sketch.shape[1]
    parts = lax.axis_size("row")
    total_rows = rows_here * parts
    total_cols = cols_here * lax.axis_size("col")
    root_rows = math.sqrt(total_rows)

    local_cols = first_product(start_sketch, activations, CHUNKS)
    partial_sketch = 0.0
    step = cols_here // CHUNKS
    shared = staggered(sum_and_share, local_cols, "row", 1.0 / root_rows)
    for c, chunk in enumerate(shared):
        span = slice(c * step, (c + 1) * step)
        partial_sketch = partial_sketch + lax.dot_general(
            activations[:, span],
            chunk,
            (((1,), (1,)), ((), ())),
            preferred_element_type=jnp.float32,
        )
    other_sketch = swap(partial_sketch, "col", 1)
    gram = row_sum(make_gram(partial_sketch, other_sketch, total_cols))
    basis, *products = make_basis(
        gram, partial_sketch, other_sketch, activations, total_cols, root_rows, CHUNKS
    )

    pieces = [total / total_rows for total in staggered(scatter_sum, products, "row")]
    return (basis, jnp.concatenate(pieces, axis=1))


def solution(mesh):
    return jax.shard_map(
        per_device,
        mesh=mesh,
        in_specs=(P(("grp", "row"), "col"), P(("grp", "row"), None)),
        out_specs=(P(("grp", "row"), None), P(("grp", "row"), "col")),
        check_vma=False,
    )
```

```python
import functools
import math

import jax
import jax.numpy as jnp
from jax import lax
from jax.experimental import pallas as pl
from jax.experimental.pallas import tpu as pltpu
from jax.sharding import PartitionSpec as P

CHUNKS = (1, 2, 1)
TILE = 512
KERNEL_VMEM = 50 * 2**20


def swap(value, axis, distance):
    size = lax.axis_size(axis)
    return lax.ppermute(value, axis, [(i, i ^ distance) for i in range(size)])


def row_sum(value):
    rows, cores = lax.axis_size("row"), lax.axis_size("col")
    assert cores == 2
    first = lax.axis_index("col") == 0
    stride = 1
    while stride < rows:
        radix = min(8, rows // stride)
        split = min(2, radix // 2)
        terms = []
        for near in [digit for digit in range(radix) if not digit & split]:
            pairs = []
            for row in range(rows):
                for core, digit in ((0, near), (1, near | split)):
                    if digit:
                        pairs.append((row * cores + core, (row ^ digit * stride) * cores + core))
            terms.append(lax.ppermute(value, ("row", "col"), pairs))
        terms[0] = jnp.where(first, value, terms[0])
        while len(terms) > 1:
            terms = [terms[i] + terms[i + 1] for i in range(0, len(terms), 2)]
        value = terms[0] + swap(terms[0], "col", 1)
        stride *= radix
    return value


def scatter_sum(value, axis, order):
    rows, cols = value.shape[0] >> len(order), value.shape[1]
    total = value.reshape([2] * len(order) + [rows, cols])
    left = sorted(order, reverse=True)
    for bit in order:
        dim = left.index(bit)
        left.remove(bit)
        low = lax.index_in_dim(total, 0, dim, keepdims=False)
        high = lax.index_in_dim(total, 1, dim, keepdims=False)
        upper = bit_of(axis, bit) == 1
        send = jnp.where(upper, low, high).astype(jnp.bfloat16)
        landed = swap(send, axis, 1 << bit)
        total = jnp.where(upper, high, low) + landed.astype(jnp.float32)
    return total


def bit_of(axis, bit):
    return lax.rem(lax.div(lax.axis_index(axis), 1 << bit), 2)


def sum_and_share(value, axis, order, scale):
    for bit in order[:-1]:
        upper = bit_of(axis, bit) == 1
        half = value.shape[1] // 2
        low, high = value[:, :half], value[:, half:]
        send = jnp.where(upper, low, high).astype(jnp.bfloat16)
        landed = swap(send, axis, 1 << bit)
        value = jnp.where(upper, high, low) + landed.astype(jnp.float32)
    landed = swap(value.astype(jnp.bfloat16), axis, 1 << order[-1])
    block = ((value + landed.astype(jnp.float32)) * scale).astype(jnp.bfloat16)
    for bit in reversed(order[:-1]):
        upper = bit_of(axis, bit) == 1
        other = swap(block, axis, 1 << bit)
        block = jnp.concatenate(
            [jnp.where(upper, other, block), jnp.where(upper, block, other)], axis=1
        )
    return block


def orders_of(axis):
    bits = list(range((lax.axis_size(axis) - 1).bit_length()))
    if len(bits) < 3:
        return [bits, bits]
    return [bits, [bits[1], bits[0]] + bits[2:]]


def fetch_tiles(slab_ref, buffer, arrived):
    copies = []
    for tile in range(buffer.shape[0]):
        span = pl.ds(tile * TILE, TILE)
        copies.append(
            pltpu.make_async_copy(slab_ref.at[:, span], buffer.at[tile], arrived.at[tile])
        )
    for copy in copies:
        copy.start()
    return copies


def store(outs, start, tile):
    for out in outs:
        if start < out.shape[1]:
            out[:, start : start + TILE] = tile
            return
        start -= out.shape[1]


def widths_of(cols):
    return [cols // sum(CHUNKS) * part for part in CHUNKS]


def sketch_kernel(start_ref, slab_ref, *refs):
    outs, (buffer, arrived) = refs[:-2], refs[-2:]
    copies = fetch_tiles(slab_ref, buffer, arrived)
    left = start_ref[...].T
    for tile, copy in enumerate(copies):
        copy.wait()
        store(
            outs,
            tile * TILE,
            lax.dot_general(
                left, buffer[tile], (((1,), (0,)), ((), ())), preferred_element_type=jnp.float32
            ),
        )


def first_product(start, slab):
    rows, width = start.shape
    cols = slab.shape[1]
    return pl.pallas_call(
        sketch_kernel,
        out_shape=[
            jax.ShapeDtypeStruct((width, part), jnp.float32) for part in widths_of(cols)
        ],
        in_specs=[
            pl.BlockSpec(memory_space=pltpu.VMEM),
            pl.BlockSpec(memory_space=pl.ANY),
        ],
        out_specs=[pl.BlockSpec(memory_space=pltpu.VMEM)] * len(CHUNKS),
        scratch_shapes=[
            pltpu.VMEM((cols // TILE, rows, TILE), jnp.bfloat16),
            pltpu.SemaphoreType.DMA((cols // TILE,)),
        ],
        compiler_params=pltpu.CompilerParams(vmem_limit_bytes=KERNEL_VMEM),
        cost_estimate=pl.CostEstimate(
            flops=2 * rows * width * cols, bytes_accessed=2 * rows * cols, transcendentals=0
        ),
        name="first_product",
    )(start, slab)


def matmul(left, right, exact=True):
    if not exact:
        left, right = left.astype(jnp.bfloat16), right.astype(jnp.bfloat16)
    return lax.dot_general(
        left,
        right,
        (((1,), (0,)), ((), ())),
        precision=lax.Precision.HIGHEST if exact else None,
        preferred_element_type=jnp.float32,
    )


def matmul_t(left, right, exact=True):
    if not exact:
        left, right = left.astype(jnp.bfloat16), right.astype(jnp.bfloat16)
    return lax.dot_general(
        left,
        right,
        (((1,), (1,)), ((), ())),
        precision=lax.Precision.HIGHEST if exact else None,
        preferred_element_type=jnp.float32,
    )


def gram_kernel(total_cols, mine_ref, other_ref, packed_ref):
    sketch = (mine_ref[...] + other_ref[...]) / total_cols
    gram = matmul(sketch.T, sketch)
    half = gram.shape[0] // 2
    row = lax.broadcasted_iota(jnp.int32, (half, 2 * half), 0)
    col = lax.broadcasted_iota(jnp.int32, (half, 2 * half), 1)
    top, bottom = gram[:half], pltpu.roll(gram[half:], half, 1)
    packed_ref[:half] = jnp.where(row > col, bottom, top)
    diagonal = jnp.sum(jnp.where(row == col, bottom, 0.0), axis=0, keepdims=True)
    packed_ref[half:] = jnp.broadcast_to(diagonal, (8, 2 * half))


def unpack_gram(packed):
    width = packed.shape[1]
    half = width // 2
    row = lax.broadcasted_iota(jnp.int32, (half, width), 0)
    col = lax.broadcasted_iota(jnp.int32, (half, width), 1)
    square = packed[:half]
    top = jnp.where(row > col, 0.0, square)
    lower = jnp.where(row > col, square, jnp.where(row == col, packed[half : half + 1], 0.0))
    parts = jnp.concatenate([top, pltpu.roll(lower, half, 1)], axis=0)
    row = lax.broadcasted_iota(jnp.int32, (width, width), 0)
    col = lax.broadcasted_iota(jnp.int32, (width, width), 1)
    return jnp.where(row == col, parts, parts + parts.T)


def make_gram(mine, other, total_cols):
    rows, width = mine.shape
    return pl.pallas_call(
        functools.partial(gram_kernel, total_cols),
        out_shape=jax.ShapeDtypeStruct((width // 2 + 8, width), jnp.float32),
        in_specs=[pl.BlockSpec(memory_space=pltpu.VMEM)] * 2,
        out_specs=pl.BlockSpec(memory_space=pltpu.VMEM),
        compiler_params=pltpu.CompilerParams(vmem_limit_bytes=16 * 2**20),
        name="make_gram",
    )(mine, other)


UPDATES = 4
LOOSE_UPDATES = 2
CLOSE = 1e-5


def basis_kernel(
    total_cols, root_rows, gram_ref, mine_ref, other_ref, slab_ref,
    basis_ref, *refs,
):
    products, (work_ref, inverse_ref, buffer, arrived) = refs[:-4], refs[-4:]
    fetch = pltpu.make_async_copy(slab_ref, buffer, arrived)
    fetch.start()
    width = gram_ref.shape[1]
    row = lax.broadcasted_iota(jnp.int32, (width, width), 0)
    col = lax.broadcasted_iota(jnp.int32, (width, width), 1)
    on_diag = row == col
    unit = jnp.where(on_diag, 1.0, 0.0)
    half = jnp.where(row > col, 1.0, jnp.where(on_diag, 0.5, 0.0))

    gram = unpack_gram(gram_ref[...])
    diagonal = jnp.where(on_diag, gram, 0.0)
    down = lax.rsqrt(jnp.sum(diagonal, axis=1, keepdims=True))
    across = lax.rsqrt(jnp.sum(diagonal, axis=0, keepdims=True))
    scaled = gram * down * across

    error = scaled - unit
    step = error * half
    inverse = unit - step + matmul(step, step, False)
    for update in range(1, UPDATES):
        exact = update >= LOOSE_UPDATES
        error = matmul_t(matmul(inverse, scaled, exact), inverse, exact) - unit
        step = error * half
        inverse = inverse - matmul(step, inverse - matmul(step, inverse, exact), exact)
    inverse_ref[...] = inverse * across
    far = jnp.sum(error * error)

    @pl.when(jnp.logical_not(far <= CLOSE))
    def _():
        work_ref[...] = gram
        inverse_ref[...] = unit

        def eliminate(k, carry):
            whole = work_ref[...]
            pivot_row = work_ref[pl.ds(k, 1), :]
            pivot = jnp.sum(
                jnp.where(col[:1] == k, pivot_row, 0.0), axis=1, keepdims=True
            )
            column = jnp.sum(jnp.where(col == k, whole, 0.0), axis=1, keepdims=True)
            factor = jnp.where(row[:, :1] > k, column / pivot, 0.0)
            work_ref[...] = whole - factor * pivot_row
            inverse_ref[...] = inverse_ref[...] - factor * inverse_ref[pl.ds(k, 1), :]
            return carry

        lax.fori_loop(0, width, eliminate, 0)
        pivots = jnp.sum(jnp.where(on_diag, work_ref[...], 0.0), axis=1, keepdims=True)
        inverse_ref[...] = inverse_ref[...] * lax.rsqrt(pivots)

    sketch = (mine_ref[...] + other_ref[...]) / total_cols
    basis = matmul_t(sketch, inverse_ref[...]) * root_rows
    basis_ref[...] = basis
    high = basis.astype(jnp.bfloat16)
    low = (basis - high.astype(jnp.float32)).astype(jnp.bfloat16)
    pair = jnp.concatenate([high, low], axis=1).T
    fetch.wait()
    for start in range(0, buffer.shape[1], TILE):
        both = lax.dot_general(
            pair,
            buffer[:, start : start + TILE],
            (((1,), (0,)), ((), ())),
            preferred_element_type=jnp.float32,
        )
        store(products, start, both[:width] + both[width:])


def make_basis(gram, mine, other, slab, total_cols, root_rows):
    rows, width = mine.shape
    cols = slab.shape[1]
    return pl.pallas_call(
        functools.partial(basis_kernel, total_cols, root_rows),
        out_shape=[jax.ShapeDtypeStruct((rows, width), jnp.float32)]
        + [jax.ShapeDtypeStruct((width, part), jnp.float32) for part in widths_of(cols)],
        in_specs=[pl.BlockSpec(memory_space=pltpu.VMEM)] * 3
        + [pl.BlockSpec(memory_space=pl.ANY)],
        out_specs=[pl.BlockSpec(memory_space=pltpu.VMEM)] * (1 + len(CHUNKS)),
        scratch_shapes=[
            pltpu.VMEM((width, width), jnp.float32),
            pltpu.VMEM((width, width), jnp.float32),
            pltpu.VMEM(slab.shape, jnp.bfloat16),
            pltpu.SemaphoreType.DMA,
        ],
        compiler_params=pltpu.CompilerParams(vmem_limit_bytes=KERNEL_VMEM),
        name="make_basis",
    )(gram, mine, other, slab)


def per_device(activations, start_sketch):
    rows_here, cols_here = activations.shape
    width = start_sketch.shape[1]
    parts = lax.axis_size("row")
    total_rows = rows_here * parts
    total_cols = cols_here * lax.axis_size("col")
    root_rows = math.sqrt(total_rows)

    local_cols = first_product(start_sketch, activations)
    partial_sketch = 0.0
    orders = orders_of("row")
    begin = 0
    for c, local in enumerate(local_cols):
        span = slice(begin, begin + local.shape[1])
        begin = span.stop
        shared = sum_and_share(local, "row", orders[c % 2], 1.0 / root_rows)
        partial_sketch = partial_sketch + lax.dot_general(
            activations[:, span],
            shared,
            (((1,), (1,)), ((), ())),
            preferred_element_type=jnp.float32,
        )
    other_sketch = swap(partial_sketch, "col", 1)
    gram = row_sum(make_gram(partial_sketch, other_sketch, total_cols))
    basis, *products = make_basis(
        gram, partial_sketch, other_sketch, activations, total_cols, root_rows
    )

    pieces = [
        scatter_sum(product, "row", orders[c % 2]) / total_rows
        for c, product in enumerate(products)
    ]
    return (basis, jnp.concatenate(pieces, axis=1))


def solution(mesh):
    return jax.shard_map(
        per_device,
        mesh=mesh,
        in_specs=(P(("grp", "row"), "col"), P(("grp", "row"), None)),
        out_specs=(P(("grp", "row"), None), P(("grp", "row"), "col")),
        check_vma=False,
    )
```

```python
import functools
import math

import jax
import jax.numpy as jnp
from jax import lax
from jax.experimental import pallas as pl
from jax.experimental.pallas import tpu as pltpu
from jax.sharding import PartitionSpec as P

CHUNKS = 4
TILE = 512
KERNEL_VMEM = 50 * 2**20


def swap(value, axis, distance):
    size = lax.axis_size(axis)
    return lax.ppermute(value, axis, [(i, i ^ distance) for i in range(size)])


def row_sum(value):
    rows, cores = lax.axis_size("row"), lax.axis_size("col")
    assert cores == 2
    first = lax.axis_index("col") == 0
    stride = 1
    while stride < rows:
        radix = min(8, rows // stride)
        split = min(2, radix // 2)
        terms = []
        for near in [digit for digit in range(radix) if not digit & split]:
            pairs = []
            for row in range(rows):
                for core, digit in ((0, near), (1, near | split)):
                    if digit:
                        pairs.append((row * cores + core, (row ^ digit * stride) * cores + core))
            terms.append(lax.ppermute(value, ("row", "col"), pairs))
        terms[0] = jnp.where(first, value, terms[0])
        while len(terms) > 1:
            terms = [terms[i] + terms[i + 1] for i in range(0, len(terms), 2)]
        value = terms[0] + swap(terms[0], "col", 1)
        stride *= radix
    return value


def scatter_sum(value, axis, order):
    rows, cols = value.shape[0] >> len(order), value.shape[1]
    total = value.reshape([2] * len(order) + [rows, cols])
    left = sorted(order, reverse=True)
    for bit in order:
        dim = left.index(bit)
        left.remove(bit)
        low = lax.index_in_dim(total, 0, dim, keepdims=False)
        high = lax.index_in_dim(total, 1, dim, keepdims=False)
        upper = bit_of(axis, bit) == 1
        send = jnp.where(upper, low, high).astype(jnp.bfloat16)
        landed = swap(send, axis, 1 << bit)
        total = jnp.where(upper, high, low) + landed.astype(jnp.float32)
    return total


def bit_of(axis, bit):
    return lax.rem(lax.div(lax.axis_index(axis), 1 << bit), 2)


def sum_and_share(value, axis, order, scale):
    for bit in order[:-1]:
        upper = bit_of(axis, bit) == 1
        half = value.shape[1] // 2
        low, high = value[:, :half], value[:, half:]
        send = jnp.where(upper, low, high).astype(jnp.bfloat16)
        landed = swap(send, axis, 1 << bit)
        value = jnp.where(upper, high, low) + landed.astype(jnp.float32)
    landed = swap(value.astype(jnp.bfloat16), axis, 1 << order[-1])
    block = ((value + landed.astype(jnp.float32)) * scale).astype(jnp.bfloat16)
    for bit in reversed(order[:-1]):
        upper = bit_of(axis, bit) == 1
        other = swap(block, axis, 1 << bit)
        block = jnp.concatenate(
            [jnp.where(upper, other, block), jnp.where(upper, block, other)], axis=1
        )
    return block


def orders_of(axis):
    bits = list(range((lax.axis_size(axis) - 1).bit_length()))
    if len(bits) < 3:
        return [bits] * 4
    heads = [(0, 1, 2), (1, 0, 2), (0, 2, 1), (1, 2, 0)]
    return [list(head) + bits[3:] for head in heads]


def fetch_tiles(slab_ref, buffer, arrived):
    copies = []
    for tile in range(buffer.shape[0]):
        span = pl.ds(tile * TILE, TILE)
        copies.append(
            pltpu.make_async_copy(slab_ref.at[:, span], buffer.at[tile], arrived.at[tile])
        )
    for copy in copies:
        copy.start()
    return copies


def sketch_kernel(start_ref, slab_ref, *refs):
    outs, (buffer, arrived) = refs[:-2], refs[-2:]
    copies = fetch_tiles(slab_ref, buffer, arrived)
    left = start_ref[...].T
    for tile, copy in enumerate(copies):
        copy.wait()
        out, inner = divmod(tile * TILE, outs[0].shape[1])
        outs[out][:, inner : inner + TILE] = lax.dot_general(
            left, buffer[tile], (((1,), (0,)), ((), ())), preferred_element_type=jnp.float32
        )


def first_product(start, slab, chunks):
    rows, width = start.shape
    cols = slab.shape[1]
    return pl.pallas_call(
        sketch_kernel,
        out_shape=[jax.ShapeDtypeStruct((width, cols // chunks), jnp.float32)] * chunks,
        in_specs=[
            pl.BlockSpec(memory_space=pltpu.VMEM),
            pl.BlockSpec(memory_space=pl.ANY),
        ],
        out_specs=[pl.BlockSpec(memory_space=pltpu.VMEM)] * chunks,
        scratch_shapes=[
            pltpu.VMEM((cols // TILE, rows, TILE), jnp.bfloat16),
            pltpu.SemaphoreType.DMA((cols // TILE,)),
        ],
        compiler_params=pltpu.CompilerParams(vmem_limit_bytes=KERNEL_VMEM),
        cost_estimate=pl.CostEstimate(
            flops=2 * rows * width * cols, bytes_accessed=2 * rows * cols, transcendentals=0
        ),
        name="first_product",
    )(start, slab)


def matmul(left, right, exact=True):
    if not exact:
        left, right = left.astype(jnp.bfloat16), right.astype(jnp.bfloat16)
    return lax.dot_general(
        left,
        right,
        (((1,), (0,)), ((), ())),
        precision=lax.Precision.HIGHEST if exact else None,
        preferred_element_type=jnp.float32,
    )


def matmul_t(left, right, exact=True):
    if not exact:
        left, right = left.astype(jnp.bfloat16), right.astype(jnp.bfloat16)
    return lax.dot_general(
        left,
        right,
        (((1,), (1,)), ((), ())),
        precision=lax.Precision.HIGHEST if exact else None,
        preferred_element_type=jnp.float32,
    )


def gram_kernel(total_cols, mine_ref, other_ref, packed_ref):
    sketch = (mine_ref[...] + other_ref[...]) / total_cols
    gram = matmul(sketch.T, sketch)
    half = gram.shape[0] // 2
    row = lax.broadcasted_iota(jnp.int32, (half, 2 * half), 0)
    col = lax.broadcasted_iota(jnp.int32, (half, 2 * half), 1)
    top, bottom = gram[:half], pltpu.roll(gram[half:], half, 1)
    packed_ref[:half] = jnp.where(row > col, bottom, top)
    diagonal = jnp.sum(jnp.where(row == col, bottom, 0.0), axis=0, keepdims=True)
    packed_ref[half:] = jnp.broadcast_to(diagonal, (8, 2 * half))


def unpack_gram(packed):
    width = packed.shape[1]
    half = width // 2
    row = lax.broadcasted_iota(jnp.int32, (half, width), 0)
    col = lax.broadcasted_iota(jnp.int32, (half, width), 1)
    square = packed[:half]
    top = jnp.where(row > col, 0.0, square)
    lower = jnp.where(row > col, square, jnp.where(row == col, packed[half : half + 1], 0.0))
    parts = jnp.concatenate([top, pltpu.roll(lower, half, 1)], axis=0)
    row = lax.broadcasted_iota(jnp.int32, (width, width), 0)
    col = lax.broadcasted_iota(jnp.int32, (width, width), 1)
    return jnp.where(row == col, parts, parts + parts.T)


def make_gram(mine, other, total_cols):
    rows, width = mine.shape
    return pl.pallas_call(
        functools.partial(gram_kernel, total_cols),
        out_shape=jax.ShapeDtypeStruct((width // 2 + 8, width), jnp.float32),
        in_specs=[pl.BlockSpec(memory_space=pltpu.VMEM)] * 2,
        out_specs=pl.BlockSpec(memory_space=pltpu.VMEM),
        compiler_params=pltpu.CompilerParams(vmem_limit_bytes=16 * 2**20),
        name="make_gram",
    )(mine, other)


UPDATES = 4
LOOSE_UPDATES = 2
CLOSE = 1e-5


def basis_kernel(
    total_cols, root_rows, gram_ref, mine_ref, other_ref, slab_ref,
    basis_ref, *refs,
):
    products, (work_ref, inverse_ref, buffer, arrived) = refs[:-4], refs[-4:]
    fetch = pltpu.make_async_copy(slab_ref, buffer, arrived)
    fetch.start()
    width = gram_ref.shape[1]
    row = lax.broadcasted_iota(jnp.int32, (width, width), 0)
    col = lax.broadcasted_iota(jnp.int32, (width, width), 1)
    on_diag = row == col
    unit = jnp.where(on_diag, 1.0, 0.0)
    half = jnp.where(row > col, 1.0, jnp.where(on_diag, 0.5, 0.0))

    gram = unpack_gram(gram_ref[...])
    diagonal = jnp.where(on_diag, gram, 0.0)
    down = lax.rsqrt(jnp.sum(diagonal, axis=1, keepdims=True))
    across = lax.rsqrt(jnp.sum(diagonal, axis=0, keepdims=True))
    scaled = gram * down * across

    error = scaled - unit
    step = error * half
    inverse = unit - step + matmul(step, step, False)
    for update in range(1, UPDATES):
        exact = update >= LOOSE_UPDATES
        error = matmul_t(matmul(inverse, scaled, exact), inverse, exact) - unit
        step = error * half
        inverse = inverse - matmul(step, inverse - matmul(step, inverse, exact), exact)
    inverse_ref[...] = inverse * across
    far = jnp.sum(error * error)

    @pl.when(jnp.logical_not(far <= CLOSE))
    def _():
        work_ref[...] = gram
        inverse_ref[...] = unit

        def eliminate(k, carry):
            whole = work_ref[...]
            pivot_row = work_ref[pl.ds(k, 1), :]
            pivot = jnp.sum(
                jnp.where(col[:1] == k, pivot_row, 0.0), axis=1, keepdims=True
            )
            column = jnp.sum(jnp.where(col == k, whole, 0.0), axis=1, keepdims=True)
            factor = jnp.where(row[:, :1] > k, column / pivot, 0.0)
            work_ref[...] = whole - factor * pivot_row
            inverse_ref[...] = inverse_ref[...] - factor * inverse_ref[pl.ds(k, 1), :]
            return carry

        lax.fori_loop(0, width, eliminate, 0)
        pivots = jnp.sum(jnp.where(on_diag, work_ref[...], 0.0), axis=1, keepdims=True)
        inverse_ref[...] = inverse_ref[...] * lax.rsqrt(pivots)

    sketch = (mine_ref[...] + other_ref[...]) / total_cols
    basis = matmul_t(sketch, inverse_ref[...]) * root_rows
    basis_ref[...] = basis
    high = basis.astype(jnp.bfloat16)
    low = (basis - high.astype(jnp.float32)).astype(jnp.bfloat16)
    pair = jnp.concatenate([high, low], axis=1).T
    fetch.wait()
    for start in range(0, buffer.shape[1], TILE):
        both = lax.dot_general(
            pair,
            buffer[:, start : start + TILE],
            (((1,), (0,)), ((), ())),
            preferred_element_type=jnp.float32,
        )
        out, inner = divmod(start, products[0].shape[1])
        products[out][:, inner : inner + TILE] = both[:width] + both[width:]


def make_basis(gram, mine, other, slab, total_cols, root_rows, chunks):
    rows, width = mine.shape
    cols = slab.shape[1]
    return pl.pallas_call(
        functools.partial(basis_kernel, total_cols, root_rows),
        out_shape=[jax.ShapeDtypeStruct((rows, width), jnp.float32)]
        + [jax.ShapeDtypeStruct((width, cols // chunks), jnp.float32)] * chunks,
        in_specs=[pl.BlockSpec(memory_space=pltpu.VMEM)] * 3
        + [pl.BlockSpec(memory_space=pl.ANY)],
        out_specs=[pl.BlockSpec(memory_space=pltpu.VMEM)] * (1 + chunks),
        scratch_shapes=[
            pltpu.VMEM((width, width), jnp.float32),
            pltpu.VMEM((width, width), jnp.float32),
            pltpu.VMEM(slab.shape, jnp.bfloat16),
            pltpu.SemaphoreType.DMA,
        ],
        compiler_params=pltpu.CompilerParams(vmem_limit_bytes=KERNEL_VMEM),
        name="make_basis",
    )(gram, mine, other, slab)


def per_device(activations, start_sketch):
    rows_here, cols_here = activations.shape
    width = start_sketch.shape[1]
    parts = lax.axis_size("row")
    total_rows = rows_here * parts
    total_cols = cols_here * lax.axis_size("col")
    root_rows = math.sqrt(total_rows)

    local_cols = first_product(start_sketch, activations, CHUNKS)
    partial_sketch = 0.0
    orders = orders_of("row")
    step = cols_here // CHUNKS
    for c in range(CHUNKS):
        span = slice(c * step, (c + 1) * step)
        shared = sum_and_share(local_cols[c], "row", orders[c % 4], 1.0 / root_rows)
        partial_sketch = partial_sketch + lax.dot_general(
            activations[:, span],
            shared,
            (((1,), (1,)), ((), ())),
            preferred_element_type=jnp.float32,
        )
    other_sketch = swap(partial_sketch, "col", 1)
    gram = row_sum(make_gram(partial_sketch, other_sketch, total_cols))
    basis, *products = make_basis(
        gram, partial_sketch, other_sketch, activations, total_cols, root_rows, CHUNKS
    )

    pieces = [
        scatter_sum(product, "row", orders[c % 2]) / total_rows
        for c, product in enumerate(products)
    ]
    return (basis, jnp.concatenate(pieces, axis=1))


def solution(mesh):
    return jax.shard_map(
        per_device,
        mesh=mesh,
        in_specs=(P(("grp", "row"), "col"), P(("grp", "row"), None)),
        out_specs=(P(("grp", "row"), None), P(("grp", "row"), "col")),
        check_vma=False,
    )
```

```python
import functools
import math

import jax
import jax.numpy as jnp
from jax import lax
from jax.experimental import pallas as pl
from jax.experimental.pallas import tpu as pltpu
from jax.sharding import PartitionSpec as P

CHUNKS = 4
TILE = 512
KERNEL_VMEM = 50 * 2**20


def swap(value, axis, distance):
    size = lax.axis_size(axis)
    return lax.ppermute(value, axis, [(i, i ^ distance) for i in range(size)])


def row_sum(value):
    rows, cores = lax.axis_size("row"), lax.axis_size("col")
    assert cores == 2
    first = lax.axis_index("col") == 0
    stride = 1
    while stride < rows:
        radix = min(8, rows // stride)
        split = min(2, radix // 2)
        terms = []
        for near in [digit for digit in range(radix) if not digit & split]:
            pairs = []
            for row in range(rows):
                for core, digit in ((0, near), (1, near | split)):
                    if digit:
                        pairs.append((row * cores + core, (row ^ digit * stride) * cores + core))
            terms.append(lax.ppermute(value, ("row", "col"), pairs))
        terms[0] = jnp.where(first, value, terms[0])
        while len(terms) > 1:
            terms = [terms[i] + terms[i + 1] for i in range(0, len(terms), 2)]
        value = terms[0] + swap(terms[0], "col", 1)
        stride *= radix
    return value


def scatter_sum(own, sends, axis):
    groups = lax.axis_size(axis) // 4
    total = own
    for distance, send in enumerate(sends, 1):
        total = total + swap(send, axis, distance).astype(jnp.float32)
    bit = 2
    while groups > 1:
        groups //= 2
        view = total.reshape(groups, 2, total.shape[0] // (2 * groups), total.shape[1])
        low, high = view[:, 0], view[:, 1]
        upper = bit_of(axis, bit) == 1
        landed = swap(jnp.where(upper, low, high).astype(jnp.bfloat16), axis, 1 << bit)
        total = (jnp.where(upper, high, low) + landed.astype(jnp.float32)).reshape(
            -1, total.shape[1]
        )
        bit += 1
    return total


def bit_of(axis, bit):
    return lax.rem(lax.div(lax.axis_index(axis), 1 << bit), 2)


def sum_and_share(value, axis, order, scale):
    for bit in order[:-1]:
        upper = bit_of(axis, bit) == 1
        half = value.shape[1] // 2
        low, high = value[:, :half], value[:, half:]
        send = jnp.where(upper, low, high).astype(jnp.bfloat16)
        landed = swap(send, axis, 1 << bit)
        value = jnp.where(upper, high, low) + landed.astype(jnp.float32)
    landed = swap(value.astype(jnp.bfloat16), axis, 1 << order[-1])
    block = ((value + landed.astype(jnp.float32)) * scale).astype(jnp.bfloat16)
    for bit in reversed(order[:-1]):
        upper = bit_of(axis, bit) == 1
        other = swap(block, axis, 1 << bit)
        block = jnp.concatenate(
            [jnp.where(upper, other, block), jnp.where(upper, block, other)], axis=1
        )
    return block


def orders_of(axis):
    bits = list(range((lax.axis_size(axis) - 1).bit_length()))
    if len(bits) < 3:
        return [bits, bits]
    return [bits, [bits[1], bits[0]] + bits[2:]]


def fetch_tiles(slab_ref, buffer, arrived):
    copies = []
    for tile in range(buffer.shape[0]):
        span = pl.ds(tile * TILE, TILE)
        copies.append(
            pltpu.make_async_copy(slab_ref.at[:, span], buffer.at[tile], arrived.at[tile])
        )
    for copy in copies:
        copy.start()
    return copies


def sketch_kernel(start_ref, slab_ref, *refs):
    outs, (buffer, arrived) = refs[:-2], refs[-2:]
    copies = fetch_tiles(slab_ref, buffer, arrived)
    left = start_ref[...].T
    for tile, copy in enumerate(copies):
        copy.wait()
        out, inner = divmod(tile * TILE, outs[0].shape[1])
        outs[out][:, inner : inner + TILE] = lax.dot_general(
            left, buffer[tile], (((1,), (0,)), ((), ())), preferred_element_type=jnp.float32
        )


def first_product(start, slab, chunks):
    rows, width = start.shape
    cols = slab.shape[1]
    return pl.pallas_call(
        sketch_kernel,
        out_shape=[jax.ShapeDtypeStruct((width, cols // chunks), jnp.float32)] * chunks,
        in_specs=[
            pl.BlockSpec(memory_space=pltpu.VMEM),
            pl.BlockSpec(memory_space=pl.ANY),
        ],
        out_specs=[pl.BlockSpec(memory_space=pltpu.VMEM)] * chunks,
        scratch_shapes=[
            pltpu.VMEM((cols // TILE, rows, TILE), jnp.bfloat16),
            pltpu.SemaphoreType.DMA((cols // TILE,)),
        ],
        compiler_params=pltpu.CompilerParams(vmem_limit_bytes=KERNEL_VMEM),
        cost_estimate=pl.CostEstimate(
            flops=2 * rows * width * cols, bytes_accessed=2 * rows * cols, transcendentals=0
        ),
        name="first_product",
    )(start, slab)


def matmul(left, right, exact=True):
    if not exact:
        left, right = left.astype(jnp.bfloat16), right.astype(jnp.bfloat16)
    return lax.dot_general(
        left,
        right,
        (((1,), (0,)), ((), ())),
        precision=lax.Precision.HIGHEST if exact else None,
        preferred_element_type=jnp.float32,
    )


def matmul_t(left, right, exact=True):
    if not exact:
        left, right = left.astype(jnp.bfloat16), right.astype(jnp.bfloat16)
    return lax.dot_general(
        left,
        right,
        (((1,), (1,)), ((), ())),
        precision=lax.Precision.HIGHEST if exact else None,
        preferred_element_type=jnp.float32,
    )


def gram_kernel(total_cols, mine_ref, other_ref, packed_ref, sketch_ref):
    sketch = (mine_ref[...] + other_ref[...]) / total_cols
    sketch_ref[...] = sketch.T
    gram = matmul(sketch_ref[...], sketch)
    half = gram.shape[0] // 2
    row = lax.broadcasted_iota(jnp.int32, (half, 2 * half), 0)
    col = lax.broadcasted_iota(jnp.int32, (half, 2 * half), 1)
    top, bottom = gram[:half], pltpu.roll(gram[half:], half, 1)
    packed_ref[:half] = jnp.where(row > col, bottom, top)
    diagonal = jnp.sum(jnp.where(row == col, bottom, 0.0), axis=0, keepdims=True)
    packed_ref[half:] = jnp.broadcast_to(diagonal, (8, 2 * half))


def unpack_gram(packed):
    width = packed.shape[1]
    half = width // 2
    row = lax.broadcasted_iota(jnp.int32, (half, width), 0)
    col = lax.broadcasted_iota(jnp.int32, (half, width), 1)
    square = packed[:half]
    top = jnp.where(row > col, 0.0, square)
    lower = jnp.where(row > col, square, jnp.where(row == col, packed[half : half + 1], 0.0))
    parts = jnp.concatenate([top, pltpu.roll(lower, half, 1)], axis=0)
    row = lax.broadcasted_iota(jnp.int32, (width, width), 0)
    col = lax.broadcasted_iota(jnp.int32, (width, width), 1)
    return jnp.where(row == col, parts, parts + parts.T)


def make_gram(mine, other, total_cols):
    rows, width = mine.shape
    return pl.pallas_call(
        functools.partial(gram_kernel, total_cols),
        out_shape=[
            jax.ShapeDtypeStruct((width // 2 + 8, width), jnp.float32),
            jax.ShapeDtypeStruct((width, rows), jnp.float32),
        ],
        in_specs=[pl.BlockSpec(memory_space=pltpu.VMEM)] * 2,
        out_specs=[pl.BlockSpec(memory_space=pltpu.VMEM)] * 2,
        compiler_params=pltpu.CompilerParams(vmem_limit_bytes=16 * 2**20),
        name="make_gram",
    )(mine, other)


UPDATES = 4
LOOSE_UPDATES = 2
CLOSE = 1e-5


def basis_kernel(
    parts, root_rows, gram_ref, sketch_ref, slab_ref,
    basis_ref, own_ref, send1_ref, send2_ref, send3_ref,
    work_ref, inverse_ref, buffer, arrived,
):
    fetch = pltpu.make_async_copy(slab_ref, buffer, arrived)
    fetch.start()
    width = gram_ref.shape[1]
    row = lax.broadcasted_iota(jnp.int32, (width, width), 0)
    col = lax.broadcasted_iota(jnp.int32, (width, width), 1)
    on_diag = row == col
    unit = jnp.where(on_diag, 1.0, 0.0)
    half = jnp.where(row > col, 1.0, jnp.where(on_diag, 0.5, 0.0))

    gram = unpack_gram(gram_ref[...])
    diagonal = jnp.where(on_diag, gram, 0.0)
    down = lax.rsqrt(jnp.sum(diagonal, axis=1, keepdims=True))
    across = lax.rsqrt(jnp.sum(diagonal, axis=0, keepdims=True))
    scaled = gram * down * across

    error = scaled - unit
    step = error * half
    inverse = unit - step + matmul(step, step, False)
    for update in range(1, UPDATES):
        exact = update >= LOOSE_UPDATES
        error = matmul_t(matmul(inverse, scaled, exact), inverse, exact) - unit
        step = error * half
        inverse = inverse - matmul(step, inverse - matmul(step, inverse, exact), exact)
    inverse_ref[...] = inverse * across
    far = jnp.sum(error * error)

    @pl.when(jnp.logical_not(far <= CLOSE))
    def _():
        work_ref[...] = gram
        inverse_ref[...] = unit

        def eliminate(k, carry):
            whole = work_ref[...]
            pivot_row = work_ref[pl.ds(k, 1), :]
            pivot = jnp.sum(
                jnp.where(col[:1] == k, pivot_row, 0.0), axis=1, keepdims=True
            )
            column = jnp.sum(jnp.where(col == k, whole, 0.0), axis=1, keepdims=True)
            factor = jnp.where(row[:, :1] > k, column / pivot, 0.0)
            work_ref[...] = whole - factor * pivot_row
            inverse_ref[...] = inverse_ref[...] - factor * inverse_ref[pl.ds(k, 1), :]
            return carry

        lax.fori_loop(0, width, eliminate, 0)
        pivots = jnp.sum(jnp.where(on_diag, work_ref[...], 0.0), axis=1, keepdims=True)
        inverse_ref[...] = inverse_ref[...] * lax.rsqrt(pivots)

    basis = matmul(inverse_ref[...], sketch_ref[...]) * root_rows
    high = basis.astype(jnp.bfloat16)
    low = (basis - high.astype(jnp.float32)).astype(jnp.bfloat16)

    share = width // parts
    quarter = width // 4
    me = lax.rem(lax.axis_index("row"), 4)
    distance, inner = row // quarter, row % quarter
    source = (inner // share * 4 + (distance ^ me)) * share + inner % share
    order = jnp.where(col == source, 1.0, 0.0).astype(jnp.bfloat16)
    pair = jnp.concatenate(
        [
            jnp.dot(order, high, preferred_element_type=jnp.float32).astype(jnp.bfloat16),
            jnp.dot(order, low, preferred_element_type=jnp.float32).astype(jnp.bfloat16),
        ],
        axis=0,
    )
    fetch.wait()
    for start in range(0, buffer.shape[1], TILE):
        span = slice(start, start + TILE)
        both = jnp.dot(pair, buffer[:, span], preferred_element_type=jnp.float32)
        product = both[:width] + both[width:]
        own_ref[:, span] = product[:quarter]
        for out_ref, begin in ((send1_ref, 1), (send2_ref, 2), (send3_ref, 3)):
            block = product[begin * quarter : (begin + 1) * quarter]
            out_ref[:, span] = block.astype(jnp.bfloat16)
    basis_ref[...] = basis.T


def make_basis(gram, sketch, slab, root_rows):
    width, rows = sketch.shape
    block = (width // 4, slab.shape[1])
    return pl.pallas_call(
        functools.partial(basis_kernel, lax.axis_size("row"), root_rows),
        out_shape=[
            jax.ShapeDtypeStruct((rows, width), jnp.float32),
            jax.ShapeDtypeStruct(block, jnp.float32),
        ]
        + [jax.ShapeDtypeStruct(block, jnp.bfloat16)] * 3,
        in_specs=[pl.BlockSpec(memory_space=pltpu.VMEM)] * 2
        + [pl.BlockSpec(memory_space=pl.ANY)],
        out_specs=[pl.BlockSpec(memory_space=pltpu.VMEM)] * 5,
        scratch_shapes=[
            pltpu.VMEM((width, width), jnp.float32),
            pltpu.VMEM((width, width), jnp.float32),
            pltpu.VMEM(slab.shape, jnp.bfloat16),
            pltpu.SemaphoreType.DMA,
        ],
        compiler_params=pltpu.CompilerParams(vmem_limit_bytes=KERNEL_VMEM),
        name="make_basis",
    )(gram, sketch, slab)


def per_device(activations, start_sketch):
    rows_here, cols_here = activations.shape
    width = start_sketch.shape[1]
    parts = lax.axis_size("row")
    total_rows = rows_here * parts
    total_cols = cols_here * lax.axis_size("col")
    root_rows = math.sqrt(total_rows)

    local_cols = first_product(start_sketch, activations, CHUNKS)
    partial_sketch = 0.0
    orders = orders_of("row")
    step = cols_here // CHUNKS
    for c in range(CHUNKS):
        span = slice(c * step, (c + 1) * step)
        shared = sum_and_share(local_cols[c], "row", orders[c % 2], 1.0 / root_rows)
        partial_sketch = partial_sketch + lax.dot_general(
            activations[:, span],
            shared,
            (((1,), (1,)), ((), ())),
            preferred_element_type=jnp.float32,
        )
    other_sketch = swap(partial_sketch, "col", 1)
    packed, sketch = make_gram(partial_sketch, other_sketch, total_cols)
    basis, own, *sends = make_basis(row_sum(packed), sketch, activations, root_rows)
    projection = scatter_sum(own, sends, "row") / total_rows
    return (basis, projection)


def solution(mesh):
    return jax.shard_map(
        per_device,
        mesh=mesh,
        in_specs=(P(("grp", "row"), "col"), P(("grp", "row"), None)),
        out_specs=(P(("grp", "row"), None), P(("grp", "row"), "col")),
        check_vma=False,
    )
```

```python
import functools
import math

import jax
import jax.numpy as jnp
from jax import lax
from jax.experimental import pallas as pl
from jax.experimental.pallas import tpu as pltpu
from jax.sharding import PartitionSpec as P

CHUNKS = 4
TILE = 512
KERNEL_VMEM = 50 * 2**20


def swap(value, axis, distance):
    size = lax.axis_size(axis)
    return lax.ppermute(value, axis, [(i, i ^ distance) for i in range(size)])


def row_sum(value):
    rows, cores = lax.axis_size("row"), lax.axis_size("col")
    assert cores == 2
    first = lax.axis_index("col") == 0
    stride = 1
    while stride < rows:
        radix = min(8, rows // stride)
        split = min(2, radix // 2)
        terms = []
        for near in [digit for digit in range(radix) if not digit & split]:
            pairs = []
            for row in range(rows):
                for core, digit in ((0, near), (1, near | split)):
                    if digit:
                        pairs.append((row * cores + core, (row ^ digit * stride) * cores + core))
            terms.append(lax.ppermute(value, ("row", "col"), pairs))
        terms[0] = jnp.where(first, value, terms[0])
        while len(terms) > 1:
            terms = [terms[i] + terms[i + 1] for i in range(0, len(terms), 2)]
        value = terms[0] + swap(terms[0], "col", 1)
        stride *= radix
    return value


def scatter_sum(value, axis, order):
    rows, cols = value.shape[0] >> len(order), value.shape[1]
    total = value.reshape([2] * len(order) + [rows, cols])
    left = sorted(order, reverse=True)
    for bit in order:
        dim = left.index(bit)
        left.remove(bit)
        low = lax.index_in_dim(total, 0, dim, keepdims=False)
        high = lax.index_in_dim(total, 1, dim, keepdims=False)
        upper = bit_of(axis, bit) == 1
        send = jnp.where(upper, low, high).astype(jnp.bfloat16)
        landed = swap(send, axis, 1 << bit)
        total = jnp.where(upper, high, low) + landed.astype(jnp.float32)
    return total


def bit_of(axis, bit):
    return lax.rem(lax.div(lax.axis_index(axis), 1 << bit), 2)


def sum_and_share(value, axis, order, scale):
    for bit in order[:-1]:
        upper = bit_of(axis, bit) == 1
        half = value.shape[1] // 2
        low, high = value[:, :half], value[:, half:]
        send = jnp.where(upper, low, high).astype(jnp.bfloat16)
        landed = swap(send, axis, 1 << bit)
        value = jnp.where(upper, high, low) + landed.astype(jnp.float32)
    landed = swap(value.astype(jnp.bfloat16), axis, 1 << order[-1])
    block = ((value + landed.astype(jnp.float32)) * scale).astype(jnp.bfloat16)
    for bit in reversed(order[:-1]):
        upper = bit_of(axis, bit) == 1
        other = swap(block, axis, 1 << bit)
        block = jnp.concatenate(
            [jnp.where(upper, other, block), jnp.where(upper, block, other)], axis=1
        )
    return block


def orders_of(axis):
    bits = list(range((lax.axis_size(axis) - 1).bit_length()))
    if len(bits) < 3:
        return [bits, bits]
    return [bits, [bits[1], bits[0]] + bits[2:]]


def fetch_tiles(slab_ref, begin, buffer, arrived):
    copies = []
    for tile in range(buffer.shape[0]):
        span = pl.ds(begin + tile * TILE, TILE)
        copies.append(
            pltpu.make_async_copy(slab_ref.at[:, span], buffer.at[tile], arrived.at[tile])
        )
    for copy in copies:
        copy.start()
    return copies


def sketch_kernel(begin, start_ref, slab_ref, *refs):
    outs, (buffer, arrived) = refs[:-2], refs[-2:]
    copies = fetch_tiles(slab_ref, begin, buffer, arrived)
    left = start_ref[...].T
    for tile, copy in enumerate(copies):
        copy.wait()
        out, inner = divmod(tile * TILE, outs[0].shape[1])
        outs[out][:, inner : inner + TILE] = lax.dot_general(
            left, buffer[tile], (((1,), (0,)), ((), ())), preferred_element_type=jnp.float32
        )


def first_product(start, slab, begin, cols, chunks):
    rows, width = start.shape
    return pl.pallas_call(
        functools.partial(sketch_kernel, begin),
        out_shape=[jax.ShapeDtypeStruct((width, cols // chunks), jnp.float32)] * chunks,
        in_specs=[
            pl.BlockSpec(memory_space=pltpu.VMEM),
            pl.BlockSpec(memory_space=pl.ANY),
        ],
        out_specs=[pl.BlockSpec(memory_space=pltpu.VMEM)] * chunks,
        scratch_shapes=[
            pltpu.VMEM((cols // TILE, rows, TILE), jnp.bfloat16),
            pltpu.SemaphoreType.DMA((cols // TILE,)),
        ],
        compiler_params=pltpu.CompilerParams(vmem_limit_bytes=KERNEL_VMEM),
        cost_estimate=pl.CostEstimate(
            flops=2 * rows * width * cols, bytes_accessed=2 * rows * cols, transcendentals=0
        ),
        name="first_product",
    )(start, slab)


def matmul(left, right, exact=True):
    if not exact:
        left, right = left.astype(jnp.bfloat16), right.astype(jnp.bfloat16)
    return lax.dot_general(
        left,
        right,
        (((1,), (0,)), ((), ())),
        precision=lax.Precision.HIGHEST if exact else None,
        preferred_element_type=jnp.float32,
    )


def matmul_t(left, right, exact=True):
    if not exact:
        left, right = left.astype(jnp.bfloat16), right.astype(jnp.bfloat16)
    return lax.dot_general(
        left,
        right,
        (((1,), (1,)), ((), ())),
        precision=lax.Precision.HIGHEST if exact else None,
        preferred_element_type=jnp.float32,
    )


def gram_kernel(total_cols, mine_ref, other_ref, packed_ref):
    sketch = (mine_ref[...] + other_ref[...]) / total_cols
    gram = matmul(sketch.T, sketch)
    half = gram.shape[0] // 2
    row = lax.broadcasted_iota(jnp.int32, (half, 2 * half), 0)
    col = lax.broadcasted_iota(jnp.int32, (half, 2 * half), 1)
    top, bottom = gram[:half], pltpu.roll(gram[half:], half, 1)
    packed_ref[:half] = jnp.where(row > col, bottom, top)
    diagonal = jnp.sum(jnp.where(row == col, bottom, 0.0), axis=0, keepdims=True)
    packed_ref[half:] = jnp.broadcast_to(diagonal, (8, 2 * half))


def unpack_gram(packed):
    width = packed.shape[1]
    half = width // 2
    row = lax.broadcasted_iota(jnp.int32, (half, width), 0)
    col = lax.broadcasted_iota(jnp.int32, (half, width), 1)
    square = packed[:half]
    top = jnp.where(row > col, 0.0, square)
    lower = jnp.where(row > col, square, jnp.where(row == col, packed[half : half + 1], 0.0))
    parts = jnp.concatenate([top, pltpu.roll(lower, half, 1)], axis=0)
    row = lax.broadcasted_iota(jnp.int32, (width, width), 0)
    col = lax.broadcasted_iota(jnp.int32, (width, width), 1)
    return jnp.where(row == col, parts, parts + parts.T)


def make_gram(mine, other, total_cols):
    rows, width = mine.shape
    return pl.pallas_call(
        functools.partial(gram_kernel, total_cols),
        out_shape=jax.ShapeDtypeStruct((width // 2 + 8, width), jnp.float32),
        in_specs=[pl.BlockSpec(memory_space=pltpu.VMEM)] * 2,
        out_specs=pl.BlockSpec(memory_space=pltpu.VMEM),
        compiler_params=pltpu.CompilerParams(vmem_limit_bytes=16 * 2**20),
        name="make_gram",
    )(mine, other)


UPDATES = 4
LOOSE_UPDATES = 2
CLOSE = 1e-5


def basis_kernel(
    total_cols, root_rows, gram_ref, mine_ref, other_ref, slab_ref,
    basis_ref, *refs,
):
    products, (work_ref, inverse_ref, buffer, arrived) = refs[:-4], refs[-4:]
    fetch = pltpu.make_async_copy(slab_ref, buffer, arrived)
    fetch.start()
    width = gram_ref.shape[1]
    row = lax.broadcasted_iota(jnp.int32, (width, width), 0)
    col = lax.broadcasted_iota(jnp.int32, (width, width), 1)
    on_diag = row == col
    unit = jnp.where(on_diag, 1.0, 0.0)
    half = jnp.where(row > col, 1.0, jnp.where(on_diag, 0.5, 0.0))

    gram = unpack_gram(gram_ref[...])
    diagonal = jnp.where(on_diag, gram, 0.0)
    down = lax.rsqrt(jnp.sum(diagonal, axis=1, keepdims=True))
    across = lax.rsqrt(jnp.sum(diagonal, axis=0, keepdims=True))
    scaled = gram * down * across

    error = scaled - unit
    step = error * half
    inverse = unit - step + matmul(step, step, False)
    for update in range(1, UPDATES):
        exact = update >= LOOSE_UPDATES
        error = matmul_t(matmul(inverse, scaled, exact), inverse, exact) - unit
        step = error * half
        inverse = inverse - matmul(step, inverse - matmul(step, inverse, exact), exact)
    inverse_ref[...] = inverse * across
    far = jnp.sum(error * error)

    @pl.when(jnp.logical_not(far <= CLOSE))
    def _():
        work_ref[...] = gram
        inverse_ref[...] = unit

        def eliminate(k, carry):
            whole = work_ref[...]
            pivot_row = work_ref[pl.ds(k, 1), :]
            pivot = jnp.sum(
                jnp.where(col[:1] == k, pivot_row, 0.0), axis=1, keepdims=True
            )
            column = jnp.sum(jnp.where(col == k, whole, 0.0), axis=1, keepdims=True)
            factor = jnp.where(row[:, :1] > k, column / pivot, 0.0)
            work_ref[...] = whole - factor * pivot_row
            inverse_ref[...] = inverse_ref[...] - factor * inverse_ref[pl.ds(k, 1), :]
            return carry

        lax.fori_loop(0, width, eliminate, 0)
        pivots = jnp.sum(jnp.where(on_diag, work_ref[...], 0.0), axis=1, keepdims=True)
        inverse_ref[...] = inverse_ref[...] * lax.rsqrt(pivots)

    sketch = (mine_ref[...] + other_ref[...]) / total_cols
    basis = matmul_t(sketch, inverse_ref[...]) * root_rows
    basis_ref[...] = basis
    high = basis.astype(jnp.bfloat16)
    low = (basis - high.astype(jnp.float32)).astype(jnp.bfloat16)
    pair = jnp.concatenate([high, low], axis=1).T
    fetch.wait()
    for start in range(0, buffer.shape[1], TILE):
        both = lax.dot_general(
            pair,
            buffer[:, start : start + TILE],
            (((1,), (0,)), ((), ())),
            preferred_element_type=jnp.float32,
        )
        out, inner = divmod(start, products[0].shape[1])
        products[out][:, inner : inner + TILE] = both[:width] + both[width:]


def make_basis(gram, mine, other, slab, total_cols, root_rows, chunks):
    rows, width = mine.shape
    cols = slab.shape[1]
    return pl.pallas_call(
        functools.partial(basis_kernel, total_cols, root_rows),
        out_shape=[jax.ShapeDtypeStruct((rows, width), jnp.float32)]
        + [jax.ShapeDtypeStruct((width, cols // chunks), jnp.float32)] * chunks,
        in_specs=[pl.BlockSpec(memory_space=pltpu.VMEM)] * 3
        + [pl.BlockSpec(memory_space=pl.ANY)],
        out_specs=[pl.BlockSpec(memory_space=pltpu.VMEM)] * (1 + chunks),
        scratch_shapes=[
            pltpu.VMEM((width, width), jnp.float32),
            pltpu.VMEM((width, width), jnp.float32),
            pltpu.VMEM(slab.shape, jnp.bfloat16),
            pltpu.SemaphoreType.DMA,
        ],
        compiler_params=pltpu.CompilerParams(vmem_limit_bytes=KERNEL_VMEM),
        name="make_basis",
    )(gram, mine, other, slab)


def per_device(activations, start_sketch):
    rows_here, cols_here = activations.shape
    width = start_sketch.shape[1]
    parts = lax.axis_size("row")
    total_rows = rows_here * parts
    total_cols = cols_here * lax.axis_size("col")
    root_rows = math.sqrt(total_rows)

    local_cols = []
    for begin in (0, cols_here // 2):
        local_cols += first_product(
            start_sketch, activations, begin, cols_here // 2, CHUNKS // 2
        )
    partial_sketch = 0.0
    orders = orders_of("row")
    step = cols_here // CHUNKS
    for c in range(CHUNKS):
        span = slice(c * step, (c + 1) * step)
        shared = sum_and_share(local_cols[c], "row", orders[c % 2], 1.0 / root_rows)
        partial_sketch = partial_sketch + lax.dot_general(
            activations[:, span],
            shared,
            (((1,), (1,)), ((), ())),
            preferred_element_type=jnp.float32,
        )
    other_sketch = swap(partial_sketch, "col", 1)
    gram = row_sum(make_gram(partial_sketch, other_sketch, total_cols))
    basis, *products = make_basis(
        gram, partial_sketch, other_sketch, activations, total_cols, root_rows, CHUNKS
    )

    pieces = [
        scatter_sum(product, "row", orders[c % 2]) / total_rows
        for c, product in enumerate(products)
    ]
    return (basis, jnp.concatenate(pieces, axis=1))


def solution(mesh):
    return jax.shard_map(
        per_device,
        mesh=mesh,
        in_specs=(P(("grp", "row"), "col"), P(("grp", "row"), None)),
        out_specs=(P(("grp", "row"), None), P(("grp", "row"), "col")),
        check_vma=False,
    )
```

```python
import functools
import math

import jax
import jax.numpy as jnp
from jax import lax
from jax.experimental import pallas as pl
from jax.experimental.pallas import tpu as pltpu
from jax.sharding import PartitionSpec as P

CHUNKS = 4
TILE = 512
KERNEL_VMEM = 50 * 2**20


def swap(value, axis, distance):
    size = lax.axis_size(axis)
    return lax.ppermute(value, axis, [(i, i ^ distance) for i in range(size)])


def row_sum(value):
    rows, cores = lax.axis_size("row"), lax.axis_size("col")
    assert cores == 2
    first = lax.axis_index("col") == 0
    stride = 1
    while stride < rows:
        radix = min(8, rows // stride)
        split = min(2, radix // 2)
        terms = []
        for near in [digit for digit in range(radix) if not digit & split]:
            pairs = []
            for row in range(rows):
                for core, digit in ((0, near), (1, near | split)):
                    if digit:
                        pairs.append((row * cores + core, (row ^ digit * stride) * cores + core))
            terms.append(lax.ppermute(value, ("row", "col"), pairs))
        terms[0] = jnp.where(first, value, terms[0])
        while len(terms) > 1:
            terms = [terms[i] + terms[i + 1] for i in range(0, len(terms), 2)]
        value = terms[0] + swap(terms[0], "col", 1)
        stride *= radix
    return value


def scatter_sum(value, axis, order):
    rows, cols = value.shape[0] >> len(order), value.shape[1]
    total = value.reshape([2] * len(order) + [rows, cols])
    left = sorted(order, reverse=True)
    for bit in order:
        dim = left.index(bit)
        left.remove(bit)
        low = lax.index_in_dim(total, 0, dim, keepdims=False)
        high = lax.index_in_dim(total, 1, dim, keepdims=False)
        upper = bit_of(axis, bit) == 1
        send = jnp.where(upper, low, high).astype(jnp.bfloat16)
        landed = swap(send, axis, 1 << bit)
        total = jnp.where(upper, high, low) + landed.astype(jnp.float32)
    return total


def bit_of(axis, bit):
    return lax.rem(lax.div(lax.axis_index(axis), 1 << bit), 2)


def sum_and_share(value, axis, order, scale):
    for bit in order[:-1]:
        upper = bit_of(axis, bit) == 1
        half = value.shape[1] // 2
        low, high = value[:, :half], value[:, half:]
        send = jnp.where(upper, low, high).astype(jnp.bfloat16)
        landed = swap(send, axis, 1 << bit)
        value = jnp.where(upper, high, low) + landed.astype(jnp.float32)
    landed = swap(value.astype(jnp.bfloat16), axis, 1 << order[-1])
    block = ((value + landed.astype(jnp.float32)) * scale).astype(jnp.bfloat16)
    for bit in reversed(order[:-1]):
        upper = bit_of(axis, bit) == 1
        other = swap(block, axis, 1 << bit)
        block = jnp.concatenate(
            [jnp.where(upper, other, block), jnp.where(upper, block, other)], axis=1
        )
    return block


def orders_of(axis):
    bits = list(range((lax.axis_size(axis) - 1).bit_length()))
    if len(bits) < 3:
        return [bits, bits]
    return [bits, [bits[1], bits[0]] + bits[2:]]


def fetch_tiles(slab_ref, begin, buffer, arrived):
    copies = []
    for tile in range(buffer.shape[0]):
        span = pl.ds(begin + tile * TILE, TILE)
        copies.append(
            pltpu.make_async_copy(slab_ref.at[:, span], buffer.at[tile], arrived.at[tile])
        )
    for copy in copies:
        copy.start()
    return copies


def sketch_kernel(begin, start_ref, slab_ref, *refs):
    outs, (buffer, arrived) = refs[:-2], refs[-2:]
    copies = fetch_tiles(slab_ref, begin, buffer, arrived)
    left = start_ref[...].T
    for tile, copy in enumerate(copies):
        copy.wait()
        out, inner = divmod(tile * TILE, outs[0].shape[1])
        outs[out][:, inner : inner + TILE] = lax.dot_general(
            left, buffer[tile], (((1,), (0,)), ((), ())), preferred_element_type=jnp.float32
        )


def first_product(start, slab, begin, cols, chunks):
    rows, width = start.shape
    return pl.pallas_call(
        functools.partial(sketch_kernel, begin),
        out_shape=[jax.ShapeDtypeStruct((width, cols // chunks), jnp.float32)] * chunks,
        in_specs=[
            pl.BlockSpec(memory_space=pltpu.VMEM),
            pl.BlockSpec(memory_space=pl.ANY),
        ],
        out_specs=[pl.BlockSpec(memory_space=pltpu.VMEM)] * chunks,
        scratch_shapes=[
            pltpu.VMEM((cols // TILE, rows, TILE), jnp.bfloat16),
            pltpu.SemaphoreType.DMA((cols // TILE,)),
        ],
        compiler_params=pltpu.CompilerParams(vmem_limit_bytes=KERNEL_VMEM),
        cost_estimate=pl.CostEstimate(
            flops=2 * rows * width * cols, bytes_accessed=2 * rows * cols, transcendentals=0
        ),
        name="first_product",
    )(start, slab)


def matmul(left, right, exact=True):
    if not exact:
        left, right = left.astype(jnp.bfloat16), right.astype(jnp.bfloat16)
    return lax.dot_general(
        left,
        right,
        (((1,), (0,)), ((), ())),
        precision=lax.Precision.HIGHEST if exact else None,
        preferred_element_type=jnp.float32,
    )


def matmul_t(left, right, exact=True):
    if not exact:
        left, right = left.astype(jnp.bfloat16), right.astype(jnp.bfloat16)
    return lax.dot_general(
        left,
        right,
        (((1,), (1,)), ((), ())),
        precision=lax.Precision.HIGHEST if exact else None,
        preferred_element_type=jnp.float32,
    )


def gram_kernel(total_cols, mine_ref, other_ref, packed_ref, sketch_ref):
    sketch = (mine_ref[...] + other_ref[...]) / total_cols
    sketch_ref[...] = sketch.T
    gram = matmul(sketch_ref[...], sketch)
    half = gram.shape[0] // 2
    row = lax.broadcasted_iota(jnp.int32, (half, 2 * half), 0)
    col = lax.broadcasted_iota(jnp.int32, (half, 2 * half), 1)
    top, bottom = gram[:half], pltpu.roll(gram[half:], half, 1)
    packed_ref[:half] = jnp.where(row > col, bottom, top)
    diagonal = jnp.sum(jnp.where(row == col, bottom, 0.0), axis=0, keepdims=True)
    packed_ref[half:] = jnp.broadcast_to(diagonal, (8, 2 * half))


def unpack_gram(packed):
    width = packed.shape[1]
    half = width // 2
    row = lax.broadcasted_iota(jnp.int32, (half, width), 0)
    col = lax.broadcasted_iota(jnp.int32, (half, width), 1)
    square = packed[:half]
    top = jnp.where(row > col, 0.0, square)
    lower = jnp.where(row > col, square, jnp.where(row == col, packed[half : half + 1], 0.0))
    parts = jnp.concatenate([top, pltpu.roll(lower, half, 1)], axis=0)
    row = lax.broadcasted_iota(jnp.int32, (width, width), 0)
    col = lax.broadcasted_iota(jnp.int32, (width, width), 1)
    return jnp.where(row == col, parts, parts + parts.T)


def make_gram(mine, other, total_cols):
    rows, width = mine.shape
    return pl.pallas_call(
        functools.partial(gram_kernel, total_cols),
        out_shape=[
            jax.ShapeDtypeStruct((width // 2 + 8, width), jnp.float32),
            jax.ShapeDtypeStruct((width, rows), jnp.float32),
        ],
        in_specs=[pl.BlockSpec(memory_space=pltpu.VMEM)] * 2,
        out_specs=[pl.BlockSpec(memory_space=pltpu.VMEM)] * 2,
        compiler_params=pltpu.CompilerParams(vmem_limit_bytes=16 * 2**20),
        name="make_gram",
    )(mine, other)


UPDATES = 4
LOOSE_UPDATES = 2
CLOSE = 1e-5


def pair_product(pair, slab, tile, products):
    width = pair.shape[0] // 2
    both = jnp.dot(pair, slab, preferred_element_type=jnp.float32)
    out, inner = divmod(tile * TILE, products[0].shape[1])
    products[out][:, inner : inner + TILE] = both[:width] + both[width:]


def last_kernel(begin, pair_ref, slab_ref, *refs):
    products, (buffer, arrived) = refs[:-2], refs[-2:]
    copies = fetch_tiles(slab_ref, begin, buffer, arrived)
    pair = pair_ref[...]
    for tile, copy in enumerate(copies):
        copy.wait()
        pair_product(pair, buffer[tile], tile, products)


def basis_kernel(root_rows, gram_ref, sketch_ref, slab_ref, basis_ref, pair_ref, *refs):
    products, (work_ref, inverse_ref, buffer, arrived) = refs[:-4], refs[-4:]
    fetch = pltpu.make_async_copy(
        slab_ref.at[:, pl.ds(0, buffer.shape[1])], buffer, arrived
    )
    fetch.start()
    width = gram_ref.shape[1]
    row = lax.broadcasted_iota(jnp.int32, (width, width), 0)
    col = lax.broadcasted_iota(jnp.int32, (width, width), 1)
    on_diag = row == col
    unit = jnp.where(on_diag, 1.0, 0.0)
    half = jnp.where(row > col, 1.0, jnp.where(on_diag, 0.5, 0.0))

    gram = unpack_gram(gram_ref[...])
    diagonal = jnp.where(on_diag, gram, 0.0)
    down = lax.rsqrt(jnp.sum(diagonal, axis=1, keepdims=True))
    across = lax.rsqrt(jnp.sum(diagonal, axis=0, keepdims=True))
    scaled = gram * down * across

    error = scaled - unit
    step = error * half
    inverse = unit - step + matmul(step, step, False)
    for update in range(1, UPDATES):
        exact = update >= LOOSE_UPDATES
        error = matmul_t(matmul(inverse, scaled, exact), inverse, exact) - unit
        step = error * half
        inverse = inverse - matmul(step, inverse - matmul(step, inverse, exact), exact)
    inverse_ref[...] = inverse * across
    far = jnp.sum(error * error)

    @pl.when(jnp.logical_not(far <= CLOSE))
    def _():
        work_ref[...] = gram
        inverse_ref[...] = unit

        def eliminate(k, carry):
            whole = work_ref[...]
            pivot_row = work_ref[pl.ds(k, 1), :]
            pivot = jnp.sum(
                jnp.where(col[:1] == k, pivot_row, 0.0), axis=1, keepdims=True
            )
            column = jnp.sum(jnp.where(col == k, whole, 0.0), axis=1, keepdims=True)
            factor = jnp.where(row[:, :1] > k, column / pivot, 0.0)
            work_ref[...] = whole - factor * pivot_row
            inverse_ref[...] = inverse_ref[...] - factor * inverse_ref[pl.ds(k, 1), :]
            return carry

        lax.fori_loop(0, width, eliminate, 0)
        pivots = jnp.sum(jnp.where(on_diag, work_ref[...], 0.0), axis=1, keepdims=True)
        inverse_ref[...] = inverse_ref[...] * lax.rsqrt(pivots)

    basis = matmul(inverse_ref[...], sketch_ref[...]) * root_rows
    high = basis.astype(jnp.bfloat16)
    pair_ref[:width] = high
    pair_ref[width:] = (basis - high.astype(jnp.float32)).astype(jnp.bfloat16)
    pair = pair_ref[...]
    fetch.wait()
    for tile in range(buffer.shape[1] // TILE):
        slab = buffer[:, tile * TILE : (tile + 1) * TILE]
        pair_product(pair, slab, tile, products)
    basis_ref[...] = basis.T


def product_shapes(width, cols, chunks):
    return [jax.ShapeDtypeStruct((width, cols // chunks), jnp.float32)] * chunks


def tile_scratch(rows, cols):
    tiles = cols // TILE
    return [pltpu.VMEM((tiles, rows, TILE), jnp.bfloat16), pltpu.SemaphoreType.DMA((tiles,))]


def make_basis(gram, sketch, slab, cols, chunks, root_rows):
    width, rows = sketch.shape
    return pl.pallas_call(
        functools.partial(basis_kernel, root_rows),
        out_shape=[
            jax.ShapeDtypeStruct((rows, width), jnp.float32),
            jax.ShapeDtypeStruct((2 * width, rows), jnp.bfloat16),
        ]
        + product_shapes(width, cols, chunks),
        in_specs=[pl.BlockSpec(memory_space=pltpu.VMEM)] * 2
        + [pl.BlockSpec(memory_space=pl.ANY)],
        out_specs=[pl.BlockSpec(memory_space=pltpu.VMEM)] * (2 + chunks),
        scratch_shapes=[
            pltpu.VMEM((width, width), jnp.float32),
            pltpu.VMEM((width, width), jnp.float32),
            pltpu.VMEM((rows, cols), jnp.bfloat16),
            pltpu.SemaphoreType.DMA,
        ],
        compiler_params=pltpu.CompilerParams(vmem_limit_bytes=KERNEL_VMEM),
        name="make_basis",
    )(gram, sketch, slab)


def last_product(pair, slab, begin, cols, chunks):
    twice, rows = pair.shape
    return pl.pallas_call(
        functools.partial(last_kernel, begin),
        out_shape=product_shapes(twice // 2, cols, chunks),
        in_specs=[
            pl.BlockSpec(memory_space=pltpu.VMEM),
            pl.BlockSpec(memory_space=pl.ANY),
        ],
        out_specs=[pl.BlockSpec(memory_space=pltpu.VMEM)] * chunks,
        scratch_shapes=tile_scratch(rows, cols),
        compiler_params=pltpu.CompilerParams(vmem_limit_bytes=KERNEL_VMEM),
        cost_estimate=pl.CostEstimate(
            flops=2 * rows * twice * cols, bytes_accessed=2 * rows * cols, transcendentals=0
        ),
        name="last_product",
    )(pair, slab)


def per_device(activations, start_sketch):
    rows_here, cols_here = activations.shape
    width = start_sketch.shape[1]
    parts = lax.axis_size("row")
    total_rows = rows_here * parts
    total_cols = cols_here * lax.axis_size("col")
    root_rows = math.sqrt(total_rows)

    local_cols = []
    for begin in (0, cols_here // 2):
        local_cols += first_product(
            start_sketch, activations, begin, cols_here // 2, CHUNKS // 2
        )
    partial_sketch = 0.0
    orders = orders_of("row")
    step = cols_here // CHUNKS
    for c in range(CHUNKS):
        span = slice(c * step, (c + 1) * step)
        shared = sum_and_share(local_cols[c], "row", orders[c % 2], 1.0 / root_rows)
        partial_sketch = partial_sketch + lax.dot_general(
            activations[:, span],
            shared,
            (((1,), (1,)), ((), ())),
            preferred_element_type=jnp.float32,
        )
    other_sketch = swap(partial_sketch, "col", 1)
    packed, sketch = make_gram(partial_sketch, other_sketch, total_cols)
    half, chunks = cols_here // 2, CHUNKS // 2
    basis, pair, *products = make_basis(
        row_sum(packed), sketch, activations, half, chunks, root_rows
    )
    products += last_product(pair, activations, half, half, chunks)
    pieces = [
        scatter_sum(product, "row", orders[c % 2]) / total_rows
        for c, product in enumerate(products)
    ]
    return (basis, jnp.concatenate(pieces, axis=1))


def solution(mesh):
    return jax.shard_map(
        per_device,
        mesh=mesh,
        in_specs=(P(("grp", "row"), "col"), P(("grp", "row"), None)),
        out_specs=(P(("grp", "row"), None), P(("grp", "row"), "col")),
        check_vma=False,
    )
```

```python
import functools
import math

import jax
import jax.numpy as jnp
from jax import lax
from jax.experimental import pallas as pl
from jax.experimental.pallas import tpu as pltpu
from jax.sharding import PartitionSpec as P

CHUNKS = 4
TILE = 512
KERNEL_VMEM = 50 * 2**20


def swap(value, axis, distance):
    size = lax.axis_size(axis)
    return lax.ppermute(value, axis, [(i, i ^ distance) for i in range(size)])


def row_sum(value):
    rows, cores = lax.axis_size("row"), lax.axis_size("col")
    assert cores == 2
    first = lax.axis_index("col") == 0
    stride = 1
    while stride < rows:
        radix = min(8, rows // stride)
        split = min(2, radix // 2)
        terms = []
        for near in [digit for digit in range(radix) if not digit & split]:
            pairs = []
            for row in range(rows):
                for core, digit in ((0, near), (1, near | split)):
                    if digit:
                        pairs.append((row * cores + core, (row ^ digit * stride) * cores + core))
            terms.append(lax.ppermute(value, ("row", "col"), pairs))
        terms[0] = jnp.where(first, value, terms[0])
        while len(terms) > 1:
            terms = [terms[i] + terms[i + 1] for i in range(0, len(terms), 2)]
        value = terms[0] + swap(terms[0], "col", 1)
        stride *= radix
    return value


def scatter_sum(value, axis, order):
    rows, cols = value.shape[0] >> len(order), value.shape[1]
    total = value.reshape([2] * len(order) + [rows, cols])
    left = sorted(order, reverse=True)
    for bit in order:
        dim = left.index(bit)
        left.remove(bit)
        low = lax.index_in_dim(total, 0, dim, keepdims=False)
        high = lax.index_in_dim(total, 1, dim, keepdims=False)
        upper = bit_of(axis, bit) == 1
        send = jnp.where(upper, low, high).astype(jnp.bfloat16)
        landed = swap(send, axis, 1 << bit)
        total = jnp.where(upper, high, low) + landed.astype(jnp.float32)
    return total


def bit_of(axis, bit):
    return lax.rem(lax.div(lax.axis_index(axis), 1 << bit), 2)


def sum_and_share(value, axis, order, scale):
    for bit in order[:-1]:
        upper = bit_of(axis, bit) == 1
        half = value.shape[1] // 2
        low, high = value[:, :half], value[:, half:]
        send = jnp.where(upper, low, high).astype(jnp.bfloat16)
        landed = swap(send, axis, 1 << bit)
        value = jnp.where(upper, high, low) + landed.astype(jnp.float32)
    landed = swap(value.astype(jnp.bfloat16), axis, 1 << order[-1])
    block = ((value + landed.astype(jnp.float32)) * scale).astype(jnp.bfloat16)
    for bit in reversed(order[:-1]):
        upper = bit_of(axis, bit) == 1
        other = swap(block, axis, 1 << bit)
        block = jnp.concatenate(
            [jnp.where(upper, other, block), jnp.where(upper, block, other)], axis=1
        )
    return block


def orders_of(axis):
    bits = list(range((lax.axis_size(axis) - 1).bit_length()))
    if len(bits) < 3:
        return [bits, bits]
    return [bits, [bits[1], bits[0]] + bits[2:]]


def fetch_tiles(slab_ref, begin, buffer, arrived):
    copies = []
    for tile in range(buffer.shape[0]):
        span = pl.ds(begin + tile * TILE, TILE)
        copies.append(
            pltpu.make_async_copy(slab_ref.at[:, span], buffer.at[tile], arrived.at[tile])
        )
    for copy in copies:
        copy.start()
    return copies


def sketch_kernel(begin, start_ref, slab_ref, *refs):
    outs, (buffer, arrived) = refs[:-2], refs[-2:]
    copies = fetch_tiles(slab_ref, begin, buffer, arrived)
    left = start_ref[...].T
    for tile, copy in enumerate(copies):
        copy.wait()
        out, inner = divmod(tile * TILE, outs[0].shape[1])
        outs[out][:, inner : inner + TILE] = lax.dot_general(
            left, buffer[tile], (((1,), (0,)), ((), ())), preferred_element_type=jnp.float32
        )


def first_product(start, slab, begin, cols, chunks):
    rows, width = start.shape
    return pl.pallas_call(
        functools.partial(sketch_kernel, begin),
        out_shape=[jax.ShapeDtypeStruct((width, cols // chunks), jnp.float32)] * chunks,
        in_specs=[
            pl.BlockSpec(memory_space=pltpu.VMEM),
            pl.BlockSpec(memory_space=pl.ANY),
        ],
        out_specs=[pl.BlockSpec(memory_space=pltpu.VMEM)] * chunks,
        scratch_shapes=[
            pltpu.VMEM((cols // TILE, rows, TILE), jnp.bfloat16),
            pltpu.SemaphoreType.DMA((cols // TILE,)),
        ],
        compiler_params=pltpu.CompilerParams(vmem_limit_bytes=KERNEL_VMEM),
        cost_estimate=pl.CostEstimate(
            flops=2 * rows * width * cols, bytes_accessed=2 * rows * cols, transcendentals=0
        ),
        name="first_product",
    )(start, slab)


def split(value):
    high = value.astype(jnp.bfloat16)
    return high, (value - high.astype(jnp.float32)).astype(jnp.bfloat16)


def matmul(left, right, exact=True, contract=0):
    if exact:
        (high, low), (other_high, other_low) = split(left), split(right)
        left = jnp.concatenate([high, high, low], axis=1)
        right = jnp.concatenate([other_high, other_low, other_high], axis=contract)
    else:
        left, right = left.astype(jnp.bfloat16), right.astype(jnp.bfloat16)
    return lax.dot_general(
        left, right, (((1,), (contract,)), ((), ())), preferred_element_type=jnp.float32
    )


def matmul_full(left, right):
    return jnp.dot(
        left, right, precision=lax.Precision.HIGHEST, preferred_element_type=jnp.float32
    )


def gram_kernel(total_cols, mine_ref, other_ref, packed_ref, sketch_ref):
    sketch = (mine_ref[...] + other_ref[...]) / total_cols
    sketch_ref[...] = sketch.T
    gram = matmul_full(sketch_ref[...], sketch)
    half = gram.shape[0] // 2
    row = lax.broadcasted_iota(jnp.int32, (half, 2 * half), 0)
    col = lax.broadcasted_iota(jnp.int32, (half, 2 * half), 1)
    top, bottom = gram[:half], pltpu.roll(gram[half:], half, 1)
    packed_ref[:half] = jnp.where(row > col, bottom, top)
    diagonal = jnp.sum(jnp.where(row == col, bottom, 0.0), axis=0, keepdims=True)
    packed_ref[half:] = jnp.broadcast_to(diagonal, (8, 2 * half))


def unpack_gram(packed):
    width = packed.shape[1]
    half = width // 2
    row = lax.broadcasted_iota(jnp.int32, (half, width), 0)
    col = lax.broadcasted_iota(jnp.int32, (half, width), 1)
    square = packed[:half]
    top = jnp.where(row > col, 0.0, square)
    lower = jnp.where(row > col, square, jnp.where(row == col, packed[half : half + 1], 0.0))
    parts = jnp.concatenate([top, pltpu.roll(lower, half, 1)], axis=0)
    row = lax.broadcasted_iota(jnp.int32, (width, width), 0)
    col = lax.broadcasted_iota(jnp.int32, (width, width), 1)
    return jnp.where(row == col, parts, parts + parts.T)


def make_gram(mine, other, total_cols):
    rows, width = mine.shape
    return pl.pallas_call(
        functools.partial(gram_kernel, total_cols),
        out_shape=[
            jax.ShapeDtypeStruct((width // 2 + 8, width), jnp.float32),
            jax.ShapeDtypeStruct((width, rows), jnp.float32),
        ],
        in_specs=[pl.BlockSpec(memory_space=pltpu.VMEM)] * 2,
        out_specs=[pl.BlockSpec(memory_space=pltpu.VMEM)] * 2,
        compiler_params=pltpu.CompilerParams(vmem_limit_bytes=16 * 2**20),
        name="make_gram",
    )(mine, other)


UPDATES = 4
LOOSE_UPDATES = 2
CLOSE = 1e-5


def basis_kernel(
    root_rows, gram_ref, sketch_ref, slab_ref,
    basis_ref, *refs,
):
    products, (work_ref, inverse_ref, buffer, arrived) = refs[:-4], refs[-4:]
    fetch = pltpu.make_async_copy(slab_ref, buffer, arrived)
    fetch.start()
    width = gram_ref.shape[1]
    row = lax.broadcasted_iota(jnp.int32, (width, width), 0)
    col = lax.broadcasted_iota(jnp.int32, (width, width), 1)
    on_diag = row == col
    unit = jnp.where(on_diag, 1.0, 0.0)
    half = jnp.where(row > col, 1.0, jnp.where(on_diag, 0.5, 0.0))

    gram = unpack_gram(gram_ref[...])
    diagonal = jnp.where(on_diag, gram, 0.0)
    down = lax.rsqrt(jnp.sum(diagonal, axis=1, keepdims=True))
    across = lax.rsqrt(jnp.sum(diagonal, axis=0, keepdims=True))
    scaled = gram * down * across

    error = scaled - unit
    step = error * half
    inverse = unit - step + matmul(step, step, False)
    for update in range(1, UPDATES):
        exact = update >= LOOSE_UPDATES
        error = matmul(matmul(inverse, scaled, exact), inverse, exact, 1) - unit
        step = error * half
        if update < UPDATES - 1:
            step = step - matmul(step, step, exact)
        inverse = inverse - matmul(step, inverse, exact)
    inverse_ref[...] = inverse * across
    far = jnp.sum(error * error)

    @pl.when(jnp.logical_not(far <= CLOSE))
    def _():
        work_ref[...] = gram
        inverse_ref[...] = unit

        def eliminate(k, carry):
            whole = work_ref[...]
            pivot_row = work_ref[pl.ds(k, 1), :]
            pivot = jnp.sum(
                jnp.where(col[:1] == k, pivot_row, 0.0), axis=1, keepdims=True
            )
            column = jnp.sum(jnp.where(col == k, whole, 0.0), axis=1, keepdims=True)
            factor = jnp.where(row[:, :1] > k, column / pivot, 0.0)
            work_ref[...] = whole - factor * pivot_row
            inverse_ref[...] = inverse_ref[...] - factor * inverse_ref[pl.ds(k, 1), :]
            return carry

        lax.fori_loop(0, width, eliminate, 0)
        pivots = jnp.sum(jnp.where(on_diag, work_ref[...], 0.0), axis=1, keepdims=True)
        inverse_ref[...] = inverse_ref[...] * lax.rsqrt(pivots)

    basis = matmul_full(inverse_ref[...], sketch_ref[...]) * root_rows
    pair = jnp.concatenate(split(basis), axis=0)
    fetch.wait()
    for start in range(0, buffer.shape[1], TILE):
        both = lax.dot_general(
            pair,
            buffer[:, start : start + TILE],
            (((1,), (0,)), ((), ())),
            preferred_element_type=jnp.float32,
        )
        out, inner = divmod(start, products[0].shape[1])
        products[out][:, inner : inner + TILE] = both[:width] + both[width:]
    basis_ref[...] = basis.T


def make_basis(gram, sketch, slab, root_rows, chunks):
    width, rows = sketch.shape
    cols = slab.shape[1]
    return pl.pallas_call(
        functools.partial(basis_kernel, root_rows),
        out_shape=[jax.ShapeDtypeStruct((rows, width), jnp.float32)]
        + [jax.ShapeDtypeStruct((width, cols // chunks), jnp.float32)] * chunks,
        in_specs=[pl.BlockSpec(memory_space=pltpu.VMEM)] * 2
        + [pl.BlockSpec(memory_space=pl.ANY)],
        out_specs=[pl.BlockSpec(memory_space=pltpu.VMEM)] * (1 + chunks),
        scratch_shapes=[
            pltpu.VMEM((width, width), jnp.float32),
            pltpu.VMEM((width, width), jnp.float32),
            pltpu.VMEM(slab.shape, jnp.bfloat16),
            pltpu.SemaphoreType.DMA,
        ],
        compiler_params=pltpu.CompilerParams(vmem_limit_bytes=KERNEL_VMEM),
        name="make_basis",
    )(gram, sketch, slab)


def per_device(activations, start_sketch):
    rows_here, cols_here = activations.shape
    width = start_sketch.shape[1]
    parts = lax.axis_size("row")
    total_rows = rows_here * parts
    total_cols = cols_here * lax.axis_size("col")
    root_rows = math.sqrt(total_rows)

    local_cols = []
    for begin in (0, cols_here // 2):
        local_cols += first_product(
            start_sketch, activations, begin, cols_here // 2, CHUNKS // 2
        )
    partial_sketch = 0.0
    orders = orders_of("row")
    step = cols_here // CHUNKS
    for c in range(CHUNKS):
        span = slice(c * step, (c + 1) * step)
        shared = sum_and_share(local_cols[c], "row", orders[c % 2], 1.0 / root_rows)
        partial_sketch = partial_sketch + lax.dot_general(
            activations[:, span],
            shared,
            (((1,), (1,)), ((), ())),
            preferred_element_type=jnp.float32,
        )
    other_sketch = swap(partial_sketch, "col", 1)
    packed, sketch = make_gram(partial_sketch, other_sketch, total_cols)
    basis, *products = make_basis(row_sum(packed), sketch, activations, root_rows, CHUNKS)
    pieces = [
        scatter_sum(product, "row", orders[c % 2]) / total_rows
        for c, product in enumerate(products)
    ]
    return (basis, jnp.concatenate(pieces, axis=1))


def solution(mesh):
    return jax.shard_map(
        per_device,
        mesh=mesh,
        in_specs=(P(("grp", "row"), "col"), P(("grp", "row"), None)),
        out_specs=(P(("grp", "row"), None), P(("grp", "row"), "col")),
        check_vma=False,
    )
```

```python
import functools
import math

import jax
import jax.numpy as jnp
from jax import lax
from jax.experimental import pallas as pl
from jax.experimental.pallas import tpu as pltpu
from jax.sharding import PartitionSpec as P

CHUNKS = 4
LAST_CHUNKS = 2
TILE = 512
KERNEL_VMEM = 50 * 2**20


def swap(value, axis, distance):
    size = lax.axis_size(axis)
    return lax.ppermute(value, axis, [(i, i ^ distance) for i in range(size)])


def row_sum(value):
    rows, cores = lax.axis_size("row"), lax.axis_size("col")
    assert cores == 2
    first = lax.axis_index("col") == 0
    stride = 1
    while stride < rows:
        radix = min(8, rows // stride)
        split = min(2, radix // 2)
        terms = []
        for near in [digit for digit in range(radix) if not digit & split]:
            pairs = []
            for row in range(rows):
                for core, digit in ((0, near), (1, near | split)):
                    if digit:
                        pairs.append((row * cores + core, (row ^ digit * stride) * cores + core))
            terms.append(lax.ppermute(value, ("row", "col"), pairs))
        terms[0] = jnp.where(first, value, terms[0])
        while len(terms) > 1:
            terms = [terms[i] + terms[i + 1] for i in range(0, len(terms), 2)]
        value = terms[0] + swap(terms[0], "col", 1)
        stride *= radix
    return value


def levels_of(size):
    levels, stride = [], 1
    while stride < size:
        radix = 2 if stride == 1 else min(4, size // stride)
        levels.append((stride, radix))
        stride *= radix
    return levels


def scatter_sum(value, axis):
    size, cols = lax.axis_size(axis), value.shape[1]
    total = value.reshape(size, value.shape[0] // size, cols)
    for stride, radix in levels_of(size):
        digit = lax.rem(lax.div(lax.axis_index(axis), stride), radix)
        view = total.reshape((total.shape[0] // radix, radix) + total.shape[1:])
        total = lax.dynamic_index_in_dim(view, digit, 1, keepdims=False)
        for t in range(1, radix):
            part = lax.dynamic_index_in_dim(view, jnp.bitwise_xor(digit, t), 1, keepdims=False)
            landed = swap(part.astype(jnp.bfloat16), axis, t * stride)
            total = total + landed.astype(jnp.float32)
    return total[0]


def bit_of(axis, bit):
    return lax.rem(lax.div(lax.axis_index(axis), 1 << bit), 2)


def sum_and_share(value, axis, order, scale):
    for bit in order[:-1]:
        upper = bit_of(axis, bit) == 1
        half = value.shape[1] // 2
        low, high = value[:, :half], value[:, half:]
        send = jnp.where(upper, low, high).astype(jnp.bfloat16)
        landed = swap(send, axis, 1 << bit)
        value = jnp.where(upper, high, low) + landed.astype(jnp.float32)
    landed = swap(value.astype(jnp.bfloat16), axis, 1 << order[-1])
    block = ((value + landed.astype(jnp.float32)) * scale).astype(jnp.bfloat16)
    for bit in reversed(order[:-1]):
        upper = bit_of(axis, bit) == 1
        other = swap(block, axis, 1 << bit)
        block = jnp.concatenate(
            [jnp.where(upper, other, block), jnp.where(upper, block, other)], axis=1
        )
    return block


def orders_of(axis):
    bits = list(range((lax.axis_size(axis) - 1).bit_length()))
    if len(bits) < 3:
        return [bits, bits]
    return [bits, [bits[1], bits[0]] + bits[2:]]


def fetch_tiles(slab_ref, begin, buffer, arrived):
    copies = []
    for tile in range(buffer.shape[0]):
        span = pl.ds(begin + tile * TILE, TILE)
        copies.append(
            pltpu.make_async_copy(slab_ref.at[:, span], buffer.at[tile], arrived.at[tile])
        )
    for copy in copies:
        copy.start()
    return copies


def sketch_kernel(begin, start_ref, slab_ref, *refs):
    outs, (buffer, arrived) = refs[:-2], refs[-2:]
    copies = fetch_tiles(slab_ref, begin, buffer, arrived)
    left = start_ref[...].T
    for tile, copy in enumerate(copies):
        copy.wait()
        out, inner = divmod(tile * TILE, outs[0].shape[1])
        outs[out][:, inner : inner + TILE] = lax.dot_general(
            left, buffer[tile], (((1,), (0,)), ((), ())), preferred_element_type=jnp.float32
        )


def first_product(start, slab, begin, cols, chunks):
    rows, width = start.shape
    return pl.pallas_call(
        functools.partial(sketch_kernel, begin),
        out_shape=[jax.ShapeDtypeStruct((width, cols // chunks), jnp.float32)] * chunks,
        in_specs=[
            pl.BlockSpec(memory_space=pltpu.VMEM),
            pl.BlockSpec(memory_space=pl.ANY),
        ],
        out_specs=[pl.BlockSpec(memory_space=pltpu.VMEM)] * chunks,
        scratch_shapes=[
            pltpu.VMEM((cols // TILE, rows, TILE), jnp.bfloat16),
            pltpu.SemaphoreType.DMA((cols // TILE,)),
        ],
        compiler_params=pltpu.CompilerParams(vmem_limit_bytes=KERNEL_VMEM),
        cost_estimate=pl.CostEstimate(
            flops=2 * rows * width * cols, bytes_accessed=2 * rows * cols, transcendentals=0
        ),
        name="first_product",
    )(start, slab)


def split(value):
    high = value.astype(jnp.bfloat16)
    return high, (value - high.astype(jnp.float32)).astype(jnp.bfloat16)


def matmul(left, right, exact=True, contract=0):
    if exact:
        (high, low), (other_high, other_low) = split(left), split(right)
        left = jnp.concatenate([high, high, low], axis=1)
        right = jnp.concatenate([other_high, other_low, other_high], axis=contract)
    else:
        left, right = left.astype(jnp.bfloat16), right.astype(jnp.bfloat16)
    return lax.dot_general(
        left, right, (((1,), (contract,)), ((), ())), preferred_element_type=jnp.float32
    )


def matmul_full(left, right):
    return jnp.dot(
        left, right, precision=lax.Precision.HIGHEST, preferred_element_type=jnp.float32
    )


def gram_kernel(total_cols, mine_ref, other_ref, packed_ref, sketch_ref):
    sketch = (mine_ref[...] + other_ref[...]) / total_cols
    sketch_ref[...] = sketch.T
    gram = matmul_full(sketch_ref[...], sketch)
    half = gram.shape[0] // 2
    row = lax.broadcasted_iota(jnp.int32, (half, 2 * half), 0)
    col = lax.broadcasted_iota(jnp.int32, (half, 2 * half), 1)
    top, bottom = gram[:half], pltpu.roll(gram[half:], half, 1)
    packed_ref[:half] = jnp.where(row > col, bottom, top)
    diagonal = jnp.sum(jnp.where(row == col, bottom, 0.0), axis=0, keepdims=True)
    packed_ref[half:] = jnp.broadcast_to(diagonal, (8, 2 * half))


def unpack_gram(packed):
    width = packed.shape[1]
    half = width // 2
    row = lax.broadcasted_iota(jnp.int32, (half, width), 0)
    col = lax.broadcasted_iota(jnp.int32, (half, width), 1)
    square = packed[:half]
    top = jnp.where(row > col, 0.0, square)
    lower = jnp.where(row > col, square, jnp.where(row == col, packed[half : half + 1], 0.0))
    parts = jnp.concatenate([top, pltpu.roll(lower, half, 1)], axis=0)
    row = lax.broadcasted_iota(jnp.int32, (width, width), 0)
    col = lax.broadcasted_iota(jnp.int32, (width, width), 1)
    return jnp.where(row == col, parts, parts + parts.T)


def make_gram(mine, other, total_cols):
    rows, width = mine.shape
    return pl.pallas_call(
        functools.partial(gram_kernel, total_cols),
        out_shape=[
            jax.ShapeDtypeStruct((width // 2 + 8, width), jnp.float32),
            jax.ShapeDtypeStruct((width, rows), jnp.float32),
        ],
        in_specs=[pl.BlockSpec(memory_space=pltpu.VMEM)] * 2,
        out_specs=[pl.BlockSpec(memory_space=pltpu.VMEM)] * 2,
        compiler_params=pltpu.CompilerParams(vmem_limit_bytes=16 * 2**20),
        name="make_gram",
    )(mine, other)


UPDATES = 4
LOOSE_UPDATES = 2
CLOSE = 1e-5


def basis_kernel(
    root_rows, gram_ref, sketch_ref, slab_ref,
    basis_ref, *refs,
):
    products, (work_ref, inverse_ref, buffer, arrived) = refs[:-4], refs[-4:]
    fetch = pltpu.make_async_copy(slab_ref, buffer, arrived)
    fetch.start()
    width = gram_ref.shape[1]
    row = lax.broadcasted_iota(jnp.int32, (width, width), 0)
    col = lax.broadcasted_iota(jnp.int32, (width, width), 1)
    on_diag = row == col
    unit = jnp.where(on_diag, 1.0, 0.0)
    half = jnp.where(row > col, 1.0, jnp.where(on_diag, 0.5, 0.0))

    gram = unpack_gram(gram_ref[...])
    diagonal = jnp.where(on_diag, gram, 0.0)
    down = lax.rsqrt(jnp.sum(diagonal, axis=1, keepdims=True))
    across = lax.rsqrt(jnp.sum(diagonal, axis=0, keepdims=True))
    scaled = gram * down * across

    error = scaled - unit
    step = error * half
    inverse = unit - step + matmul(step, step, False)
    for update in range(1, UPDATES):
        exact = update >= LOOSE_UPDATES
        error = matmul(matmul(inverse, scaled, exact), inverse, exact, 1) - unit
        step = error * half
        if update < UPDATES - 1:
            step = step - matmul(step, step, exact)
        inverse = inverse - matmul(step, inverse, exact)
    inverse_ref[...] = inverse * across
    far = jnp.sum(error * error)

    @pl.when(jnp.logical_not(far <= CLOSE))
    def _():
        work_ref[...] = gram
        inverse_ref[...] = unit

        def eliminate(k, carry):
            whole = work_ref[...]
            pivot_row = work_ref[pl.ds(k, 1), :]
            pivot = jnp.sum(
                jnp.where(col[:1] == k, pivot_row, 0.0), axis=1, keepdims=True
            )
            column = jnp.sum(jnp.where(col == k, whole, 0.0), axis=1, keepdims=True)
            factor = jnp.where(row[:, :1] > k, column / pivot, 0.0)
            work_ref[...] = whole - factor * pivot_row
            inverse_ref[...] = inverse_ref[...] - factor * inverse_ref[pl.ds(k, 1), :]
            return carry

        lax.fori_loop(0, width, eliminate, 0)
        pivots = jnp.sum(jnp.where(on_diag, work_ref[...], 0.0), axis=1, keepdims=True)
        inverse_ref[...] = inverse_ref[...] * lax.rsqrt(pivots)

    basis = matmul_full(inverse_ref[...], sketch_ref[...]) * root_rows
    pair = jnp.concatenate(split(basis), axis=0)
    fetch.wait()
    for start in range(0, buffer.shape[1], TILE):
        both = lax.dot_general(
            pair,
            buffer[:, start : start + TILE],
            (((1,), (0,)), ((), ())),
            preferred_element_type=jnp.float32,
        )
        out, inner = divmod(start, products[0].shape[1])
        products[out][:, inner : inner + TILE] = both[:width] + both[width:]
    basis_ref[...] = basis.T


def make_basis(gram, sketch, slab, root_rows, chunks):
    width, rows = sketch.shape
    cols = slab.shape[1]
    return pl.pallas_call(
        functools.partial(basis_kernel, root_rows),
        out_shape=[jax.ShapeDtypeStruct((rows, width), jnp.float32)]
        + [jax.ShapeDtypeStruct((width, cols // chunks), jnp.float32)] * chunks,
        in_specs=[pl.BlockSpec(memory_space=pltpu.VMEM)] * 2
        + [pl.BlockSpec(memory_space=pl.ANY)],
        out_specs=[pl.BlockSpec(memory_space=pltpu.VMEM)] * (1 + chunks),
        scratch_shapes=[
            pltpu.VMEM((width, width), jnp.float32),
            pltpu.VMEM((width, width), jnp.float32),
            pltpu.VMEM(slab.shape, jnp.bfloat16),
            pltpu.SemaphoreType.DMA,
        ],
        compiler_params=pltpu.CompilerParams(vmem_limit_bytes=KERNEL_VMEM),
        name="make_basis",
    )(gram, sketch, slab)


def per_device(activations, start_sketch):
    rows_here, cols_here = activations.shape
    width = start_sketch.shape[1]
    parts = lax.axis_size("row")
    total_rows = rows_here * parts
    total_cols = cols_here * lax.axis_size("col")
    root_rows = math.sqrt(total_rows)

    local_cols = []
    for begin in (0, cols_here // 2):
        local_cols += first_product(
            start_sketch, activations, begin, cols_here // 2, CHUNKS // 2
        )
    partial_sketch = 0.0
    orders = orders_of("row")
    step = cols_here // CHUNKS
    for c in range(CHUNKS):
        span = slice(c * step, (c + 1) * step)
        shared = sum_and_share(local_cols[c], "row", orders[c % 2], 1.0 / root_rows)
        partial_sketch = partial_sketch + lax.dot_general(
            activations[:, span],
            shared,
            (((1,), (1,)), ((), ())),
            preferred_element_type=jnp.float32,
        )
    other_sketch = swap(partial_sketch, "col", 1)
    packed, sketch = make_gram(partial_sketch, other_sketch, total_cols)
    basis, *products = make_basis(row_sum(packed), sketch, activations, root_rows, LAST_CHUNKS)
    pieces = [scatter_sum(product, "row") / total_rows for product in products]
    return (basis, jnp.concatenate(pieces, axis=1))


def solution(mesh):
    return jax.shard_map(
        per_device,
        mesh=mesh,
        in_specs=(P(("grp", "row"), "col"), P(("grp", "row"), None)),
        out_specs=(P(("grp", "row"), None), P(("grp", "row"), "col")),
        check_vma=False,
    )
```

```python
import functools
import math

import jax
import jax.numpy as jnp
from jax import lax
from jax.experimental import pallas as pl
from jax.experimental.pallas import tpu as pltpu
from jax.sharding import PartitionSpec as P

CHUNKS = 4
LINK_TYPES = (jnp.bfloat16, jnp.float32, jnp.bfloat16)
TILE = 512
KERNEL_VMEM = 50 * 2**20


def swap(value, axis, distance):
    size = lax.axis_size(axis)
    return lax.ppermute(value, axis, [(i, i ^ distance) for i in range(size)])


def row_sum(value):
    rows, cores = lax.axis_size("row"), lax.axis_size("col")
    assert cores == 2
    first = lax.axis_index("col") == 0
    stride = 1
    while stride < rows:
        if rows // stride < 8:
            value = value + swap(value, "row", stride)
            stride *= 2
            continue
        terms = []
        for near in range(2):
            pairs = [
                (row * 2 + core, (row ^ (near + 2 * core) * stride) * 2 + core)
                for row in range(rows)
                for core in range(2)
                if near + core
            ]
            terms.append(lax.ppermute(value, ("row", "col"), pairs))
        here = jnp.where(first, value, terms[0]) + terms[1]
        far = []
        for cross in range(2):
            pairs = [
                (row * 2 + core, (row ^ 4 * stride) * 2 + (core ^ cross))
                for row in range(rows)
                for core in range(2)
            ]
            far.append(lax.ppermute(here, ("row", "col"), pairs))
        value = (here + swap(here, "col", 1)) + (far[0] + far[1])
        stride *= 8
    return value


def scatter_sum(value, axis, order):
    rows, cols = value.shape[0] >> len(order), value.shape[1]
    total = value.reshape([2] * len(order) + [rows, cols])
    left = sorted(order, reverse=True)
    for step, bit in enumerate(order):
        dim = left.index(bit)
        left.remove(bit)
        low = lax.index_in_dim(total, 0, dim, keepdims=False)
        high = lax.index_in_dim(total, 1, dim, keepdims=False)
        upper = bit_of(axis, bit) == 1
        send = jnp.where(upper, low, high).astype(LINK_TYPES[min(step, 2)])
        landed = swap(send, axis, 1 << bit)
        total = jnp.where(upper, high, low) + landed.astype(jnp.float32)
    return total


def bit_of(axis, bit):
    return lax.rem(lax.div(lax.axis_index(axis), 1 << bit), 2)


def sum_and_share(value, axis, order, scale):
    for step, bit in enumerate(order[:-1]):
        upper = bit_of(axis, bit) == 1
        half = value.shape[1] // 2
        low, high = value[:, :half], value[:, half:]
        send = jnp.where(upper, low, high).astype(LINK_TYPES[min(step, 2)])
        landed = swap(send, axis, 1 << bit)
        value = jnp.where(upper, high, low) + landed.astype(jnp.float32)
    landed = swap(value.astype(jnp.bfloat16), axis, 1 << order[-1])
    block = ((value + landed.astype(jnp.float32)) * scale).astype(jnp.bfloat16)
    for bit in reversed(order[:-1]):
        upper = bit_of(axis, bit) == 1
        other = swap(block, axis, 1 << bit)
        block = jnp.concatenate(
            [jnp.where(upper, other, block), jnp.where(upper, block, other)], axis=1
        )
    return block


def orders_of(axis):
    bits = list(range((lax.axis_size(axis) - 1).bit_length()))
    if len(bits) < 3:
        return [bits, bits]
    return [bits, [bits[1], bits[0]] + bits[2:]]


def fetch_tiles(slab_ref, begin, buffer, arrived):
    copies = []
    for tile in range(buffer.shape[0]):
        span = pl.ds(begin + tile * TILE, TILE)
        copies.append(
            pltpu.make_async_copy(slab_ref.at[:, span], buffer.at[tile], arrived.at[tile])
        )
    for copy in copies:
        copy.start()
    return copies


def sketch_kernel(begin, start_ref, slab_ref, *refs):
    outs, (buffer, arrived) = refs[:-2], refs[-2:]
    copies = fetch_tiles(slab_ref, begin, buffer, arrived)
    left = start_ref[...].T
    for tile, copy in enumerate(copies):
        copy.wait()
        out, inner = divmod(tile * TILE, outs[0].shape[1])
        outs[out][:, inner : inner + TILE] = lax.dot_general(
            left, buffer[tile], (((1,), (0,)), ((), ())), preferred_element_type=jnp.float32
        )


def first_product(start, slab, begin, cols, chunks):
    rows, width = start.shape
    return pl.pallas_call(
        functools.partial(sketch_kernel, begin),
        out_shape=[jax.ShapeDtypeStruct((width, cols // chunks), jnp.float32)] * chunks,
        in_specs=[
            pl.BlockSpec(memory_space=pltpu.VMEM),
            pl.BlockSpec(memory_space=pl.ANY),
        ],
        out_specs=[pl.BlockSpec(memory_space=pltpu.VMEM)] * chunks,
        scratch_shapes=[
            pltpu.VMEM((cols // TILE, rows, TILE), jnp.bfloat16),
            pltpu.SemaphoreType.DMA((cols // TILE,)),
        ],
        compiler_params=pltpu.CompilerParams(vmem_limit_bytes=KERNEL_VMEM),
        cost_estimate=pl.CostEstimate(
            flops=2 * rows * width * cols, bytes_accessed=2 * rows * cols, transcendentals=0
        ),
        name="first_product",
    )(start, slab)


def split(value):
    high = value.astype(jnp.bfloat16)
    return high, (value - high.astype(jnp.float32)).astype(jnp.bfloat16)


def matmul(left, right, exact=True, contract=0):
    if exact:
        (high, low), (other_high, other_low) = split(left), split(right)
        left = jnp.concatenate([high, high, low], axis=1)
        right = jnp.concatenate([other_high, other_low, other_high], axis=contract)
    else:
        left, right = left.astype(jnp.bfloat16), right.astype(jnp.bfloat16)
    return lax.dot_general(
        left, right, (((1,), (contract,)), ((), ())), preferred_element_type=jnp.float32
    )


def matmul_full(left, right):
    return jnp.dot(
        left, right, precision=lax.Precision.HIGHEST, preferred_element_type=jnp.float32
    )


def gram_kernel(total_cols, mine_ref, other_ref, packed_ref, sketch_ref):
    sketch = (mine_ref[...] + other_ref[...]) / total_cols
    sketch_ref[...] = sketch.T
    gram = matmul_full(sketch_ref[...], sketch)
    half = gram.shape[0] // 2
    row = lax.broadcasted_iota(jnp.int32, (half, 2 * half), 0)
    col = lax.broadcasted_iota(jnp.int32, (half, 2 * half), 1)
    top, bottom = gram[:half], pltpu.roll(gram[half:], half, 1)
    packed_ref[:half] = jnp.where(row > col, bottom, top)
    diagonal = jnp.sum(jnp.where(row == col, bottom, 0.0), axis=0, keepdims=True)
    packed_ref[half:] = jnp.broadcast_to(diagonal, (8, 2 * half))


def unpack_gram(packed):
    width = packed.shape[1]
    half = width // 2
    row = lax.broadcasted_iota(jnp.int32, (half, width), 0)
    col = lax.broadcasted_iota(jnp.int32, (half, width), 1)
    square = packed[:half]
    top = jnp.where(row > col, 0.0, square)
    lower = jnp.where(row > col, square, jnp.where(row == col, packed[half : half + 1], 0.0))
    parts = jnp.concatenate([top, pltpu.roll(lower, half, 1)], axis=0)
    row = lax.broadcasted_iota(jnp.int32, (width, width), 0)
    col = lax.broadcasted_iota(jnp.int32, (width, width), 1)
    return jnp.where(row == col, parts, parts + parts.T)


def make_gram(mine, other, total_cols):
    rows, width = mine.shape
    return pl.pallas_call(
        functools.partial(gram_kernel, total_cols),
        out_shape=[
            jax.ShapeDtypeStruct((width // 2 + 8, width), jnp.float32),
            jax.ShapeDtypeStruct((width, rows), jnp.float32),
        ],
        in_specs=[pl.BlockSpec(memory_space=pltpu.VMEM)] * 2,
        out_specs=[pl.BlockSpec(memory_space=pltpu.VMEM)] * 2,
        compiler_params=pltpu.CompilerParams(vmem_limit_bytes=16 * 2**20),
        name="make_gram",
    )(mine, other)


UPDATES = 4
LOOSE_UPDATES = 2
CLOSE = 1e-5


def basis_kernel(
    root_rows, gram_ref, sketch_ref, slab_ref,
    basis_ref, *refs,
):
    products, (work_ref, inverse_ref, buffer, arrived) = refs[:-4], refs[-4:]
    fetch = pltpu.make_async_copy(slab_ref, buffer, arrived)
    fetch.start()
    width = gram_ref.shape[1]
    row = lax.broadcasted_iota(jnp.int32, (width, width), 0)
    col = lax.broadcasted_iota(jnp.int32, (width, width), 1)
    on_diag = row == col
    unit = jnp.where(on_diag, 1.0, 0.0)
    half = jnp.where(row > col, 1.0, jnp.where(on_diag, 0.5, 0.0))

    gram = unpack_gram(gram_ref[...])
    diagonal = jnp.where(on_diag, gram, 0.0)
    down = lax.rsqrt(jnp.sum(diagonal, axis=1, keepdims=True))
    across = lax.rsqrt(jnp.sum(diagonal, axis=0, keepdims=True))
    scaled = gram * down * across

    error = scaled - unit
    step = error * half
    inverse = unit - step + matmul(step, step, False)
    for update in range(1, UPDATES):
        exact = update >= LOOSE_UPDATES
        error = matmul(matmul(inverse, scaled, exact), inverse, exact, 1) - unit
        step = error * half
        if update < UPDATES - 1:
            step = step - matmul(step, step, exact)
        inverse = inverse - matmul(step, inverse, exact)
    inverse_ref[...] = inverse * across
    far = jnp.sum(error * error)

    @pl.when(jnp.logical_not(far <= CLOSE))
    def _():
        work_ref[...] = gram
        inverse_ref[...] = unit

        def eliminate(k, carry):
            whole = work_ref[...]
            pivot_row = work_ref[pl.ds(k, 1), :]
            pivot = jnp.sum(
                jnp.where(col[:1] == k, pivot_row, 0.0), axis=1, keepdims=True
            )
            column = jnp.sum(jnp.where(col == k, whole, 0.0), axis=1, keepdims=True)
            factor = jnp.where(row[:, :1] > k, column / pivot, 0.0)
            work_ref[...] = whole - factor * pivot_row
            inverse_ref[...] = inverse_ref[...] - factor * inverse_ref[pl.ds(k, 1), :]
            return carry

        lax.fori_loop(0, width, eliminate, 0)
        pivots = jnp.sum(jnp.where(on_diag, work_ref[...], 0.0), axis=1, keepdims=True)
        inverse_ref[...] = inverse_ref[...] * lax.rsqrt(pivots)

    basis = matmul_full(inverse_ref[...], sketch_ref[...]) * root_rows
    pair = jnp.concatenate(split(basis), axis=0)
    fetch.wait()
    for start in range(0, buffer.shape[1], TILE):
        both = lax.dot_general(
            pair,
            buffer[:, start : start + TILE],
            (((1,), (0,)), ((), ())),
            preferred_element_type=jnp.float32,
        )
        out, inner = divmod(start, products[0].shape[1])
        products[out][:, inner : inner + TILE] = both[:width] + both[width:]
    basis_ref[...] = basis.T


def make_basis(gram, sketch, slab, root_rows, chunks):
    width, rows = sketch.shape
    cols = slab.shape[1]
    return pl.pallas_call(
        functools.partial(basis_kernel, root_rows),
        out_shape=[jax.ShapeDtypeStruct((rows, width), jnp.float32)]
        + [jax.ShapeDtypeStruct((width, cols // chunks), jnp.float32)] * chunks,
        in_specs=[pl.BlockSpec(memory_space=pltpu.VMEM)] * 2
        + [pl.BlockSpec(memory_space=pl.ANY)],
        out_specs=[pl.BlockSpec(memory_space=pltpu.VMEM)] * (1 + chunks),
        scratch_shapes=[
            pltpu.VMEM((width, width), jnp.float32),
            pltpu.VMEM((width, width), jnp.float32),
            pltpu.VMEM(slab.shape, jnp.bfloat16),
            pltpu.SemaphoreType.DMA,
        ],
        compiler_params=pltpu.CompilerParams(vmem_limit_bytes=KERNEL_VMEM),
        name="make_basis",
    )(gram, sketch, slab)


def per_device(activations, start_sketch):
    rows_here, cols_here = activations.shape
    width = start_sketch.shape[1]
    parts = lax.axis_size("row")
    total_rows = rows_here * parts
    total_cols = cols_here * lax.axis_size("col")
    root_rows = math.sqrt(total_rows)

    local_cols = []
    for begin in (0, cols_here // 2):
        local_cols += first_product(
            start_sketch, activations, begin, cols_here // 2, CHUNKS // 2
        )
    partial_sketch = 0.0
    orders = orders_of("row")
    step = cols_here // CHUNKS
    for c in range(CHUNKS):
        span = slice(c * step, (c + 1) * step)
        shared = sum_and_share(local_cols[c], "row", orders[c % 2], 1.0 / root_rows)
        partial_sketch = partial_sketch + lax.dot_general(
            activations[:, span],
            shared,
            (((1,), (1,)), ((), ())),
            preferred_element_type=jnp.float32,
        )
    other_sketch = swap(partial_sketch, "col", 1)
    packed, sketch = make_gram(partial_sketch, other_sketch, total_cols)
    basis, *products = make_basis(row_sum(packed), sketch, activations, root_rows, CHUNKS)
    pieces = [
        scatter_sum(product, "row", orders[c % 2]) / total_rows
        for c, product in enumerate(products)
    ]
    return (basis, jnp.concatenate(pieces, axis=1))


def solution(mesh):
    return jax.shard_map(
        per_device,
        mesh=mesh,
        in_specs=(P(("grp", "row"), "col"), P(("grp", "row"), None)),
        out_specs=(P(("grp", "row"), None), P(("grp", "row"), "col")),
        check_vma=False,
    )
```

```python
import functools
import math

import jax
import jax.numpy as jnp
from jax import lax
from jax.experimental import pallas as pl
from jax.experimental.pallas import tpu as pltpu
from jax.sharding import PartitionSpec as P

CHUNKS = 4
LINK_TYPES = (jnp.bfloat16, jnp.float32, jnp.bfloat16)
TILE = 512
KERNEL_VMEM = 50 * 2**20


def swap(value, axis, distance):
    size = lax.axis_size(axis)
    return lax.ppermute(value, axis, [(i, i ^ distance) for i in range(size)])


def row_sum(value):
    rows, cores = lax.axis_size("row"), lax.axis_size("col")
    assert cores == 2
    first = lax.axis_index("col") == 0
    stride = 1
    while stride < rows:
        radix = min(8, rows // stride)
        split = min(2, radix // 2)
        terms = []
        for near in [digit for digit in range(radix) if not digit & split]:
            pairs = []
            for row in range(rows):
                for core, digit in ((0, near), (1, near | split)):
                    if digit:
                        pairs.append((row * cores + core, (row ^ digit * stride) * cores + core))
            terms.append(lax.ppermute(value, ("row", "col"), pairs))
        terms[0] = jnp.where(first, value, terms[0])
        while len(terms) > 1:
            terms = [terms[i] + terms[i + 1] for i in range(0, len(terms), 2)]
        value = terms[0] + swap(terms[0], "col", 1)
        stride *= radix
    return value


def scatter_sum(value, axis, order):
    rows, cols = value.shape[0] >> len(order), value.shape[1]
    total = value.reshape([2] * len(order) + [rows, cols])
    left = sorted(order, reverse=True)
    for step, bit in enumerate(order):
        dim = left.index(bit)
        left.remove(bit)
        low = lax.index_in_dim(total, 0, dim, keepdims=False)
        high = lax.index_in_dim(total, 1, dim, keepdims=False)
        upper = bit_of(axis, bit) == 1
        send = jnp.where(upper, low, high).astype(LINK_TYPES[min(step, 2)])
        landed = swap(send, axis, 1 << bit)
        total = jnp.where(upper, high, low) + landed.astype(jnp.float32)
    return total


def bit_of(axis, bit):
    return lax.rem(lax.div(lax.axis_index(axis), 1 << bit), 2)


def sum_and_share(value, axis, order, scale):
    for step, bit in enumerate(order[:-1]):
        upper = bit_of(axis, bit) == 1
        half = value.shape[1] // 2
        low, high = value[:, :half], value[:, half:]
        send = jnp.where(upper, low, high).astype(LINK_TYPES[min(step, 2)])
        landed = swap(send, axis, 1 << bit)
        value = jnp.where(upper, high, low) + landed.astype(jnp.float32)
    landed = swap(value.astype(jnp.bfloat16), axis, 1 << order[-1])
    block = ((value + landed.astype(jnp.float32)) * scale).astype(jnp.bfloat16)
    for bit in reversed(order[:-1]):
        upper = bit_of(axis, bit) == 1
        other = swap(block, axis, 1 << bit)
        block = jnp.concatenate(
            [jnp.where(upper, other, block), jnp.where(upper, block, other)], axis=1
        )
    return block


def orders_of(axis):
    bits = list(range((lax.axis_size(axis) - 1).bit_length()))
    if len(bits) < 3:
        return [bits, bits]
    return [bits, [bits[1], bits[0]] + bits[2:]]


def fetch_tiles(slab_ref, begin, buffer, arrived):
    copies = []
    for tile in range(buffer.shape[0]):
        span = pl.ds(begin + tile * TILE, TILE)
        copies.append(
            pltpu.make_async_copy(slab_ref.at[:, span], buffer.at[tile], arrived.at[tile])
        )
    for copy in copies:
        copy.start()
    return copies


def sketch_kernel(begin, start_ref, slab_ref, *refs):
    outs, (buffer, arrived) = refs[:-2], refs[-2:]
    copies = fetch_tiles(slab_ref, begin, buffer, arrived)
    left = start_ref[...].T
    for tile, copy in enumerate(copies):
        copy.wait()
        out, inner = divmod(tile * TILE, outs[0].shape[1])
        outs[out][:, inner : inner + TILE] = lax.dot_general(
            left, buffer[tile], (((1,), (0,)), ((), ())), preferred_element_type=jnp.float32
        )


def first_product(start, slab, begin, cols, chunks):
    rows, width = start.shape
    return pl.pallas_call(
        functools.partial(sketch_kernel, begin),
        out_shape=[jax.ShapeDtypeStruct((width, cols // chunks), jnp.float32)] * chunks,
        in_specs=[
            pl.BlockSpec(memory_space=pltpu.VMEM),
            pl.BlockSpec(memory_space=pl.ANY),
        ],
        out_specs=[pl.BlockSpec(memory_space=pltpu.VMEM)] * chunks,
        scratch_shapes=[
            pltpu.VMEM((cols // TILE, rows, TILE), jnp.bfloat16),
            pltpu.SemaphoreType.DMA((cols // TILE,)),
        ],
        compiler_params=pltpu.CompilerParams(vmem_limit_bytes=KERNEL_VMEM),
        cost_estimate=pl.CostEstimate(
            flops=2 * rows * width * cols, bytes_accessed=2 * rows * cols, transcendentals=0
        ),
        name="first_product",
    )(start, slab)


def split(value):
    high = value.astype(jnp.bfloat16)
    return high, (value - high.astype(jnp.float32)).astype(jnp.bfloat16)


def matmul(left, right, exact=True, contract=0):
    if exact:
        (high, low), (other_high, other_low) = split(left), split(right)
        left = jnp.concatenate([high, high, low], axis=1)
        right = jnp.concatenate([other_high, other_low, other_high], axis=contract)
    else:
        left, right = left.astype(jnp.bfloat16), right.astype(jnp.bfloat16)
    return lax.dot_general(
        left, right, (((1,), (contract,)), ((), ())), preferred_element_type=jnp.float32
    )


def matmul_full(left, right):
    return jnp.dot(
        left, right, precision=lax.Precision.HIGHEST, preferred_element_type=jnp.float32
    )


def gram_kernel(total_cols, mine_ref, other_ref, packed_ref, sketch_ref):
    sketch = (mine_ref[...] + other_ref[...]) / total_cols
    sketch_ref[...] = sketch.T
    gram = matmul_full(sketch_ref[...], sketch)
    half = gram.shape[0] // 2
    row = lax.broadcasted_iota(jnp.int32, (half, 2 * half), 0)
    col = lax.broadcasted_iota(jnp.int32, (half, 2 * half), 1)
    top, bottom = gram[:half], pltpu.roll(gram[half:], half, 1)
    packed_ref[:half] = jnp.where(row > col, bottom, top)
    diagonal = jnp.sum(jnp.where(row == col, bottom, 0.0), axis=0, keepdims=True)
    packed_ref[half:] = jnp.broadcast_to(diagonal, (8, 2 * half))


def unpack_gram(packed):
    width = packed.shape[1]
    half = width // 2
    row = lax.broadcasted_iota(jnp.int32, (half, width), 0)
    col = lax.broadcasted_iota(jnp.int32, (half, width), 1)
    square = packed[:half]
    top = jnp.where(row > col, 0.0, square)
    lower = jnp.where(row > col, square, jnp.where(row == col, packed[half : half + 1], 0.0))
    parts = jnp.concatenate([top, pltpu.roll(lower, half, 1)], axis=0)
    row = lax.broadcasted_iota(jnp.int32, (width, width), 0)
    col = lax.broadcasted_iota(jnp.int32, (width, width), 1)
    return jnp.where(row == col, parts, parts + parts.T)


def make_gram(mine, other, total_cols):
    rows, width = mine.shape
    return pl.pallas_call(
        functools.partial(gram_kernel, total_cols),
        out_shape=[
            jax.ShapeDtypeStruct((width // 2 + 8, width), jnp.float32),
            jax.ShapeDtypeStruct((width, rows), jnp.float32),
        ],
        in_specs=[pl.BlockSpec(memory_space=pltpu.VMEM)] * 2,
        out_specs=[pl.BlockSpec(memory_space=pltpu.VMEM)] * 2,
        compiler_params=pltpu.CompilerParams(vmem_limit_bytes=16 * 2**20),
        name="make_gram",
    )(mine, other)


UPDATES = 4
LOOSE_UPDATES = 2
CLOSE = 1e-5


def basis_kernel(
    root_rows, gram_ref, sketch_ref, slab_ref,
    basis_ref, *refs,
):
    products, (work_ref, inverse_ref, buffer, arrived) = refs[:-4], refs[-4:]
    fetch = pltpu.make_async_copy(slab_ref, buffer, arrived)
    fetch.start()
    width = gram_ref.shape[1]
    row = lax.broadcasted_iota(jnp.int32, (width, width), 0)
    col = lax.broadcasted_iota(jnp.int32, (width, width), 1)
    on_diag = row == col
    unit = jnp.where(on_diag, 1.0, 0.0)
    half = jnp.where(row > col, 1.0, jnp.where(on_diag, 0.5, 0.0))

    gram = unpack_gram(gram_ref[...])
    diagonal = jnp.where(on_diag, gram, 0.0)
    down = lax.rsqrt(jnp.sum(diagonal, axis=1, keepdims=True))
    across = lax.rsqrt(jnp.sum(diagonal, axis=0, keepdims=True))
    scaled = gram * down * across

    error = scaled - unit
    step = error * half
    inverse = unit - step + matmul(step, step, False)
    for update in range(1, UPDATES):
        exact = update >= LOOSE_UPDATES
        error = matmul(matmul(inverse, scaled, exact), inverse, exact, 1) - unit
        step = error * half
        if update < UPDATES - 1:
            step = step - matmul(step, step, exact)
        inverse = inverse - matmul(step, inverse, exact)
    inverse_ref[...] = inverse * across
    far = jnp.sum(error * error)

    @pl.when(jnp.logical_not(far <= CLOSE))
    def _():
        work_ref[...] = gram
        inverse_ref[...] = unit

        def eliminate(k, carry):
            whole = work_ref[...]
            pivot_row = work_ref[pl.ds(k, 1), :]
            pivot = jnp.sum(
                jnp.where(col[:1] == k, pivot_row, 0.0), axis=1, keepdims=True
            )
            column = jnp.sum(jnp.where(col == k, whole, 0.0), axis=1, keepdims=True)
            factor = jnp.where(row[:, :1] > k, column / pivot, 0.0)
            work_ref[...] = whole - factor * pivot_row
            inverse_ref[...] = inverse_ref[...] - factor * inverse_ref[pl.ds(k, 1), :]
            return carry

        lax.fori_loop(0, width, eliminate, 0)
        pivots = jnp.sum(jnp.where(on_diag, work_ref[...], 0.0), axis=1, keepdims=True)
        inverse_ref[...] = inverse_ref[...] * lax.rsqrt(pivots)

    basis = matmul_full(inverse_ref[...], sketch_ref[...]) * root_rows
    pair = jnp.concatenate(split(basis), axis=0)
    fetch.wait()
    for start in range(0, buffer.shape[1], TILE):
        both = lax.dot_general(
            pair,
            buffer[:, start : start + TILE],
            (((1,), (0,)), ((), ())),
            preferred_element_type=jnp.float32,
        )
        out, inner = divmod(start, products[0].shape[1])
        products[out][:, inner : inner + TILE] = both[:width] + both[width:]
    basis_ref[...] = basis.T


def make_basis(gram, sketch, slab, root_rows, chunks):
    width, rows = sketch.shape
    cols = slab.shape[1]
    return pl.pallas_call(
        functools.partial(basis_kernel, root_rows),
        out_shape=[jax.ShapeDtypeStruct((rows, width), jnp.float32)]
        + [jax.ShapeDtypeStruct((width, cols // chunks), jnp.float32)] * chunks,
        in_specs=[pl.BlockSpec(memory_space=pltpu.VMEM)] * 2
        + [pl.BlockSpec(memory_space=pl.ANY)],
        out_specs=[pl.BlockSpec(memory_space=pltpu.VMEM)] * (1 + chunks),
        scratch_shapes=[
            pltpu.VMEM((width, width), jnp.float32),
            pltpu.VMEM((width, width), jnp.float32),
            pltpu.VMEM(slab.shape, jnp.bfloat16),
            pltpu.SemaphoreType.DMA,
        ],
        compiler_params=pltpu.CompilerParams(vmem_limit_bytes=KERNEL_VMEM),
        name="make_basis",
    )(gram, sketch, slab)


def per_device(activations, start_sketch):
    rows_here, cols_here = activations.shape
    width = start_sketch.shape[1]
    parts = lax.axis_size("row")
    total_rows = rows_here * parts
    total_cols = cols_here * lax.axis_size("col")
    root_rows = math.sqrt(total_rows)

    local_cols = []
    for begin in (0, cols_here // 2):
        local_cols += first_product(
            start_sketch, activations, begin, cols_here // 2, CHUNKS // 2
        )
    partial_sketch = 0.0
    orders = orders_of("row")
    step = cols_here // CHUNKS
    for c in range(CHUNKS):
        span = slice(c * step, (c + 1) * step)
        shared = sum_and_share(local_cols[c], "row", orders[c % 2], 1.0 / root_rows)
        partial_sketch = partial_sketch + lax.dot_general(
            activations[:, span],
            shared,
            (((1,), (1,)), ((), ())),
            preferred_element_type=jnp.float32,
        )
    other_sketch = swap(partial_sketch, "col", 1)
    packed, sketch = make_gram(partial_sketch, other_sketch, total_cols)
    basis, *products = make_basis(row_sum(packed), sketch, activations, root_rows, CHUNKS)
    pieces = [
        scatter_sum(product, "row", orders[c % 2]) / total_rows
        for c, product in enumerate(products)
    ]
    return (basis, jnp.concatenate(pieces, axis=1))


def solution(mesh):
    return jax.shard_map(
        per_device,
        mesh=mesh,
        in_specs=(P(("grp", "row"), "col"), P(("grp", "row"), None)),
        out_specs=(P(("grp", "row"), None), P(("grp", "row"), "col")),
        check_vma=False,
    )
```

```python
import functools
import math

import jax
import jax.numpy as jnp
from jax import lax
from jax.experimental import pallas as pl
from jax.experimental.pallas import tpu as pltpu
from jax.sharding import PartitionSpec as P

CHUNKS = 4
LINK_TYPES = (jnp.bfloat16, jnp.float32, jnp.bfloat16)
TILE = 512
KERNEL_VMEM = 50 * 2**20


def swap(value, axis, distance):
    size = lax.axis_size(axis)
    return lax.ppermute(value, axis, [(i, i ^ distance) for i in range(size)])


def row_sum(value):
    rows, cores = lax.axis_size("row"), lax.axis_size("col")
    assert cores == 2
    first = lax.axis_index("col") == 0
    stride = 1
    while stride < rows:
        radix = min(8, rows // stride)
        split = min(2, radix // 2)
        terms = []
        for near in [digit for digit in range(radix) if not digit & split]:
            pairs = []
            for row in range(rows):
                for core, digit in ((0, near), (1, near | split)):
                    if digit:
                        pairs.append((row * cores + core, (row ^ digit * stride) * cores + core))
            terms.append(lax.ppermute(value, ("row", "col"), pairs))
        terms[0] = jnp.where(first, value, terms[0])
        while len(terms) > 1:
            terms = [terms[i] + terms[i + 1] for i in range(0, len(terms), 2)]
        value = terms[0] + swap(terms[0], "col", 1)
        stride *= radix
    return value


def scatter_sum(value, axis, order):
    rows, cols = value.shape[0] >> len(order), value.shape[1]
    total = value.reshape([2] * len(order) + [rows, cols])
    left = sorted(order, reverse=True)
    for bit in order:
        dim = left.index(bit)
        left.remove(bit)
        low = lax.index_in_dim(total, 0, dim, keepdims=False)
        high = lax.index_in_dim(total, 1, dim, keepdims=False)
        upper = bit_of(axis, bit) == 1
        send = jnp.where(upper, low, high).astype(jnp.bfloat16)
        landed = swap(send, axis, 1 << bit)
        total = jnp.where(upper, high, low) + landed.astype(jnp.float32)
    return total


def bit_of(axis, bit):
    return lax.rem(lax.div(lax.axis_index(axis), 1 << bit), 2)


def sum_and_share(value, axis, order, scale):
    for step, bit in enumerate(order[:-1]):
        upper = bit_of(axis, bit) == 1
        half = value.shape[1] // 2
        low, high = value[:, :half], value[:, half:]
        send = jnp.where(upper, low, high).astype(LINK_TYPES[min(step, 2)])
        landed = swap(send, axis, 1 << bit)
        value = jnp.where(upper, high, low) + landed.astype(jnp.float32)
    landed = swap(value.astype(jnp.bfloat16), axis, 1 << order[-1])
    block = ((value + landed.astype(jnp.float32)) * scale).astype(jnp.bfloat16)
    for bit in reversed(order[:-1]):
        upper = bit_of(axis, bit) == 1
        other = swap(block, axis, 1 << bit)
        block = jnp.concatenate(
            [jnp.where(upper, other, block), jnp.where(upper, block, other)], axis=1
        )
    return block


def orders_of(axis):
    bits = list(range((lax.axis_size(axis) - 1).bit_length()))
    if len(bits) < 3:
        return [bits, bits]
    return [bits, [bits[1], bits[0]] + bits[2:]]


def fetch_tiles(slab_ref, begin, buffer, arrived):
    copies = []
    for tile in range(buffer.shape[0]):
        span = pl.ds(begin + tile * TILE, TILE)
        copies.append(
            pltpu.make_async_copy(slab_ref.at[:, span], buffer.at[tile], arrived.at[tile])
        )
    for copy in copies:
        copy.start()
    return copies


def sketch_kernel(begin, start_ref, slab_ref, *refs):
    outs, (buffer, arrived) = refs[:-2], refs[-2:]
    copies = fetch_tiles(slab_ref, begin, buffer, arrived)
    left = start_ref[...].T
    for tile, copy in enumerate(copies):
        copy.wait()
        out, inner = divmod(tile * TILE, outs[0].shape[1])
        outs[out][:, inner : inner + TILE] = lax.dot_general(
            left, buffer[tile], (((1,), (0,)), ((), ())), preferred_element_type=jnp.float32
        )


def first_product(start, slab, begin, cols, chunks):
    rows, width = start.shape
    return pl.pallas_call(
        functools.partial(sketch_kernel, begin),
        out_shape=[jax.ShapeDtypeStruct((width, cols // chunks), jnp.float32)] * chunks,
        in_specs=[
            pl.BlockSpec(memory_space=pltpu.VMEM),
            pl.BlockSpec(memory_space=pl.ANY),
        ],
        out_specs=[pl.BlockSpec(memory_space=pltpu.VMEM)] * chunks,
        scratch_shapes=[
            pltpu.VMEM((cols // TILE, rows, TILE), jnp.bfloat16),
            pltpu.SemaphoreType.DMA((cols // TILE,)),
        ],
        compiler_params=pltpu.CompilerParams(vmem_limit_bytes=KERNEL_VMEM),
        cost_estimate=pl.CostEstimate(
            flops=2 * rows * width * cols, bytes_accessed=2 * rows * cols, transcendentals=0
        ),
        name="first_product",
    )(start, slab)


def split(value):
    high = value.astype(jnp.bfloat16)
    return high, (value - high.astype(jnp.float32)).astype(jnp.bfloat16)


def matmul(left, right, exact=True, contract=0):
    if exact:
        (high, low), (other_high, other_low) = split(left), split(right)
        left = jnp.concatenate([high, high, low], axis=1)
        right = jnp.concatenate([other_high, other_low, other_high], axis=contract)
    else:
        left, right = left.astype(jnp.bfloat16), right.astype(jnp.bfloat16)
    return lax.dot_general(
        left, right, (((1,), (contract,)), ((), ())), preferred_element_type=jnp.float32
    )


def matmul_full(left, right):
    return jnp.dot(
        left, right, precision=lax.Precision.HIGHEST, preferred_element_type=jnp.float32
    )


def gram_kernel(total_cols, mine_ref, other_ref, packed_ref, sketch_ref):
    sketch = (mine_ref[...] + other_ref[...]) / total_cols
    sketch_ref[...] = sketch.T
    gram = matmul_full(sketch_ref[...], sketch)
    half = gram.shape[0] // 2
    row = lax.broadcasted_iota(jnp.int32, (half, 2 * half), 0)
    col = lax.broadcasted_iota(jnp.int32, (half, 2 * half), 1)
    top, bottom = gram[:half], pltpu.roll(gram[half:], half, 1)
    packed_ref[:half] = jnp.where(row > col, bottom, top)
    diagonal = jnp.sum(jnp.where(row == col, bottom, 0.0), axis=0, keepdims=True)
    packed_ref[half:] = jnp.broadcast_to(diagonal, (8, 2 * half))


def unpack_gram(packed):
    width = packed.shape[1]
    half = width // 2
    row = lax.broadcasted_iota(jnp.int32, (half, width), 0)
    col = lax.broadcasted_iota(jnp.int32, (half, width), 1)
    square = packed[:half]
    top = jnp.where(row > col, 0.0, square)
    lower = jnp.where(row > col, square, jnp.where(row == col, packed[half : half + 1], 0.0))
    parts = jnp.concatenate([top, pltpu.roll(lower, half, 1)], axis=0)
    row = lax.broadcasted_iota(jnp.int32, (width, width), 0)
    col = lax.broadcasted_iota(jnp.int32, (width, width), 1)
    return jnp.where(row == col, parts, parts + parts.T)


def make_gram(mine, other, total_cols):
    rows, width = mine.shape
    return pl.pallas_call(
        functools.partial(gram_kernel, total_cols),
        out_shape=[
            jax.ShapeDtypeStruct((width // 2 + 8, width), jnp.float32),
            jax.ShapeDtypeStruct((width, rows), jnp.float32),
        ],
        in_specs=[pl.BlockSpec(memory_space=pltpu.VMEM)] * 2,
        out_specs=[pl.BlockSpec(memory_space=pltpu.VMEM)] * 2,
        compiler_params=pltpu.CompilerParams(vmem_limit_bytes=16 * 2**20),
        name="make_gram",
    )(mine, other)


UPDATES = 4
LOOSE_UPDATES = 2
CLOSE = 1e-5


def basis_kernel(
    root_rows, gram_ref, sketch_ref, slab_ref,
    basis_ref, *refs,
):
    products, (work_ref, inverse_ref, buffer, arrived) = refs[:-4], refs[-4:]
    fetch = pltpu.make_async_copy(slab_ref, buffer, arrived)
    fetch.start()
    width = gram_ref.shape[1]
    row = lax.broadcasted_iota(jnp.int32, (width, width), 0)
    col = lax.broadcasted_iota(jnp.int32, (width, width), 1)
    on_diag = row == col
    unit = jnp.where(on_diag, 1.0, 0.0)
    half = jnp.where(row > col, 1.0, jnp.where(on_diag, 0.5, 0.0))

    gram = unpack_gram(gram_ref[...])
    diagonal = jnp.where(on_diag, gram, 0.0)
    down = lax.rsqrt(jnp.sum(diagonal, axis=1, keepdims=True))
    across = lax.rsqrt(jnp.sum(diagonal, axis=0, keepdims=True))
    scaled = gram * down * across

    error = scaled - unit
    step = error * half
    inverse = unit - step + matmul(step, step, False)
    for update in range(1, UPDATES):
        exact = update >= LOOSE_UPDATES
        error = matmul(matmul(inverse, scaled, exact), inverse, exact, 1) - unit
        step = error * half
        if update < UPDATES - 1:
            step = step - matmul(step, step, exact)
        inverse = inverse - matmul(step, inverse, exact)
    inverse_ref[...] = inverse * across
    far = jnp.sum(error * error)

    @pl.when(jnp.logical_not(far <= CLOSE))
    def _():
        work_ref[...] = gram
        inverse_ref[...] = unit

        def eliminate(k, carry):
            whole = work_ref[...]
            pivot_row = work_ref[pl.ds(k, 1), :]
            pivot = jnp.sum(
                jnp.where(col[:1] == k, pivot_row, 0.0), axis=1, keepdims=True
            )
            column = jnp.sum(jnp.where(col == k, whole, 0.0), axis=1, keepdims=True)
            factor = jnp.where(row[:, :1] > k, column / pivot, 0.0)
            work_ref[...] = whole - factor * pivot_row
            inverse_ref[...] = inverse_ref[...] - factor * inverse_ref[pl.ds(k, 1), :]
            return carry

        lax.fori_loop(0, width, eliminate, 0)
        pivots = jnp.sum(jnp.where(on_diag, work_ref[...], 0.0), axis=1, keepdims=True)
        inverse_ref[...] = inverse_ref[...] * lax.rsqrt(pivots)

    basis = matmul_full(inverse_ref[...], sketch_ref[...]) * root_rows
    pair = jnp.concatenate(split(basis), axis=0)
    fetch.wait()
    for start in range(0, buffer.shape[1], TILE):
        both = lax.dot_general(
            pair,
            buffer[:, start : start + TILE],
            (((1,), (0,)), ((), ())),
            preferred_element_type=jnp.float32,
        )
        out, inner = divmod(start, products[0].shape[1])
        products[out][:, inner : inner + TILE] = both[:width] + both[width:]
    basis_ref[...] = basis.T


def make_basis(gram, sketch, slab, root_rows, chunks):
    width, rows = sketch.shape
    cols = slab.shape[1]
    return pl.pallas_call(
        functools.partial(basis_kernel, root_rows),
        out_shape=[jax.ShapeDtypeStruct((rows, width), jnp.float32)]
        + [jax.ShapeDtypeStruct((width, cols // chunks), jnp.float32)] * chunks,
        in_specs=[pl.BlockSpec(memory_space=pltpu.VMEM)] * 2
        + [pl.BlockSpec(memory_space=pl.ANY)],
        out_specs=[pl.BlockSpec(memory_space=pltpu.VMEM)] * (1 + chunks),
        scratch_shapes=[
            pltpu.VMEM((width, width), jnp.float32),
            pltpu.VMEM((width, width), jnp.float32),
            pltpu.VMEM(slab.shape, jnp.bfloat16),
            pltpu.SemaphoreType.DMA,
        ],
        compiler_params=pltpu.CompilerParams(vmem_limit_bytes=KERNEL_VMEM),
        name="make_basis",
    )(gram, sketch, slab)


def per_device(activations, start_sketch):
    rows_here, cols_here = activations.shape
    width = start_sketch.shape[1]
    parts = lax.axis_size("row")
    total_rows = rows_here * parts
    total_cols = cols_here * lax.axis_size("col")
    root_rows = math.sqrt(total_rows)

    local_cols = []
    for begin in (0, cols_here // 2):
        local_cols += first_product(
            start_sketch, activations, begin, cols_here // 2, CHUNKS // 2
        )
    partial_sketch = 0.0
    orders = orders_of("row")
    step = cols_here // CHUNKS
    for c in range(CHUNKS):
        span = slice(c * step, (c + 1) * step)
        shared = sum_and_share(local_cols[c], "row", orders[c % 2], 1.0 / root_rows)
        partial_sketch = partial_sketch + lax.dot_general(
            activations[:, span],
            shared,
            (((1,), (1,)), ((), ())),
            preferred_element_type=jnp.float32,
        )
    other_sketch = swap(partial_sketch, "col", 1)
    packed, sketch = make_gram(partial_sketch, other_sketch, total_cols)
    basis, *products = make_basis(row_sum(packed), sketch, activations, root_rows, CHUNKS)
    pieces = [
        scatter_sum(product, "row", orders[c % 2]) / total_rows
        for c, product in enumerate(products)
    ]
    return (basis, jnp.concatenate(pieces, axis=1))


def solution(mesh):
    return jax.shard_map(
        per_device,
        mesh=mesh,
        in_specs=(P(("grp", "row"), "col"), P(("grp", "row"), None)),
        out_specs=(P(("grp", "row"), None), P(("grp", "row"), "col")),
        check_vma=False,
    )
```

```python
import functools
import math

import jax
import jax.numpy as jnp
from jax import lax
from jax.experimental import pallas as pl
from jax.experimental.pallas import tpu as pltpu
from jax.sharding import PartitionSpec as P

CHUNKS = 4
TILE = 512
KERNEL_VMEM = 50 * 2**20


def swap(value, axis, distance):
    size = lax.axis_size(axis)
    return lax.ppermute(value, axis, [(i, i ^ distance) for i in range(size)])


def row_sum(value):
    rows, cores = lax.axis_size("row"), lax.axis_size("col")
    assert cores == 2
    first = lax.axis_index("col") == 0
    stride = 1
    while stride < rows:
        radix = min(8, rows // stride)
        split = min(2, radix // 2)
        terms = []
        for near in [digit for digit in range(radix) if not digit & split]:
            pairs = []
            for row in range(rows):
                for core, digit in ((0, near), (1, near | split)):
                    if digit:
                        pairs.append((row * cores + core, (row ^ digit * stride) * cores + core))
            terms.append(lax.ppermute(value, ("row", "col"), pairs))
        terms[0] = jnp.where(first, value, terms[0])
        while len(terms) > 1:
            terms = [terms[i] + terms[i + 1] for i in range(0, len(terms), 2)]
        value = terms[0] + swap(terms[0], "col", 1)
        stride *= radix
    return value


def scatter_sum(value, axis, order):
    rows, cols = value.shape[0] >> len(order), value.shape[1]
    total = value.reshape([2] * len(order) + [rows, cols])
    left = sorted(order, reverse=True)
    for bit in order:
        dim = left.index(bit)
        left.remove(bit)
        low = lax.index_in_dim(total, 0, dim, keepdims=False)
        high = lax.index_in_dim(total, 1, dim, keepdims=False)
        upper = bit_of(axis, bit) == 1
        send = jnp.where(upper, low, high).astype(jnp.bfloat16)
        landed = swap(send, axis, 1 << bit)
        total = jnp.where(upper, high, low) + landed.astype(jnp.float32)
    return total


def bit_of(axis, bit):
    return lax.rem(lax.div(lax.axis_index(axis), 1 << bit), 2)


def sum_and_share(value, axis, order, scale):
    for bit in order[:-1]:
        upper = bit_of(axis, bit) == 1
        half = value.shape[1] // 2
        low, high = value[:, :half], value[:, half:]
        send = jnp.where(upper, low, high).astype(jnp.bfloat16)
        landed = swap(send, axis, 1 << bit)
        value = jnp.where(upper, high, low) + landed.astype(jnp.float32)
    landed = swap(value.astype(jnp.bfloat16), axis, 1 << order[-1])
    block = ((value + landed.astype(jnp.float32)) * scale).astype(jnp.bfloat16)
    for bit in reversed(order[:-1]):
        upper = bit_of(axis, bit) == 1
        other = swap(block, axis, 1 << bit)
        block = jnp.concatenate(
            [jnp.where(upper, other, block), jnp.where(upper, block, other)], axis=1
        )
    return block


def orders_of(axis):
    bits = list(range((lax.axis_size(axis) - 1).bit_length()))
    if len(bits) < 3:
        return [bits] * 4
    heads = [(0, 1, 2), (1, 0, 2), (0, 2, 1), (1, 2, 0)]
    return [list(head) + bits[3:] for head in heads]


def fetch_tiles(slab_ref, begin, buffer, arrived):
    copies = []
    for tile in range(buffer.shape[0]):
        span = pl.ds(begin + tile * TILE, TILE)
        copies.append(
            pltpu.make_async_copy(slab_ref.at[:, span], buffer.at[tile], arrived.at[tile])
        )
    for copy in copies:
        copy.start()
    return copies


def sketch_kernel(begin, start_ref, slab_ref, *refs):
    outs, (buffer, arrived) = refs[:-2], refs[-2:]
    copies = fetch_tiles(slab_ref, begin, buffer, arrived)
    left = start_ref[...].T
    for tile, copy in enumerate(copies):
        copy.wait()
        out, inner = divmod(tile * TILE, outs[0].shape[1])
        outs[out][:, inner : inner + TILE] = lax.dot_general(
            left, buffer[tile], (((1,), (0,)), ((), ())), preferred_element_type=jnp.float32
        )


def first_product(start, slab, begin, cols, chunks):
    rows, width = start.shape
    return pl.pallas_call(
        functools.partial(sketch_kernel, begin),
        out_shape=[jax.ShapeDtypeStruct((width, cols // chunks), jnp.float32)] * chunks,
        in_specs=[
            pl.BlockSpec(memory_space=pltpu.VMEM),
            pl.BlockSpec(memory_space=pl.ANY),
        ],
        out_specs=[pl.BlockSpec(memory_space=pltpu.VMEM)] * chunks,
        scratch_shapes=[
            pltpu.VMEM((cols // TILE, rows, TILE), jnp.bfloat16),
            pltpu.SemaphoreType.DMA((cols // TILE,)),
        ],
        compiler_params=pltpu.CompilerParams(vmem_limit_bytes=KERNEL_VMEM),
        cost_estimate=pl.CostEstimate(
            flops=2 * rows * width * cols, bytes_accessed=2 * rows * cols, transcendentals=0
        ),
        name="first_product",
    )(start, slab)


def split(value):
    high = value.astype(jnp.bfloat16)
    return high, (value - high.astype(jnp.float32)).astype(jnp.bfloat16)


def matmul(left, right, exact=True, contract=0):
    if exact:
        (high, low), (other_high, other_low) = split(left), split(right)
        left = jnp.concatenate([high, high, low], axis=1)
        right = jnp.concatenate([other_high, other_low, other_high], axis=contract)
    else:
        left, right = left.astype(jnp.bfloat16), right.astype(jnp.bfloat16)
    return lax.dot_general(
        left, right, (((1,), (contract,)), ((), ())), preferred_element_type=jnp.float32
    )


def matmul_full(left, right):
    return jnp.dot(
        left, right, precision=lax.Precision.HIGHEST, preferred_element_type=jnp.float32
    )


def gram_kernel(total_cols, mine_ref, other_ref, packed_ref, sketch_ref):
    sketch = (mine_ref[...] + other_ref[...]) / total_cols
    sketch_ref[...] = sketch.T
    gram = matmul_full(sketch_ref[...], sketch)
    half = gram.shape[0] // 2
    row = lax.broadcasted_iota(jnp.int32, (half, 2 * half), 0)
    col = lax.broadcasted_iota(jnp.int32, (half, 2 * half), 1)
    top, bottom = gram[:half], pltpu.roll(gram[half:], half, 1)
    packed_ref[:half] = jnp.where(row > col, bottom, top)
    diagonal = jnp.sum(jnp.where(row == col, bottom, 0.0), axis=0, keepdims=True)
    packed_ref[half:] = jnp.broadcast_to(diagonal, (8, 2 * half))


def unpack_gram(packed):
    width = packed.shape[1]
    half = width // 2
    row = lax.broadcasted_iota(jnp.int32, (half, width), 0)
    col = lax.broadcasted_iota(jnp.int32, (half, width), 1)
    square = packed[:half]
    top = jnp.where(row > col, 0.0, square)
    lower = jnp.where(row > col, square, jnp.where(row == col, packed[half : half + 1], 0.0))
    parts = jnp.concatenate([top, pltpu.roll(lower, half, 1)], axis=0)
    row = lax.broadcasted_iota(jnp.int32, (width, width), 0)
    col = lax.broadcasted_iota(jnp.int32, (width, width), 1)
    return jnp.where(row == col, parts, parts + parts.T)


def make_gram(mine, other, total_cols):
    rows, width = mine.shape
    return pl.pallas_call(
        functools.partial(gram_kernel, total_cols),
        out_shape=[
            jax.ShapeDtypeStruct((width // 2 + 8, width), jnp.float32),
            jax.ShapeDtypeStruct((width, rows), jnp.float32),
        ],
        in_specs=[pl.BlockSpec(memory_space=pltpu.VMEM)] * 2,
        out_specs=[pl.BlockSpec(memory_space=pltpu.VMEM)] * 2,
        compiler_params=pltpu.CompilerParams(vmem_limit_bytes=16 * 2**20),
        name="make_gram",
    )(mine, other)


UPDATES = 4
LOOSE_UPDATES = 2
CLOSE = 1e-5


def basis_kernel(
    root_rows, gram_ref, sketch_ref, slab_ref,
    basis_ref, *refs,
):
    products, (work_ref, inverse_ref, buffer, arrived) = refs[:-4], refs[-4:]
    fetch = pltpu.make_async_copy(slab_ref, buffer, arrived)
    fetch.start()
    width = gram_ref.shape[1]
    row = lax.broadcasted_iota(jnp.int32, (width, width), 0)
    col = lax.broadcasted_iota(jnp.int32, (width, width), 1)
    on_diag = row == col
    unit = jnp.where(on_diag, 1.0, 0.0)
    half = jnp.where(row > col, 1.0, jnp.where(on_diag, 0.5, 0.0))

    gram = unpack_gram(gram_ref[...])
    diagonal = jnp.where(on_diag, gram, 0.0)
    down = lax.rsqrt(jnp.sum(diagonal, axis=1, keepdims=True))
    across = lax.rsqrt(jnp.sum(diagonal, axis=0, keepdims=True))
    scaled = gram * down * across

    error = scaled - unit
    step = error * half
    inverse = unit - step + matmul(step, step, False)
    for update in range(1, UPDATES):
        exact = update >= LOOSE_UPDATES
        error = matmul(matmul(inverse, scaled, exact), inverse, exact, 1) - unit
        step = error * half
        if update < UPDATES - 1:
            step = step - matmul(step, step, exact)
        inverse = inverse - matmul(step, inverse, exact)
    inverse_ref[...] = inverse * across
    far = jnp.sum(error * error)

    @pl.when(jnp.logical_not(far <= CLOSE))
    def _():
        work_ref[...] = gram
        inverse_ref[...] = unit

        def eliminate(k, carry):
            whole = work_ref[...]
            pivot_row = work_ref[pl.ds(k, 1), :]
            pivot = jnp.sum(
                jnp.where(col[:1] == k, pivot_row, 0.0), axis=1, keepdims=True
            )
            column = jnp.sum(jnp.where(col == k, whole, 0.0), axis=1, keepdims=True)
            factor = jnp.where(row[:, :1] > k, column / pivot, 0.0)
            work_ref[...] = whole - factor * pivot_row
            inverse_ref[...] = inverse_ref[...] - factor * inverse_ref[pl.ds(k, 1), :]
            return carry

        lax.fori_loop(0, width, eliminate, 0)
        pivots = jnp.sum(jnp.where(on_diag, work_ref[...], 0.0), axis=1, keepdims=True)
        inverse_ref[...] = inverse_ref[...] * lax.rsqrt(pivots)

    basis = matmul_full(inverse_ref[...], sketch_ref[...]) * root_rows
    pair = jnp.concatenate(split(basis), axis=0)
    fetch.wait()
    for start in range(0, buffer.shape[1], TILE):
        both = lax.dot_general(
            pair,
            buffer[:, start : start + TILE],
            (((1,), (0,)), ((), ())),
            preferred_element_type=jnp.float32,
        )
        out, inner = divmod(start, products[0].shape[1])
        products[out][:, inner : inner + TILE] = both[:width] + both[width:]
    basis_ref[...] = basis.T


def make_basis(gram, sketch, slab, root_rows, chunks):
    width, rows = sketch.shape
    cols = slab.shape[1]
    return pl.pallas_call(
        functools.partial(basis_kernel, root_rows),
        out_shape=[jax.ShapeDtypeStruct((rows, width), jnp.float32)]
        + [jax.ShapeDtypeStruct((width, cols // chunks), jnp.float32)] * chunks,
        in_specs=[pl.BlockSpec(memory_space=pltpu.VMEM)] * 2
        + [pl.BlockSpec(memory_space=pl.ANY)],
        out_specs=[pl.BlockSpec(memory_space=pltpu.VMEM)] * (1 + chunks),
        scratch_shapes=[
            pltpu.VMEM((width, width), jnp.float32),
            pltpu.VMEM((width, width), jnp.float32),
            pltpu.VMEM(slab.shape, jnp.bfloat16),
            pltpu.SemaphoreType.DMA,
        ],
        compiler_params=pltpu.CompilerParams(vmem_limit_bytes=KERNEL_VMEM),
        name="make_basis",
    )(gram, sketch, slab)


def per_device(activations, start_sketch):
    rows_here, cols_here = activations.shape
    width = start_sketch.shape[1]
    parts = lax.axis_size("row")
    total_rows = rows_here * parts
    total_cols = cols_here * lax.axis_size("col")
    root_rows = math.sqrt(total_rows)

    local_cols = []
    for begin in (0, cols_here // 2):
        local_cols += first_product(
            start_sketch, activations, begin, cols_here // 2, CHUNKS // 2
        )
    partial_sketch = 0.0
    orders = orders_of("row")
    step = cols_here // CHUNKS
    for c in range(CHUNKS):
        span = slice(c * step, (c + 1) * step)
        shared = sum_and_share(local_cols[c], "row", orders[c % 2], 1.0 / root_rows)
        partial_sketch = partial_sketch + lax.dot_general(
            activations[:, span],
            shared,
            (((1,), (1,)), ((), ())),
            preferred_element_type=jnp.float32,
        )
    other_sketch = swap(partial_sketch, "col", 1)
    packed, sketch = make_gram(partial_sketch, other_sketch, total_cols)
    basis, *products = make_basis(row_sum(packed), sketch, activations, root_rows, CHUNKS)
    pieces = [
        scatter_sum(product, "row", orders[c % 4]) / total_rows
        for c, product in enumerate(products)
    ]
    return (basis, jnp.concatenate(pieces, axis=1))


def solution(mesh):
    return jax.shard_map(
        per_device,
        mesh=mesh,
        in_specs=(P(("grp", "row"), "col"), P(("grp", "row"), None)),
        out_specs=(P(("grp", "row"), None), P(("grp", "row"), "col")),
        check_vma=False,
    )
```

```python
import functools
import math

import jax
import jax.numpy as jnp
from jax import lax
from jax.experimental import pallas as pl
from jax.experimental.pallas import tpu as pltpu
from jax.sharding import PartitionSpec as P

CHUNKS = 4
TILE = 256
KERNEL_VMEM = 50 * 2**20


def swap(value, axis, distance):
    size = lax.axis_size(axis)
    return lax.ppermute(value, axis, [(i, i ^ distance) for i in range(size)])


def row_sum(value):
    rows, cores = lax.axis_size("row"), lax.axis_size("col")
    assert cores == 2
    first = lax.axis_index("col") == 0
    stride = 1
    while stride < rows:
        radix = min(8, rows // stride)
        split = min(2, radix // 2)
        terms = []
        for near in [digit for digit in range(radix) if not digit & split]:
            pairs = []
            for row in range(rows):
                for core, digit in ((0, near), (1, near | split)):
                    if digit:
                        pairs.append((row * cores + core, (row ^ digit * stride) * cores + core))
            terms.append(lax.ppermute(value, ("row", "col"), pairs))
        terms[0] = jnp.where(first, value, terms[0])
        while len(terms) > 1:
            terms = [terms[i] + terms[i + 1] for i in range(0, len(terms), 2)]
        value = terms[0] + swap(terms[0], "col", 1)
        stride *= radix
    return value


def scatter_sum(value, axis, order):
    rows, cols = value.shape[0] >> len(order), value.shape[1]
    total = value.reshape([2] * len(order) + [rows, cols])
    left = sorted(order, reverse=True)
    for bit in order:
        dim = left.index(bit)
        left.remove(bit)
        low = lax.index_in_dim(total, 0, dim, keepdims=False)
        high = lax.index_in_dim(total, 1, dim, keepdims=False)
        upper = bit_of(axis, bit) == 1
        send = jnp.where(upper, low, high).astype(jnp.bfloat16)
        landed = swap(send, axis, 1 << bit)
        total = jnp.where(upper, high, low) + landed.astype(jnp.float32)
    return total


def bit_of(axis, bit):
    return lax.rem(lax.div(lax.axis_index(axis), 1 << bit), 2)


def sum_and_share(value, axis, order, scale):
    for bit in order[:-1]:
        upper = bit_of(axis, bit) == 1
        half = value.shape[1] // 2
        low, high = value[:, :half], value[:, half:]
        send = jnp.where(upper, low, high).astype(jnp.bfloat16)
        landed = swap(send, axis, 1 << bit)
        value = jnp.where(upper, high, low) + landed.astype(jnp.float32)
    landed = swap(value.astype(jnp.bfloat16), axis, 1 << order[-1])
    block = ((value + landed.astype(jnp.float32)) * scale).astype(jnp.bfloat16)
    for bit in reversed(order[:-1]):
        upper = bit_of(axis, bit) == 1
        other = swap(block, axis, 1 << bit)
        block = jnp.concatenate(
            [jnp.where(upper, other, block), jnp.where(upper, block, other)], axis=1
        )
    return block


def orders_of(axis):
    bits = list(range((lax.axis_size(axis) - 1).bit_length()))
    if len(bits) < 3:
        return [bits, bits]
    return [bits, [bits[1], bits[0]] + bits[2:]]


def fetch_tiles(slab_ref, begin, buffer, arrived):
    copies = []
    for tile in range(buffer.shape[0]):
        span = pl.ds(begin + tile * TILE, TILE)
        copies.append(
            pltpu.make_async_copy(slab_ref.at[:, span], buffer.at[tile], arrived.at[tile])
        )
    for copy in copies:
        copy.start()
    return copies


def sketch_kernel(begin, start_ref, slab_ref, *refs):
    outs, (buffer, arrived) = refs[:-2], refs[-2:]
    copies = fetch_tiles(slab_ref, begin, buffer, arrived)
    left = start_ref[...].T
    for tile, copy in enumerate(copies):
        copy.wait()
        out, inner = divmod(tile * TILE, outs[0].shape[1])
        outs[out][:, inner : inner + TILE] = lax.dot_general(
            left, buffer[tile], (((1,), (0,)), ((), ())), preferred_element_type=jnp.float32
        )


def first_product(start, slab, begin, cols, chunks):
    rows, width = start.shape
    return pl.pallas_call(
        functools.partial(sketch_kernel, begin),
        out_shape=[jax.ShapeDtypeStruct((width, cols // chunks), jnp.float32)] * chunks,
        in_specs=[
            pl.BlockSpec(memory_space=pltpu.VMEM),
            pl.BlockSpec(memory_space=pl.ANY),
        ],
        out_specs=[pl.BlockSpec(memory_space=pltpu.VMEM)] * chunks,
        scratch_shapes=[
            pltpu.VMEM((cols // TILE, rows, TILE), jnp.bfloat16),
            pltpu.SemaphoreType.DMA((cols // TILE,)),
        ],
        compiler_params=pltpu.CompilerParams(vmem_limit_bytes=KERNEL_VMEM),
        cost_estimate=pl.CostEstimate(
            flops=2 * rows * width * cols, bytes_accessed=2 * rows * cols, transcendentals=0
        ),
        name="first_product",
    )(start, slab)


def split(value):
    high = value.astype(jnp.bfloat16)
    return high, (value - high.astype(jnp.float32)).astype(jnp.bfloat16)


def matmul(left, right, exact=True, contract=0):
    if exact:
        (high, low), (other_high, other_low) = split(left), split(right)
        left = jnp.concatenate([high, high, low], axis=1)
        right = jnp.concatenate([other_high, other_low, other_high], axis=contract)
    else:
        left, right = left.astype(jnp.bfloat16), right.astype(jnp.bfloat16)
    return lax.dot_general(
        left, right, (((1,), (contract,)), ((), ())), preferred_element_type=jnp.float32
    )


def matmul_full(left, right):
    return jnp.dot(
        left, right, precision=lax.Precision.HIGHEST, preferred_element_type=jnp.float32
    )


def gram_kernel(total_cols, mine_ref, other_ref, packed_ref, sketch_ref):
    sketch = (mine_ref[...] + other_ref[...]) / total_cols
    sketch_ref[...] = sketch.T
    gram = matmul_full(sketch_ref[...], sketch)
    half = gram.shape[0] // 2
    row = lax.broadcasted_iota(jnp.int32, (half, 2 * half), 0)
    col = lax.broadcasted_iota(jnp.int32, (half, 2 * half), 1)
    top, bottom = gram[:half], pltpu.roll(gram[half:], half, 1)
    packed_ref[:half] = jnp.where(row > col, bottom, top)
    diagonal = jnp.sum(jnp.where(row == col, bottom, 0.0), axis=0, keepdims=True)
    packed_ref[half:] = jnp.broadcast_to(diagonal, (8, 2 * half))


def unpack_gram(packed):
    width = packed.shape[1]
    half = width // 2
    row = lax.broadcasted_iota(jnp.int32, (half, width), 0)
    col = lax.broadcasted_iota(jnp.int32, (half, width), 1)
    square = packed[:half]
    top = jnp.where(row > col, 0.0, square)
    lower = jnp.where(row > col, square, jnp.where(row == col, packed[half : half + 1], 0.0))
    parts = jnp.concatenate([top, pltpu.roll(lower, half, 1)], axis=0)
    row = lax.broadcasted_iota(jnp.int32, (width, width), 0)
    col = lax.broadcasted_iota(jnp.int32, (width, width), 1)
    return jnp.where(row == col, parts, parts + parts.T)


def make_gram(mine, other, total_cols):
    rows, width = mine.shape
    return pl.pallas_call(
        functools.partial(gram_kernel, total_cols),
        out_shape=[
            jax.ShapeDtypeStruct((width // 2 + 8, width), jnp.float32),
            jax.ShapeDtypeStruct((width, rows), jnp.float32),
        ],
        in_specs=[pl.BlockSpec(memory_space=pltpu.VMEM)] * 2,
        out_specs=[pl.BlockSpec(memory_space=pltpu.VMEM)] * 2,
        compiler_params=pltpu.CompilerParams(vmem_limit_bytes=16 * 2**20),
        name="make_gram",
    )(mine, other)


UPDATES = 4
LOOSE_UPDATES = 2
CLOSE = 1e-5


def basis_kernel(
    root_rows, gram_ref, sketch_ref, slab_ref,
    basis_ref, *refs,
):
    products, (work_ref, inverse_ref, buffer, arrived) = refs[:-4], refs[-4:]
    fetch = pltpu.make_async_copy(slab_ref, buffer, arrived)
    fetch.start()
    width = gram_ref.shape[1]
    row = lax.broadcasted_iota(jnp.int32, (width, width), 0)
    col = lax.broadcasted_iota(jnp.int32, (width, width), 1)
    on_diag = row == col
    unit = jnp.where(on_diag, 1.0, 0.0)
    half = jnp.where(row > col, 1.0, jnp.where(on_diag, 0.5, 0.0))

    gram = unpack_gram(gram_ref[...])
    diagonal = jnp.where(on_diag, gram, 0.0)
    down = lax.rsqrt(jnp.sum(diagonal, axis=1, keepdims=True))
    across = lax.rsqrt(jnp.sum(diagonal, axis=0, keepdims=True))
    scaled = gram * down * across

    error = scaled - unit
    step = error * half
    inverse = unit - step + matmul(step, step, False)
    for update in range(1, UPDATES):
        exact = update >= LOOSE_UPDATES
        error = matmul(matmul(inverse, scaled, exact), inverse, exact, 1) - unit
        step = error * half
        if update < UPDATES - 1:
            step = step - matmul(step, step, exact)
        inverse = inverse - matmul(step, inverse, exact)
    inverse_ref[...] = inverse * across
    far = jnp.sum(error * error)

    @pl.when(jnp.logical_not(far <= CLOSE))
    def _():
        work_ref[...] = gram
        inverse_ref[...] = unit

        def eliminate(k, carry):
            whole = work_ref[...]
            pivot_row = work_ref[pl.ds(k, 1), :]
            pivot = jnp.sum(
                jnp.where(col[:1] == k, pivot_row, 0.0), axis=1, keepdims=True
            )
            column = jnp.sum(jnp.where(col == k, whole, 0.0), axis=1, keepdims=True)
            factor = jnp.where(row[:, :1] > k, column / pivot, 0.0)
            work_ref[...] = whole - factor * pivot_row
            inverse_ref[...] = inverse_ref[...] - factor * inverse_ref[pl.ds(k, 1), :]
            return carry

        lax.fori_loop(0, width, eliminate, 0)
        pivots = jnp.sum(jnp.where(on_diag, work_ref[...], 0.0), axis=1, keepdims=True)
        inverse_ref[...] = inverse_ref[...] * lax.rsqrt(pivots)

    basis = matmul_full(inverse_ref[...], sketch_ref[...]) * root_rows
    pair = jnp.concatenate(split(basis), axis=0)
    fetch.wait()
    for start in range(0, buffer.shape[1], TILE):
        both = lax.dot_general(
            pair,
            buffer[:, start : start + TILE],
            (((1,), (0,)), ((), ())),
            preferred_element_type=jnp.float32,
        )
        out, inner = divmod(start, products[0].shape[1])
        products[out][:, inner : inner + TILE] = both[:width] + both[width:]
    basis_ref[...] = basis.T


def make_basis(gram, sketch, slab, root_rows, chunks):
    width, rows = sketch.shape
    cols = slab.shape[1]
    return pl.pallas_call(
        functools.partial(basis_kernel, root_rows),
        out_shape=[jax.ShapeDtypeStruct((rows, width), jnp.float32)]
        + [jax.ShapeDtypeStruct((width, cols // chunks), jnp.float32)] * chunks,
        in_specs=[pl.BlockSpec(memory_space=pltpu.VMEM)] * 2
        + [pl.BlockSpec(memory_space=pl.ANY)],
        out_specs=[pl.BlockSpec(memory_space=pltpu.VMEM)] * (1 + chunks),
        scratch_shapes=[
            pltpu.VMEM((width, width), jnp.float32),
            pltpu.VMEM((width, width), jnp.float32),
            pltpu.VMEM(slab.shape, jnp.bfloat16),
            pltpu.SemaphoreType.DMA,
        ],
        compiler_params=pltpu.CompilerParams(vmem_limit_bytes=KERNEL_VMEM),
        name="make_basis",
    )(gram, sketch, slab)


def per_device(activations, start_sketch):
    rows_here, cols_here = activations.shape
    width = start_sketch.shape[1]
    parts = lax.axis_size("row")
    total_rows = rows_here * parts
    total_cols = cols_here * lax.axis_size("col")
    root_rows = math.sqrt(total_rows)

    local_cols = []
    for begin in (0, cols_here // 2):
        local_cols += first_product(
            start_sketch, activations, begin, cols_here // 2, CHUNKS // 2
        )
    partial_sketch = 0.0
    orders = orders_of("row")
    step = cols_here // CHUNKS
    for c in range(CHUNKS):
        span = slice(c * step, (c + 1) * step)
        shared = sum_and_share(local_cols[c], "row", orders[c % 2], 1.0 / root_rows)
        partial_sketch = partial_sketch + lax.dot_general(
            activations[:, span],
            shared,
            (((1,), (1,)), ((), ())),
            preferred_element_type=jnp.float32,
        )
    other_sketch = swap(partial_sketch, "col", 1)
    packed, sketch = make_gram(partial_sketch, other_sketch, total_cols)
    basis, *products = make_basis(row_sum(packed), sketch, activations, root_rows, CHUNKS)
    pieces = [
        scatter_sum(product, "row", orders[c % 2]) / total_rows
        for c, product in enumerate(products)
    ]
    return (basis, jnp.concatenate(pieces, axis=1))


def solution(mesh):
    return jax.shard_map(
        per_device,
        mesh=mesh,
        in_specs=(P(("grp", "row"), "col"), P(("grp", "row"), None)),
        out_specs=(P(("grp", "row"), None), P(("grp", "row"), "col")),
        check_vma=False,
    )
```

```python
import functools
import math

import jax
import jax.numpy as jnp
from jax import lax
from jax.experimental import pallas as pl
from jax.experimental.pallas import tpu as pltpu
from jax.sharding import PartitionSpec as P

CHUNKS = 4
TILE = 1024
KERNEL_VMEM = 50 * 2**20


def swap(value, axis, distance):
    size = lax.axis_size(axis)
    return lax.ppermute(value, axis, [(i, i ^ distance) for i in range(size)])


def row_sum(value):
    rows, cores = lax.axis_size("row"), lax.axis_size("col")
    assert cores == 2
    first = lax.axis_index("col") == 0
    stride = 1
    while stride < rows:
        radix = min(8, rows // stride)
        split = min(2, radix // 2)
        terms = []
        for near in [digit for digit in range(radix) if not digit & split]:
            pairs = []
            for row in range(rows):
                for core, digit in ((0, near), (1, near | split)):
                    if digit:
                        pairs.append((row * cores + core, (row ^ digit * stride) * cores + core))
            terms.append(lax.ppermute(value, ("row", "col"), pairs))
        terms[0] = jnp.where(first, value, terms[0])
        while len(terms) > 1:
            terms = [terms[i] + terms[i + 1] for i in range(0, len(terms), 2)]
        value = terms[0] + swap(terms[0], "col", 1)
        stride *= radix
    return value


def scatter_sum(value, axis, order):
    rows, cols = value.shape[0] >> len(order), value.shape[1]
    total = value.reshape([2] * len(order) + [rows, cols])
    left = sorted(order, reverse=True)
    for bit in order:
        dim = left.index(bit)
        left.remove(bit)
        low = lax.index_in_dim(total, 0, dim, keepdims=False)
        high = lax.index_in_dim(total, 1, dim, keepdims=False)
        upper = bit_of(axis, bit) == 1
        send = jnp.where(upper, low, high).astype(jnp.bfloat16)
        landed = swap(send, axis, 1 << bit)
        total = jnp.where(upper, high, low) + landed.astype(jnp.float32)
    return total


def bit_of(axis, bit):
    return lax.rem(lax.div(lax.axis_index(axis), 1 << bit), 2)


def sum_and_share(value, axis, order, scale):
    for bit in order[:-1]:
        upper = bit_of(axis, bit) == 1
        half = value.shape[1] // 2
        low, high = value[:, :half], value[:, half:]
        send = jnp.where(upper, low, high).astype(jnp.bfloat16)
        landed = swap(send, axis, 1 << bit)
        value = jnp.where(upper, high, low) + landed.astype(jnp.float32)
    landed = swap(value.astype(jnp.bfloat16), axis, 1 << order[-1])
    block = ((value + landed.astype(jnp.float32)) * scale).astype(jnp.bfloat16)
    for bit in reversed(order[:-1]):
        upper = bit_of(axis, bit) == 1
        other = swap(block, axis, 1 << bit)
        block = jnp.concatenate(
            [jnp.where(upper, other, block), jnp.where(upper, block, other)], axis=1
        )
    return block


def orders_of(axis):
    bits = list(range((lax.axis_size(axis) - 1).bit_length()))
    if len(bits) < 3:
        return [bits, bits]
    return [bits, [bits[1], bits[0]] + bits[2:]]


def fetch_tiles(slab_ref, begin, buffer, arrived):
    copies = []
    for tile in range(buffer.shape[0]):
        span = pl.ds(begin + tile * TILE, TILE)
        copies.append(
            pltpu.make_async_copy(slab_ref.at[:, span], buffer.at[tile], arrived.at[tile])
        )
    for copy in copies:
        copy.start()
    return copies


def sketch_kernel(begin, start_ref, slab_ref, *refs):
    outs, (buffer, arrived) = refs[:-2], refs[-2:]
    copies = fetch_tiles(slab_ref, begin, buffer, arrived)
    left = start_ref[...].T
    for tile, copy in enumerate(copies):
        copy.wait()
        out, inner = divmod(tile * TILE, outs[0].shape[1])
        outs[out][:, inner : inner + TILE] = lax.dot_general(
            left, buffer[tile], (((1,), (0,)), ((), ())), preferred_element_type=jnp.float32
        )


def first_product(start, slab, begin, cols, chunks):
    rows, width = start.shape
    return pl.pallas_call(
        functools.partial(sketch_kernel, begin),
        out_shape=[jax.ShapeDtypeStruct((width, cols // chunks), jnp.float32)] * chunks,
        in_specs=[
            pl.BlockSpec(memory_space=pltpu.VMEM),
            pl.BlockSpec(memory_space=pl.ANY),
        ],
        out_specs=[pl.BlockSpec(memory_space=pltpu.VMEM)] * chunks,
        scratch_shapes=[
            pltpu.VMEM((cols // TILE, rows, TILE), jnp.bfloat16),
            pltpu.SemaphoreType.DMA((cols // TILE,)),
        ],
        compiler_params=pltpu.CompilerParams(vmem_limit_bytes=KERNEL_VMEM),
        cost_estimate=pl.CostEstimate(
            flops=2 * rows * width * cols, bytes_accessed=2 * rows * cols, transcendentals=0
        ),
        name="first_product",
    )(start, slab)


def split(value):
    high = value.astype(jnp.bfloat16)
    return high, (value - high.astype(jnp.float32)).astype(jnp.bfloat16)


def matmul(left, right, exact=True, contract=0):
    if exact:
        (high, low), (other_high, other_low) = split(left), split(right)
        left = jnp.concatenate([high, high, low], axis=1)
        right = jnp.concatenate([other_high, other_low, other_high], axis=contract)
    else:
        left, right = left.astype(jnp.bfloat16), right.astype(jnp.bfloat16)
    return lax.dot_general(
        left, right, (((1,), (contract,)), ((), ())), preferred_element_type=jnp.float32
    )


def matmul_full(left, right):
    return jnp.dot(
        left, right, precision=lax.Precision.HIGHEST, preferred_element_type=jnp.float32
    )


def gram_kernel(total_cols, mine_ref, other_ref, packed_ref, sketch_ref):
    sketch = (mine_ref[...] + other_ref[...]) / total_cols
    sketch_ref[...] = sketch.T
    gram = matmul_full(sketch_ref[...], sketch)
    half = gram.shape[0] // 2
    row = lax.broadcasted_iota(jnp.int32, (half, 2 * half), 0)
    col = lax.broadcasted_iota(jnp.int32, (half, 2 * half), 1)
    top, bottom = gram[:half], pltpu.roll(gram[half:], half, 1)
    packed_ref[:half] = jnp.where(row > col, bottom, top)
    diagonal = jnp.sum(jnp.where(row == col, bottom, 0.0), axis=0, keepdims=True)
    packed_ref[half:] = jnp.broadcast_to(diagonal, (8, 2 * half))


def unpack_gram(packed):
    width = packed.shape[1]
    half = width // 2
    row = lax.broadcasted_iota(jnp.int32, (half, width), 0)
    col = lax.broadcasted_iota(jnp.int32, (half, width), 1)
    square = packed[:half]
    top = jnp.where(row > col, 0.0, square)
    lower = jnp.where(row > col, square, jnp.where(row == col, packed[half : half + 1], 0.0))
    parts = jnp.concatenate([top, pltpu.roll(lower, half, 1)], axis=0)
    row = lax.broadcasted_iota(jnp.int32, (width, width), 0)
    col = lax.broadcasted_iota(jnp.int32, (width, width), 1)
    return jnp.where(row == col, parts, parts + parts.T)


def make_gram(mine, other, total_cols):
    rows, width = mine.shape
    return pl.pallas_call(
        functools.partial(gram_kernel, total_cols),
        out_shape=[
            jax.ShapeDtypeStruct((width // 2 + 8, width), jnp.float32),
            jax.ShapeDtypeStruct((width, rows), jnp.float32),
        ],
        in_specs=[pl.BlockSpec(memory_space=pltpu.VMEM)] * 2,
        out_specs=[pl.BlockSpec(memory_space=pltpu.VMEM)] * 2,
        compiler_params=pltpu.CompilerParams(vmem_limit_bytes=16 * 2**20),
        name="make_gram",
    )(mine, other)


UPDATES = 4
LOOSE_UPDATES = 2
CLOSE = 1e-5


def basis_kernel(
    root_rows, gram_ref, sketch_ref, slab_ref,
    basis_ref, *refs,
):
    products, (work_ref, inverse_ref, buffer, arrived) = refs[:-4], refs[-4:]
    fetch = pltpu.make_async_copy(slab_ref, buffer, arrived)
    fetch.start()
    width = gram_ref.shape[1]
    row = lax.broadcasted_iota(jnp.int32, (width, width), 0)
    col = lax.broadcasted_iota(jnp.int32, (width, width), 1)
    on_diag = row == col
    unit = jnp.where(on_diag, 1.0, 0.0)
    half = jnp.where(row > col, 1.0, jnp.where(on_diag, 0.5, 0.0))

    gram = unpack_gram(gram_ref[...])
    diagonal = jnp.where(on_diag, gram, 0.0)
    down = lax.rsqrt(jnp.sum(diagonal, axis=1, keepdims=True))
    across = lax.rsqrt(jnp.sum(diagonal, axis=0, keepdims=True))
    scaled = gram * down * across

    error = scaled - unit
    step = error * half
    inverse = unit - step + matmul(step, step, False)
    for update in range(1, UPDATES):
        exact = update >= LOOSE_UPDATES
        error = matmul(matmul(inverse, scaled, exact), inverse, exact, 1) - unit
        step = error * half
        if update < UPDATES - 1:
            step = step - matmul(step, step, exact)
        inverse = inverse - matmul(step, inverse, exact)
    inverse_ref[...] = inverse * across
    far = jnp.sum(error * error)

    @pl.when(jnp.logical_not(far <= CLOSE))
    def _():
        work_ref[...] = gram
        inverse_ref[...] = unit

        def eliminate(k, carry):
            whole = work_ref[...]
            pivot_row = work_ref[pl.ds(k, 1), :]
            pivot = jnp.sum(
                jnp.where(col[:1] == k, pivot_row, 0.0), axis=1, keepdims=True
            )
            column = jnp.sum(jnp.where(col == k, whole, 0.0), axis=1, keepdims=True)
            factor = jnp.where(row[:, :1] > k, column / pivot, 0.0)
            work_ref[...] = whole - factor * pivot_row
            inverse_ref[...] = inverse_ref[...] - factor * inverse_ref[pl.ds(k, 1), :]
            return carry

        lax.fori_loop(0, width, eliminate, 0)
        pivots = jnp.sum(jnp.where(on_diag, work_ref[...], 0.0), axis=1, keepdims=True)
        inverse_ref[...] = inverse_ref[...] * lax.rsqrt(pivots)

    basis = matmul_full(inverse_ref[...], sketch_ref[...]) * root_rows
    pair = jnp.concatenate(split(basis), axis=0)
    fetch.wait()
    for start in range(0, buffer.shape[1], TILE):
        both = lax.dot_general(
            pair,
            buffer[:, start : start + TILE],
            (((1,), (0,)), ((), ())),
            preferred_element_type=jnp.float32,
        )
        out, inner = divmod(start, products[0].shape[1])
        products[out][:, inner : inner + TILE] = both[:width] + both[width:]
    basis_ref[...] = basis.T


def make_basis(gram, sketch, slab, root_rows, chunks):
    width, rows = sketch.shape
    cols = slab.shape[1]
    return pl.pallas_call(
        functools.partial(basis_kernel, root_rows),
        out_shape=[jax.ShapeDtypeStruct((rows, width), jnp.float32)]
        + [jax.ShapeDtypeStruct((width, cols // chunks), jnp.float32)] * chunks,
        in_specs=[pl.BlockSpec(memory_space=pltpu.VMEM)] * 2
        + [pl.BlockSpec(memory_space=pl.ANY)],
        out_specs=[pl.BlockSpec(memory_space=pltpu.VMEM)] * (1 + chunks),
        scratch_shapes=[
            pltpu.VMEM((width, width), jnp.float32),
            pltpu.VMEM((width, width), jnp.float32),
            pltpu.VMEM(slab.shape, jnp.bfloat16),
            pltpu.SemaphoreType.DMA,
        ],
        compiler_params=pltpu.CompilerParams(vmem_limit_bytes=KERNEL_VMEM),
        name="make_basis",
    )(gram, sketch, slab)


def per_device(activations, start_sketch):
    rows_here, cols_here = activations.shape
    width = start_sketch.shape[1]
    parts = lax.axis_size("row")
    total_rows = rows_here * parts
    total_cols = cols_here * lax.axis_size("col")
    root_rows = math.sqrt(total_rows)

    local_cols = []
    for begin in (0, cols_here // 2):
        local_cols += first_product(
            start_sketch, activations, begin, cols_here // 2, CHUNKS // 2
        )
    partial_sketch = 0.0
    orders = orders_of("row")
    step = cols_here // CHUNKS
    for c in range(CHUNKS):
        span = slice(c * step, (c + 1) * step)
        shared = sum_and_share(local_cols[c], "row", orders[c % 2], 1.0 / root_rows)
        partial_sketch = partial_sketch + lax.dot_general(
            activations[:, span],
            shared,
            (((1,), (1,)), ((), ())),
            preferred_element_type=jnp.float32,
        )
    other_sketch = swap(partial_sketch, "col", 1)
    packed, sketch = make_gram(partial_sketch, other_sketch, total_cols)
    basis, *products = make_basis(row_sum(packed), sketch, activations, root_rows, CHUNKS)
    pieces = [
        scatter_sum(product, "row", orders[c % 2]) / total_rows
        for c, product in enumerate(products)
    ]
    return (basis, jnp.concatenate(pieces, axis=1))


def solution(mesh):
    return jax.shard_map(
        per_device,
        mesh=mesh,
        in_specs=(P(("grp", "row"), "col"), P(("grp", "row"), None)),
        out_specs=(P(("grp", "row"), None), P(("grp", "row"), "col")),
        check_vma=False,
    )
```

```python
import functools
import math

import jax
import jax.numpy as jnp
from jax import lax
from jax.experimental import pallas as pl
from jax.experimental.pallas import tpu as pltpu
from jax.sharding import PartitionSpec as P

CHUNKS = 4
TILE = 1024
KERNEL_VMEM = 50 * 2**20


def swap(value, axis, distance):
    size = lax.axis_size(axis)
    return lax.ppermute(value, axis, [(i, i ^ distance) for i in range(size)])


def row_sum(value):
    rows, cores = lax.axis_size("row"), lax.axis_size("col")
    assert cores == 2
    first = lax.axis_index("col") == 0
    stride = 1
    while stride < rows:
        radix = min(8, rows // stride)
        split = min(2, radix // 2)
        terms = []
        for near in [digit for digit in range(radix) if not digit & split]:
            pairs = []
            for row in range(rows):
                for core, digit in ((0, near), (1, near | split)):
                    if digit:
                        pairs.append((row * cores + core, (row ^ digit * stride) * cores + core))
            terms.append(lax.ppermute(value, ("row", "col"), pairs))
        terms[0] = jnp.where(first, value, terms[0])
        while len(terms) > 1:
            terms = [terms[i] + terms[i + 1] for i in range(0, len(terms), 2)]
        value = terms[0] + swap(terms[0], "col", 1)
        stride *= radix
    return value


def scatter_sum(value, axis, order):
    rows, cols = value.shape[0] >> len(order), value.shape[1]
    total = value.reshape([2] * len(order) + [rows, cols])
    left = sorted(order, reverse=True)
    for bit in order:
        dim = left.index(bit)
        left.remove(bit)
        low = lax.index_in_dim(total, 0, dim, keepdims=False)
        high = lax.index_in_dim(total, 1, dim, keepdims=False)
        upper = bit_of(axis, bit) == 1
        send = jnp.where(upper, low, high).astype(jnp.bfloat16)
        landed = swap(send, axis, 1 << bit)
        total = jnp.where(upper, high, low) + landed.astype(jnp.float32)
    return total


def bit_of(axis, bit):
    return lax.rem(lax.div(lax.axis_index(axis), 1 << bit), 2)


def sum_and_share(value, axis, order, scale):
    for bit in order[:-1]:
        upper = bit_of(axis, bit) == 1
        half = value.shape[1] // 2
        low, high = value[:, :half], value[:, half:]
        send = jnp.where(upper, low, high).astype(jnp.bfloat16)
        landed = swap(send, axis, 1 << bit)
        value = jnp.where(upper, high, low) + landed.astype(jnp.float32)
    landed = swap(value.astype(jnp.bfloat16), axis, 1 << order[-1])
    block = ((value + landed.astype(jnp.float32)) * scale).astype(jnp.bfloat16)
    for bit in reversed(order[:-1]):
        upper = bit_of(axis, bit) == 1
        other = swap(block, axis, 1 << bit)
        block = jnp.concatenate(
            [jnp.where(upper, other, block), jnp.where(upper, block, other)], axis=1
        )
    return block


def orders_of(axis):
    bits = list(range((lax.axis_size(axis) - 1).bit_length()))
    if len(bits) < 3:
        return [bits, bits]
    return [bits, [bits[1], bits[0]] + bits[2:]]


def fetch_tiles(slab_ref, begin, buffer, arrived):
    copies = []
    for tile in range(buffer.shape[0]):
        span = pl.ds(begin + tile * TILE, TILE)
        copies.append(
            pltpu.make_async_copy(slab_ref.at[:, span], buffer.at[tile], arrived.at[tile])
        )
    for copy in copies:
        copy.start()
    return copies


def sketch_kernel(begin, start_ref, slab_ref, *refs):
    outs, (buffer, arrived) = refs[:-2], refs[-2:]
    copies = fetch_tiles(slab_ref, begin, buffer, arrived)
    left = start_ref[...].T
    for tile, copy in enumerate(copies):
        copy.wait()
        out, inner = divmod(tile * TILE, outs[0].shape[1])
        outs[out][:, inner : inner + TILE] = lax.dot_general(
            left, buffer[tile], (((1,), (0,)), ((), ())), preferred_element_type=jnp.float32
        )


def first_product(start, slab, begin, cols, chunks):
    rows, width = start.shape
    return pl.pallas_call(
        functools.partial(sketch_kernel, begin),
        out_shape=[jax.ShapeDtypeStruct((width, cols // chunks), jnp.float32)] * chunks,
        in_specs=[
            pl.BlockSpec(memory_space=pltpu.VMEM),
            pl.BlockSpec(memory_space=pl.ANY),
        ],
        out_specs=[pl.BlockSpec(memory_space=pltpu.VMEM)] * chunks,
        scratch_shapes=[
            pltpu.VMEM((cols // TILE, rows, TILE), jnp.bfloat16),
            pltpu.SemaphoreType.DMA((cols // TILE,)),
        ],
        compiler_params=pltpu.CompilerParams(vmem_limit_bytes=KERNEL_VMEM),
        cost_estimate=pl.CostEstimate(
            flops=2 * rows * width * cols, bytes_accessed=2 * rows * cols, transcendentals=0
        ),
        name="first_product",
    )(start, slab)


def split(value):
    high = value.astype(jnp.bfloat16)
    return high, (value - high.astype(jnp.float32)).astype(jnp.bfloat16)


def matmul(left, right, exact=True, contract=0):
    if exact:
        (high, low), (other_high, other_low) = split(left), split(right)
        left = jnp.concatenate([high, high, low], axis=1)
        right = jnp.concatenate([other_high, other_low, other_high], axis=contract)
    else:
        left, right = left.astype(jnp.bfloat16), right.astype(jnp.bfloat16)
    return lax.dot_general(
        left, right, (((1,), (contract,)), ((), ())), preferred_element_type=jnp.float32
    )


def matmul_full(left, right):
    return jnp.dot(
        left, right, precision=lax.Precision.HIGHEST, preferred_element_type=jnp.float32
    )


def gram_kernel(total_cols, mine_ref, other_ref, packed_ref, sketch_ref):
    sketch = (mine_ref[...] + other_ref[...]) / total_cols
    sketch_ref[...] = sketch.T
    gram = matmul_full(sketch_ref[...], sketch)
    half = gram.shape[0] // 2
    row = lax.broadcasted_iota(jnp.int32, (half, 2 * half), 0)
    col = lax.broadcasted_iota(jnp.int32, (half, 2 * half), 1)
    top, bottom = gram[:half], pltpu.roll(gram[half:], half, 1)
    packed_ref[:half] = jnp.where(row > col, bottom, top)
    diagonal = jnp.sum(jnp.where(row == col, bottom, 0.0), axis=0, keepdims=True)
    packed_ref[half:] = jnp.broadcast_to(diagonal, (8, 2 * half))


def unpack_gram(packed):
    width = packed.shape[1]
    half = width // 2
    row = lax.broadcasted_iota(jnp.int32, (half, width), 0)
    col = lax.broadcasted_iota(jnp.int32, (half, width), 1)
    square = packed[:half]
    top = jnp.where(row > col, 0.0, square)
    lower = jnp.where(row > col, square, jnp.where(row == col, packed[half : half + 1], 0.0))
    parts = jnp.concatenate([top, pltpu.roll(lower, half, 1)], axis=0)
    row = lax.broadcasted_iota(jnp.int32, (width, width), 0)
    col = lax.broadcasted_iota(jnp.int32, (width, width), 1)
    return jnp.where(row == col, parts, parts + parts.T)


def make_gram(mine, other, total_cols):
    rows, width = mine.shape
    return pl.pallas_call(
        functools.partial(gram_kernel, total_cols),
        out_shape=[
            jax.ShapeDtypeStruct((width // 2 + 8, width), jnp.float32),
            jax.ShapeDtypeStruct((width, rows), jnp.float32),
        ],
        in_specs=[pl.BlockSpec(memory_space=pltpu.VMEM)] * 2,
        out_specs=[pl.BlockSpec(memory_space=pltpu.VMEM)] * 2,
        compiler_params=pltpu.CompilerParams(vmem_limit_bytes=16 * 2**20),
        name="make_gram",
    )(mine, other)


UPDATES = 4
LOOSE_UPDATES = 2
CLOSE = 1e-5


def basis_kernel(
    root_rows, gram_ref, sketch_ref, slab_ref,
    basis_ref, *refs,
):
    products, (work_ref, inverse_ref, buffer, arrived) = refs[:-4], refs[-4:]
    fetch = pltpu.make_async_copy(slab_ref, buffer, arrived)
    fetch.start()
    width = gram_ref.shape[1]
    row = lax.broadcasted_iota(jnp.int32, (width, width), 0)
    col = lax.broadcasted_iota(jnp.int32, (width, width), 1)
    on_diag = row == col
    unit = jnp.where(on_diag, 1.0, 0.0)
    half = jnp.where(row > col, 1.0, jnp.where(on_diag, 0.5, 0.0))

    gram = unpack_gram(gram_ref[...])
    diagonal = jnp.where(on_diag, gram, 0.0)
    down = lax.rsqrt(jnp.sum(diagonal, axis=1, keepdims=True))
    across = lax.rsqrt(jnp.sum(diagonal, axis=0, keepdims=True))
    scaled = gram * down * across

    error = scaled - unit
    step = error * half
    inverse = unit - step + matmul(step, step, False)
    for update in range(1, UPDATES):
        exact = update >= LOOSE_UPDATES
        error = matmul(matmul(inverse, scaled, exact), inverse, exact, 1) - unit
        step = error * half
        if update < UPDATES - 1:
            step = step - matmul(step, step, exact)
        inverse = inverse - matmul(step, inverse, exact)
    inverse_ref[...] = inverse * across
    far = jnp.sum(error * error)

    @pl.when(jnp.logical_not(far <= CLOSE))
    def _():
        work_ref[...] = gram
        inverse_ref[...] = unit

        def eliminate(k, carry):
            whole = work_ref[...]
            pivot_row = work_ref[pl.ds(k, 1), :]
            pivot = jnp.sum(
                jnp.where(col[:1] == k, pivot_row, 0.0), axis=1, keepdims=True
            )
            column = jnp.sum(jnp.where(col == k, whole, 0.0), axis=1, keepdims=True)
            factor = jnp.where(row[:, :1] > k, column / pivot, 0.0)
            work_ref[...] = whole - factor * pivot_row
            inverse_ref[...] = inverse_ref[...] - factor * inverse_ref[pl.ds(k, 1), :]
            return carry

        lax.fori_loop(0, width, eliminate, 0)
        pivots = jnp.sum(jnp.where(on_diag, work_ref[...], 0.0), axis=1, keepdims=True)
        inverse_ref[...] = inverse_ref[...] * lax.rsqrt(pivots)

    basis = matmul_full(inverse_ref[...], sketch_ref[...]) * root_rows
    pair = jnp.concatenate(split(basis), axis=0)
    fetch.wait()
    for start in range(0, buffer.shape[1], TILE):
        both = lax.dot_general(
            pair,
            buffer[:, start : start + TILE],
            (((1,), (0,)), ((), ())),
            preferred_element_type=jnp.float32,
        )
        out, inner = divmod(start, products[0].shape[1])
        products[out][:, inner : inner + TILE] = both[:width] + both[width:]
    basis_ref[...] = basis.T


def make_basis(gram, sketch, slab, root_rows, chunks):
    width, rows = sketch.shape
    cols = slab.shape[1]
    return pl.pallas_call(
        functools.partial(basis_kernel, root_rows),
        out_shape=[jax.ShapeDtypeStruct((rows, width), jnp.float32)]
        + [jax.ShapeDtypeStruct((width, cols // chunks), jnp.float32)] * chunks,
        in_specs=[pl.BlockSpec(memory_space=pltpu.VMEM)] * 2
        + [pl.BlockSpec(memory_space=pl.ANY)],
        out_specs=[pl.BlockSpec(memory_space=pltpu.VMEM)] * (1 + chunks),
        scratch_shapes=[
            pltpu.VMEM((width, width), jnp.float32),
            pltpu.VMEM((width, width), jnp.float32),
            pltpu.VMEM(slab.shape, jnp.bfloat16),
            pltpu.SemaphoreType.DMA,
        ],
        compiler_params=pltpu.CompilerParams(vmem_limit_bytes=KERNEL_VMEM),
        name="make_basis",
    )(gram, sketch, slab)


def per_device(activations, start_sketch):
    rows_here, cols_here = activations.shape
    width = start_sketch.shape[1]
    parts = lax.axis_size("row")
    total_rows = rows_here * parts
    total_cols = cols_here * lax.axis_size("col")
    root_rows = math.sqrt(total_rows)

    local_cols = []
    for begin in (0, cols_here // 2):
        local_cols += first_product(
            start_sketch, activations, begin, cols_here // 2, CHUNKS // 2
        )
    partial_sketch = 0.0
    orders = orders_of("row")
    step = cols_here // CHUNKS
    for c in range(CHUNKS):
        span = slice(c * step, (c + 1) * step)
        shared = sum_and_share(local_cols[c], "row", orders[1 - c % 2], 1.0 / root_rows)
        partial_sketch = partial_sketch + lax.dot_general(
            activations[:, span],
            shared,
            (((1,), (1,)), ((), ())),
            preferred_element_type=jnp.float32,
        )
    other_sketch = swap(partial_sketch, "col", 1)
    packed, sketch = make_gram(partial_sketch, other_sketch, total_cols)
    basis, *products = make_basis(row_sum(packed), sketch, activations, root_rows, CHUNKS)
    pieces = [
        scatter_sum(product, "row", orders[c % 2]) / total_rows
        for c, product in enumerate(products)
    ]
    return (basis, jnp.concatenate(pieces, axis=1))


def solution(mesh):
    return jax.shard_map(
        per_device,
        mesh=mesh,
        in_specs=(P(("grp", "row"), "col"), P(("grp", "row"), None)),
        out_specs=(P(("grp", "row"), None), P(("grp", "row"), "col")),
        check_vma=False,
    )
```
